32 devices in a mesh: ctx: 4 (over y, x), tp: 2 (over core), fsdp: 4 (over z).
Axes of the slice: x: 2, y: 2, z: 4, core: 2. Of those that a mesh axis runs over, the one named last changes fastest.
Arguments:
- block_input: bfloat16 [8, 2048, 2048], P('fsdp', 'ctx'), may hold values from -6 to 6
- doc_start: int32 [8, 2048], P('fsdp', 'ctx'), may hold values from 0 to 2047, as said below
- gain_mix: float32 [2048], replicated, may hold values from 0.5 to 1.5
- query_weight: float32 [2048, 2048], P(('ctx', 'fsdp'), 'tp'), may hold values from -0.125 to 0.125
- key_weight: float32 [2048, 2048], P(('ctx', 'fsdp'), 'tp'), may hold values from -0.125 to 0.125
- value_weight: float32 [2048, 2048], P(('ctx', 'fsdp'), 'tp'), may hold values from -0.125 to 0.125
- beta_weight: float32 [2048, 16], P(('ctx', 'fsdp'), 'tp'), may hold values from -0.125 to 0.125
- beta_bias: float32 [16], P('tp'), may hold values from -5 to 0
- conv_weight: float32 [3, 4, 2048], P(None, None, 'tp'), may hold values from -3 to 3
- gain_o: float32 [128], replicated, may hold values from 0.5 to 1.5
- out_weight: float32 [2048, 2048], P('tp', ('ctx', 'fsdp')), may hold values from -0.25 to 0.25
- gain_ffn: float32 [2048], replicated, may hold values from 0.5 to 1.5
- gate_weight: float32 [2048, 5632], P(('ctx', 'fsdp'), 'tp'), may hold values from -0.125 to 0.125
- up_weight: float32 [2048, 5632], P(('ctx', 'fsdp'), 'tp'), may hold values from -0.125 to 0.125
- down_weight: float32 [5632, 2048], P('tp', ('ctx', 'fsdp')), may hold values from -0.15625 to 0.15625
- out_grad: bfloat16 [8, 2048, 2048], P('fsdp', 'ctx'), may hold values from -6 to 6
Outputs:
- block_output: bfloat16 [8, 2048, 2048], P('fsdp', 'ctx')
- input_grad: bfloat16 [8, 2048, 2048], P('fsdp', 'ctx')
- gain_mix_grad: float32 [2048], replicated
- query_weight_grad: float32 [2048, 2048], P(('ctx', 'fsdp'), 'tp')
- key_weight_grad: float32 [2048, 2048], P(('ctx', 'fsdp'), 'tp')
- value_weight_grad: float32 [2048, 2048], P(('ctx', 'fsdp'), 'tp')
- beta_weight_grad: float32 [2048, 16], P(('ctx', 'fsdp'), 'tp')
- beta_bias_grad: float32 [16], P('tp')
- conv_weight_grad: float32 [3, 4, 2048], P(None, None, 'tp')
- gain_o_grad: float32 [128], replicated
- out_weight_grad: float32 [2048, 2048], P('tp', ('ctx', 'fsdp'))
- gain_ffn_grad: float32 [2048], replicated
- gate_weight_grad: float32 [2048, 5632], P(('ctx', 'fsdp'), 'tp')
- up_weight_grad: float32 [2048, 5632], P(('ctx', 'fsdp'), 'tp')
- down_weight_grad: float32 [5632, 2048], P('tp', ('ctx', 'fsdp'))
The draws below stay inside these ranges and needn't reach their ends.
Inputs may be any that keep to these rules, and one draw needn't show every extreme that they name: doc_start[s, t] is the position in sequence s of the first token of the document that holds token t; documents are contiguous runs and doc_start[s, 0] = 0.
All inputs are finite; a program needn't handle non-finite values.
Results may differ from the reference program's by a relative error of at most 0.024.
Values may be sent and summed in bfloat16 or wider, within the bound.
No kernel may reach another device: no remote copies, remote signals or barrier semaphores. Data moves between devices by JAX's collectives and lax.ppermute only.
A program may use at most 512 MiB of HBM per device.

```python
import jax
import jax.numpy as jnp
from jax import lax

D = 2048
FF = 5632
HEADS = 16
HEAD = 128
CONV = 4
GROUP = 64
SEQ_ALL = 8
LENGTH = 2048


def draw_doc_start(key, part):
    rate_key, start_key = jax.random.split(jax.random.fold_in(key, 7))
    offset = jax.random.randint(rate_key, (), 0, 4)
    kinds = (jnp.arange(SEQ_ALL, dtype=jnp.int32) + offset) % 4
    denominators = jnp.array([8, 64, 512, 4096], dtype=jnp.int32)[kinds]
    rolls = jax.random.randint(start_key, (SEQ_ALL, LENGTH), 0, 1 << 20)
    fresh = (rolls % denominators[:, None] == 0) & (kinds[:, None] != 3)
    positions = jnp.arange(LENGTH, dtype=jnp.int32)[None, :]
    fresh = fresh | (positions == 0)
    fresh = fresh.at[0, LENGTH - 1].set(True)
    return lax.cummax(jnp.where(fresh, positions, 0), axis=1).astype(jnp.int32)


def block_scale(stream_key, extent, cuts, smallest, largest):
    def one(axis_at, parts):
        heights = jax.random.uniform(jax.random.fold_in(jax.random.fold_in(stream_key, 6), axis_at), (parts,), jnp.float32, smallest / len(cuts), largest / len(cuts))
        return jnp.repeat(jnp.exp(heights), extent[axis_at] // parts).reshape((-1,) + (1,) * (len(extent) - axis_at - 1))

    factor_of = one(*cuts[0])
    for cut in cuts[1:]:
        factor_of = factor_of * one(*cut)
    return factor_of


def gaussian(rng, extent, deviation, bound, pieces=(), kind=jnp.bfloat16):
    values = jax.random.normal(rng, extent, jnp.float32) * deviation
    if len(pieces) > 0:
        values = block_scale(rng, extent, pieces, -0.22, 0.18) * values
    return jnp.clip(values, min=-bound, max=bound).astype(kind)


def setup_inputs(seed: int = 0) -> dict:
    key_of = jax.random.split(jax.random.key(seed), 17)
    block_input = gaussian(key_of[0], (SEQ_ALL, LENGTH, D), 1.0, 6.0, ((0, 4), (1, 4)))
    doc_start = draw_doc_start(jax.random.fold_in(key_of[16], 71), 0)
    gain_mix = jnp.clip(1.0 + 0.1 * jax.random.normal(key_of[2], (D,), jnp.float32), 0.5, 1.5)
    query_weight = gaussian(key_of[3], (D, HEADS * HEAD), D ** -0.5, 0.125, ((0, 16), (1, 2)), jnp.float32)
    key_weight = gaussian(key_of[4], (D, HEADS * HEAD), D ** -0.5, 0.125, ((0, 16), (1, 2)), jnp.float32)
    value_weight = gaussian(key_of[5], (D, HEADS * HEAD), D ** -0.5, 0.125, ((0, 16), (1, 2)), jnp.float32)
    beta_weight = gaussian(key_of[6], (D, HEADS), D ** -0.5, 0.125, ((0, 16), (1, 2)), jnp.float32)
    beta_bias = jnp.clip(-5.0 + 5.0 * jax.random.uniform(key_of[7], (HEADS,), jnp.float32) ** block_scale(key_of[7], (HEADS,), ((0, 2),), -0.2, 0.2), -5.0, 0.0)
    conv_weight = gaussian(key_of[8], (3, CONV, HEADS * HEAD), 0.5, 3.0, ((2, 2),), jnp.float32)
    gain_o = jnp.clip(jax.random.uniform(key_of[9], (HEAD,), jnp.float32, 0.5, 1.5), 0.5, 1.5)
    out_weight = gaussian(key_of[10], (HEADS * HEAD, D), (HEADS * HEAD // 4) ** -0.5, 0.25, ((0, 2), (1, 16)), jnp.float32)
    gain_ffn = jnp.clip(1.0 + 0.1 * jax.random.normal(key_of[11], (D,), jnp.float32), 0.5, 1.5)
    gate_weight = gaussian(key_of[12], (D, FF), D ** -0.5, 0.125, ((0, 16), (1, 2)), jnp.float32)
    up_weight = gaussian(key_of[13], (D, FF), D ** -0.5, 0.125, ((0, 16), (1, 2)), jnp.float32)
    down_weight = gaussian(key_of[14], (FF, D), (FF // 4) ** -0.5, 0.15625, ((0, 2), (1, 16)), jnp.float32)
    out_grad = gaussian(key_of[15], (SEQ_ALL, LENGTH, D), 1.0, 6.0, ((0, 4), (1, 4)))
    return dict(block_input=block_input, doc_start=doc_start, gain_mix=gain_mix, query_weight=query_weight, key_weight=key_weight, value_weight=value_weight, beta_weight=beta_weight, beta_bias=beta_bias, conv_weight=conv_weight, gain_o=gain_o, out_weight=out_weight, gain_ffn=gain_ffn, gate_weight=gate_weight, up_weight=up_weight, down_weight=down_weight, out_grad=out_grad)


EPSILON = 1e-06
HEAD_FLOOR = 0.01
HIGHEST = lax.Precision.HIGHEST

@jax.custom_vjp
def low(v):
    return lax.optimization_barrier(v.astype(jnp.bfloat16)).astype(jnp.float32)

@jax.custom_vjp
def low_back(v):
    return v

def low_keep(v):
    return (low(v), None)

def low_pass(kept, grad):
    return (grad,)

def back_keep(v):
    return (v, None)

def back_low(kept, grad):
    return (low(grad),)
low.defvjp(low_keep, low_pass)
low_back.defvjp(back_keep, back_low)

def matmul_high(left, right):
    return jnp.dot(left, right, precision=HIGHEST, preferred_element_type=jnp.float32)

def rms_norm(values, gain, floor_value):
    return values * lax.rsqrt(lax.optimization_barrier(jnp.mean(values * values, axis=-1, keepdims=True)) + floor_value) * gain

def unit_norm(values):
    return values * lax.rsqrt(lax.optimization_barrier(jnp.sum(values * values, axis=-1, keepdims=True)) + EPSILON)

def invert_unit_lower(strict):
    size = strict.shape[-1]
    identity = jnp.eye(size, dtype=jnp.float32)
    power = -strict
    result = identity + power
    for repeat in range(size.bit_length() - 2):
        power = jnp.matmul(power, power, precision=HIGHEST)
        result = jnp.matmul(result, identity + power, precision=HIGHEST)
    return result

def block_step(state_mat, inputs):
    queries, key_vecs, values, strengths, starts, first_pos = inputs
    size = key_vecs.shape[-2]
    order = jnp.arange(size)
    carried = (starts < first_pos).astype(jnp.float32)
    same_doc = starts[..., :, None] == starts[..., None, :]
    below = order[:, None] > order[None, :]
    upto = order[:, None] >= order[None, :]
    key_gram = jnp.einsum('...td,...sd->...ts', key_vecs, key_vecs, precision=HIGHEST)
    strict = jnp.where(same_doc & below, strengths[..., :, None] * key_gram, 0.0)
    from_state = jnp.einsum('...td,...de->...te', key_vecs, state_mat, precision=HIGHEST)
    targets = strengths[..., None] * (values - carried[..., None] * from_state)
    updates = jnp.matmul(invert_unit_lower(strict), targets, precision=HIGHEST)
    scores = jnp.where(same_doc & upto, jnp.einsum('...td,...sd->...ts', queries, key_vecs, precision=HIGHEST), 0.0)
    outputs = carried[..., None] * jnp.einsum('...td,...de->...te', queries, state_mat, precision=HIGHEST)
    outputs = outputs + jnp.einsum('...ts,...se->...te', scores, updates, precision=HIGHEST)
    last_doc = (starts == starts[..., -1:]).astype(jnp.float32)
    new_state = carried[..., -1:, None] * state_mat + jnp.einsum('...sd,...se->...de', key_vecs * last_doc[..., None], updates, precision=HIGHEST)
    return (new_state, outputs)

def delta_rule(queries, key_vecs, values, strengths, starts):
    heads, length, head_dim = queries.shape
    blocks = length // GROUP

    def by_block(array):
        return array.reshape(heads, blocks, GROUP, -1).transpose(1, 0, 2, 3)
    block_strengths = strengths.reshape(heads, blocks, GROUP).transpose(1, 0, 2)
    block_starts = starts.reshape(blocks, 1, GROUP)
    firsts = jnp.arange(blocks, dtype=jnp.int32) * GROUP
    start_state = jnp.zeros((heads, head_dim, values.shape[-1]), jnp.float32)
    final, outputs = lax.scan(jax.checkpoint(block_step), start_state, (by_block(queries), by_block(key_vecs), by_block(values), block_strengths, block_starts, firsts))
    return outputs.transpose(1, 0, 2, 3).reshape(heads, length, -1)

def short_conv(pre, weight, starts):
    length, channels = pre.shape
    positions = jnp.arange(length, dtype=jnp.int32)
    total = jnp.zeros((length, channels), jnp.float32)
    for tap_index in range(CONV):
        shift_back = CONV - 1 - tap_index
        moved = jnp.concatenate([jnp.zeros((shift_back, channels), jnp.float32), pre[:length - shift_back]], axis=0)
        valid = (positions - shift_back >= starts).astype(jnp.float32)
        total = total + weight[tap_index] * moved * valid[:, None]
    return total

def reference(block_input, doc_start, gain_mix, query_weight, key_weight, value_weight, beta_weight, beta_bias, conv_weight, gain_o, out_weight, gain_ffn, gate_weight, up_weight, down_weight, out_grad):

    def forward(inputs, gain_a, query_w, key_w, value_w, beta_w, bias_b, conv_w, gain_head, out_w, gain_b, gate_w, up_w, down_w):
        low_query = low(query_w)
        low_key = low(key_w)
        low_value = low(value_w)
        low_beta = low(beta_w)
        low_out = low(out_w)
        low_gate = low(gate_w)
        low_up = low(up_w)
        low_down = low(down_w)

        def one_sequence(couple):
            tokens, starts = couple
            length = tokens.shape[0]
            normed = low(rms_norm(tokens, gain_a, EPSILON))
            query_pre = low_back(matmul_high(normed, low_query))
            key_pre = low_back(matmul_high(normed, low_key))
            value_pre = low_back(matmul_high(normed, low_value))
            strength = jax.nn.sigmoid(low_back(matmul_high(normed, low_beta)) + bias_b)
            query_act = jax.nn.silu(short_conv(query_pre, conv_w[0], starts))
            key_act = jax.nn.silu(short_conv(key_pre, conv_w[1], starts))
            value_act = jax.nn.silu(short_conv(value_pre, conv_w[2], starts))
            queries = unit_norm(query_act.reshape(length, HEADS, HEAD)).transpose(1, 0, 2)
            key_vecs = unit_norm(key_act.reshape(length, HEADS, HEAD)).transpose(1, 0, 2)
            values = value_act.reshape(length, HEADS, HEAD).transpose(1, 0, 2)
            mixed = delta_rule(queries, key_vecs, values, strength.T, starts)
            mixed_normed = rms_norm(mixed, gain_head, HEAD_FLOOR)
            mixed_rows = mixed_normed.transpose(1, 0, 2).reshape(length, HEADS * HEAD)
            residual = tokens + low_back(matmul_high(low(mixed_rows), low_out))
            normed_ffn = low(rms_norm(residual, gain_b, EPSILON))
            gate = low_back(matmul_high(normed_ffn, low_gate))
            up_val = low_back(matmul_high(normed_ffn, low_up))
            hidden = low(jax.nn.silu(gate) * up_val)
            return residual + low_back(matmul_high(hidden, low_down))
        return lax.map(jax.checkpoint(one_sequence), (inputs, doc_start))
    primal, pullback = jax.vjp(forward, block_input.astype(jnp.float32), gain_mix, query_weight, key_weight, value_weight, beta_weight, beta_bias, conv_weight, gain_o, out_weight, gain_ffn, gate_weight, up_weight, down_weight)
    grads = pullback(out_grad.astype(jnp.float32))
    return (primal.astype(jnp.bfloat16), grads[0].astype(jnp.bfloat16), grads[1], grads[2], grads[3], grads[4], grads[5], grads[6], grads[7], grads[8], grads[9], grads[10], grads[11], grads[12], grads[13])
```

```python
import functools
import jax
import jax.numpy as jnp
from jax import lax
from jax.experimental import pallas as pl
from jax.experimental.pallas import tpu as pltpu
from jax.sharding import PartitionSpec as P

LANES = 128
CHUNK = 128
HALO = 8
EPSILON = 1e-06
HEAD_FLOOR = 0.01
VMEM_BYTES = 60 * 1024 * 1024


def low(value):
    return value.astype(jnp.bfloat16)


def mul_nn(left, right):
    return lax.dot_general(low(left), low(right), (((1,), (0,)), ((), ())), preferred_element_type=jnp.float32)


def mul_nt(left, right):
    return lax.dot_general(low(left), low(right), (((1,), (1,)), ((), ())), preferred_element_type=jnp.float32)


def mul_tn(left, right):
    return lax.dot_general(low(left), low(right), (((0,), (0,)), ((), ())), preferred_element_type=jnp.float32)


def iota(shape, axis):
    return lax.broadcasted_iota(jnp.int32, shape, axis)


def chunk_masks(col, row, first):
    size = col.shape[0]
    same = col == row
    order, other = iota((size, size), 0), iota((size, size), 1)
    upto = same & (order >= other)
    below = same & (order > other)
    carried = (col < first).astype(jnp.float32)
    last = (col == row[:, size - 1 :]).astype(jnp.float32)
    keep = (row[:, size - 1 :] < first).astype(jnp.float32)
    return upto, below, carried, last, keep


def invert_units(systems):
    size = systems[0].shape[0]
    order, other = iota((size, size), 0), iota((size, size), 1)
    identity = (order == other).astype(jnp.float32)
    span = 1
    found = None
    while span < size:
        pair = (order // (2 * span) == other // (2 * span)) & (order // span != other // span)
        parts = [jnp.where(pair, system, 0.0) for system in systems]
        if found is None:
            found = [identity - part for part in parts]
        else:
            right = [mul_nn(part, value) for part, value in zip(parts, found)]
            found = [value - mul_nn(value, part) for value, part in zip(found, right)]
        span *= 2
    return found


def conv_rows(ext, conv, col, offset, size, lane, taps):
    total = None
    moved = []
    position = iota((size, 1), 0) + offset
    for tap in range(taps):
        back = taps - 1 - tap
        values = ext[pl.ds(HALO + offset - back, size), lane : lane + LANES]
        values = jnp.where(position - back >= col, values, 0.0)
        moved.append(values)
        term = conv[tap : tap + 1, lane : lane + LANES] * values
        total = term if total is None else total + term
    return total, moved


def unit(values):
    return values * lax.rsqrt(jnp.sum(values * values, axis=-1, keepdims=True) + EPSILON)


def head_column(values, head):
    return jnp.sum(jnp.where(iota(values.shape, 1) == head, values, 0.0), axis=-1, keepdims=True)


def forward_kernel(taps, heads, pre, beta, bias, halo, conv, col_ref, row_ref, own, carry, final, inv, upd, states, ext):
    length = pre.shape[0]
    ext[:HALO] = halo[0]
    ext[HALO:] = pre[...]
    head = pl.program_id(1) * heads
    jobs = [(i, j) for j in range(length // CHUNK) for i in range(heads)]
    data = {}
    for j in range(length // CHUNK):
        rows = pl.ds(j * CHUNK, CHUNK)
        col, row = col_ref[0, rows], row_ref[0, :, rows]
        masks = chunk_masks(col, row, j * CHUNK)
        strengths = jax.nn.sigmoid(beta[rows] + bias[...])
        for i in range(heads):
            acts = []
            for kind in range(3):
                total, _ = conv_rows(ext, conv, col, j * CHUNK, CHUNK, (3 * i + kind) * LANES, taps)
                acts.append(total * jax.nn.sigmoid(total))
            query, key, value = unit(acts[0]), unit(acts[1]), acts[2]
            strength = head_column(strengths, head + i)
            grams = mul_nt(jnp.concatenate([low(key), low(query)], axis=0), key)
            system = jnp.where(masks[1], strength * grams[:CHUNK], 0.0)
            scores = low(jnp.where(masks[0], grams[CHUNK:], 0.0))
            data[i, j] = (low(query), low(key), value, strength, scores, masks, system)
    inverses = dict(zip(jobs, invert_units([data[job][6] for job in jobs])))
    for i in range(heads):
        state = jnp.concatenate(
            [
                jnp.zeros((LANES, LANES), jnp.float32),
                (iota((LANES, LANES), 0) == iota((LANES, LANES), 1)).astype(jnp.float32),
            ],
            axis=1,
        )
        final[0, i] = state
    for j in range(length // CHUNK):
        rows = pl.ds(j * CHUNK, CHUNK)
        for i in range(heads):
            query, key, value, strength, scores, masks, _ = data[i, j]
            _, _, carried, last, keep = masks
            inverse = low(inverses[i, j])
            state = final[0, i]
            state_low = low(state)
            read = mul_nn(jnp.concatenate([key, query], axis=0), state_low)
            wide = jnp.concatenate([value, jnp.zeros_like(value)], axis=1)
            targets = strength * (wide - carried * read[:CHUNK])
            update = low(mul_nn(inverse, targets))
            result = carried * read[CHUNK:] + mul_nn(scores, update)
            final[0, i] = keep * state + mul_tn(key * low(last), update)
            lanes = slice(i * LANES, (i + 1) * LANES)
            own[rows, lanes] = result[:, :LANES]
            carry[rows, lanes] = low(result[:, LANES:])
            inv[0, i, j] = inverse
            upd[0, i, j] = update
            states[0, i, j] = state_low


def mixer_forward(pre, bias, halo, conv, col, row, taps, heads_here, group):
    seqs, length = col.shape[0], col.shape[1]
    steps = heads_here // group
    chunks = length // CHUNK
    wide = 3 * LANES * group
    rows = seqs * length

    def tile(*tail, kind):
        return jax.ShapeDtypeStruct((seqs, heads_here) + tail, kind)

    def spec(*tail):
        return pl.BlockSpec((1, group) + tail, lambda s, h: (s, h) + (0,) * len(tail))

    flat = pl.BlockSpec((length, LANES * group), lambda s, h: (s, h))
    last = 3 * heads_here
    return pl.pallas_call(
        functools.partial(forward_kernel, taps, group),
        grid=(seqs, steps),
        in_specs=[
            pl.BlockSpec((length, wide), lambda s, h: (s, h)),
            pl.BlockSpec((length, LANES), lambda s, h: (s, last)),
            pl.BlockSpec((1, LANES), lambda s, h: (0, 0)),
            pl.BlockSpec((1, HALO, wide), lambda s, h: (s, 0, h)),
            pl.BlockSpec((conv.shape[0], wide), lambda s, h: (0, h)),
            pl.BlockSpec((1, length, 1), lambda s, h: (s, 0, 0)),
            pl.BlockSpec((1, 1, length), lambda s, h: (s, 0, 0)),
        ],
        out_specs=[
            flat,
            flat,
            spec(LANES, 2 * LANES),
            spec(chunks, CHUNK, CHUNK),
            spec(chunks, CHUNK, 2 * LANES),
            spec(chunks, LANES, 2 * LANES),
        ],
        out_shape=[
            jax.ShapeDtypeStruct((rows, heads_here * LANES), jnp.float32),
            jax.ShapeDtypeStruct((rows, heads_here * LANES), jnp.bfloat16),
            tile(LANES, 2 * LANES, kind=jnp.float32),
            tile(chunks, CHUNK, CHUNK, kind=jnp.bfloat16),
            tile(chunks, CHUNK, 2 * LANES, kind=jnp.bfloat16),
            tile(chunks, LANES, 2 * LANES, kind=jnp.bfloat16),
        ],
        scratch_shapes=[pltpu.VMEM((length + HALO, wide), jnp.float32)],
        compiler_params=pltpu.CompilerParams(vmem_limit_bytes=VMEM_BYTES),
        cost_estimate=pl.CostEstimate(
            flops=60 * rows * heads_here * CHUNK * LANES, bytes_accessed=40 * rows * heads_here * LANES, transcendentals=0
        ),
    )(pre, pre, bias, halo, conv, col, row)


def backward_kernel(
    taps, heads, pre, beta, bias, halo, conv, col_ref, row_ref, grad_ref, inv, upd, states, start, end,
    grad_pre, tail, before, conv_grad, bias_grad, ext, grad_ext, logits,
):
    length = pre.shape[0]
    step = pl.program_id(1)
    head = step * heads
    ext[:HALO] = halo[0]
    ext[HALO:] = pre[...]
    grad_ext[...] = jnp.zeros_like(grad_ext)

    @pl.when(step == 0)
    def _():
        logits[...] = jnp.zeros_like(logits)

    grad_states = [end[0, i] for i in range(heads)]
    entry = [low(start[0, i]) for i in range(heads)]
    tap_sums = {}
    for j in reversed(range(length // CHUNK)):
        offset = j * CHUNK
        rows = pl.ds(offset, CHUNK)
        col, row = col_ref[0, rows], row_ref[0, :, rows]
        upto, below, carried, last, keep = chunk_masks(col, row, offset)
        strengths = jax.nn.sigmoid(beta[rows] + bias[...])
        grad_logit = jnp.zeros((CHUNK, LANES), jnp.float32)
        for i in range(heads):
            raw, taps_in = [], []
            for kind in range(3):
                total, moved = conv_rows(ext, conv, col, offset, CHUNK, (3 * i + kind) * LANES, taps)
                raw.append(total)
                taps_in.append(moved)
            gates = [jax.nn.sigmoid(total) for total in raw]
            acts = [total * gate for total, gate in zip(raw, gates)]
            scales = [lax.rsqrt(jnp.sum(act * act, axis=-1, keepdims=True) + EPSILON) for act in acts[:2]]
            query, key, value = acts[0] * scales[0], acts[1] * scales[1], acts[2]
            strength = head_column(strengths, head + i)
            lanes = slice(i * LANES, (i + 1) * LANES)
            query_low, key_low = low(query), low(key)
            grams = mul_nt(jnp.concatenate([key_low, query_low], axis=0), key_low)
            gram = jnp.where(below, grams[:CHUNK], 0.0)
            scores = jnp.where(upto, grams[CHUNK:], 0.0)
            inverse = inv[0, i, j]
            update = upd[0, i, j]
            update = low(update[:, :LANES].astype(jnp.float32) + mul_nn(update[:, LANES:], entry[i]))
            state = states[0, i, j]
            state = low(state[:, :LANES].astype(jnp.float32) + mul_nn(state[:, LANES:], entry[i]))
            grad_out = grad_ref[rows, lanes]
            grad_state = grad_states[i]
            grad_state_low = low(grad_state)
            key_last = key_low * low(last)
            grad_update = mul_tn(scores, grad_out) + mul_nn(key_last, grad_state_low)
            grad_target = mul_tn(inverse, grad_update)
            weighted = strength * grad_target
            passed = carried * weighted
            out_carried = carried * grad_out.astype(jnp.float32)
            query_carried = query_low * low(carried)
            grad_states[i] = (
                keep * grad_state + mul_tn(query_carried, grad_out) - mul_tn(key_low, passed)
            )
            grad_scores = jnp.where(upto, mul_nt(grad_out, update), 0.0)
            grad_system = jnp.where(below, mul_nt(grad_target, update), 0.0)
            remainder = value - carried * mul_nn(key_low, state)
            grad_strength = jnp.sum(grad_target * remainder - grad_system * gram, axis=-1, keepdims=True)
            scaled = strength * grad_system
            from_state = mul_nt(jnp.concatenate([low(out_carried), low(passed)], axis=0), state)
            from_keys = mul_nn(jnp.concatenate([low(grad_scores), low(scaled + scaled.T)], axis=0), key_low)
            grad_query = from_state[:CHUNK] + from_keys[:CHUNK]
            grad_key = (
                mul_tn(grad_scores, query_low)
                + last * mul_nt(update, grad_state_low)
                - from_state[CHUNK:]
                - from_keys[CHUNK:]
            )
            grad_logit = grad_logit + jnp.where(
                iota((CHUNK, LANES), 1) == head + i, grad_strength * strength * (1.0 - strength), 0.0
            )
            grads = [
                scales[0] * (grad_query - query * jnp.sum(grad_query * query, axis=-1, keepdims=True)),
                scales[1] * (grad_key - key * jnp.sum(grad_key * key, axis=-1, keepdims=True)),
                weighted,
            ]
            position = iota((CHUNK, 1), 0) + offset
            for kind in range(3):
                gate, total = gates[kind], raw[kind]
                grad_conv = grads[kind] * gate * (1.0 + total * (1.0 - gate))
                lane = (3 * i + kind) * LANES
                for tap in range(taps):
                    back = taps - 1 - tap
                    part = jnp.sum(grad_conv * taps_in[kind][tap], axis=0, keepdims=True)
                    spot = (i, kind, tap)
                    tap_sums[spot] = part if spot not in tap_sums else tap_sums[spot] + part
                    back_part = jnp.where(
                        position - back >= col, grad_conv * conv[tap : tap + 1, lane : lane + LANES], 0.0
                    )
                    where = pl.ds(HALO + offset - back, CHUNK)
                    grad_ext[where, lane : lane + LANES] += back_part
        logits[rows] += grad_logit
    wide = 3 * LANES * heads
    place = pl.multiple_of(step * wide, LANES)
    grad_pre[:, pl.ds(place, wide)] = low(grad_ext[HALO:])
    before[0] = grad_ext[:HALO]
    tail[0] = grad_ext[length:]
    for i in range(heads):
        for kind in range(3):
            lane = (3 * i + kind) * LANES
            for tap in range(taps):
                conv_grad[0, tap : tap + 1, lane : lane + LANES] = tap_sums[i, kind, tap]

    @pl.when(step == pl.num_programs(1) - 1)
    def _():
        total = logits[...]
        grad_pre[:, grad_pre.shape[1] - LANES :] = low(total)
        bias_grad[0] = jnp.sum(total, axis=0, keepdims=True)


def mixer_backward(pre, bias, halo, conv, col, row, grad_mixed, inv, upd, states, start, end, taps, heads_here, group):
    seqs, length = col.shape[0], col.shape[1]
    steps = heads_here // group
    chunks = length // CHUNK
    wide = 3 * LANES * group
    rows = seqs * length
    total = pre.shape[1]

    def spec(*tail):
        return pl.BlockSpec((1, group) + tail, lambda s, h: (s, h) + (0,) * len(tail))

    last = 3 * heads_here
    part = pl.BlockSpec((1, HALO, wide), lambda s, h: (s, 0, h))
    edge = jax.ShapeDtypeStruct((seqs, HALO, 3 * LANES * heads_here), jnp.float32)
    return pl.pallas_call(
        functools.partial(backward_kernel, taps, group),
        grid=(seqs, steps),
        in_specs=[
            pl.BlockSpec((length, wide), lambda s, h: (s, h)),
            pl.BlockSpec((length, LANES), lambda s, h: (s, last)),
            pl.BlockSpec((1, LANES), lambda s, h: (0, 0)),
            part,
            pl.BlockSpec((conv.shape[0], wide), lambda s, h: (0, h)),
            pl.BlockSpec((1, length, 1), lambda s, h: (s, 0, 0)),
            pl.BlockSpec((1, 1, length), lambda s, h: (s, 0, 0)),
            pl.BlockSpec((length, LANES * group), lambda s, h: (s, h)),
            spec(chunks, CHUNK, CHUNK),
            spec(chunks, CHUNK, 2 * LANES),
            spec(chunks, LANES, 2 * LANES),
            spec(LANES, LANES),
            spec(LANES, LANES),
        ],
        out_specs=[
            pl.BlockSpec((length, total), lambda s, h: (s, 0)),
            part,
            part,
            part,
            pl.BlockSpec((1, 1, LANES), lambda s, h: (s, 0, 0)),
        ],
        out_shape=[
            jax.ShapeDtypeStruct((rows, total), jnp.bfloat16),
            edge,
            edge,
            edge,
            jax.ShapeDtypeStruct((seqs, 1, LANES), jnp.float32),
        ],
        scratch_shapes=[
            pltpu.VMEM((length + HALO, wide), jnp.float32),
            pltpu.VMEM((length + HALO, wide), jnp.float32),
            pltpu.VMEM((length, LANES), jnp.float32),
        ],
        compiler_params=pltpu.CompilerParams(vmem_limit_bytes=VMEM_BYTES),
        cost_estimate=pl.CostEstimate(
            flops=60 * rows * heads_here * CHUNK * LANES, bytes_accessed=40 * rows * heads_here * LANES, transcendentals=0
        ),
    )(pre, pre, bias, halo, conv, col, row, grad_mixed, inv, upd, states, start, end)


def mixed_rows_of(own, carry, start):
    return own + mul_nn(carry, start)


def output_kernel(heads, own, carry, start, gain, out):
    for i in range(heads):
        lanes = slice(i * LANES, (i + 1) * LANES)
        mixed = mixed_rows_of(own[:, lanes], carry[:, lanes], start[0, i])
        scale = lax.rsqrt(jnp.mean(mixed * mixed, axis=-1, keepdims=True) + HEAD_FLOOR)
        out[:, lanes] = low(mixed * scale * gain[...])


def output_backward_kernel(heads, own, carry, start, gain, grad, out, across, gain_grad):
    total = jnp.zeros((1, LANES), jnp.float32)
    for i in range(heads):
        lanes = slice(i * LANES, (i + 1) * LANES)
        carried = carry[:, lanes]
        mixed = mixed_rows_of(own[:, lanes], carried, start[0, i])
        scale = lax.rsqrt(jnp.mean(mixed * mixed, axis=-1, keepdims=True) + HEAD_FLOOR)
        normed = mixed * scale
        upper = grad[:, lanes].astype(jnp.float32)
        total = total + jnp.sum(upper * normed, axis=0, keepdims=True)
        weighted = upper * gain[...]
        back = scale * (weighted - normed * jnp.mean(weighted * normed, axis=-1, keepdims=True))
        out[:, lanes] = low(back)
        across[0, i] = mul_tn(carried, back)
    gain_grad[0, 0] = total


def mixer_output(own, carry, start, gain, group):
    seqs, heads_here = start.shape[:2]
    rows = own.shape[0]
    length = rows // seqs
    flat = pl.BlockSpec((length, LANES * group), lambda s, h: (s, h))
    square = pl.BlockSpec((1, group, LANES, LANES), lambda s, h: (s, h, 0, 0))
    return pl.pallas_call(
        functools.partial(output_kernel, group),
        grid=(seqs, heads_here // group),
        in_specs=[flat, flat, square, pl.BlockSpec((1, LANES), lambda s, h: (0, 0))],
        out_specs=flat,
        out_shape=jax.ShapeDtypeStruct(own.shape, jnp.bfloat16),
        compiler_params=pltpu.CompilerParams(vmem_limit_bytes=VMEM_BYTES),
        cost_estimate=pl.CostEstimate(
            flops=2 * own.size * LANES, bytes_accessed=8 * own.size, transcendentals=0
        ),
    )(own, carry, start, gain)


def mixer_output_backward(own, carry, start, gain, grad, group):
    seqs, heads_here = start.shape[:2]
    rows = own.shape[0]
    length = rows // seqs
    steps = heads_here // group
    flat = pl.BlockSpec((length, LANES * group), lambda s, h: (s, h))
    square = pl.BlockSpec((1, group, LANES, LANES), lambda s, h: (s, h, 0, 0))
    return pl.pallas_call(
        functools.partial(output_backward_kernel, group),
        grid=(seqs, steps),
        in_specs=[flat, flat, square, pl.BlockSpec((1, LANES), lambda s, h: (0, 0)), flat],
        out_specs=[flat, square, pl.BlockSpec((1, 1, 1, LANES), lambda s, h: (s, h, 0, 0))],
        out_shape=[
            jax.ShapeDtypeStruct(own.shape, jnp.bfloat16),
            jax.ShapeDtypeStruct(start.shape, jnp.float32),
            jax.ShapeDtypeStruct((seqs, steps, 1, LANES), jnp.float32),
        ],
        compiler_params=pltpu.CompilerParams(vmem_limit_bytes=VMEM_BYTES),
        cost_estimate=pl.CostEstimate(
            flops=4 * own.size * LANES, bytes_accessed=12 * own.size, transcendentals=0
        ),
    )(own, carry, start, gain, grad)


def flip(value, axis, bit):
    devices = range(lax.axis_size(axis))
    return lax.ppermute(value, axis, [(i, i ^ bit) for i in devices])


def shift(value, axis, distance):
    count = lax.axis_size(axis)
    return lax.ppermute(value, axis, [(i, (i + distance) % count) for i in range(count)])


def put(buffer, piece, index):
    start = (index,) + (0,) * piece.ndim
    return lax.dynamic_update_slice(buffer, piece[None], start)


def after(value, *earlier):
    return lax.optimization_barrier((value,) + earlier)[0]


def gather_line(shard):
    count, place = lax.axis_size("fsdp"), lax.axis_index("fsdp")
    buffer = put(jnp.zeros((count,) + shard.shape, shard.dtype), shard, place)
    for distance in range(1, count):
        buffer = put(buffer, shift(shard, "fsdp", distance), (place - distance) % count)
    return buffer.reshape(count * shard.shape[0], shard.shape[1])


def gather_square(piece):
    place = lax.axis_index("ctx")
    half = piece.shape[0] // 2
    beside = flip(piece, "ctx", 1)
    across = flip(piece, "ctx", 2)
    upper = flip(beside[:half], "ctx", 2)
    lower = flip(across[half:], "ctx", 1)
    buffer = put(jnp.zeros((4,) + piece.shape, piece.dtype), piece, place)
    buffer = put(buffer, beside, place ^ 1)
    buffer = put(buffer, across, place ^ 2)
    buffer = put(buffer, jnp.concatenate([upper, lower], axis=0), place ^ 3)
    return buffer.reshape(4 * piece.shape[0], piece.shape[1])


def gather_groups(shards):
    if lax.axis_size("ctx") != 4:
        return [lax.all_gather(shard, ("ctx", "fsdp"), axis=0, tiled=True) for shard in shards]
    full = []
    line = None
    for shard in shards:
        line = gather_line(shard if line is None else after(shard, line))
        full.append(gather_square(line if not full else after(line, full[-1])))
    return full


def relative_columns(rows):
    width = rows.shape[1] // 4
    part = width // lax.axis_size("fsdp")
    place, line = lax.axis_index("ctx"), lax.axis_index("fsdp")
    blocks = []
    for bit in range(4):
        block = lax.dynamic_slice_in_dim(rows, (place ^ bit) * width, width, 1)
        twice = jnp.concatenate([block, block], axis=1)
        blocks.append(lax.dynamic_slice_in_dim(twice, line * part, width, 1))
    return blocks


def outer_scatter(rows, grads, blocks=None):
    if lax.axis_size("ctx") != 4:
        return lax.psum_scatter(
            outer_rows(rows, grads).astype(jnp.bfloat16), ("ctx", "fsdp"), scatter_dimension=0, tiled=True
        ).astype(jnp.float32)
    if blocks is None:
        blocks = relative_columns(rows)
    half = blocks[0].shape[1] // 2
    low = jnp.bfloat16

    def halves(bit):
        block = blocks[bit]
        return outer_rows(block[:, :half], grads), outer_rows(block[:, half:], grads)

    diag_up, diag_down = halves(3)
    from_across = flip(diag_up.astype(low), "ctx", 2)
    from_beside = flip(diag_down.astype(low), "ctx", 1)
    beside_up, beside_down = halves(1)
    across_up, across_down = halves(2)
    beside_down = flip(beside_down.astype(low), "ctx", 1)
    across_up = flip(across_up.astype(low), "ctx", 2)
    beside_up = flip((beside_up + from_across).astype(low), "ctx", 1)
    across_down = flip((across_down + from_beside).astype(low), "ctx", 2)
    own_up, own_down = halves(0)
    own_up = own_up + beside_up + across_up
    own_down = own_down + beside_down + across_down
    count = lax.axis_size("fsdp")
    part = 2 * half // count
    own = jnp.concatenate([own_up, own_down], axis=0)
    total = own[:part]
    for distance in range(1, count):
        piece = own[distance * part : (distance + 1) * part].astype(low)
        total = total + shift(piece, "fsdp", distance)
    return total


def butterfly(value, axes):
    for axis in axes:
        count, bit = lax.axis_size(axis), 1
        while bit < count:
            value = value + flip(value, axis, bit)
            bit *= 2
    return value


def from_behind(block, axis, distance):
    devices = range(lax.axis_size(axis))
    route = [(i - distance, i) for i in devices if i - distance in devices]
    return lax.ppermute(block, axis, route)


def rms_scale(values, floor_value):
    return lax.rsqrt(jnp.mean(values * values, axis=-1, keepdims=True) + floor_value)


def norm_backward(grad_normed, inputs, scale, gain):
    normed = inputs * scale
    weighted = grad_normed * gain
    return (
        scale * (weighted - normed * jnp.mean(weighted * normed, axis=-1, keepdims=True)),
        normed,
    )


def times(left, right):
    return jnp.dot(left, right, preferred_element_type=jnp.float32)


def times_transposed(left, right):
    return lax.dot_general(
        left, right, (((1,), (1,)), ((), ())), preferred_element_type=jnp.float32
    )


def outer_rows(left, right):
    return lax.dot_general(
        left, right, (((0,), (0,)), ((), ())), preferred_element_type=jnp.float32
    )


def heads_combine(partial_value):
    part = low(partial_value)
    if lax.axis_size("tp") != 2:
        return lax.psum(part, "tp").astype(jnp.float32)
    return part.astype(jnp.float32) + flip(part, "tp", 1).astype(jnp.float32)


def rows_own(held):
    count = held.shape[0] // lax.axis_size("tp")
    return lax.dynamic_slice_in_dim(held, lax.axis_index("tp") * count, count, 0)


def by_head(parts):
    lead = parts[0].shape[:-1]
    split = [part.reshape(lead + (-1, LANES)) for part in parts]
    return jnp.stack(split, axis=-2).reshape(lead + (-1,))


def by_kind(joined):
    lead = joined.shape[:-1]
    split = joined.reshape(lead + (-1, 3, LANES))
    return [split[..., kind, :].reshape(lead + (-1,)) for kind in range(3)]


def local(
    block_input,
    doc_start,
    gain_mix,
    query_weight,
    key_weight,
    value_weight,
    beta_weight,
    beta_bias,
    conv_weight,
    gain_o,
    out_weight,
    gain_ffn,
    gate_weight,
    up_weight,
    down_weight,
    out_grad,
):
    seq_count, local_len, width = block_input.shape
    row_count = seq_count * local_len
    heads_here = beta_weight.shape[1]
    taps = conv_weight.shape[1]
    group = 2 if heads_here % 2 == 0 else 1
    hidden_cols = gate_weight.shape[1]
    head_cols = 3 * heads_here * LANES
    spare = LANES - heads_here
    mix_full, out_full, ffn_full, down_full = gather_groups(
        [
            jnp.concatenate(
                [
                    by_head([low(query_weight), low(key_weight), low(value_weight)]),
                    jnp.pad(low(beta_weight), ((0, 0), (0, spare))),
                ],
                axis=1,
            ),
            low(out_weight).T,
            jnp.concatenate([low(gate_weight), low(up_weight)], axis=1),
            low(down_weight).T,
        ]
    )
    first_pos = lax.axis_index("ctx") * local_len
    starts = doc_start - first_pos
    col, row = starts[:, :, None], starts[:, None, :]
    conv = by_head([conv_weight[0], conv_weight[1], conv_weight[2]])
    bias = jnp.pad(beta_bias, (0, spare))[None]
    gain_head = gain_o[None]

    inputs = block_input.astype(jnp.float32).reshape(row_count, width)
    scale_mix = rms_scale(inputs, EPSILON)
    normed_mix = low(inputs * scale_mix * gain_mix)
    pre = times(normed_mix, mix_full)
    ends = pre.reshape(seq_count, local_len, -1)[:, local_len - HALO :, :head_cols]
    halo = from_behind(ends, "ctx", 1)
    own, carry, final, inverses, updates, states = mixer_forward(
        pre, bias, halo, conv, col, row, taps, heads_here, group
    )
    transfer = low(final[..., LANES:])
    entered = jnp.zeros_like(final[..., :LANES])
    leaving = final[..., :LANES]
    for repeat in range(lax.axis_size("ctx") - 1):
        entered = from_behind(low(leaving), "ctx", 1)
        leaving = final[..., :LANES] + jnp.einsum(
            "shij,shjk->shik", transfer, entered, preferred_element_type=jnp.float32
        )
    entered = entered.astype(jnp.float32)
    mixed_rows = mixer_output(own, carry, entered, gain_head, group)
    residual = inputs + heads_combine(times_transposed(mixed_rows, out_full))
    scale_ffn = rms_scale(residual, EPSILON)
    normed_ffn = low(residual * scale_ffn * gain_ffn)

    both = times(normed_ffn, ffn_full)
    gate, up_val = both[:, :hidden_cols], both[:, hidden_cols:]
    sigmoid_gate = jax.nn.sigmoid(gate)
    activated = gate * sigmoid_gate
    hidden = low(activated * up_val)
    grad_rows = out_grad.reshape(row_count, width)
    grad_hidden = times(grad_rows, down_full)
    grad_gate = low(grad_hidden * up_val * sigmoid_gate * (1.0 + gate * (1.0 - sigmoid_gate)))
    grad_up = low(grad_hidden * activated)
    grad_both = jnp.concatenate([grad_gate, grad_up], axis=1)
    grad_normed = heads_combine(times_transposed(grad_both, ffn_full))
    output_held = low(residual + heads_combine(times_transposed(hidden, down_full)))
    down_grad = outer_scatter(grad_rows, hidden).T
    both_grad = outer_scatter(normed_ffn, grad_both)
    gate_grad, up_grad = both_grad[:, :hidden_cols], both_grad[:, hidden_cols:]

    back_ffn, unit_ffn = norm_backward(grad_normed, residual, scale_ffn, gain_ffn)
    grad_residual = grad_rows.astype(jnp.float32) + back_ffn
    gain_ffn_part = jnp.sum(rows_own(grad_normed * unit_ffn), axis=0)
    grad_branch = low(grad_residual)
    out_grad_w = outer_scatter(grad_branch, mixed_rows).T
    grad_heads = times(grad_branch, out_full)
    grad_mixed, across, gain_o_part = mixer_output_backward(
        own, carry, entered, gain_head, grad_heads, group
    )
    grad_end = jnp.zeros_like(across)
    grad_now = across
    for repeat in range(lax.axis_size("ctx") - 1):
        grad_end = from_behind(low(grad_now), "ctx", -1)
        grad_now = across + jnp.einsum(
            "shji,shjk->shik", transfer, grad_end, preferred_element_type=jnp.float32
        )
    grad_end = grad_end.astype(jnp.float32)
    grad_mix, tail, before, conv_part, bias_part = mixer_backward(
        pre, bias, halo, conv, col, row, grad_mixed, inverses, updates, states, entered, grad_end,
        taps, heads_here, group,
    )
    tail = low(tail + from_behind(before, "ctx", -1))
    grad_mix = lax.dynamic_update_slice(
        grad_mix.reshape(seq_count, local_len, -1), tail, (0, local_len - HALO, 0)
    ).reshape(row_count, -1)
    mix_back = heads_combine(times_transposed(grad_mix, mix_full))
    mix_grad = outer_scatter(normed_mix, grad_mix)
    query_grad, key_grad, value_grad = by_kind(mix_grad[:, :head_cols])
    beta_grad = mix_grad[:, head_cols : head_cols + heads_here]
    back_mix, unit_mix = norm_backward(mix_back, inputs, scale_mix, gain_mix)
    input_held = low(grad_residual + back_mix)
    gain_mix_part = jnp.sum(rows_own(mix_back * unit_mix), axis=0)

    small = butterfly(
        jnp.concatenate([gain_mix_part, gain_ffn_part, jnp.sum(gain_o_part, axis=(0, 1, 2))]),
        ("tp", "ctx", "fsdp"),
    )
    gain_mix_grad, gain_ffn_grad, gain_o_grad = jnp.split(small, [width, 2 * width])
    conv_grad = butterfly(jnp.sum(conv_part, axis=0)[:taps], ("ctx", "fsdp"))
    conv_grad = jnp.stack(by_kind(conv_grad))
    bias_grad = butterfly(jnp.sum(bias_part, axis=(0, 1))[:heads_here], ("ctx", "fsdp"))
    return (
        output_held.reshape(seq_count, local_len, width),
        input_held.reshape(seq_count, local_len, width),
        gain_mix_grad,
        query_grad,
        key_grad,
        value_grad,
        beta_grad,
        bias_grad,
        conv_grad,
        gain_o_grad,
        out_grad_w,
        gain_ffn_grad,
        gate_grad,
        up_grad,
        down_grad,
    )


def solution(mesh):
    placed = (
        P("fsdp", "ctx", None),
        P("fsdp", "ctx"),
        P(),
        P(("ctx", "fsdp"), "tp"),
        P(("ctx", "fsdp"), "tp"),
        P(("ctx", "fsdp"), "tp"),
        P(("ctx", "fsdp"), "tp"),
        P("tp"),
        P(None, None, "tp"),
        P(),
        P("tp", ("ctx", "fsdp")),
        P(),
        P(("ctx", "fsdp"), "tp"),
        P(("ctx", "fsdp"), "tp"),
        P("tp", ("ctx", "fsdp")),
        P("fsdp", "ctx", None),
    )
    return jax.shard_map(
        local,
        mesh=mesh,
        in_specs=placed,
        out_specs=(
            P("fsdp", "ctx", None),
            P("fsdp", "ctx", None),
            P(),
            P(("ctx", "fsdp"), "tp"),
            P(("ctx", "fsdp"), "tp"),
            P(("ctx", "fsdp"), "tp"),
            P(("ctx", "fsdp"), "tp"),
            P("tp"),
            P(None, None, "tp"),
            P(),
            P("tp", ("ctx", "fsdp")),
            P(),
            P(("ctx", "fsdp"), "tp"),
            P(("ctx", "fsdp"), "tp"),
            P("tp", ("ctx", "fsdp")),
        ),
        check_vma=False,
    )
```

```python
import functools
import jax
import jax.numpy as jnp
from jax import lax
from jax.experimental import pallas as pl
from jax.experimental.pallas import tpu as pltpu
from jax.sharding import PartitionSpec as P

LANES = 128
CHUNK = 128
HALO = 8
EPSILON = 1e-06
HEAD_FLOOR = 0.01
VMEM_BYTES = 60 * 1024 * 1024


def low(value):
    return value.astype(jnp.bfloat16)


def mul_nn(left, right):
    return lax.dot_general(low(left), low(right), (((1,), (0,)), ((), ())), preferred_element_type=jnp.float32)


def mul_nt(left, right):
    return lax.dot_general(low(left), low(right), (((1,), (1,)), ((), ())), preferred_element_type=jnp.float32)


def mul_tn(left, right):
    return lax.dot_general(low(left), low(right), (((0,), (0,)), ((), ())), preferred_element_type=jnp.float32)


def iota(shape, axis):
    return lax.broadcasted_iota(jnp.int32, shape, axis)


def chunk_masks(col, row, first):
    size = col.shape[0]
    same = col == row
    order, other = iota((size, size), 0), iota((size, size), 1)
    upto = same & (order >= other)
    below = same & (order > other)
    carried = (col < first).astype(jnp.float32)
    last = (col == row[:, size - 1 :]).astype(jnp.float32)
    keep = (row[:, size - 1 :] < first).astype(jnp.float32)
    return upto, below, carried, last, keep


def invert_units(systems):
    size = systems[0].shape[0]
    order, other = iota((size, size), 0), iota((size, size), 1)
    identity = (order == other).astype(jnp.float32)
    span = 1
    found = None
    while span < size:
        pair = (order // (2 * span) == other // (2 * span)) & (order // span != other // span)
        parts = [jnp.where(pair, system, 0.0) for system in systems]
        if found is None:
            found = [identity - part for part in parts]
        else:
            right = [mul_nn(part, value) for part, value in zip(parts, found)]
            found = [value - mul_nn(value, part) for value, part in zip(found, right)]
        span *= 2
    return found


def conv_rows(ext, conv, col, offset, size, lane, taps):
    total = None
    moved = []
    position = iota((size, 1), 0) + offset
    for tap in range(taps):
        back = taps - 1 - tap
        values = ext[pl.ds(HALO + offset - back, size), lane : lane + LANES]
        values = jnp.where(position - back >= col, values, 0.0)
        moved.append(values)
        term = conv[tap : tap + 1, lane : lane + LANES] * values
        total = term if total is None else total + term
    return total, moved


def unit(values):
    return values * lax.rsqrt(jnp.sum(values * values, axis=-1, keepdims=True) + EPSILON)


def head_column(values, head):
    return jnp.sum(jnp.where(iota(values.shape, 1) == head, values, 0.0), axis=-1, keepdims=True)


def forward_kernel(taps, heads, first, pre, beta, bias, halo, conv, col_ref, row_ref, own, carry, final, inv, upd, states, ext):
    length = pre.shape[0]
    ext[:HALO] = halo[0]
    ext[HALO:] = pre[...]
    head = first + pl.program_id(1) * heads
    jobs = [(i, j) for j in range(length // CHUNK) for i in range(heads)]
    data = {}
    for j in range(length // CHUNK):
        rows = pl.ds(j * CHUNK, CHUNK)
        col, row = col_ref[0, rows], row_ref[0, :, rows]
        masks = chunk_masks(col, row, j * CHUNK)
        strengths = jax.nn.sigmoid(beta[rows] + bias[...])
        for i in range(heads):
            acts = []
            for kind in range(3):
                total, _ = conv_rows(ext, conv, col, j * CHUNK, CHUNK, (3 * i + kind) * LANES, taps)
                acts.append(total * jax.nn.sigmoid(total))
            query, key, value = unit(acts[0]), unit(acts[1]), acts[2]
            strength = head_column(strengths, head + i)
            grams = mul_nt(jnp.concatenate([low(key), low(query)], axis=0), key)
            system = jnp.where(masks[1], strength * grams[:CHUNK], 0.0)
            scores = low(jnp.where(masks[0], grams[CHUNK:], 0.0))
            data[i, j] = (low(query), low(key), value, strength, scores, masks, system)
    inverses = dict(zip(jobs, invert_units([data[job][6] for job in jobs])))
    for i in range(heads):
        state = jnp.concatenate(
            [
                jnp.zeros((LANES, LANES), jnp.float32),
                (iota((LANES, LANES), 0) == iota((LANES, LANES), 1)).astype(jnp.float32),
            ],
            axis=1,
        )
        final[0, i] = state
    for j in range(length // CHUNK):
        rows = pl.ds(j * CHUNK, CHUNK)
        for i in range(heads):
            query, key, value, strength, scores, masks, _ = data[i, j]
            _, _, carried, last, keep = masks
            inverse = low(inverses[i, j])
            state = final[0, i]
            state_low = low(state)
            read = mul_nn(jnp.concatenate([key, query], axis=0), state_low)
            wide = jnp.concatenate([value, jnp.zeros_like(value)], axis=1)
            targets = strength * (wide - carried * read[:CHUNK])
            update = low(mul_nn(inverse, targets))
            result = carried * read[CHUNK:] + mul_nn(scores, update)
            final[0, i] = keep * state + mul_tn(key * low(last), update)
            lanes = slice(i * LANES, (i + 1) * LANES)
            own[rows, lanes] = result[:, :LANES]
            carry[rows, lanes] = low(result[:, LANES:])
            inv[0, i, j] = inverse
            upd[0, i, j] = update
            states[0, i, j] = state_low


def mixer_forward(pre, logit, bias, halo, conv, col, row, taps, first, heads_here, group):
    seqs, length = col.shape[0], col.shape[1]
    steps = heads_here // group
    chunks = length // CHUNK
    wide = 3 * LANES * group
    rows = seqs * length

    def tile(*tail, kind):
        return jax.ShapeDtypeStruct((seqs, heads_here) + tail, kind)

    def spec(*tail):
        return pl.BlockSpec((1, group) + tail, lambda s, h: (s, h) + (0,) * len(tail))

    flat = pl.BlockSpec((length, LANES * group), lambda s, h: (s, h))
    last = logit.shape[1] // LANES - 1
    return pl.pallas_call(
        functools.partial(forward_kernel, taps, group, first),
        grid=(seqs, steps),
        in_specs=[
            pl.BlockSpec((length, wide), lambda s, h: (s, h)),
            pl.BlockSpec((length, LANES), lambda s, h: (s, last)),
            pl.BlockSpec((1, LANES), lambda s, h: (0, 0)),
            pl.BlockSpec((1, HALO, wide), lambda s, h: (s, 0, h)),
            pl.BlockSpec((conv.shape[0], wide), lambda s, h: (0, h)),
            pl.BlockSpec((1, length, 1), lambda s, h: (s, 0, 0)),
            pl.BlockSpec((1, 1, length), lambda s, h: (s, 0, 0)),
        ],
        out_specs=[
            flat,
            flat,
            spec(LANES, 2 * LANES),
            spec(chunks, CHUNK, CHUNK),
            spec(chunks, CHUNK, 2 * LANES),
            spec(chunks, LANES, 2 * LANES),
        ],
        out_shape=[
            jax.ShapeDtypeStruct((rows, heads_here * LANES), jnp.float32),
            jax.ShapeDtypeStruct((rows, heads_here * LANES), jnp.bfloat16),
            tile(LANES, 2 * LANES, kind=jnp.float32),
            tile(chunks, CHUNK, CHUNK, kind=jnp.bfloat16),
            tile(chunks, CHUNK, 2 * LANES, kind=jnp.bfloat16),
            tile(chunks, LANES, 2 * LANES, kind=jnp.bfloat16),
        ],
        scratch_shapes=[pltpu.VMEM((length + HALO, wide), jnp.float32)],
        compiler_params=pltpu.CompilerParams(vmem_limit_bytes=VMEM_BYTES),
        cost_estimate=pl.CostEstimate(
            flops=60 * rows * heads_here * CHUNK * LANES, bytes_accessed=40 * rows * heads_here * LANES, transcendentals=0
        ),
    )(pre, logit, bias, halo, conv, col, row)


def backward_kernel(
    taps, heads, first, pre, beta, bias, halo, conv, col_ref, row_ref, grad_ref, inv, upd, states, start, end,
    grad_pre, tail, before, conv_grad, logits, ext, grad_ext,
):
    length = pre.shape[0]
    step = pl.program_id(1)
    head = first + step * heads
    ext[:HALO] = halo[0]
    ext[HALO:] = pre[...]
    grad_ext[...] = jnp.zeros_like(grad_ext)

    @pl.when(step == 0)
    def _():
        logits[...] = jnp.zeros_like(logits)

    grad_states = [end[0, i] for i in range(heads)]
    entry = [low(start[0, i]) for i in range(heads)]
    tap_sums = {}
    for j in reversed(range(length // CHUNK)):
        offset = j * CHUNK
        rows = pl.ds(offset, CHUNK)
        col, row = col_ref[0, rows], row_ref[0, :, rows]
        upto, below, carried, last, keep = chunk_masks(col, row, offset)
        strengths = jax.nn.sigmoid(beta[rows] + bias[...])
        grad_logit = jnp.zeros((CHUNK, LANES), jnp.float32)
        for i in range(heads):
            raw, taps_in = [], []
            for kind in range(3):
                total, moved = conv_rows(ext, conv, col, offset, CHUNK, (3 * i + kind) * LANES, taps)
                raw.append(total)
                taps_in.append(moved)
            gates = [jax.nn.sigmoid(total) for total in raw]
            acts = [total * gate for total, gate in zip(raw, gates)]
            scales = [lax.rsqrt(jnp.sum(act * act, axis=-1, keepdims=True) + EPSILON) for act in acts[:2]]
            query, key, value = acts[0] * scales[0], acts[1] * scales[1], acts[2]
            strength = head_column(strengths, head + i)
            lanes = slice(i * LANES, (i + 1) * LANES)
            query_low, key_low = low(query), low(key)
            grams = mul_nt(jnp.concatenate([key_low, query_low], axis=0), key_low)
            gram = jnp.where(below, grams[:CHUNK], 0.0)
            scores = jnp.where(upto, grams[CHUNK:], 0.0)
            inverse = inv[0, i, j]
            update = upd[0, i, j]
            update = low(update[:, :LANES].astype(jnp.float32) + mul_nn(update[:, LANES:], entry[i]))
            state = states[0, i, j]
            state = low(state[:, :LANES].astype(jnp.float32) + mul_nn(state[:, LANES:], entry[i]))
            grad_out = grad_ref[rows, lanes]
            grad_state = grad_states[i]
            grad_state_low = low(grad_state)
            key_last = key_low * low(last)
            grad_update = mul_tn(scores, grad_out) + mul_nn(key_last, grad_state_low)
            grad_target = mul_tn(inverse, grad_update)
            weighted = strength * grad_target
            passed = carried * weighted
            out_carried = carried * grad_out.astype(jnp.float32)
            query_carried = query_low * low(carried)
            grad_states[i] = (
                keep * grad_state + mul_tn(query_carried, grad_out) - mul_tn(key_low, passed)
            )
            grad_scores = jnp.where(upto, mul_nt(grad_out, update), 0.0)
            grad_system = jnp.where(below, mul_nt(grad_target, update), 0.0)
            remainder = value - carried * mul_nn(key_low, state)
            grad_strength = jnp.sum(grad_target * remainder - grad_system * gram, axis=-1, keepdims=True)
            scaled = strength * grad_system
            from_state = mul_nt(jnp.concatenate([low(out_carried), low(passed)], axis=0), state)
            from_keys = mul_nn(jnp.concatenate([low(grad_scores), low(scaled + scaled.T)], axis=0), key_low)
            grad_query = from_state[:CHUNK] + from_keys[:CHUNK]
            grad_key = (
                mul_tn(grad_scores, query_low)
                + last * mul_nt(update, grad_state_low)
                - from_state[CHUNK:]
                - from_keys[CHUNK:]
            )
            grad_logit = grad_logit + jnp.where(
                iota((CHUNK, LANES), 1) == head + i, grad_strength * strength * (1.0 - strength), 0.0
            )
            grads = [
                scales[0] * (grad_query - query * jnp.sum(grad_query * query, axis=-1, keepdims=True)),
                scales[1] * (grad_key - key * jnp.sum(grad_key * key, axis=-1, keepdims=True)),
                weighted,
            ]
            position = iota((CHUNK, 1), 0) + offset
            for kind in range(3):
                gate, total = gates[kind], raw[kind]
                grad_conv = grads[kind] * gate * (1.0 + total * (1.0 - gate))
                lane = (3 * i + kind) * LANES
                for tap in range(taps):
                    back = taps - 1 - tap
                    part = jnp.sum(grad_conv * taps_in[kind][tap], axis=0, keepdims=True)
                    spot = (i, kind, tap)
                    tap_sums[spot] = part if spot not in tap_sums else tap_sums[spot] + part
                    back_part = jnp.where(
                        position - back >= col, grad_conv * conv[tap : tap + 1, lane : lane + LANES], 0.0
                    )
                    where = pl.ds(HALO + offset - back, CHUNK)
                    grad_ext[where, lane : lane + LANES] += back_part
        logits[rows] += grad_logit
    grad_pre[...] = low(grad_ext[HALO:])
    before[0] = grad_ext[:HALO]
    tail[0] = grad_ext[length:]
    for i in range(heads):
        for kind in range(3):
            lane = (3 * i + kind) * LANES
            for tap in range(taps):
                conv_grad[0, tap : tap + 1, lane : lane + LANES] = tap_sums[i, kind, tap]


def mixer_backward(
    pre, logit, bias, halo, conv, col, row, grad_mixed, inv, upd, states, start, end, taps, first, heads_here, group
):
    seqs, length = col.shape[0], col.shape[1]
    steps = heads_here // group
    chunks = length // CHUNK
    wide = 3 * LANES * group
    rows = seqs * length

    def spec(*tail):
        return pl.BlockSpec((1, group) + tail, lambda s, h: (s, h) + (0,) * len(tail))

    last = logit.shape[1] // LANES - 1
    part = pl.BlockSpec((1, HALO, wide), lambda s, h: (s, 0, h))
    edge = jax.ShapeDtypeStruct((seqs, HALO, 3 * LANES * heads_here), jnp.float32)
    return pl.pallas_call(
        functools.partial(backward_kernel, taps, group, first),
        grid=(seqs, steps),
        in_specs=[
            pl.BlockSpec((length, wide), lambda s, h: (s, h)),
            pl.BlockSpec((length, LANES), lambda s, h: (s, last)),
            pl.BlockSpec((1, LANES), lambda s, h: (0, 0)),
            part,
            pl.BlockSpec((conv.shape[0], wide), lambda s, h: (0, h)),
            pl.BlockSpec((1, length, 1), lambda s, h: (s, 0, 0)),
            pl.BlockSpec((1, 1, length), lambda s, h: (s, 0, 0)),
            pl.BlockSpec((length, LANES * group), lambda s, h: (s, h)),
            spec(chunks, CHUNK, CHUNK),
            spec(chunks, CHUNK, 2 * LANES),
            spec(chunks, LANES, 2 * LANES),
            spec(LANES, LANES),
            spec(LANES, LANES),
        ],
        out_specs=[
            pl.BlockSpec((length, wide), lambda s, h: (s, h)),
            part,
            part,
            part,
            pl.BlockSpec((length, LANES), lambda s, h: (s, 0)),
        ],
        out_shape=[
            jax.ShapeDtypeStruct((rows, 3 * LANES * heads_here), jnp.bfloat16),
            edge,
            edge,
            edge,
            jax.ShapeDtypeStruct((rows, LANES), jnp.float32),
        ],
        scratch_shapes=[
            pltpu.VMEM((length + HALO, wide), jnp.float32),
            pltpu.VMEM((length + HALO, wide), jnp.float32),
        ],
        compiler_params=pltpu.CompilerParams(vmem_limit_bytes=VMEM_BYTES),
        cost_estimate=pl.CostEstimate(
            flops=60 * rows * heads_here * CHUNK * LANES, bytes_accessed=40 * rows * heads_here * LANES, transcendentals=0
        ),
    )(pre, logit, bias, halo, conv, col, row, grad_mixed, inv, upd, states, start, end)


def mixed_rows_of(own, carry, start):
    return own + mul_nn(carry, start)


def output_kernel(heads, own, carry, start, gain, out):
    for i in range(heads):
        lanes = slice(i * LANES, (i + 1) * LANES)
        mixed = mixed_rows_of(own[:, lanes], carry[:, lanes], start[0, i])
        scale = lax.rsqrt(jnp.mean(mixed * mixed, axis=-1, keepdims=True) + HEAD_FLOOR)
        out[:, lanes] = low(mixed * scale * gain[...])


def output_backward_kernel(heads, own, carry, start, gain, grad, out, across, gain_grad):
    total = jnp.zeros((1, LANES), jnp.float32)
    for i in range(heads):
        lanes = slice(i * LANES, (i + 1) * LANES)
        carried = carry[:, lanes]
        mixed = mixed_rows_of(own[:, lanes], carried, start[0, i])
        scale = lax.rsqrt(jnp.mean(mixed * mixed, axis=-1, keepdims=True) + HEAD_FLOOR)
        normed = mixed * scale
        upper = grad[:, lanes].astype(jnp.float32)
        total = total + jnp.sum(upper * normed, axis=0, keepdims=True)
        weighted = upper * gain[...]
        back = scale * (weighted - normed * jnp.mean(weighted * normed, axis=-1, keepdims=True))
        out[:, lanes] = low(back)
        across[0, i] = mul_tn(carried, back)
    gain_grad[0, 0] = total


def mixer_output(own, carry, start, gain, group):
    seqs, heads_here = start.shape[:2]
    rows = own.shape[0]
    length = rows // seqs
    flat = pl.BlockSpec((length, LANES * group), lambda s, h: (s, h))
    square = pl.BlockSpec((1, group, LANES, LANES), lambda s, h: (s, h, 0, 0))
    return pl.pallas_call(
        functools.partial(output_kernel, group),
        grid=(seqs, heads_here // group),
        in_specs=[flat, flat, square, pl.BlockSpec((1, LANES), lambda s, h: (0, 0))],
        out_specs=flat,
        out_shape=jax.ShapeDtypeStruct(own.shape, jnp.bfloat16),
        compiler_params=pltpu.CompilerParams(vmem_limit_bytes=VMEM_BYTES),
        cost_estimate=pl.CostEstimate(
            flops=2 * own.size * LANES, bytes_accessed=8 * own.size, transcendentals=0
        ),
    )(own, carry, start, gain)


def mixer_output_backward(own, carry, start, gain, grad, first, group):
    seqs, heads_here = start.shape[:2]
    rows = own.shape[0]
    length = rows // seqs
    steps = heads_here // group
    flat = pl.BlockSpec((length, LANES * group), lambda s, h: (s, h))
    base = first // group
    shifted = pl.BlockSpec((length, LANES * group), lambda s, h: (s, base + h))
    square = pl.BlockSpec((1, group, LANES, LANES), lambda s, h: (s, h, 0, 0))
    return pl.pallas_call(
        functools.partial(output_backward_kernel, group),
        grid=(seqs, steps),
        in_specs=[flat, flat, square, pl.BlockSpec((1, LANES), lambda s, h: (0, 0)), shifted],
        out_specs=[flat, square, pl.BlockSpec((1, 1, 1, LANES), lambda s, h: (s, h, 0, 0))],
        out_shape=[
            jax.ShapeDtypeStruct(own.shape, jnp.bfloat16),
            jax.ShapeDtypeStruct(start.shape, jnp.float32),
            jax.ShapeDtypeStruct((seqs, steps, 1, LANES), jnp.float32),
        ],
        compiler_params=pltpu.CompilerParams(vmem_limit_bytes=VMEM_BYTES),
        cost_estimate=pl.CostEstimate(
            flops=4 * own.size * LANES, bytes_accessed=12 * own.size, transcendentals=0
        ),
    )(own, carry, start, gain, grad)


def ffn_kernel(rows, grads, gate_w, up_w, down_w, hidden, grad_gate, grad_up, grad_rows, result):
    gate = mul_nt(rows[...], gate_w[...])
    up = mul_nt(rows[...], up_w[...])
    grad_hidden = mul_nt(grads[...], down_w[...])
    sigmoid = jax.nn.sigmoid(gate)
    active = gate * sigmoid
    kept = low(active * up)
    back_gate = low(grad_hidden * up * sigmoid * (1.0 + gate * (1.0 - sigmoid)))
    back_up = low(grad_hidden * active)
    hidden[...] = kept
    grad_gate[...] = back_gate
    grad_up[...] = back_up
    grad_rows[...] = low(mul_nn(back_gate, gate_w[...]) + mul_nn(back_up, up_w[...]))
    result[...] = low(mul_nn(kept, down_w[...]))


def ffn_both(rows, grads, weights):
    count, width = rows.shape
    units = weights.shape[0] // 3
    tile = min(256, count)
    wide = pl.BlockSpec((tile, width), lambda i: (i, 0))
    narrow = pl.BlockSpec((tile, units), lambda i: (i, 0))

    def third(index):
        return pl.BlockSpec((units, width), lambda i: (index, 0))

    return pl.pallas_call(
        ffn_kernel,
        grid=(count // tile,),
        in_specs=[wide, wide, third(0), third(1), third(2)],
        out_specs=[narrow, narrow, narrow, wide, wide],
        out_shape=[jax.ShapeDtypeStruct((count, units), jnp.bfloat16)] * 3
        + [jax.ShapeDtypeStruct((count, width), jnp.bfloat16)] * 2,
        compiler_params=pltpu.CompilerParams(vmem_limit_bytes=VMEM_BYTES),
        cost_estimate=pl.CostEstimate(
            flops=12 * count * width * units, bytes_accessed=8 * count * width + 6 * units * width, transcendentals=0
        ),
    )(rows, grads, weights, weights, weights)


def flip(value, axis, bit):
    devices = range(lax.axis_size(axis))
    return lax.ppermute(value, axis, [(i, i ^ bit) for i in devices])


def shift(value, axis, distance):
    count = lax.axis_size(axis)
    return lax.ppermute(value, axis, [(i, (i + distance) % count) for i in range(count)])


def from_behind(block, axis, distance):
    devices = range(lax.axis_size(axis))
    route = [(i - distance, i) for i in devices if i - distance in devices]
    return lax.ppermute(block, axis, route)


def tie(value, *earlier):
    return lax.optimization_barrier((value,) + earlier)[0]


def put(buffer, piece, *start):
    return lax.dynamic_update_slice(buffer, piece, start)


def wide(value):
    return value.astype(jnp.float32)


def features(rows):
    count, width = rows.shape
    squares, lines = lax.axis_size("ctx"), lax.axis_size("fsdp")
    part = width // (squares * lines)
    order = rows.reshape(count, squares, lines, part).transpose(0, 2, 1, 3).reshape(count, width)
    twice = jnp.concatenate([order, order], axis=1)
    return lax.dynamic_slice_in_dim(twice, lax.axis_index("fsdp") * squares * part, width, 1)


def features_back(rows):
    count, width = rows.shape
    squares, lines = lax.axis_size("ctx"), lax.axis_size("fsdp")
    part = width // (squares * lines)
    twice = jnp.concatenate([rows, rows], axis=1)
    turn = (lines - lax.axis_index("fsdp")) % lines
    order = lax.dynamic_slice_in_dim(twice, turn * squares * part, width, 1)
    return order.reshape(count, lines, squares, part).transpose(0, 2, 1, 3).reshape(count, width)


def gather_line(shard):
    count = lax.axis_size("fsdp")
    return jnp.stack([shard] + [shift(shard, "fsdp", count - r) for r in range(1, count)])


class Square:
    def __init__(self, own):
        self.own = own
        self.half = own.shape[0] // 2
        self.beside = flip(own, "ctx", 1)
        self.across = flip(own, "ctx", 2)

    def forward(self, *earlier):
        upper = self.beside[: self.half]
        lower = self.across[self.half :]
        if earlier:
            upper, lower = lax.optimization_barrier((upper, lower) + earlier)[:2]
        self.upper = flip(upper, "ctx", 2)
        self.lower = flip(lower, "ctx", 1)
        return self

    def done(self):
        return (self.upper, self.lower)

    def weights(self):
        lines, rows, columns = self.own.shape
        place = lax.axis_index("ctx")
        buffer = jnp.zeros((lines, 4, rows, columns), self.own.dtype)
        buffer = put(buffer, self.own[:, None], 0, place, 0, 0)
        buffer = put(buffer, self.beside[:, None], 0, place ^ 1, 0, 0)
        buffer = put(buffer, self.across[:, None], 0, place ^ 2, 0, 0)
        buffer = put(buffer, self.upper[:, None], 0, place ^ 3, 0, 0)
        buffer = put(buffer, self.lower[:, None], self.half, place ^ 3, 0, 0)
        return buffer.reshape(4 * lines * rows, columns)

    def rows(self):
        parts = [self.own, self.beside, self.across, self.upper, self.lower]
        if lax.axis_size("tp") == 2:
            return jnp.concatenate(parts + [flip(part, "tp", 1) for part in parts], axis=0)
        return lax.all_gather(jnp.concatenate(parts, axis=0), "tp", axis=0, tiled=True)


def square_sum(blocks):
    from_across = flip(low(blocks(3, 0)), "ctx", 2)
    from_beside = flip(low(blocks(3, 1)), "ctx", 1)
    beside_down = flip(low(blocks(1, 1)), "ctx", 1)
    across_up = flip(low(blocks(2, 0)), "ctx", 2)
    beside_up = flip(low(blocks(1, 0) + wide(from_across)), "ctx", 1)
    across_down = flip(low(blocks(2, 1) + wide(from_beside)), "ctx", 2)
    upper = blocks(0, 0) + wide(beside_up) + wide(across_up)
    lower = blocks(0, 1) + wide(beside_down) + wide(across_down)
    return jnp.concatenate([upper, lower], axis=0)


def collect_rows(partial):
    count = lax.axis_size("tp")
    size = partial.shape[0] // count
    if count == 2:
        total = wide(partial[:size]) + wide(flip(partial[size:], "tp", 1))
    else:
        total = wide(lax.psum_scatter(partial, "tp", scatter_dimension=0, tiled=True))
    half = size // 8
    return square_sum(lambda bit, low_half: total[(2 * bit + low_half) * half :][:half])


def neighbour_columns(rows):
    lines = lax.axis_size("fsdp")
    count, width = rows.shape
    split = rows.reshape(count, lines, 4, width // (4 * lines))
    place = lax.axis_index("ctx")
    return [
        lax.dynamic_index_in_dim(split, place ^ bit, 2, keepdims=False).reshape(count, width // 4)
        for bit in range(4)
    ]


def line_sum(own):
    total = own[0]
    for distance in range(1, own.shape[0]):
        total = total + wide(shift(low(own[distance]), "fsdp", distance))
    return total


def outer_scatter(columns, grads):
    half = columns[0].shape[1] // 2

    def block(bit, low_half):
        return outer_rows(columns[bit][:, low_half * half : (low_half + 1) * half], grads)

    own = square_sum(block)
    lines = lax.axis_size("fsdp")
    return line_sum(own.reshape(lines, own.shape[0] // lines, own.shape[1]))


def swap_square(pieces):
    place = lax.axis_index("ctx")
    arrived = jnp.zeros(pieces.shape, jnp.bfloat16)
    for bit in range(4):
        piece = low(lax.dynamic_index_in_dim(pieces, place ^ bit, 0))
        arrived = put(arrived, flip(piece, "ctx", bit) if bit else piece, place ^ bit, 0, 0)
    return arrived


def butterfly(value, axes):
    for axis in axes:
        count, bit = lax.axis_size(axis), 1
        while bit < count:
            value = value + flip(value, axis, bit)
            bit *= 2
    return value


def rms_scale(values, floor_value):
    return lax.rsqrt(jnp.mean(values * values, axis=-1, keepdims=True) + floor_value)


def norm_backward(grad_normed, inputs, scale, gain):
    normed = inputs * scale
    weighted = grad_normed * gain
    return (
        scale * (weighted - normed * jnp.mean(weighted * normed, axis=-1, keepdims=True)),
        normed,
    )


def times(left, right):
    return jnp.dot(left, right, preferred_element_type=jnp.float32)


def times_transposed(left, right):
    return lax.dot_general(
        left, right, (((1,), (1,)), ((), ())), preferred_element_type=jnp.float32
    )


def outer_rows(left, right):
    return lax.dot_general(
        left, right, (((0,), (0,)), ((), ())), preferred_element_type=jnp.float32
    )


def rows_mine(rows):
    count = rows.shape[1] // lax.axis_size("tp")
    return lax.dynamic_slice_in_dim(rows, lax.axis_index("tp") * count, count, 1)


def rows_scatter(partial):
    if lax.axis_size("tp") != 2:
        return wide(lax.psum_scatter(partial, "tp", scatter_dimension=1, tiled=True))
    count = partial.shape[1] // 2
    other = lax.dynamic_slice_in_dim(partial, (1 - lax.axis_index("tp")) * count, count, 1)
    return wide(rows_mine(partial)) + wide(flip(other, "tp", 1))


def rows_full(mine):
    if lax.axis_size("tp") != 2:
        return lax.all_gather(mine, "tp", axis=1, tiled=True)
    other = flip(mine, "tp", 1)
    pair = jnp.concatenate([mine, other, mine], axis=1)
    count = mine.shape[1]
    return lax.dynamic_slice_in_dim(pair, lax.axis_index("tp") * count, 2 * count, 1)


def by_head(parts):
    lead = parts[0].shape[:-1]
    split = [part.reshape(lead + (-1, LANES)) for part in parts]
    return jnp.stack(split, axis=-2).reshape(lead + (-1,))


def by_kind(joined):
    lead = joined.shape[:-1]
    split = joined.reshape(lead + (-1, 3, LANES))
    return [split[..., kind, :].reshape(lead + (-1,)) for kind in range(3)]


def pass_states(own, transfer, forward):
    rule = "shij,shjk->shik" if forward == 1 else "shji,shjk->shik"
    leaving = own
    entered = low(jnp.zeros_like(own))
    for repeat in range(lax.axis_size("ctx") - 1):
        entered = from_behind(low(leaving), "ctx", forward)
        leaving = own + jnp.einsum(rule, transfer, entered, preferred_element_type=jnp.float32)
    return wide(entered)


def local(
    block_input,
    doc_start,
    gain_mix,
    query_weight,
    key_weight,
    value_weight,
    beta_weight,
    beta_bias,
    conv_weight,
    gain_o,
    out_weight,
    gain_ffn,
    gate_weight,
    up_weight,
    down_weight,
    out_grad,
):
    seq_count, local_len, width = block_input.shape
    row_count = seq_count * local_len
    heads_here = beta_weight.shape[1]
    taps = conv_weight.shape[1]
    parts = 2 if heads_here % 2 == 0 else 1
    part_heads = heads_here // parts
    group = 2 if part_heads % 2 == 0 else 1
    part_cols = 3 * part_heads * LANES
    spare = LANES - heads_here
    units_here = gate_weight.shape[1]
    shard_rows = gate_weight.shape[0]
    seqs = range(seq_count)

    joined = by_head([low(query_weight), low(key_weight), low(value_weight)])
    shards = [joined[:, p * part_cols : (p + 1) * part_cols] for p in range(parts)]
    shards[0] = jnp.concatenate([shards[0], jnp.pad(low(beta_weight), ((0, 0), (0, spare)))], axis=1)
    shards.append(low(out_weight).T)
    lines = []
    for shard in shards:
        lines.append(gather_line(tie(shard, lines[-1]) if lines else shard))
    units = units_here // 4
    pieces = jnp.stack([low(gate_weight).T, low(up_weight).T, low(down_weight)])
    pieces = pieces.reshape(3, 4, units, shard_rows).transpose(1, 0, 2, 3)
    ffn_line = swap_square(pieces.reshape(4, 3 * units, shard_rows))
    ffn_line = ffn_line.transpose(1, 0, 2).reshape(3 * units, 4 * shard_rows)
    ffn_parts = gather_line(tie(ffn_line, lines[-1]))

    first_pos = lax.axis_index("ctx") * local_len
    starts = doc_start - first_pos
    col, row = starts[:, :, None], starts[:, None, :]
    conv = by_head([conv_weight[0], conv_weight[1], conv_weight[2]])
    bias = jnp.pad(beta_bias, (0, spare))[None]
    gain_head = gain_o[None]
    gain_mix, gain_ffn = features(gain_mix[None]), features(gain_ffn[None])

    tokens = features(block_input.reshape(row_count, width))
    inputs = wide(tokens)
    normed_mix = low(inputs * rms_scale(inputs, EPSILON) * gain_mix)
    inputs_mine = wide(rows_mine(tokens.reshape(seq_count, local_len, width)))
    grads_mine = rows_mine(features(out_grad.reshape(row_count, width)).reshape(seq_count, local_len, width))

    square = Square(lines[0]).forward()
    mix_full, kept, pre = [], [], []
    for p in range(parts):
        mix_full.append(square.weights())
        square = Square(tie(lines[p + 1], *square.done()))
        if p == parts - 1:
            grad_squares = [Square(tie(grads_mine[0], mix_full[-1]))]
        pre.append(times(normed_mix, mix_full[p]))
        ends = pre[p].reshape(seq_count, local_len, -1)[:, local_len - HALO :, :part_cols]
        halo = from_behind(ends, "ctx", 1)
        convs = conv[:, p * part_cols : (p + 1) * part_cols]
        kept.append(
            [halo, convs]
            + list(
                mixer_forward(
                    pre[p], pre[0], bias, halo, convs, col, row, taps, p * part_heads, part_heads, group
                )
            )
        )
        square.forward(kept[p][2])
    grad_squares[0].forward(kept[-1][2])
    for s in seqs[1:]:
        grad_squares.append(Square(tie(grads_mine[s], *grad_squares[-1].done())).forward())
    out_full = square.weights()

    entered, transfers, mixed_rows = [], [], []
    for _, _, own, carry, final, _, _, _ in kept:
        transfers.append(low(final[..., LANES:]))
        entered.append(pass_states(final[..., :LANES], transfers[-1], 1))
        mixed_rows.append(mixer_output(own, carry, entered[-1], gain_head, group))
    mixed_rows = jnp.concatenate(mixed_rows, axis=1)

    residual, scale_ffn, normed_ffn, squares = [], [], [], []
    for s in seqs:
        branch = times_transposed(mixed_rows[s * local_len : (s + 1) * local_len], out_full)
        residual.append(inputs_mine[s] + rows_scatter(low(branch)[None])[0])
        scale_ffn.append(rms_scale(residual[s], EPSILON))
        squares.append(Square(low(residual[s] * scale_ffn[s] * gain_ffn)).forward())
    ffn_parts = tie(ffn_parts, squares[0].own)
    ffn_full = jnp.concatenate([ffn_parts[i] for i in range(ffn_parts.shape[0])], axis=1)
    ffn_rows, grad_rows, ffn_out = [], [], []
    for s in seqs:
        ffn_rows.append(squares[s].rows())
        grad_rows.append(grad_squares[s].rows())
        ffn_out.append(ffn_both(ffn_rows[s], grad_rows[s], ffn_full))

    grad_residual, grad_branch, gain_ffn_part = [], [], 0.0
    for s in seqs:
        grad_normed = collect_rows(ffn_out[s][3])
        back_ffn, unit_ffn = norm_backward(grad_normed, residual[s], scale_ffn[s], gain_ffn)
        grad_residual.append(wide(grads_mine[s]) + back_ffn)
        gain_ffn_part = gain_ffn_part + jnp.sum(grad_normed * unit_ffn, axis=0)
        grad_branch.append(rows_full(low(grad_residual[s])[None])[0])
    grad_branch = jnp.concatenate(grad_branch, axis=0)
    held = []
    for s in seqs:
        total = collect_rows(tie(ffn_out[s][4], grad_branch))
        held.append(low(residual[s] + total))
    block_output = features_back(rows_full(jnp.stack(held)).reshape(row_count, width))

    grad_heads = times(grad_branch, out_full)
    backs, acrosses, gain_o_part = [], [], 0.0
    for p in range(parts):
        _, _, own, carry, _, _, _, _ = kept[p]
        back, across, gain_part = mixer_output_backward(
            own, carry, entered[p], gain_head, grad_heads, p * part_heads, group
        )
        backs.append(back)
        acrosses.append(across)
        gain_o_part = gain_o_part + jnp.sum(gain_part, axis=(0, 1, 2))
    grad_end = pass_states(jnp.concatenate(acrosses, axis=1), jnp.concatenate(transfers, axis=1), -1)

    sums = []
    for kind, sources in ((1, ffn_rows), (2, ffn_rows), (0, grad_rows)):
        total = 0.0
        for s in seqs:
            total = total + outer_rows(ffn_out[s][kind], sources[s])
        count = lax.axis_size("fsdp")
        sums.append(line_sum(jnp.stack([total[:, i * 4 * shard_rows : (i + 1) * 4 * shard_rows] for i in range(count)])))
    sums = jnp.stack(sums).reshape(3 * units, 4, shard_rows).transpose(1, 0, 2)
    arrived = swap_square(sums).reshape(4, 3, units, shard_rows)
    gate_grad, up_grad, down_grad = (wide(arrived[:, i].reshape(units_here, shard_rows)) for i in range(3))

    out_grad_w = outer_scatter(neighbour_columns(grad_branch), mixed_rows).T

    columns = neighbour_columns(normed_mix)
    mix_back, mix_grads, conv_parts = 0.0, [None] * parts, [None] * parts
    logits = 0.0
    for p in reversed(range(parts)):
        halo, convs, own, carry, final, inverses, updates, states = kept[p]
        heads = slice(p * part_heads, (p + 1) * part_heads)
        grad_mix, tail, before, conv_parts[p], logit = mixer_backward(
            pre[p], pre[0], bias, halo, convs, col, row, backs[p], inverses, updates, states,
            entered[p], grad_end[:, heads], taps, p * part_heads, part_heads, group,
        )
        logits = logits + logit
        tail = low(tail + from_behind(before, "ctx", -1))
        grad_mix = put(grad_mix.reshape(seq_count, local_len, -1), tail, 0, local_len - HALO, 0)
        grad_mix = grad_mix.reshape(row_count, -1)
        if p == 0:
            grad_mix = jnp.concatenate([grad_mix, low(logits)], axis=1)
        mix_back = mix_back + times_transposed(grad_mix, mix_full[p])
        mix_grads[p] = outer_scatter(columns, grad_mix)
    joined = jnp.concatenate([grad[:, :part_cols] for grad in mix_grads], axis=1)
    query_grad, key_grad, value_grad = by_kind(joined)
    beta_grad = mix_grads[0][:, part_cols : part_cols + heads_here]

    mix_back = rows_scatter(low(mix_back).reshape(seq_count, local_len, width))
    back_mix, unit_mix = norm_backward(mix_back, inputs_mine, rms_scale(inputs_mine, EPSILON), gain_mix)
    input_held = low(jnp.stack(grad_residual) + back_mix)
    input_grad = features_back(rows_full(input_held).reshape(row_count, width))
    gain_mix_part = jnp.sum(mix_back * unit_mix, axis=(0, 1))

    gains = features_back(jnp.stack([gain_mix_part, gain_ffn_part]))
    small = butterfly(
        jnp.concatenate([gains[0], gains[1], gain_o_part]), ("tp", "ctx", "fsdp")
    )
    gain_mix_grad, gain_ffn_grad, gain_o_grad = jnp.split(small, [width, 2 * width])
    conv_cols = jnp.concatenate([jnp.sum(part, axis=0)[:taps] for part in conv_parts], axis=1)
    sums = jnp.concatenate([conv_cols.reshape(-1), jnp.sum(logits, axis=0)])
    sums = butterfly(sums, ("ctx", "fsdp"))
    conv_grad = jnp.stack(by_kind(sums[:-LANES].reshape(taps, -1)))
    bias_grad = sums[sums.shape[0] - LANES :][:heads_here]
    return (
        block_output.reshape(seq_count, local_len, width),
        input_grad.reshape(seq_count, local_len, width),
        gain_mix_grad,
        query_grad,
        key_grad,
        value_grad,
        beta_grad,
        bias_grad,
        conv_grad,
        gain_o_grad,
        out_grad_w,
        gain_ffn_grad,
        gate_grad.T,
        up_grad.T,
        down_grad,
    )


def solution(mesh):
    placed = (
        P("fsdp", "ctx", None),
        P("fsdp", "ctx"),
        P(),
        P(("ctx", "fsdp"), "tp"),
        P(("ctx", "fsdp"), "tp"),
        P(("ctx", "fsdp"), "tp"),
        P(("ctx", "fsdp"), "tp"),
        P("tp"),
        P(None, None, "tp"),
        P(),
        P("tp", ("ctx", "fsdp")),
        P(),
        P(("ctx", "fsdp"), "tp"),
        P(("ctx", "fsdp"), "tp"),
        P("tp", ("ctx", "fsdp")),
        P("fsdp", "ctx", None),
    )
    return jax.shard_map(
        local,
        mesh=mesh,
        in_specs=placed,
        out_specs=(
            P("fsdp", "ctx", None),
            P("fsdp", "ctx", None),
            P(),
            P(("ctx", "fsdp"), "tp"),
            P(("ctx", "fsdp"), "tp"),
            P(("ctx", "fsdp"), "tp"),
            P(("ctx", "fsdp"), "tp"),
            P("tp"),
            P(None, None, "tp"),
            P(),
            P("tp", ("ctx", "fsdp")),
            P(),
            P(("ctx", "fsdp"), "tp"),
            P(("ctx", "fsdp"), "tp"),
            P("tp", ("ctx", "fsdp")),
        ),
        check_vma=False,
    )
```

```python
import functools
import math
import jax
import jax.numpy as jnp
from jax import lax
from jax.experimental import pallas as pl
from jax.experimental.pallas import tpu as pltpu
from jax.sharding import PartitionSpec as P

LANES = 128
CHUNK = 128
HALO = 8
EPSILON = 1e-06
HEAD_FLOOR = 0.01
VMEM_BYTES = 60 * 1024 * 1024


def low(value):
    return value.astype(jnp.bfloat16)


def mul_nn(left, right):
    return lax.dot_general(low(left), low(right), (((1,), (0,)), ((), ())), preferred_element_type=jnp.float32)


def mul_nt(left, right):
    return lax.dot_general(low(left), low(right), (((1,), (1,)), ((), ())), preferred_element_type=jnp.float32)


def mul_tn(left, right):
    return lax.dot_general(low(left), low(right), (((0,), (0,)), ((), ())), preferred_element_type=jnp.float32)


def iota(shape, axis):
    return lax.broadcasted_iota(jnp.int32, shape, axis)


def chunk_masks(col, row, first):
    size = col.shape[0]
    same = col == row
    order, other = iota((size, size), 0), iota((size, size), 1)
    upto = same & (order >= other)
    below = same & (order > other)
    carried = (col < first).astype(jnp.float32)
    last = (col == row[:, size - 1 :]).astype(jnp.float32)
    keep = (row[:, size - 1 :] < first).astype(jnp.float32)
    return upto, below, carried, last, keep


def invert_units(systems):
    size = systems[0].shape[0]
    order, other = iota((size, size), 0), iota((size, size), 1)
    identity = (order == other).astype(jnp.float32)
    span = 1
    found = None
    while span < size:
        pair = (order // (2 * span) == other // (2 * span)) & (order // span != other // span)
        parts = [jnp.where(pair, system, 0.0) for system in systems]
        if found is None:
            found = [identity - part for part in parts]
        else:
            right = [mul_nn(part, value) for part, value in zip(parts, found)]
            found = [value - mul_nn(value, part) for value, part in zip(found, right)]
        span *= 2
    return found


def conv_rows(ext, conv, col, offset, size, lane, taps):
    total = None
    moved = []
    position = iota((size, 1), 0) + offset
    for tap in range(taps):
        back = taps - 1 - tap
        values = ext[pl.ds(HALO + offset - back, size), lane : lane + LANES]
        values = jnp.where(position - back >= col, values, 0.0)
        moved.append(values)
        term = conv[tap : tap + 1, lane : lane + LANES] * values
        total = term if total is None else total + term
    return total, moved


def unit(values):
    return values * lax.rsqrt(jnp.sum(values * values, axis=-1, keepdims=True) + EPSILON)


def head_column(values, head):
    return jnp.sum(jnp.where(iota(values.shape, 1) == head, values, 0.0), axis=-1, keepdims=True)


def forward_kernel(taps, heads, first, pre, beta, bias, halo, conv, col_ref, row_ref, own, carry, final, inv, upd, states, ext):
    length = pre.shape[0]
    ext[:HALO] = halo[0]
    ext[HALO:] = pre[...]
    head = first + pl.program_id(1) * heads
    jobs = [(i, j) for j in range(length // CHUNK) for i in range(heads)]
    data = {}
    for j in range(length // CHUNK):
        rows = pl.ds(j * CHUNK, CHUNK)
        col, row = col_ref[0, rows], row_ref[0, :, rows]
        masks = chunk_masks(col, row, j * CHUNK)
        strengths = jax.nn.sigmoid(beta[rows] + bias[...])
        for i in range(heads):
            acts = []
            for kind in range(3):
                total, _ = conv_rows(ext, conv, col, j * CHUNK, CHUNK, (3 * i + kind) * LANES, taps)
                acts.append(total * jax.nn.sigmoid(total))
            query, key, value = unit(acts[0]), unit(acts[1]), acts[2]
            strength = head_column(strengths, head + i)
            grams = mul_nt(jnp.concatenate([low(key), low(query)], axis=0), key)
            system = jnp.where(masks[1], strength * grams[:CHUNK], 0.0)
            scores = low(jnp.where(masks[0], grams[CHUNK:], 0.0))
            data[i, j] = (low(query), low(key), value, strength, scores, masks, system)
    inverses = dict(zip(jobs, invert_units([data[job][6] for job in jobs])))
    for i in range(heads):
        state = jnp.concatenate(
            [
                jnp.zeros((LANES, LANES), jnp.float32),
                (iota((LANES, LANES), 0) == iota((LANES, LANES), 1)).astype(jnp.float32),
            ],
            axis=1,
        )
        final[0, i] = state
    for j in range(length // CHUNK):
        rows = pl.ds(j * CHUNK, CHUNK)
        for i in range(heads):
            query, key, value, strength, scores, masks, _ = data[i, j]
            _, _, carried, last, keep = masks
            inverse = low(inverses[i, j])
            state = final[0, i]
            state_low = low(state)
            read = mul_nn(jnp.concatenate([key, query], axis=0), state_low)
            wide = jnp.concatenate([value, jnp.zeros_like(value)], axis=1)
            targets = strength * (wide - carried * read[:CHUNK])
            update = low(mul_nn(inverse, targets))
            result = carried * read[CHUNK:] + mul_nn(scores, update)
            final[0, i] = keep * state + mul_tn(key * low(last), update)
            lanes = slice(i * LANES, (i + 1) * LANES)
            own[rows, lanes] = result[:, :LANES]
            carry[rows, lanes] = low(result[:, LANES:])
            inv[0, i, j] = inverse
            upd[0, i, j] = update
            states[0, i, j] = state_low


def mixer_forward(pre, logit, bias, halo, conv, col, row, taps, first, heads_here, group):
    seqs, length = col.shape[0], col.shape[1]
    steps = heads_here // group
    chunks = length // CHUNK
    wide = 3 * LANES * group
    rows = seqs * length

    def tile(*tail, kind):
        return jax.ShapeDtypeStruct((seqs, heads_here) + tail, kind)

    def spec(*tail):
        return pl.BlockSpec((1, group) + tail, lambda s, h: (s, h) + (0,) * len(tail))

    flat = pl.BlockSpec((length, LANES * group), lambda s, h: (s, h))
    last = logit.shape[1] // LANES - 1
    return pl.pallas_call(
        functools.partial(forward_kernel, taps, group, first),
        grid=(seqs, steps),
        in_specs=[
            pl.BlockSpec((length, wide), lambda s, h: (s, h)),
            pl.BlockSpec((length, LANES), lambda s, h: (s, last)),
            pl.BlockSpec((1, LANES), lambda s, h: (0, 0)),
            pl.BlockSpec((1, HALO, wide), lambda s, h: (s, 0, h)),
            pl.BlockSpec((conv.shape[0], wide), lambda s, h: (0, h)),
            pl.BlockSpec((1, length, 1), lambda s, h: (s, 0, 0)),
            pl.BlockSpec((1, 1, length), lambda s, h: (s, 0, 0)),
        ],
        out_specs=[
            flat,
            flat,
            spec(LANES, 2 * LANES),
            spec(chunks, CHUNK, CHUNK),
            spec(chunks, CHUNK, 2 * LANES),
            spec(chunks, LANES, 2 * LANES),
        ],
        out_shape=[
            jax.ShapeDtypeStruct((rows, heads_here * LANES), jnp.float32),
            jax.ShapeDtypeStruct((rows, heads_here * LANES), jnp.bfloat16),
            tile(LANES, 2 * LANES, kind=jnp.float32),
            tile(chunks, CHUNK, CHUNK, kind=jnp.bfloat16),
            tile(chunks, CHUNK, 2 * LANES, kind=jnp.bfloat16),
            tile(chunks, LANES, 2 * LANES, kind=jnp.bfloat16),
        ],
        scratch_shapes=[pltpu.VMEM((length + HALO, wide), jnp.float32)],
        compiler_params=pltpu.CompilerParams(vmem_limit_bytes=VMEM_BYTES),
        cost_estimate=pl.CostEstimate(
            flops=60 * rows * heads_here * CHUNK * LANES, bytes_accessed=40 * rows * heads_here * LANES, transcendentals=0
        ),
    )(pre, logit, bias, halo, conv, col, row)


def backward_kernel(
    taps, heads, first, pre, beta, bias, halo, conv, col_ref, row_ref, grad_ref, inv, upd, states, start, end,
    grad_pre, tail, before, conv_grad, logits, ext, grad_ext,
):
    length = pre.shape[0]
    step = pl.program_id(1)
    head = first + step * heads
    ext[:HALO] = halo[0]
    ext[HALO:] = pre[...]
    grad_ext[...] = jnp.zeros_like(grad_ext)

    @pl.when(step == 0)
    def _():
        logits[...] = jnp.zeros_like(logits)

    grad_states = [end[0, i] for i in range(heads)]
    entry = [low(start[0, i]) for i in range(heads)]
    tap_sums = {}
    for j in reversed(range(length // CHUNK)):
        offset = j * CHUNK
        rows = pl.ds(offset, CHUNK)
        col, row = col_ref[0, rows], row_ref[0, :, rows]
        upto, below, carried, last, keep = chunk_masks(col, row, offset)
        strengths = jax.nn.sigmoid(beta[rows] + bias[...])
        grad_logit = jnp.zeros((CHUNK, LANES), jnp.float32)
        for i in range(heads):
            raw, taps_in = [], []
            for kind in range(3):
                total, moved = conv_rows(ext, conv, col, offset, CHUNK, (3 * i + kind) * LANES, taps)
                raw.append(total)
                taps_in.append(moved)
            gates = [jax.nn.sigmoid(total) for total in raw]
            acts = [total * gate for total, gate in zip(raw, gates)]
            scales = [lax.rsqrt(jnp.sum(act * act, axis=-1, keepdims=True) + EPSILON) for act in acts[:2]]
            query, key, value = acts[0] * scales[0], acts[1] * scales[1], acts[2]
            strength = head_column(strengths, head + i)
            lanes = slice(i * LANES, (i + 1) * LANES)
            query_low, key_low = low(query), low(key)
            grams = mul_nt(jnp.concatenate([key_low, query_low], axis=0), key_low)
            gram = jnp.where(below, grams[:CHUNK], 0.0)
            scores = jnp.where(upto, grams[CHUNK:], 0.0)
            inverse = inv[0, i, j]
            update = upd[0, i, j]
            update = low(update[:, :LANES].astype(jnp.float32) + mul_nn(update[:, LANES:], entry[i]))
            state = states[0, i, j]
            state = low(state[:, :LANES].astype(jnp.float32) + mul_nn(state[:, LANES:], entry[i]))
            grad_out = grad_ref[rows, lanes]
            grad_state = grad_states[i]
            grad_state_low = low(grad_state)
            key_last = key_low * low(last)
            grad_update = mul_tn(scores, grad_out) + mul_nn(key_last, grad_state_low)
            grad_target = mul_tn(inverse, grad_update)
            weighted = strength * grad_target
            passed = carried * weighted
            out_carried = carried * grad_out.astype(jnp.float32)
            query_carried = query_low * low(carried)
            grad_states[i] = (
                keep * grad_state + mul_tn(query_carried, grad_out) - mul_tn(key_low, passed)
            )
            grad_scores = jnp.where(upto, mul_nt(grad_out, update), 0.0)
            grad_system = jnp.where(below, mul_nt(grad_target, update), 0.0)
            remainder = value - carried * mul_nn(key_low, state)
            grad_strength = jnp.sum(grad_target * remainder - grad_system * gram, axis=-1, keepdims=True)
            scaled = strength * grad_system
            from_state = mul_nt(jnp.concatenate([low(out_carried), low(passed)], axis=0), state)
            from_keys = mul_nn(jnp.concatenate([low(grad_scores), low(scaled + scaled.T)], axis=0), key_low)
            grad_query = from_state[:CHUNK] + from_keys[:CHUNK]
            grad_key = (
                mul_tn(grad_scores, query_low)
                + last * mul_nt(update, grad_state_low)
                - from_state[CHUNK:]
                - from_keys[CHUNK:]
            )
            grad_logit = grad_logit + jnp.where(
                iota((CHUNK, LANES), 1) == head + i, grad_strength * strength * (1.0 - strength), 0.0
            )
            grads = [
                scales[0] * (grad_query - query * jnp.sum(grad_query * query, axis=-1, keepdims=True)),
                scales[1] * (grad_key - key * jnp.sum(grad_key * key, axis=-1, keepdims=True)),
                weighted,
            ]
            position = iota((CHUNK, 1), 0) + offset
            for kind in range(3):
                gate, total = gates[kind], raw[kind]
                grad_conv = grads[kind] * gate * (1.0 + total * (1.0 - gate))
                lane = (3 * i + kind) * LANES
                for tap in range(taps):
                    back = taps - 1 - tap
                    part = jnp.sum(grad_conv * taps_in[kind][tap], axis=0, keepdims=True)
                    spot = (i, kind, tap)
                    tap_sums[spot] = part if spot not in tap_sums else tap_sums[spot] + part
                    back_part = jnp.where(
                        position - back >= col, grad_conv * conv[tap : tap + 1, lane : lane + LANES], 0.0
                    )
                    where = pl.ds(HALO + offset - back, CHUNK)
                    grad_ext[where, lane : lane + LANES] += back_part
        logits[rows] += grad_logit
    grad_pre[...] = low(grad_ext[HALO:])
    before[0] = grad_ext[:HALO]
    tail[0] = grad_ext[length:]
    for i in range(heads):
        for kind in range(3):
            lane = (3 * i + kind) * LANES
            for tap in range(taps):
                conv_grad[0, tap : tap + 1, lane : lane + LANES] = tap_sums[i, kind, tap]


def mixer_backward(
    pre, logit, bias, halo, conv, col, row, grad_mixed, inv, upd, states, start, end, taps, first, heads_here, group
):
    seqs, length = col.shape[0], col.shape[1]
    steps = heads_here // group
    chunks = length // CHUNK
    wide = 3 * LANES * group
    rows = seqs * length

    def spec(*tail):
        return pl.BlockSpec((1, group) + tail, lambda s, h: (s, h) + (0,) * len(tail))

    last = logit.shape[1] // LANES - 1
    part = pl.BlockSpec((1, HALO, wide), lambda s, h: (s, 0, h))
    edge = jax.ShapeDtypeStruct((seqs, HALO, 3 * LANES * heads_here), jnp.float32)
    return pl.pallas_call(
        functools.partial(backward_kernel, taps, group, first),
        grid=(seqs, steps),
        in_specs=[
            pl.BlockSpec((length, wide), lambda s, h: (s, h)),
            pl.BlockSpec((length, LANES), lambda s, h: (s, last)),
            pl.BlockSpec((1, LANES), lambda s, h: (0, 0)),
            part,
            pl.BlockSpec((conv.shape[0], wide), lambda s, h: (0, h)),
            pl.BlockSpec((1, length, 1), lambda s, h: (s, 0, 0)),
            pl.BlockSpec((1, 1, length), lambda s, h: (s, 0, 0)),
            pl.BlockSpec((length, LANES * group), lambda s, h: (s, h)),
            spec(chunks, CHUNK, CHUNK),
            spec(chunks, CHUNK, 2 * LANES),
            spec(chunks, LANES, 2 * LANES),
            spec(LANES, LANES),
            spec(LANES, LANES),
        ],
        out_specs=[
            pl.BlockSpec((length, wide), lambda s, h: (s, h)),
            part,
            part,
            part,
            pl.BlockSpec((length, LANES), lambda s, h: (s, 0)),
        ],
        out_shape=[
            jax.ShapeDtypeStruct((rows, 3 * LANES * heads_here), jnp.bfloat16),
            edge,
            edge,
            edge,
            jax.ShapeDtypeStruct((rows, LANES), jnp.float32),
        ],
        scratch_shapes=[
            pltpu.VMEM((length + HALO, wide), jnp.float32),
            pltpu.VMEM((length + HALO, wide), jnp.float32),
        ],
        compiler_params=pltpu.CompilerParams(vmem_limit_bytes=VMEM_BYTES),
        cost_estimate=pl.CostEstimate(
            flops=60 * rows * heads_here * CHUNK * LANES, bytes_accessed=40 * rows * heads_here * LANES, transcendentals=0
        ),
    )(pre, logit, bias, halo, conv, col, row, grad_mixed, inv, upd, states, start, end)


def mixed_rows_of(own, carry, start):
    return own + mul_nn(carry, start)


def output_kernel(heads, own, carry, start, gain, out):
    for i in range(heads):
        lanes = slice(i * LANES, (i + 1) * LANES)
        mixed = mixed_rows_of(own[:, lanes], carry[:, lanes], start[0, i])
        scale = lax.rsqrt(jnp.mean(mixed * mixed, axis=-1, keepdims=True) + HEAD_FLOOR)
        out[:, lanes] = low(mixed * scale * gain[...])


def output_backward_kernel(heads, own, carry, start, gain, grad, out, across, gain_grad):
    total = jnp.zeros((1, LANES), jnp.float32)
    for i in range(heads):
        lanes = slice(i * LANES, (i + 1) * LANES)
        carried = carry[:, lanes]
        mixed = mixed_rows_of(own[:, lanes], carried, start[0, i])
        scale = lax.rsqrt(jnp.mean(mixed * mixed, axis=-1, keepdims=True) + HEAD_FLOOR)
        normed = mixed * scale
        upper = grad[:, lanes].astype(jnp.float32)
        total = total + jnp.sum(upper * normed, axis=0, keepdims=True)
        weighted = upper * gain[...]
        back = scale * (weighted - normed * jnp.mean(weighted * normed, axis=-1, keepdims=True))
        out[:, lanes] = low(back)
        across[0, i] = mul_tn(carried, back)
    gain_grad[0, 0] = total


def mixer_output(own, carry, start, gain, group):
    seqs, heads_here = start.shape[:2]
    rows = own.shape[0]
    length = rows // seqs
    flat = pl.BlockSpec((length, LANES * group), lambda s, h: (s, h))
    square = pl.BlockSpec((1, group, LANES, LANES), lambda s, h: (s, h, 0, 0))
    return pl.pallas_call(
        functools.partial(output_kernel, group),
        grid=(seqs, heads_here // group),
        in_specs=[flat, flat, square, pl.BlockSpec((1, LANES), lambda s, h: (0, 0))],
        out_specs=flat,
        out_shape=jax.ShapeDtypeStruct(own.shape, jnp.bfloat16),
        compiler_params=pltpu.CompilerParams(vmem_limit_bytes=VMEM_BYTES),
        cost_estimate=pl.CostEstimate(
            flops=2 * own.size * LANES, bytes_accessed=8 * own.size, transcendentals=0
        ),
    )(own, carry, start, gain)


def mixer_output_backward(own, carry, start, gain, grad, first, group):
    seqs, heads_here = start.shape[:2]
    rows = own.shape[0]
    length = rows // seqs
    steps = heads_here // group
    flat = pl.BlockSpec((length, LANES * group), lambda s, h: (s, h))
    base = first // group
    shifted = pl.BlockSpec((length, LANES * group), lambda s, h: (s, base + h))
    square = pl.BlockSpec((1, group, LANES, LANES), lambda s, h: (s, h, 0, 0))
    return pl.pallas_call(
        functools.partial(output_backward_kernel, group),
        grid=(seqs, steps),
        in_specs=[flat, flat, square, pl.BlockSpec((1, LANES), lambda s, h: (0, 0)), shifted],
        out_specs=[flat, square, pl.BlockSpec((1, 1, 1, LANES), lambda s, h: (s, h, 0, 0))],
        out_shape=[
            jax.ShapeDtypeStruct(own.shape, jnp.bfloat16),
            jax.ShapeDtypeStruct(start.shape, jnp.float32),
            jax.ShapeDtypeStruct((seqs, steps, 1, LANES), jnp.float32),
        ],
        compiler_params=pltpu.CompilerParams(vmem_limit_bytes=VMEM_BYTES),
        cost_estimate=pl.CostEstimate(
            flops=4 * own.size * LANES, bytes_accessed=12 * own.size, transcendentals=0
        ),
    )(own, carry, start, gain, grad)


def ffn_kernel(rows, grads, gate_w, up_w, down_w, hidden, grad_gate, grad_up, grad_rows, result):
    gate = mul_nt(rows[...], gate_w[...])
    up = mul_nt(rows[...], up_w[...])
    grad_hidden = mul_nt(grads[...], down_w[...])
    sigmoid = jax.nn.sigmoid(gate)
    active = gate * sigmoid
    kept = low(active * up)
    back_gate = low(grad_hidden * up * sigmoid * (1.0 + gate * (1.0 - sigmoid)))
    back_up = low(grad_hidden * active)
    hidden[...] = kept
    grad_gate[...] = back_gate
    grad_up[...] = back_up
    grad_rows[...] = low(mul_nn(back_gate, gate_w[...]) + mul_nn(back_up, up_w[...]))
    result[...] = low(mul_nn(kept, down_w[...]))


def ffn_both(rows, grads, weights):
    count, width = rows.shape
    units = weights.shape[0] // 3
    tile = min(256, count)
    wide = pl.BlockSpec((tile, width), lambda i: (i, 0))
    narrow = pl.BlockSpec((tile, units), lambda i: (i, 0))

    def third(index):
        return pl.BlockSpec((units, width), lambda i: (index, 0))

    return pl.pallas_call(
        ffn_kernel,
        grid=(count // tile,),
        in_specs=[wide, wide, third(0), third(1), third(2)],
        out_specs=[narrow, narrow, narrow, wide, wide],
        out_shape=[jax.ShapeDtypeStruct((count, units), jnp.bfloat16)] * 3
        + [jax.ShapeDtypeStruct((count, width), jnp.bfloat16)] * 2,
        compiler_params=pltpu.CompilerParams(vmem_limit_bytes=VMEM_BYTES),
        cost_estimate=pl.CostEstimate(
            flops=12 * count * width * units, bytes_accessed=8 * count * width + 6 * units * width, transcendentals=0
        ),
    )(rows, grads, weights, weights, weights)


def place_kernel(count, targets, *refs):
    pieces, out, done = refs[:count], refs[count], refs[count + 1]
    copies = []
    for i, piece in enumerate(pieces):
        target = out.at[pl.ds(targets[i], piece.shape[0])]
        copies.append(pltpu.make_async_copy(piece, target, done.at[i]))
    for copy in copies:
        copy.start()
    for copy in copies:
        copy.wait()


def place_blocks(pieces, targets, blocks):
    count = len(pieces)
    shape = (blocks,) + pieces[0].shape[1:]
    anywhere = pl.BlockSpec(memory_space=pl.ANY)
    return pl.pallas_call(
        functools.partial(place_kernel, count),
        grid_spec=pltpu.PrefetchScalarGridSpec(
            num_scalar_prefetch=1,
            grid=(1,),
            in_specs=[anywhere] * count,
            out_specs=anywhere,
            scratch_shapes=[pltpu.SemaphoreType.DMA((count,))],
        ),
        out_shape=jax.ShapeDtypeStruct(shape, pieces[0].dtype),
        cost_estimate=pl.CostEstimate(flops=0, bytes_accessed=4 * math.prod(shape), transcendentals=0),
    )(jnp.stack(targets).astype(jnp.int32), *pieces)


def join_kernel(line, source, *refs):
    refs[-1][...] = source[...]


def columns_join(full, piece, line, lines, squares):
    rows, columns = piece.shape
    part = columns // squares
    known = [] if full is None else [full]
    return pl.pallas_call(
        join_kernel,
        grid_spec=pltpu.PrefetchScalarGridSpec(
            num_scalar_prefetch=1,
            grid=(squares,),
            in_specs=[pl.BlockSpec((rows, part), lambda j, line: (0, j))]
            + [pl.BlockSpec(memory_space=pl.ANY) for _ in known],
            out_specs=pl.BlockSpec((rows, part), lambda j, line: (0, j * lines + line[0])),
        ),
        out_shape=jax.ShapeDtypeStruct((rows, lines * columns), piece.dtype),
        input_output_aliases={2: 0} if known else {},
        compiler_params=pltpu.CompilerParams(vmem_limit_bytes=VMEM_BYTES),
        cost_estimate=pl.CostEstimate(flops=0, bytes_accessed=4 * piece.size, transcendentals=0),
    )(jnp.reshape(line, (1,)).astype(jnp.int32), piece, *known)


def columns_split_kernel(first, second, third, out):
    for i, ref in enumerate((first, second, third)):
        out[0, i] = low(ref[...])


def columns_split(arrays, lines, squares):
    rows, columns = arrays[0].shape
    part = columns // (lines * squares)
    return pl.pallas_call(
        columns_split_kernel,
        grid=(lines, squares),
        in_specs=[pl.BlockSpec((rows, part), lambda i, j: (0, j * lines + i))] * 3,
        out_specs=pl.BlockSpec((1, 3, rows, part), lambda i, j: (i, 0, 0, j)),
        out_shape=jax.ShapeDtypeStruct((lines, 3, rows, squares * part), jnp.bfloat16),
        compiler_params=pltpu.CompilerParams(vmem_limit_bytes=VMEM_BYTES),
        cost_estimate=pl.CostEstimate(flops=0, bytes_accessed=18 * arrays[0].size, transcendentals=0),
    )(*arrays)


def flip(value, axis, bit):
    devices = range(lax.axis_size(axis))
    return lax.ppermute(value, axis, [(i, i ^ bit) for i in devices])


def shift(value, axis, distance):
    count = lax.axis_size(axis)
    return lax.ppermute(value, axis, [(i, (i + distance) % count) for i in range(count)])


def from_behind(block, axis, distance):
    devices = range(lax.axis_size(axis))
    route = [(i - distance, i) for i in devices if i - distance in devices]
    return lax.ppermute(block, axis, route)


def tie(value, *earlier):
    return lax.optimization_barrier((value,) + earlier)[0]


def put(buffer, piece, *start):
    return lax.dynamic_update_slice(buffer, piece, start)


def wide(value):
    return value.astype(jnp.float32)


def gather_line(shard):
    count, place = lax.axis_size("fsdp"), lax.axis_index("fsdp")
    pieces = [shard[None]] + [shift(shard, "fsdp", d)[None] for d in range(1, count)]
    return place_blocks(pieces, [(place - d) % count for d in range(count)], count)


class Square:
    def __init__(self, own):
        self.own = own
        self.half = own.shape[0] // 2
        self.beside = flip(own, "ctx", 1)
        self.across = flip(own, "ctx", 2)

    def forward(self, *earlier):
        upper = self.beside[: self.half]
        lower = self.across[self.half :]
        if earlier:
            upper, lower = lax.optimization_barrier((upper, lower) + earlier)[:2]
        self.upper = flip(upper, "ctx", 2)
        self.lower = flip(lower, "ctx", 1)
        return self

    def done(self):
        return (self.upper, self.lower)

    def weights(self):
        lines, rows, columns = self.own.shape
        place = lax.axis_index("ctx")
        starts = [(place ^ bit) * lines for bit in range(4)]
        full = place_blocks(
            [self.own, self.beside, self.across, self.upper, self.lower],
            starts + [starts[3] + self.half],
            4 * lines,
        )
        return full.reshape(4 * lines * rows, columns)

    def far(self):
        return jnp.concatenate([self.upper, self.lower], axis=0)


def all_cores(rows):
    if lax.axis_size("tp") != 2:
        return lax.all_gather(rows, "tp", axis=0, tiled=True)
    return jnp.concatenate([rows, flip(rows, "tp", 1)], axis=0)


def core_sum(partial):
    if lax.axis_size("tp") != 2:
        return wide(lax.psum_scatter(partial, "tp", scatter_dimension=0, tiled=True))
    half = partial.shape[0] // 2
    return wide(partial[:half]) + wide(flip(partial[half:], "tp", 1))


def neighbour_columns(rows):
    width = rows.shape[1] // 4
    place = lax.axis_index("ctx")
    return [lax.dynamic_slice_in_dim(rows, (place ^ bit) * width, width, 1) for bit in range(4)]


def line_sum(own):
    count, place = own.shape[0], lax.axis_index("fsdp")
    total = lax.dynamic_index_in_dim(own, place, 0, keepdims=False)
    for distance in range(1, count):
        piece = lax.dynamic_index_in_dim(own, (place + distance) % count, 0, keepdims=False)
        total = total + wide(shift(low(piece), "fsdp", distance))
    return total


class Scatter:
    def __init__(self, columns, grads):
        self.columns, self.grads = columns, grads
        self.half = columns[0].shape[1] // 2
        self.sent = [low(self.block(*which)) for which in ((3, 0), (3, 1), (1, 1), (2, 0))]
        self.first = tuple(flip(part, "ctx", bit) for part, bit in zip(self.sent, (2, 1, 1, 2)))

    def block(self, bit, lower):
        return outer_rows(self.columns[bit][:, lower * self.half : (lower + 1) * self.half], self.grads)

    def finish(self, *earlier):
        first = self.first
        if earlier:
            first = lax.optimization_barrier(first + earlier)[:4]
        from_across, from_beside, beside_lower, across_upper = first
        beside_upper = flip(low(self.block(1, 0) + wide(from_across)), "ctx", 1)
        across_lower = flip(low(self.block(2, 1) + wide(from_beside)), "ctx", 2)
        self.last = (beside_upper, across_lower)
        upper = self.block(0, 0) + wide(beside_upper) + wide(across_upper)
        lower = self.block(0, 1) + wide(beside_lower) + wide(across_lower)
        own = jnp.concatenate([upper, lower], axis=0)
        lines = lax.axis_size("fsdp")
        return line_sum(own.reshape(lines, own.shape[0] // lines, own.shape[1]))


def butterfly(value, axes):
    for axis in axes:
        count, bit = lax.axis_size(axis), 1
        while bit < count:
            value = value + flip(value, axis, bit)
            bit *= 2
    return value


def rms_scale(values, floor_value):
    return lax.rsqrt(jnp.mean(values * values, axis=-1, keepdims=True) + floor_value)


def norm_backward(grad_normed, inputs, scale, gain):
    normed = inputs * scale
    weighted = grad_normed * gain
    return (
        scale * (weighted - normed * jnp.mean(weighted * normed, axis=-1, keepdims=True)),
        normed,
    )


def times(left, right):
    return jnp.dot(left, right, preferred_element_type=jnp.float32)


def times_transposed(left, right):
    return lax.dot_general(
        left, right, (((1,), (1,)), ((), ())), preferred_element_type=jnp.float32
    )


def outer_rows(left, right):
    return lax.dot_general(
        left, right, (((0,), (0,)), ((), ())), preferred_element_type=jnp.float32
    )


def rows_mine(rows):
    count = rows.shape[1] // lax.axis_size("tp")
    return lax.dynamic_slice_in_dim(rows, lax.axis_index("tp") * count, count, 1)


def rows_scatter(partial):
    if lax.axis_size("tp") != 2:
        return wide(lax.psum_scatter(partial, "tp", scatter_dimension=1, tiled=True))
    count = partial.shape[1] // 2
    other = lax.dynamic_slice_in_dim(partial, (1 - lax.axis_index("tp")) * count, count, 1)
    return wide(rows_mine(partial)) + wide(flip(other, "tp", 1))


def rows_full(mine):
    if lax.axis_size("tp") != 2:
        return lax.all_gather(mine, "tp", axis=1, tiled=True)
    other = flip(mine, "tp", 1)
    pair = jnp.concatenate([mine, other, mine], axis=1)
    count = mine.shape[1]
    return lax.dynamic_slice_in_dim(pair, lax.axis_index("tp") * count, 2 * count, 1)


def by_head(parts):
    lead = parts[0].shape[:-1]
    split = [part.reshape(lead + (-1, LANES)) for part in parts]
    return jnp.stack(split, axis=-2).reshape(lead + (-1,))


def by_kind(joined):
    lead = joined.shape[:-1]
    split = joined.reshape(lead + (-1, 3, LANES))
    return [split[..., kind, :].reshape(lead + (-1,)) for kind in range(3)]


def pass_states(own, transfer, forward):
    rule = "shij,shjk->shik" if forward == 1 else "shji,shjk->shik"
    leaving = own
    entered = low(jnp.zeros_like(own))
    for repeat in range(lax.axis_size("ctx") - 1):
        entered = from_behind(low(leaving), "ctx", forward)
        leaving = own + jnp.einsum(rule, transfer, entered, preferred_element_type=jnp.float32)
    return wide(entered)


def local(
    block_input,
    doc_start,
    gain_mix,
    query_weight,
    key_weight,
    value_weight,
    beta_weight,
    beta_bias,
    conv_weight,
    gain_o,
    out_weight,
    gain_ffn,
    gate_weight,
    up_weight,
    down_weight,
    out_grad,
):
    seq_count, local_len, width = block_input.shape
    row_count = seq_count * local_len
    heads_here = beta_weight.shape[1]
    taps = conv_weight.shape[1]
    parts = 2 if heads_here % 2 == 0 else 1
    part_heads = heads_here // parts
    group = 2 if part_heads % 2 == 0 else 1
    part_cols = 3 * part_heads * LANES
    spare = LANES - heads_here
    units_here = gate_weight.shape[1]
    shard_rows = gate_weight.shape[0]

    joined = by_head([low(query_weight), low(key_weight), low(value_weight)])
    shards = [joined[:, p * part_cols : (p + 1) * part_cols] for p in range(parts)]
    shards[0] = jnp.concatenate([shards[0], jnp.pad(low(beta_weight), ((0, 0), (0, spare)))], axis=1)
    shards.append(low(out_weight).T)
    lines = []
    for shard in shards:
        lines.append(gather_line(tie(shard, lines[-1]) if lines else shard))
    units = units_here // 4
    pieces = jnp.stack([low(gate_weight).T, low(up_weight).T, low(down_weight)])
    pieces = pieces.reshape(3, 4, units, shard_rows).transpose(1, 0, 2, 3)
    ffn_line = lax.all_to_all(pieces.reshape(4, 3 * units, shard_rows), "ctx", 0, 0)
    ffn_line = ffn_line.transpose(1, 0, 2).reshape(3 * units, 4 * shard_rows)
    line_count, line_place = lax.axis_size("fsdp"), lax.axis_index("fsdp")
    ffn_full = columns_join(None, ffn_line, line_place, line_count, 4)
    ends_apart = sorted({1 % line_count, line_count - 1} - {0})
    ffn_near = {d: shift(tie(ffn_line, lines[parts - 1]), "fsdp", d) for d in ends_apart}

    first_pos = lax.axis_index("ctx") * local_len
    starts = doc_start - first_pos
    col, row = starts[:, :, None], starts[:, None, :]
    conv = by_head([conv_weight[0], conv_weight[1], conv_weight[2]])
    bias = jnp.pad(beta_bias, (0, spare))[None]
    gain_head = gain_o[None]
    tokens = block_input.reshape(row_count, width)
    inputs = wide(tokens)
    normed_mix = low(inputs * rms_scale(inputs, EPSILON) * gain_mix)
    inputs_mine = wide(rows_mine(block_input).reshape(-1, width))
    grads_mine = rows_mine(out_grad).reshape(-1, width)

    square = Square(tie(lines[0], ffn_line)).forward()
    mix_full, kept, pre = [], [], []
    for p in range(parts):
        mix_full.append(square.weights())
        square = Square(tie(lines[p + 1], *square.done()))
        if p == 0:
            pre.append(times(normed_mix, mix_full[p]))
        else:
            pre.append(times(tie(normed_mix, lines[-1]), mix_full[p]))
        ends = pre[p].reshape(seq_count, local_len, -1)[:, local_len - HALO :, :part_cols]
        halo = from_behind(ends, "ctx", 1)
        convs = conv[:, p * part_cols : (p + 1) * part_cols]
        held = pre[p]
        if p > 0:
            held = tie(held, grad_square.beside, grad_square.across)
        kept.append(
            [halo, convs]
            + list(
                mixer_forward(
                    held, pre[0], bias, halo, convs, col, row, taps, p * part_heads, part_heads, group
                )
            )
        )
        square.forward(kept[p][2])
        if p == 0:
            ffn_near = dict(zip(ends_apart, lax.optimization_barrier(tuple(ffn_near.values()))))
            for d in ends_apart:
                ffn_full = columns_join(ffn_full, ffn_near[d], (line_place - d) % line_count, line_count, 4)
            cut = 3 * units // 2
            ffn_far = {
                d: shift(tie(ffn_line[:cut], *ffn_near.values()), "fsdp", d) for d in range(2, line_count - 1)
            }
            square.upper = tie(square.upper, *ffn_near.values())
            grad_square = Square(tie(grads_mine, kept[p][2]))
        if p == parts - 1:
            grad_square.forward()
    out_full = square.weights()

    entered, transfers, mixed_rows = [], [], []
    for _, _, own, carry, final, _, _, _ in kept:
        transfers.append(low(final[..., LANES:]))
        first = final[..., :LANES]
        if len(entered) == parts - 1:
            first = tie(first, *grad_square.done(), *ffn_far.values())
            ffn_far = {
                d: [piece, shift(tie(ffn_line[cut:], piece), "fsdp", d)] for d, piece in ffn_far.items()
            }
        entered.append(pass_states(first, transfers[-1], 1))
        if len(entered) == parts:
            carry = tie(carry, *(piece[1] for piece in ffn_far.values()))
        mixed_rows.append(mixer_output(own, carry, entered[-1], gain_head, group))
    mixed_rows = jnp.concatenate(mixed_rows, axis=1)

    branch = low(times_transposed(mixed_rows, out_full)).reshape(seq_count, local_len, width)
    residual = inputs_mine + rows_scatter(branch).reshape(-1, width)
    scale_ffn = rms_scale(residual, EPSILON)
    square = Square(low(residual * scale_ffn * gain_ffn))
    for d, pieces in ffn_far.items():
        piece = jnp.concatenate(pieces, axis=0)
        ffn_full = columns_join(ffn_full, piece, (line_place - d) % line_count, line_count, 4)

    ffn_rows = [all_cores(square.own)]
    grad_rows = [all_cores(part) for part in (grad_square.own, grad_square.beside, grad_square.across, grad_square.far())]
    ffn_out = [ffn_both(ffn_rows[0], grad_rows[0], ffn_full)]
    square.forward(ffn_out[0][0])
    ffn_rows.append(all_cores(tie(square.beside, ffn_out[0][0])))
    ffn_out.append(ffn_both(ffn_rows[1], grad_rows[1], ffn_full))
    ffn_rows.append(all_cores(tie(square.across, ffn_out[0][0], *square.done())))
    ffn_out.append(ffn_both(tie(ffn_rows[2], ffn_out[1][0]), grad_rows[2], ffn_full))
    beside_sums, across_sums = low(core_sum(ffn_out[1][3])), low(core_sum(ffn_out[2][3]))
    ffn_rows.append(tie(all_cores(square.far()), beside_sums, across_sums))
    ffn_out.append(ffn_both(ffn_rows[3], grad_rows[3], ffn_full))
    near_sums = (flip(beside_sums, "ctx", 1), flip(across_sums, "ctx", 2))
    far_sums = core_sum(tie(ffn_out[3][3], *near_sums))
    ffn_rows[0] = tie(ffn_rows[0], ffn_out[2][3])
    for i in (1, 2, 3):
        ffn_rows[i], grad_rows[i] = tie(ffn_rows[i], far_sums), tie(grad_rows[i], far_sums)
    far_sums = flip(low(far_sums), "ctx", 3)
    grad_normed = core_sum(ffn_out[0][3]) + wide(near_sums[0]) + wide(near_sums[1]) + wide(far_sums)
    back_ffn, unit_ffn = norm_backward(grad_normed, residual, scale_ffn, gain_ffn)
    grad_residual = wide(grads_mine) + back_ffn
    gain_ffn_part = jnp.sum(grad_normed * unit_ffn, axis=0)
    grad_branch = rows_full(low(grad_residual).reshape(seq_count, -1, width)).reshape(row_count, width)
    grad_heads = times(grad_branch, out_full)
    backs, acrosses, gain_o_part = [], [], 0.0
    for p in range(parts):
        _, _, own, carry, _, _, _, _ = kept[p]
        back, across, gain_part = mixer_output_backward(
            own, carry, entered[p], gain_head, grad_heads, p * part_heads, group
        )
        backs.append(back)
        acrosses.append(across)
        gain_o_part = gain_o_part + jnp.sum(gain_part, axis=(0, 1, 2))
    grad_end = pass_states(jnp.concatenate(acrosses, axis=1), jnp.concatenate(transfers, axis=1), -1)
    result_near = [
        flip(tie(low(core_sum(tie(ffn_out[bit][4], grad_branch))), grad_end), "ctx", bit) for bit in (1, 2)
    ]
    result_far = core_sum(tie(ffn_out[3][4], grad_branch))
    result_own = core_sum(tie(ffn_out[0][4], grad_branch))

    sums = []
    for kind, sources in ((1, ffn_rows), (2, ffn_rows), (0, grad_rows)):
        total = 0.0
        for out, source in zip(ffn_out, sources):
            total = total + outer_rows(out[kind], source)
        sums.append(total)
    sums = columns_split(sums, line_count, 4).reshape(line_count, 3 * units, 4 * shard_rows)

    def line_piece(distance):
        return lax.dynamic_index_in_dim(sums, (line_place + distance) % line_count, 0, keepdims=False)

    total = wide(line_piece(0))
    cut = 3 * units // 2
    line_sends = [(d, 0, 3 * units) for d in ends_apart]
    line_sends += [(d, at, at + cut) for d in range(2, line_count - 1) for at in (0, cut)]
    line_got = []
    for d, low_row, high_row in line_sends:
        piece = line_piece(d)[low_row:high_row]
        if line_got:
            piece = tie(piece, grad_end, line_got[-1])
        line_got.append(shift(piece, "fsdp", d))

    out_grad_w = low(outer_rows(grad_branch, mixed_rows))
    out_grad_w = wide(lax.psum_scatter(out_grad_w, ("ctx", "fsdp"), scatter_dimension=0, tiled=True)).T

    columns = neighbour_columns(normed_mix)
    mix_back, mix_grads, conv_parts = 0.0, [None] * parts, [None] * parts
    logits = 0.0
    scatter = None
    for p in reversed(range(parts)):
        halo, convs, own, carry, final, inverses, updates, states = kept[p]
        heads = slice(p * part_heads, (p + 1) * part_heads)
        back = tie(backs[p], *line_got[:1]) if scatter is None else tie(backs[p], *scatter.sent)
        grad_mix, tail, before, conv_parts[p], logit = mixer_backward(
            pre[p], pre[0], bias, halo, convs, col, row, back, inverses, updates, states,
            entered[p], grad_end[:, heads], taps, p * part_heads, part_heads, group,
        )
        logits = logits + logit
        tail = low(tail + from_behind(before, "ctx", -1))
        grad_mix = put(grad_mix.reshape(seq_count, local_len, -1), tail, 0, local_len - HALO, 0)
        grad_mix = grad_mix.reshape(row_count, -1)
        if scatter is not None:
            mix_grads[p + 1] = scatter.finish(grad_mix)
        else:
            grad_mix = tie(grad_mix, *result_near, *line_got[1:2])
        if p == 0:
            grad_mix = tie(jnp.concatenate([grad_mix, low(logits)], axis=1), *line_got[2:3])
        mix_back = mix_back + times_transposed(grad_mix, mix_full[p])
        scatter = Scatter(columns, grad_mix)
    mix_grads[0] = scatter.finish()
    for (_, low_row, high_row), part in zip(line_sends, line_got):
        total = total + jnp.pad(wide(part), ((low_row, total.shape[0] - high_row), (0, 0)))
    sums = tie(low(total), grad_mix).reshape(3 * units, 4, shard_rows).transpose(1, 0, 2)
    arrived = lax.all_to_all(sums, "ctx", 0, 0).reshape(4, 3, units, shard_rows)
    gate_grad, up_grad, down_grad = (wide(arrived[:, i].reshape(units_here, shard_rows)) for i in range(3))
    result = result_own + wide(result_near[0]) + wide(result_near[1])
    result = result + wide(flip(low(tie(result_far, *scatter.last)), "ctx", 3))
    block_output = rows_full(low(residual + result).reshape(seq_count, -1, width))
    joined = jnp.concatenate([grad[:, :part_cols] for grad in mix_grads], axis=1)
    query_grad, key_grad, value_grad = by_kind(joined)
    beta_grad = mix_grads[0][:, part_cols : part_cols + heads_here]

    mix_back = rows_scatter(low(mix_back).reshape(seq_count, local_len, width)).reshape(-1, width)
    back_mix, unit_mix = norm_backward(mix_back, inputs_mine, rms_scale(inputs_mine, EPSILON), gain_mix)
    input_grad = rows_full(low(grad_residual + back_mix).reshape(seq_count, -1, width))
    gain_mix_part = jnp.sum(mix_back * unit_mix, axis=0)

    conv_cols = jnp.concatenate([jnp.sum(part, axis=0)[:taps] for part in conv_parts], axis=1)
    gains = butterfly(jnp.concatenate([gain_mix_part, gain_ffn_part, gain_o_part]), ("tp",))
    sums = jnp.concatenate([gains, conv_cols.reshape(-1), jnp.sum(logits, axis=0)])
    sums = butterfly(sums, ("ctx", "fsdp"))
    ends = [width, 2 * width, 2 * width + LANES, sums.shape[0] - LANES]
    gain_mix_grad, gain_ffn_grad, gain_o_grad, conv_grad, bias_grad = jnp.split(sums, ends)
    conv_grad = jnp.stack(by_kind(conv_grad.reshape(taps, -1)))
    bias_grad = bias_grad[:heads_here]
    return (
        block_output,
        input_grad,
        gain_mix_grad,
        query_grad,
        key_grad,
        value_grad,
        beta_grad,
        bias_grad,
        conv_grad,
        gain_o_grad,
        out_grad_w,
        gain_ffn_grad,
        gate_grad.T,
        up_grad.T,
        down_grad,
    )


def solution(mesh):
    placed = (
        P("fsdp", "ctx", None),
        P("fsdp", "ctx"),
        P(),
        P(("ctx", "fsdp"), "tp"),
        P(("ctx", "fsdp"), "tp"),
        P(("ctx", "fsdp"), "tp"),
        P(("ctx", "fsdp"), "tp"),
        P("tp"),
        P(None, None, "tp"),
        P(),
        P("tp", ("ctx", "fsdp")),
        P(),
        P(("ctx", "fsdp"), "tp"),
        P(("ctx", "fsdp"), "tp"),
        P("tp", ("ctx", "fsdp")),
        P("fsdp", "ctx", None),
    )
    return jax.shard_map(
        local,
        mesh=mesh,
        in_specs=placed,
        out_specs=(
            P("fsdp", "ctx", None),
            P("fsdp", "ctx", None),
            P(),
            P(("ctx", "fsdp"), "tp"),
            P(("ctx", "fsdp"), "tp"),
            P(("ctx", "fsdp"), "tp"),
            P(("ctx", "fsdp"), "tp"),
            P("tp"),
            P(None, None, "tp"),
            P(),
            P("tp", ("ctx", "fsdp")),
            P(),
            P(("ctx", "fsdp"), "tp"),
            P(("ctx", "fsdp"), "tp"),
            P("tp", ("ctx", "fsdp")),
        ),
        check_vma=False,
    )
```

```python
import functools
import math
import jax
import jax.numpy as jnp
from jax import lax
from jax.experimental import pallas as pl
from jax.experimental.pallas import tpu as pltpu
from jax.sharding import PartitionSpec as P

LANES = 128
CHUNK = 128
HALO = 8
EPSILON = 1e-06
HEAD_FLOOR = 0.01
VMEM_BYTES = 60 * 1024 * 1024


def low(value):
    return value.astype(jnp.bfloat16)


def mul_nn(left, right):
    return lax.dot_general(low(left), low(right), (((1,), (0,)), ((), ())), preferred_element_type=jnp.float32)


def mul_nt(left, right):
    return lax.dot_general(low(left), low(right), (((1,), (1,)), ((), ())), preferred_element_type=jnp.float32)


def mul_tn(left, right):
    return lax.dot_general(low(left), low(right), (((0,), (0,)), ((), ())), preferred_element_type=jnp.float32)


def iota(shape, axis):
    return lax.broadcasted_iota(jnp.int32, shape, axis)


def chunk_masks(col, row, first):
    size = col.shape[0]
    same = col == row
    order, other = iota((size, size), 0), iota((size, size), 1)
    upto = same & (order >= other)
    below = same & (order > other)
    carried = (col < first).astype(jnp.float32)
    last = (col == row[:, size - 1 :]).astype(jnp.float32)
    keep = (row[:, size - 1 :] < first).astype(jnp.float32)
    return upto, below, carried, last, keep


def invert_units(systems):
    size = systems[0].shape[0]
    order, other = iota((size, size), 0), iota((size, size), 1)
    identity = (order == other).astype(jnp.float32)
    span = 1
    found = None
    while span < size:
        pair = (order // (2 * span) == other // (2 * span)) & (order // span != other // span)
        parts = [jnp.where(pair, system, 0.0) for system in systems]
        if found is None:
            found = [identity - part for part in parts]
        else:
            right = [mul_nn(part, value) for part, value in zip(parts, found)]
            found = [value - mul_nn(value, part) for value, part in zip(found, right)]
        span *= 2
    return found


def conv_rows(ext, conv, col, offset, size, lane, taps):
    total = None
    moved = []
    position = iota((size, 1), 0) + offset
    for tap in range(taps):
        back = taps - 1 - tap
        values = ext[pl.ds(HALO + offset - back, size), lane : lane + LANES]
        values = jnp.where(position - back >= col, values, 0.0)
        moved.append(values)
        term = conv[tap : tap + 1, lane : lane + LANES] * values
        total = term if total is None else total + term
    return total, moved


def unit(values):
    return values * lax.rsqrt(jnp.sum(values * values, axis=-1, keepdims=True) + EPSILON)


def head_column(values, head):
    return jnp.sum(jnp.where(iota(values.shape, 1) == head, values, 0.0), axis=-1, keepdims=True)


def forward_kernel(taps, heads, first, pre, beta, bias, halo, conv, col_ref, row_ref, own, carry, final, inv, upd, states, ext):
    length = pre.shape[0]
    ext[:HALO] = halo[0]
    ext[HALO:] = pre[...]
    head = first + pl.program_id(1) * heads
    jobs = [(i, j) for j in range(length // CHUNK) for i in range(heads)]
    data = {}
    for j in range(length // CHUNK):
        rows = pl.ds(j * CHUNK, CHUNK)
        col, row = col_ref[0, rows], row_ref[0, :, rows]
        masks = chunk_masks(col, row, j * CHUNK)
        strengths = jax.nn.sigmoid(beta[rows] + bias[...])
        for i in range(heads):
            acts = []
            for kind in range(3):
                total, _ = conv_rows(ext, conv, col, j * CHUNK, CHUNK, (3 * i + kind) * LANES, taps)
                acts.append(total * jax.nn.sigmoid(total))
            query, key, value = unit(acts[0]), unit(acts[1]), acts[2]
            strength = head_column(strengths, head + i)
            grams = mul_nt(jnp.concatenate([low(key), low(query)], axis=0), key)
            system = jnp.where(masks[1], strength * grams[:CHUNK], 0.0)
            scores = low(jnp.where(masks[0], grams[CHUNK:], 0.0))
            data[i, j] = (low(query), low(key), value, strength, scores, masks, system)
    inverses = dict(zip(jobs, invert_units([data[job][6] for job in jobs])))
    for i in range(heads):
        state = jnp.concatenate(
            [
                jnp.zeros((LANES, LANES), jnp.float32),
                (iota((LANES, LANES), 0) == iota((LANES, LANES), 1)).astype(jnp.float32),
            ],
            axis=1,
        )
        final[0, i] = state
    for j in range(length // CHUNK):
        rows = pl.ds(j * CHUNK, CHUNK)
        for i in range(heads):
            query, key, value, strength, scores, masks, _ = data[i, j]
            _, _, carried, last, keep = masks
            inverse = low(inverses[i, j])
            state = final[0, i]
            state_low = low(state)
            read = mul_nn(jnp.concatenate([key, query], axis=0), state_low)
            wide = jnp.concatenate([value, jnp.zeros_like(value)], axis=1)
            targets = strength * (wide - carried * read[:CHUNK])
            update = low(mul_nn(inverse, targets))
            result = carried * read[CHUNK:] + mul_nn(scores, update)
            final[0, i] = keep * state + mul_tn(key * low(last), update)
            lanes = slice(i * LANES, (i + 1) * LANES)
            own[rows, lanes] = result[:, :LANES]
            carry[rows, lanes] = low(result[:, LANES:])
            inv[0, i, j] = inverse
            upd[0, i, j] = update
            states[0, i, j] = state_low


def mixer_forward(pre, logit, bias, halo, conv, col, row, taps, first, heads_here, group):
    seqs, length = col.shape[0], col.shape[1]
    steps = heads_here // group
    chunks = length // CHUNK
    wide = 3 * LANES * group
    rows = seqs * length

    def tile(*tail, kind):
        return jax.ShapeDtypeStruct((seqs, heads_here) + tail, kind)

    def spec(*tail):
        return pl.BlockSpec((1, group) + tail, lambda s, h: (s, h) + (0,) * len(tail))

    flat = pl.BlockSpec((length, LANES * group), lambda s, h: (s, h))
    last = logit.shape[1] // LANES - 1
    return pl.pallas_call(
        functools.partial(forward_kernel, taps, group, first),
        grid=(seqs, steps),
        in_specs=[
            pl.BlockSpec((length, wide), lambda s, h: (s, h)),
            pl.BlockSpec((length, LANES), lambda s, h: (s, last)),
            pl.BlockSpec((1, LANES), lambda s, h: (0, 0)),
            pl.BlockSpec((1, HALO, wide), lambda s, h: (s, 0, h)),
            pl.BlockSpec((conv.shape[0], wide), lambda s, h: (0, h)),
            pl.BlockSpec((1, length, 1), lambda s, h: (s, 0, 0)),
            pl.BlockSpec((1, 1, length), lambda s, h: (s, 0, 0)),
        ],
        out_specs=[
            flat,
            flat,
            spec(LANES, 2 * LANES),
            spec(chunks, CHUNK, CHUNK),
            spec(chunks, CHUNK, 2 * LANES),
            spec(chunks, LANES, 2 * LANES),
        ],
        out_shape=[
            jax.ShapeDtypeStruct((rows, heads_here * LANES), jnp.float32),
            jax.ShapeDtypeStruct((rows, heads_here * LANES), jnp.bfloat16),
            tile(LANES, 2 * LANES, kind=jnp.float32),
            tile(chunks, CHUNK, CHUNK, kind=jnp.bfloat16),
            tile(chunks, CHUNK, 2 * LANES, kind=jnp.bfloat16),
            tile(chunks, LANES, 2 * LANES, kind=jnp.bfloat16),
        ],
        scratch_shapes=[pltpu.VMEM((length + HALO, wide), jnp.float32)],
        compiler_params=pltpu.CompilerParams(vmem_limit_bytes=VMEM_BYTES),
        cost_estimate=pl.CostEstimate(
            flops=60 * rows * heads_here * CHUNK * LANES, bytes_accessed=40 * rows * heads_here * LANES, transcendentals=0
        ),
    )(pre, logit, bias, halo, conv, col, row)


def backward_kernel(
    taps, heads, first, pre, beta, bias, halo, conv, col_ref, row_ref, grad_ref, inv, upd, states, start, end,
    grad_pre, tail, before, conv_grad, logits, ext, grad_ext,
):
    length = pre.shape[0]
    step = pl.program_id(1)
    head = first + step * heads
    ext[:HALO] = halo[0]
    ext[HALO:] = pre[...]
    grad_ext[...] = jnp.zeros_like(grad_ext)

    @pl.when(step == 0)
    def _():
        logits[...] = jnp.zeros_like(logits)

    grad_states = [end[0, i] for i in range(heads)]
    entry = [low(start[0, i]) for i in range(heads)]
    tap_sums = {}
    for j in reversed(range(length // CHUNK)):
        offset = j * CHUNK
        rows = pl.ds(offset, CHUNK)
        col, row = col_ref[0, rows], row_ref[0, :, rows]
        upto, below, carried, last, keep = chunk_masks(col, row, offset)
        strengths = jax.nn.sigmoid(beta[rows] + bias[...])
        grad_logit = jnp.zeros((CHUNK, LANES), jnp.float32)
        for i in range(heads):
            raw, taps_in = [], []
            for kind in range(3):
                total, moved = conv_rows(ext, conv, col, offset, CHUNK, (3 * i + kind) * LANES, taps)
                raw.append(total)
                taps_in.append(moved)
            gates = [jax.nn.sigmoid(total) for total in raw]
            acts = [total * gate for total, gate in zip(raw, gates)]
            scales = [lax.rsqrt(jnp.sum(act * act, axis=-1, keepdims=True) + EPSILON) for act in acts[:2]]
            query, key, value = acts[0] * scales[0], acts[1] * scales[1], acts[2]
            strength = head_column(strengths, head + i)
            lanes = slice(i * LANES, (i + 1) * LANES)
            query_low, key_low = low(query), low(key)
            grams = mul_nt(jnp.concatenate([key_low, query_low], axis=0), key_low)
            gram = jnp.where(below, grams[:CHUNK], 0.0)
            scores = jnp.where(upto, grams[CHUNK:], 0.0)
            inverse = inv[0, i, j]
            update = upd[0, i, j]
            update = low(update[:, :LANES].astype(jnp.float32) + mul_nn(update[:, LANES:], entry[i]))
            state = states[0, i, j]
            state = low(state[:, :LANES].astype(jnp.float32) + mul_nn(state[:, LANES:], entry[i]))
            grad_out = grad_ref[rows, lanes]
            grad_state = grad_states[i]
            grad_state_low = low(grad_state)
            key_last = key_low * low(last)
            grad_update = mul_tn(scores, grad_out) + mul_nn(key_last, grad_state_low)
            grad_target = mul_tn(inverse, grad_update)
            weighted = strength * grad_target
            passed = carried * weighted
            out_carried = carried * grad_out.astype(jnp.float32)
            query_carried = query_low * low(carried)
            grad_states[i] = (
                keep * grad_state + mul_tn(query_carried, grad_out) - mul_tn(key_low, passed)
            )
            grad_scores = jnp.where(upto, mul_nt(grad_out, update), 0.0)
            grad_system = jnp.where(below, mul_nt(grad_target, update), 0.0)
            remainder = value - carried * mul_nn(key_low, state)
            grad_strength = jnp.sum(grad_target * remainder - grad_system * gram, axis=-1, keepdims=True)
            scaled = strength * grad_system
            from_state = mul_nt(jnp.concatenate([low(out_carried), low(passed)], axis=0), state)
            from_keys = mul_nn(jnp.concatenate([low(grad_scores), low(scaled + scaled.T)], axis=0), key_low)
            grad_query = from_state[:CHUNK] + from_keys[:CHUNK]
            grad_key = (
                mul_tn(grad_scores, query_low)
                + last * mul_nt(update, grad_state_low)
                - from_state[CHUNK:]
                - from_keys[CHUNK:]
            )
            grad_logit = grad_logit + jnp.where(
                iota((CHUNK, LANES), 1) == head + i, grad_strength * strength * (1.0 - strength), 0.0
            )
            grads = [
                scales[0] * (grad_query - query * jnp.sum(grad_query * query, axis=-1, keepdims=True)),
                scales[1] * (grad_key - key * jnp.sum(grad_key * key, axis=-1, keepdims=True)),
                weighted,
            ]
            position = iota((CHUNK, 1), 0) + offset
            for kind in range(3):
                gate, total = gates[kind], raw[kind]
                grad_conv = grads[kind] * gate * (1.0 + total * (1.0 - gate))
                lane = (3 * i + kind) * LANES
                for tap in range(taps):
                    back = taps - 1 - tap
                    part = jnp.sum(grad_conv * taps_in[kind][tap], axis=0, keepdims=True)
                    spot = (i, kind, tap)
                    tap_sums[spot] = part if spot not in tap_sums else tap_sums[spot] + part
                    back_part = jnp.where(
                        position - back >= col, grad_conv * conv[tap : tap + 1, lane : lane + LANES], 0.0
                    )
                    where = pl.ds(HALO + offset - back, CHUNK)
                    grad_ext[where, lane : lane + LANES] += back_part
        logits[rows] += grad_logit
    grad_pre[...] = low(grad_ext[HALO:])
    before[0] = grad_ext[:HALO]
    tail[0] = grad_ext[length:]
    for i in range(heads):
        for kind in range(3):
            lane = (3 * i + kind) * LANES
            for tap in range(taps):
                conv_grad[0, tap : tap + 1, lane : lane + LANES] = tap_sums[i, kind, tap]


def mixer_backward(
    pre, logit, bias, halo, conv, col, row, grad_mixed, inv, upd, states, start, end, taps, first, heads_here, group
):
    seqs, length = col.shape[0], col.shape[1]
    steps = heads_here // group
    chunks = length // CHUNK
    wide = 3 * LANES * group
    rows = seqs * length

    def spec(*tail):
        return pl.BlockSpec((1, group) + tail, lambda s, h: (s, h) + (0,) * len(tail))

    last = logit.shape[1] // LANES - 1
    part = pl.BlockSpec((1, HALO, wide), lambda s, h: (s, 0, h))
    edge = jax.ShapeDtypeStruct((seqs, HALO, 3 * LANES * heads_here), jnp.float32)
    return pl.pallas_call(
        functools.partial(backward_kernel, taps, group, first),
        grid=(seqs, steps),
        in_specs=[
            pl.BlockSpec((length, wide), lambda s, h: (s, h)),
            pl.BlockSpec((length, LANES), lambda s, h: (s, last)),
            pl.BlockSpec((1, LANES), lambda s, h: (0, 0)),
            part,
            pl.BlockSpec((conv.shape[0], wide), lambda s, h: (0, h)),
            pl.BlockSpec((1, length, 1), lambda s, h: (s, 0, 0)),
            pl.BlockSpec((1, 1, length), lambda s, h: (s, 0, 0)),
            pl.BlockSpec((length, LANES * group), lambda s, h: (s, h)),
            spec(chunks, CHUNK, CHUNK),
            spec(chunks, CHUNK, 2 * LANES),
            spec(chunks, LANES, 2 * LANES),
            spec(LANES, LANES),
            spec(LANES, LANES),
        ],
        out_specs=[
            pl.BlockSpec((length, wide), lambda s, h: (s, h)),
            part,
            part,
            part,
            pl.BlockSpec((length, LANES), lambda s, h: (s, 0)),
        ],
        out_shape=[
            jax.ShapeDtypeStruct((rows, 3 * LANES * heads_here), jnp.bfloat16),
            edge,
            edge,
            edge,
            jax.ShapeDtypeStruct((rows, LANES), jnp.float32),
        ],
        scratch_shapes=[
            pltpu.VMEM((length + HALO, wide), jnp.float32),
            pltpu.VMEM((length + HALO, wide), jnp.float32),
        ],
        compiler_params=pltpu.CompilerParams(vmem_limit_bytes=VMEM_BYTES),
        cost_estimate=pl.CostEstimate(
            flops=60 * rows * heads_here * CHUNK * LANES, bytes_accessed=40 * rows * heads_here * LANES, transcendentals=0
        ),
    )(pre, logit, bias, halo, conv, col, row, grad_mixed, inv, upd, states, start, end)


def mixed_rows_of(own, carry, start):
    return own + mul_nn(carry, start)


def output_kernel(heads, own, carry, start, gain, out):
    for i in range(heads):
        lanes = slice(i * LANES, (i + 1) * LANES)
        mixed = mixed_rows_of(own[:, lanes], carry[:, lanes], start[0, i])
        scale = lax.rsqrt(jnp.mean(mixed * mixed, axis=-1, keepdims=True) + HEAD_FLOOR)
        out[:, lanes] = low(mixed * scale * gain[...])


def output_backward_kernel(heads, own, carry, start, gain, grad, out, across, gain_grad):
    total = jnp.zeros((1, LANES), jnp.float32)
    for i in range(heads):
        lanes = slice(i * LANES, (i + 1) * LANES)
        carried = carry[:, lanes]
        mixed = mixed_rows_of(own[:, lanes], carried, start[0, i])
        scale = lax.rsqrt(jnp.mean(mixed * mixed, axis=-1, keepdims=True) + HEAD_FLOOR)
        normed = mixed * scale
        upper = grad[:, lanes].astype(jnp.float32)
        total = total + jnp.sum(upper * normed, axis=0, keepdims=True)
        weighted = upper * gain[...]
        back = scale * (weighted - normed * jnp.mean(weighted * normed, axis=-1, keepdims=True))
        out[:, lanes] = low(back)
        across[0, i] = mul_tn(carried, back)
    gain_grad[0, 0] = total


def mixer_output(own, carry, start, gain, group):
    seqs, heads_here = start.shape[:2]
    rows = own.shape[0]
    length = rows // seqs
    flat = pl.BlockSpec((length, LANES * group), lambda s, h: (s, h))
    square = pl.BlockSpec((1, group, LANES, LANES), lambda s, h: (s, h, 0, 0))
    return pl.pallas_call(
        functools.partial(output_kernel, group),
        grid=(seqs, heads_here // group),
        in_specs=[flat, flat, square, pl.BlockSpec((1, LANES), lambda s, h: (0, 0))],
        out_specs=flat,
        out_shape=jax.ShapeDtypeStruct(own.shape, jnp.bfloat16),
        compiler_params=pltpu.CompilerParams(vmem_limit_bytes=VMEM_BYTES),
        cost_estimate=pl.CostEstimate(
            flops=2 * own.size * LANES, bytes_accessed=8 * own.size, transcendentals=0
        ),
    )(own, carry, start, gain)


def mixer_output_backward(own, carry, start, gain, grad, first, group):
    seqs, heads_here = start.shape[:2]
    rows = own.shape[0]
    length = rows // seqs
    steps = heads_here // group
    flat = pl.BlockSpec((length, LANES * group), lambda s, h: (s, h))
    base = first // group
    shifted = pl.BlockSpec((length, LANES * group), lambda s, h: (s, base + h))
    square = pl.BlockSpec((1, group, LANES, LANES), lambda s, h: (s, h, 0, 0))
    return pl.pallas_call(
        functools.partial(output_backward_kernel, group),
        grid=(seqs, steps),
        in_specs=[flat, flat, square, pl.BlockSpec((1, LANES), lambda s, h: (0, 0)), shifted],
        out_specs=[flat, square, pl.BlockSpec((1, 1, 1, LANES), lambda s, h: (s, h, 0, 0))],
        out_shape=[
            jax.ShapeDtypeStruct(own.shape, jnp.bfloat16),
            jax.ShapeDtypeStruct(start.shape, jnp.float32),
            jax.ShapeDtypeStruct((seqs, steps, 1, LANES), jnp.float32),
        ],
        compiler_params=pltpu.CompilerParams(vmem_limit_bytes=VMEM_BYTES),
        cost_estimate=pl.CostEstimate(
            flops=4 * own.size * LANES, bytes_accessed=12 * own.size, transcendentals=0
        ),
    )(own, carry, start, gain, grad)


def ffn_kernel(mine, other, mine_grads, other_grads, gate_w, up_w, down_w, *outs):
    rows = jnp.concatenate([mine[...], other[...]], axis=0)
    grads = jnp.concatenate([mine_grads[...], other_grads[...]], axis=0)
    half = mine.shape[0]
    gate = mul_nt(rows, gate_w[...])
    up = mul_nt(rows, up_w[...])
    grad_hidden = mul_nt(grads, down_w[...])
    sigmoid = jax.nn.sigmoid(gate)
    active = gate * sigmoid
    kept = low(active * up)
    back_gate = low(grad_hidden * up * sigmoid * (1.0 + gate * (1.0 - sigmoid)))
    back_up = low(grad_hidden * active)
    grad_rows = low(mul_nn(back_gate, gate_w[...]) + mul_nn(back_up, up_w[...]))
    result = low(mul_nn(kept, down_w[...]))
    for side in range(2):
        here = slice(side * half, (side + 1) * half)
        acts, grad_out, result_out = outs[3 * side : 3 * side + 3]
        for kind, value in enumerate((back_gate, back_up, kept)):
            acts[kind] = value[here]
        grad_out[...] = grad_rows[here]
        result_out[...] = result[here]


def ffn_both(rows, grads, weights):
    count, width = rows[0].shape
    units = weights.shape[0] // 3
    tile = min(256, count)
    wide_rows = pl.BlockSpec((tile, width), lambda i: (i, 0))
    narrow = pl.BlockSpec((3, tile, units), lambda i: (0, i, 0))

    def third(index):
        return pl.BlockSpec((units, width), lambda i: (index, 0))

    flat = jax.ShapeDtypeStruct((count, width), jnp.bfloat16)
    outs = pl.pallas_call(
        ffn_kernel,
        grid=(count // tile,),
        in_specs=[wide_rows] * 4 + [third(0), third(1), third(2)],
        out_specs=[narrow, wide_rows, wide_rows] * 2,
        out_shape=[jax.ShapeDtypeStruct((3, count, units), jnp.bfloat16), flat, flat] * 2,
        compiler_params=pltpu.CompilerParams(vmem_limit_bytes=VMEM_BYTES),
        cost_estimate=pl.CostEstimate(
            flops=24 * count * width * units, bytes_accessed=16 * count * width + 6 * units * width, transcendentals=0
        ),
    )(*rows, *grads, weights, weights, weights)
    return outs[:3], outs[3:]


def ffn_weights_kernel(count, lines, *refs):
    acts, rows, grads = refs[:count], refs[count : 2 * count], refs[2 * count : 3 * count]
    out, total = refs[-2:]
    part = out.shape[-1]

    def add(sources):
        for i in range(count):
            value = mul_tn(acts[i][0], sources[i][...])
            if i == 0:
                total[...] = value
            else:
                total[...] += value

    @pl.when(pl.program_id(0) < 2)
    def _():
        add(rows)

    @pl.when(pl.program_id(0) == 2)
    def _():
        add(grads)

    for line in range(lines):
        out[line, 0] = low(total[:, line * part : (line + 1) * part])


def ffn_weights(acts, rows, grads, lines, squares):
    count, width = len(acts), rows[0].shape[1]
    size, units = acts[0].shape[1:]
    block = width // squares
    part = block // lines
    act_spec = pl.BlockSpec((1, size, units), lambda k, c: (k, 0, 0))
    row_spec = pl.BlockSpec((size, block), lambda k, c: (0, jnp.where(k < 2, c, squares - 1)))
    grad_spec = pl.BlockSpec((size, block), lambda k, c: (0, jnp.where(k < 2, 0, c)))
    return pl.pallas_call(
        functools.partial(ffn_weights_kernel, count, lines),
        grid=(3, squares),
        in_specs=[act_spec] * count + [row_spec] * count + [grad_spec] * count,
        out_specs=pl.BlockSpec((lines, 1, units, part), lambda k, c: (0, k, 0, c)),
        out_shape=jax.ShapeDtypeStruct((lines, 3, units, squares * part), jnp.bfloat16),
        scratch_shapes=[pltpu.VMEM((units, block), jnp.float32)],
        compiler_params=pltpu.CompilerParams(vmem_limit_bytes=VMEM_BYTES),
        cost_estimate=pl.CostEstimate(
            flops=6 * count * size * width * units, bytes_accessed=8 * count * size * width, transcendentals=0
        ),
    )(*acts, *rows, *grads)


def block_columns(place, bit, size):
    return pl.multiple_of((place[0] ^ bit) * size, size)


def gathered_kernel(place, rows, *refs):
    out = refs[-1]
    own, beside, across, upper, lower = refs[:-1]
    size, half = own.shape[0], upper.shape[0]
    total = None
    for bit, skip, ref in ((0, 0, own), (1, 0, beside), (2, 0, across), (3, 0, upper), (3, half, lower)):
        start = pl.multiple_of(block_columns(place, bit, size) + skip, half)
        value = mul_nn(rows[:, pl.ds(start, ref.shape[0])], ref[...])
        total = value if total is None else total + value
    out[...] = total


def gathered_times(rows, place, pieces):
    count, width = rows.shape
    columns = pieces[0].shape[1]
    tile = min(256, count)
    whole = [pl.BlockSpec(piece.shape, lambda i, place: (0, 0)) for piece in pieces]
    return pl.pallas_call(
        gathered_kernel,
        grid_spec=pltpu.PrefetchScalarGridSpec(
            num_scalar_prefetch=1,
            grid=(count // tile,),
            in_specs=[pl.BlockSpec((tile, width), lambda i, place: (i, 0))] + whole,
            out_specs=pl.BlockSpec((tile, columns), lambda i, place: (i, 0)),
        ),
        out_shape=jax.ShapeDtypeStruct((count, columns), jnp.float32),
        compiler_params=pltpu.CompilerParams(vmem_limit_bytes=VMEM_BYTES),
        cost_estimate=pl.CostEstimate(
            flops=2 * count * width * columns, bytes_accessed=2 * (count + columns) * width, transcendentals=0
        ),
    )(jnp.reshape(place, (1,)).astype(jnp.int32), rows, *pieces)


def gathered_transposed_kernel(count, place, *refs):
    factors, pieces, out = refs[:count], refs[count:-1], refs[-1]
    size, half = pieces[0].shape[0], pieces[3].shape[0]
    for i, (bit, skip) in enumerate(((0, 0), (1, 0), (2, 0), (3, 0), (3, half))):
        start = pl.multiple_of(block_columns(place, bit, size) + skip, half)
        total = None
        for p in range(count):
            value = mul_nt(factors[p][...], pieces[5 * p + i][...])
            total = value if total is None else total + value
        out[:, pl.ds(start, pieces[i].shape[0])] = low(total)


def gathered_times_transposed(factors, place, pieces):
    count, rows = len(factors), factors[0].shape[0]
    width = 4 * pieces[0][0].shape[0]
    tile = min(256, rows)
    flat = [piece for some in pieces for piece in some]
    whole = [pl.BlockSpec(piece.shape, lambda i, place: (0, 0)) for piece in flat]
    wides = [pl.BlockSpec((tile, factor.shape[1]), lambda i, place: (i, 0)) for factor in factors]
    columns = sum(factor.shape[1] for factor in factors)
    return pl.pallas_call(
        functools.partial(gathered_transposed_kernel, count),
        grid_spec=pltpu.PrefetchScalarGridSpec(
            num_scalar_prefetch=1,
            grid=(rows // tile,),
            in_specs=wides + whole,
            out_specs=pl.BlockSpec((tile, width), lambda i, place: (i, 0)),
        ),
        out_shape=jax.ShapeDtypeStruct((rows, width), jnp.bfloat16),
        compiler_params=pltpu.CompilerParams(vmem_limit_bytes=VMEM_BYTES),
        cost_estimate=pl.CostEstimate(
            flops=2 * rows * width * columns, bytes_accessed=2 * (rows + columns) * width, transcendentals=0
        ),
    )(jnp.reshape(place, (1,)).astype(jnp.int32), *factors, *flat)


def join_kernel(line, source, *refs):
    refs[-1][...] = source[...]


def columns_join(full, piece, line, lines, squares):
    rows, columns = piece.shape
    part = columns // squares
    known = [] if full is None else [full]
    return pl.pallas_call(
        join_kernel,
        grid_spec=pltpu.PrefetchScalarGridSpec(
            num_scalar_prefetch=1,
            grid=(squares,),
            in_specs=[pl.BlockSpec((rows, part), lambda j, line: (0, j))]
            + [pl.BlockSpec(memory_space=pl.ANY) for _ in known],
            out_specs=pl.BlockSpec((rows, part), lambda j, line: (0, j * lines + line[0])),
        ),
        out_shape=jax.ShapeDtypeStruct((rows, lines * columns), piece.dtype),
        input_output_aliases={2: 0} if known else {},
        compiler_params=pltpu.CompilerParams(vmem_limit_bytes=VMEM_BYTES),
        cost_estimate=pl.CostEstimate(flops=0, bytes_accessed=4 * piece.size, transcendentals=0),
    )(jnp.reshape(line, (1,)).astype(jnp.int32), piece, *known)


def flip(value, axis, bit):
    devices = range(lax.axis_size(axis))
    return lax.ppermute(value, axis, [(i, i ^ bit) for i in devices])


def shift(value, axis, distance):
    count = lax.axis_size(axis)
    return lax.ppermute(value, axis, [(i, (i + distance) % count) for i in range(count)])


def from_behind(block, axis, distance):
    devices = range(lax.axis_size(axis))
    route = [(i - distance, i) for i in devices if i - distance in devices]
    return lax.ppermute(block, axis, route)


def tie(value, *earlier):
    return lax.optimization_barrier((value,) + earlier)[0]


def put(buffer, piece, *start):
    return lax.dynamic_update_slice(buffer, piece, start)


def wide(value):
    return value.astype(jnp.float32)


def gather_line(shard):
    count, place = lax.axis_size("fsdp"), lax.axis_index("fsdp")
    pieces = [shard] + [shift(shard, "fsdp", d) for d in range(1, count)]
    order = [(place - i) % count for i in range(count)]
    return jnp.concatenate([lax.select_n(which, *pieces) for which in order], axis=0)


class Square:
    def __init__(self, own):
        self.own = own
        self.half = own.shape[0] // 2
        self.beside = flip(own, "ctx", 1)
        self.across = flip(own, "ctx", 2)

    def forward(self, *earlier):
        upper = self.beside[: self.half]
        lower = self.across[self.half :]
        if earlier:
            upper, lower = lax.optimization_barrier((upper, lower) + earlier)[:2]
        self.upper = flip(upper, "ctx", 2)
        self.lower = flip(lower, "ctx", 1)
        return self

    def done(self):
        return (self.upper, self.lower)

    def pieces(self):
        return [self.own, self.beside, self.across, self.upper, self.lower]

    def far(self):
        return jnp.concatenate([self.upper, self.lower], axis=0)


def both_sides(rows):
    if lax.axis_size("tp") == 2:
        return rows, flip(rows, "tp", 1)
    every = lax.all_gather(rows, "tp", axis=0, tiled=True)
    half = every.shape[0] // 2
    return every[:half], every[half:]


def core_sum(mine, other):
    if lax.axis_size("tp") == 2:
        return wide(mine) + wide(flip(other, "tp", 1))
    both = jnp.concatenate([mine, other], axis=0)
    return wide(lax.psum_scatter(both, "tp", scatter_dimension=0, tiled=True))


def neighbour_columns(rows):
    width = rows.shape[1] // 4
    place = lax.axis_index("ctx")
    return [lax.dynamic_slice_in_dim(rows, (place ^ bit) * width, width, 1) for bit in range(4)]


def line_sum(own):
    count, place = own.shape[0], lax.axis_index("fsdp")
    total = lax.dynamic_index_in_dim(own, place, 0, keepdims=False)
    for distance in range(1, count):
        piece = lax.dynamic_index_in_dim(own, (place + distance) % count, 0, keepdims=False)
        total = total + wide(shift(low(piece), "fsdp", distance))
    return total


class Scatter:
    def __init__(self, columns, grads):
        self.columns, self.grads = columns, grads
        self.half = columns[0].shape[1] // 2
        self.sent = [low(self.block(*which)) for which in ((3, 0), (3, 1), (1, 1), (2, 0))]
        self.first = tuple(flip(part, "ctx", bit) for part, bit in zip(self.sent, (2, 1, 1, 2)))

    def block(self, bit, lower):
        return outer_rows(self.columns[bit][:, lower * self.half : (lower + 1) * self.half], self.grads)

    def finish(self, *earlier):
        first = self.first
        if earlier:
            first = lax.optimization_barrier(first + earlier)[:4]
        from_across, from_beside, beside_lower, across_upper = first
        beside_upper = flip(low(self.block(1, 0) + wide(from_across)), "ctx", 1)
        across_lower = flip(low(self.block(2, 1) + wide(from_beside)), "ctx", 2)
        self.last = (beside_upper, across_lower)
        upper = self.block(0, 0) + wide(beside_upper) + wide(across_upper)
        lower = self.block(0, 1) + wide(beside_lower) + wide(across_lower)
        own = jnp.concatenate([upper, lower], axis=0)
        lines = lax.axis_size("fsdp")
        return line_sum(own.reshape(lines, own.shape[0] // lines, own.shape[1]))


def butterfly(value, axes):
    for axis in axes:
        count, bit = lax.axis_size(axis), 1
        while bit < count:
            value = value + flip(value, axis, bit)
            bit *= 2
    return value


def rms_scale(values, floor_value):
    return lax.rsqrt(jnp.mean(values * values, axis=-1, keepdims=True) + floor_value)


def norm_backward(grad_normed, inputs, scale, gain):
    normed = inputs * scale
    weighted = grad_normed * gain
    return (
        scale * (weighted - normed * jnp.mean(weighted * normed, axis=-1, keepdims=True)),
        normed,
    )


def times(left, right):
    return jnp.dot(left, right, preferred_element_type=jnp.float32)


def times_transposed(left, right):
    return lax.dot_general(
        left, right, (((1,), (1,)), ((), ())), preferred_element_type=jnp.float32
    )


def outer_rows(left, right):
    return lax.dot_general(
        left, right, (((0,), (0,)), ((), ())), preferred_element_type=jnp.float32
    )


def rows_mine(rows):
    count = rows.shape[1] // lax.axis_size("tp")
    return lax.dynamic_slice_in_dim(rows, lax.axis_index("tp") * count, count, 1)


def rows_scatter(partial):
    if lax.axis_size("tp") != 2:
        return wide(lax.psum_scatter(partial, "tp", scatter_dimension=1, tiled=True))
    count = partial.shape[1] // 2
    other = lax.dynamic_slice_in_dim(partial, (1 - lax.axis_index("tp")) * count, count, 1)
    return wide(rows_mine(partial)) + wide(flip(other, "tp", 1))


def rows_full(mine):
    if lax.axis_size("tp") != 2:
        return lax.all_gather(mine, "tp", axis=1, tiled=True)
    other = flip(mine, "tp", 1)
    lower = lax.axis_index("tp") == 0
    return jnp.concatenate([jnp.where(lower, mine, other), jnp.where(lower, other, mine)], axis=1)


def by_head(parts):
    lead = parts[0].shape[:-1]
    split = [part.reshape(lead + (-1, LANES)) for part in parts]
    return jnp.stack(split, axis=-2).reshape(lead + (-1,))


def by_kind(joined):
    lead = joined.shape[:-1]
    split = joined.reshape(lead + (-1, 3, LANES))
    return [split[..., kind, :].reshape(lead + (-1,)) for kind in range(3)]


def pass_states(own, transfer, forward):
    rule = "shij,shjk->shik" if forward == 1 else "shji,shjk->shik"
    leaving = own
    entered = low(jnp.zeros_like(own))
    for repeat in range(lax.axis_size("ctx") - 1):
        entered = from_behind(low(leaving), "ctx", forward)
        leaving = own + jnp.einsum(rule, transfer, entered, preferred_element_type=jnp.float32)
    return wide(entered)


def local(
    block_input,
    doc_start,
    gain_mix,
    query_weight,
    key_weight,
    value_weight,
    beta_weight,
    beta_bias,
    conv_weight,
    gain_o,
    out_weight,
    gain_ffn,
    gate_weight,
    up_weight,
    down_weight,
    out_grad,
):
    seq_count, local_len, width = block_input.shape
    row_count = seq_count * local_len
    heads_here = beta_weight.shape[1]
    taps = conv_weight.shape[1]
    parts = 2 if heads_here % 2 == 0 else 1
    part_heads = heads_here // parts
    group = 2 if part_heads % 2 == 0 else 1
    part_cols = 3 * part_heads * LANES
    spare = LANES - heads_here
    units_here = gate_weight.shape[1]
    shard_rows = gate_weight.shape[0]

    joined = by_head([low(query_weight), low(key_weight), low(value_weight)])
    shards = [joined[:, p * part_cols : (p + 1) * part_cols] for p in range(parts)]
    shards[0] = jnp.concatenate([shards[0], jnp.pad(low(beta_weight), ((0, 0), (0, spare)))], axis=1)
    shards.append(low(out_weight).T)
    lines = []
    for shard in shards:
        lines.append(gather_line(tie(shard, lines[-1]) if lines else shard))
    units = units_here // 4
    pieces = jnp.stack([low(gate_weight).T, low(up_weight).T, low(down_weight)])
    pieces = pieces.reshape(3, 4, units, shard_rows).transpose(1, 0, 2, 3)
    ffn_line = lax.all_to_all(pieces.reshape(4, 3 * units, shard_rows), "ctx", 0, 0)
    ffn_line = ffn_line.transpose(1, 0, 2).reshape(3 * units, 4 * shard_rows)
    line_count, line_place = lax.axis_size("fsdp"), lax.axis_index("fsdp")
    ffn_full = columns_join(None, ffn_line, line_place, line_count, 4)
    ends_apart = sorted({1 % line_count, line_count - 1} - {0})
    ffn_near = {d: shift(tie(ffn_line, lines[parts - 1]), "fsdp", d) for d in ends_apart}

    ctx_place = lax.axis_index("ctx")
    first_pos = ctx_place * local_len
    starts = doc_start - first_pos
    col, row = starts[:, :, None], starts[:, None, :]
    conv = by_head([conv_weight[0], conv_weight[1], conv_weight[2]])
    bias = jnp.pad(beta_bias, (0, spare))[None]
    gain_head = gain_o[None]
    tokens = block_input.reshape(row_count, width)
    inputs = wide(tokens)
    normed_mix = low(inputs * rms_scale(inputs, EPSILON) * gain_mix)
    inputs_mine = wide(rows_mine(block_input).reshape(-1, width))
    grads_mine = rows_mine(out_grad).reshape(-1, width)

    square = Square(tie(lines[0], ffn_line)).forward()
    mix_full, kept, pre = [], [], []
    for p in range(parts):
        mix_full.append(square.pieces())
        square = Square(tie(lines[p + 1], *square.done()))
        if p == 0:
            pre.append(gathered_times(normed_mix, ctx_place, mix_full[p]))
        else:
            pre.append(gathered_times(tie(normed_mix, lines[-1]), ctx_place, mix_full[p]))
        ends = pre[p].reshape(seq_count, local_len, -1)[:, local_len - HALO :, :part_cols]
        halo = from_behind(ends, "ctx", 1)
        convs = conv[:, p * part_cols : (p + 1) * part_cols]
        held = pre[p]
        if p > 0:
            held, ffn_full = lax.optimization_barrier((held, ffn_full, grad_square.beside, grad_square.across))[:2]
        kept.append(
            [halo, convs]
            + list(
                mixer_forward(
                    held, pre[0], bias, halo, convs, col, row, taps, p * part_heads, part_heads, group
                )
            )
        )
        square.forward(kept[p][2])
        if p == 0:
            ffn_near = dict(zip(ends_apart, lax.optimization_barrier(tuple(ffn_near.values()))))
            for d in ends_apart:
                ffn_full = columns_join(ffn_full, ffn_near[d], (line_place - d) % line_count, line_count, 4)
            cut = 3 * units // 2
            ffn_far = {
                d: shift(tie(ffn_line[:cut], *ffn_near.values()), "fsdp", d) for d in range(2, line_count - 1)
            }
            square.upper = tie(square.upper, *ffn_near.values())
            grad_square = Square(tie(grads_mine, kept[p][2]))
        if p == parts - 1:
            grad_square.forward()
    out_full = square.pieces()

    entered, transfers, mixed_rows = [], [], []
    for _, _, own, carry, final, _, _, _ in kept:
        transfers.append(low(final[..., LANES:]))
        first = final[..., :LANES]
        if len(entered) == parts - 1:
            first = tie(first, *grad_square.done(), *ffn_far.values())
            ffn_far = {
                d: [piece, shift(tie(ffn_line[cut:], piece), "fsdp", d)] for d, piece in ffn_far.items()
            }
        entered.append(pass_states(first, transfers[-1], 1))
        if len(entered) == parts:
            carry = tie(carry, *(piece[1] for piece in ffn_far.values()))
        mixed_rows.append(mixer_output(own, carry, entered[-1], gain_head, group))
    mixed_rows = jnp.concatenate(mixed_rows, axis=1)

    branch = gathered_times_transposed([mixed_rows], ctx_place, [out_full]).reshape(seq_count, local_len, width)
    residual = inputs_mine + rows_scatter(branch).reshape(-1, width)
    scale_ffn = rms_scale(residual, EPSILON)
    square = Square(low(residual * scale_ffn * gain_ffn))
    for d, pieces in ffn_far.items():
        piece = jnp.concatenate(pieces, axis=0)
        ffn_full = columns_join(ffn_full, piece, (line_place - d) % line_count, line_count, 4)

    ffn_rows = [both_sides(square.own)]
    grad_rows = [
        both_sides(part) for part in (grad_square.own, grad_square.beside, grad_square.across, grad_square.far())
    ]
    ffn_out = [ffn_both(ffn_rows[0], grad_rows[0], ffn_full)]
    square.forward(ffn_out[0][0][0])
    ffn_rows.append(both_sides(tie(square.beside, ffn_out[0][0][0])))
    ffn_out.append(ffn_both(ffn_rows[1], grad_rows[1], ffn_full))
    ffn_rows.append(both_sides(tie(square.across, ffn_out[0][0][0], *square.done())))
    mine, other = ffn_rows[2]
    ffn_out.append(ffn_both((tie(mine, ffn_out[1][0][0]), other), grad_rows[2], ffn_full))
    beside_sums, across_sums = (low(core_sum(*(side[1] for side in ffn_out[bit]))) for bit in (1, 2))
    ffn_rows.append(both_sides(square.far()))
    mine, other = ffn_rows[3]
    ffn_out.append(ffn_both((tie(mine, beside_sums, across_sums), other), grad_rows[3], ffn_full))
    near_sums = (flip(beside_sums, "ctx", 1), flip(across_sums, "ctx", 2))
    mine, other = (side[1] for side in ffn_out[3])
    far_sums = low(core_sum(mine, tie(other, *near_sums)))
    acts = [side[0] for outs in ffn_out for side in outs]
    acts[0] = tie(acts[0], far_sums)
    far_sums = flip(far_sums, "ctx", 3)
    sums = ffn_weights(
        acts,
        [side for sides in ffn_rows for side in sides],
        [side for sides in grad_rows for side in sides],
        line_count,
        4,
    ).reshape(line_count, 3 * units, 4 * shard_rows)

    far_sums, sums = lax.optimization_barrier((far_sums, sums))
    grad_normed = core_sum(*(side[1] for side in ffn_out[0]))
    grad_normed = grad_normed + wide(near_sums[0]) + wide(near_sums[1]) + wide(far_sums)
    back_ffn, unit_ffn = norm_backward(grad_normed, residual, scale_ffn, gain_ffn)
    grad_residual = wide(grads_mine) + back_ffn
    gain_ffn_part = jnp.sum(grad_normed * unit_ffn, axis=0)
    grad_branch = rows_full(low(grad_residual).reshape(seq_count, -1, width)).reshape(row_count, width)
    grad_heads = gathered_times(grad_branch, ctx_place, out_full)
    backs, acrosses, gain_o_part = [], [], 0.0
    for p in range(parts):
        _, _, own, carry, _, _, _, _ = kept[p]
        back, across, gain_part = mixer_output_backward(
            own, carry, entered[p], gain_head, grad_heads, p * part_heads, group
        )
        backs.append(back)
        acrosses.append(across)
        gain_o_part = gain_o_part + jnp.sum(gain_part, axis=(0, 1, 2))
    grad_end = pass_states(jnp.concatenate(acrosses, axis=1), jnp.concatenate(transfers, axis=1), -1)
    results = []
    for outs in ffn_out:
        mine, other = (side[2] for side in outs)
        results.append(core_sum(mine, tie(other, grad_branch)))
    result_near = [flip(tie(low(results[bit]), grad_end), "ctx", bit) for bit in (1, 2)]
    result_own, result_far = results[0], results[3]

    def line_piece(distance):
        return lax.dynamic_index_in_dim(sums, (line_place + distance) % line_count, 0, keepdims=False)

    total = wide(line_piece(0))
    cut = 3 * units // 2
    line_sends = [(d, 0, 3 * units) for d in ends_apart]
    line_sends += [(d, at, at + cut) for d in range(2, line_count - 1) for at in (0, cut)]
    line_got = []
    for d, low_row, high_row in line_sends:
        piece = line_piece(d)[low_row:high_row]
        if line_got:
            piece = tie(piece, grad_end, line_got[-1])
        line_got.append(shift(piece, "fsdp", d))

    out_grad_w = low(outer_rows(grad_branch, mixed_rows))
    out_grad_w = wide(lax.psum_scatter(out_grad_w, ("ctx", "fsdp"), scatter_dimension=0, tiled=True)).T

    columns = neighbour_columns(normed_mix)
    grad_mixes, mix_grads, conv_parts = [None] * parts, [None] * parts, [None] * parts
    logits = 0.0
    scatter = None
    for p in reversed(range(parts)):
        halo, convs, own, carry, final, inverses, updates, states = kept[p]
        heads = slice(p * part_heads, (p + 1) * part_heads)
        back = tie(backs[p], *line_got[:1]) if scatter is None else tie(backs[p], *scatter.sent)
        grad_mix, tail, before, conv_parts[p], logit = mixer_backward(
            pre[p], pre[0], bias, halo, convs, col, row, back, inverses, updates, states,
            entered[p], grad_end[:, heads], taps, p * part_heads, part_heads, group,
        )
        logits = logits + logit
        tail = low(tail + from_behind(before, "ctx", -1))
        grad_mix = put(grad_mix.reshape(seq_count, local_len, -1), tail, 0, local_len - HALO, 0)
        grad_mix = grad_mix.reshape(row_count, -1)
        if scatter is not None:
            mix_grads[p + 1] = scatter.finish(grad_mix)
        else:
            grad_mix = tie(grad_mix, *result_near, *line_got[1:2])
        if p == 0:
            grad_mix = tie(jnp.concatenate([grad_mix, low(logits)], axis=1), *line_got[2:3])
        grad_mixes[p] = grad_mix
        scatter = Scatter(columns, grad_mix)
    mix_grads[0] = scatter.finish()
    for (_, low_row, high_row), part in zip(line_sends, line_got):
        total = total + jnp.pad(wide(part), ((low_row, total.shape[0] - high_row), (0, 0)))
    sums = tie(low(total), grad_mix).reshape(3 * units, 4, shard_rows).transpose(1, 0, 2)
    arrived = lax.all_to_all(sums, "ctx", 0, 0).reshape(4, 3, units, shard_rows)
    gate_grad, up_grad, down_grad = (wide(arrived[:, i].reshape(units_here, shard_rows)) for i in range(3))
    result = result_own + wide(result_near[0]) + wide(result_near[1])
    result = result + wide(flip(low(tie(result_far, *scatter.last)), "ctx", 3))
    block_output = rows_full(low(residual + result).reshape(seq_count, -1, width))
    joined = jnp.concatenate([grad[:, :part_cols] for grad in mix_grads], axis=1)
    query_grad, key_grad, value_grad = by_kind(joined)
    beta_grad = mix_grads[0][:, part_cols : part_cols + heads_here]

    mix_back = gathered_times_transposed(grad_mixes, ctx_place, mix_full)
    mix_back = rows_scatter(mix_back.reshape(seq_count, local_len, width)).reshape(-1, width)
    back_mix, unit_mix = norm_backward(mix_back, inputs_mine, rms_scale(inputs_mine, EPSILON), gain_mix)
    input_grad = rows_full(low(grad_residual + back_mix).reshape(seq_count, -1, width))
    gain_mix_part = jnp.sum(mix_back * unit_mix, axis=0)

    conv_cols = jnp.concatenate([jnp.sum(part, axis=0)[:taps] for part in conv_parts], axis=1)
    gains = butterfly(jnp.concatenate([gain_mix_part, gain_ffn_part, gain_o_part]), ("tp",))
    sums = jnp.concatenate([gains, conv_cols.reshape(-1), jnp.sum(logits, axis=0)])
    sums = butterfly(sums, ("ctx", "fsdp"))
    ends = [width, 2 * width, 2 * width + LANES, sums.shape[0] - LANES]
    gain_mix_grad, gain_ffn_grad, gain_o_grad, conv_grad, bias_grad = jnp.split(sums, ends)
    conv_grad = jnp.stack(by_kind(conv_grad.reshape(taps, -1)))
    bias_grad = bias_grad[:heads_here]
    return (
        block_output,
        input_grad,
        gain_mix_grad,
        query_grad,
        key_grad,
        value_grad,
        beta_grad,
        bias_grad,
        conv_grad,
        gain_o_grad,
        out_grad_w,
        gain_ffn_grad,
        gate_grad.T,
        up_grad.T,
        down_grad,
    )


def solution(mesh):
    placed = (
        P("fsdp", "ctx", None),
        P("fsdp", "ctx"),
        P(),
        P(("ctx", "fsdp"), "tp"),
        P(("ctx", "fsdp"), "tp"),
        P(("ctx", "fsdp"), "tp"),
        P(("ctx", "fsdp"), "tp"),
        P("tp"),
        P(None, None, "tp"),
        P(),
        P("tp", ("ctx", "fsdp")),
        P(),
        P(("ctx", "fsdp"), "tp"),
        P(("ctx", "fsdp"), "tp"),
        P("tp", ("ctx", "fsdp")),
        P("fsdp", "ctx", None),
    )
    return jax.shard_map(
        local,
        mesh=mesh,
        in_specs=placed,
        out_specs=(
            P("fsdp", "ctx", None),
            P("fsdp", "ctx", None),
            P(),
            P(("ctx", "fsdp"), "tp"),
            P(("ctx", "fsdp"), "tp"),
            P(("ctx", "fsdp"), "tp"),
            P(("ctx", "fsdp"), "tp"),
            P("tp"),
            P(None, None, "tp"),
            P(),
            P("tp", ("ctx", "fsdp")),
            P(),
            P(("ctx", "fsdp"), "tp"),
            P(("ctx", "fsdp"), "tp"),
            P("tp", ("ctx", "fsdp")),
        ),
        check_vma=False,
    )
```

```python
import functools
import math
import jax
import jax.numpy as jnp
from jax import lax
from jax.experimental import pallas as pl
from jax.experimental.pallas import tpu as pltpu
from jax.sharding import PartitionSpec as P

LANES = 128
CHUNK = 128
HALO = 8
EPSILON = 1e-06
HEAD_FLOOR = 0.01
VMEM_BYTES = 60 * 1024 * 1024


def low(value):
    return value.astype(jnp.bfloat16)


def mul_nn(left, right):
    return lax.dot_general(low(left), low(right), (((1,), (0,)), ((), ())), preferred_element_type=jnp.float32)


def mul_nt(left, right):
    return lax.dot_general(low(left), low(right), (((1,), (1,)), ((), ())), preferred_element_type=jnp.float32)


def mul_tn(left, right):
    return lax.dot_general(low(left), low(right), (((0,), (0,)), ((), ())), preferred_element_type=jnp.float32)


def iota(shape, axis):
    return lax.broadcasted_iota(jnp.int32, shape, axis)


def chunk_masks(col, row, first):
    size = col.shape[0]
    same = col == row
    order, other = iota((size, size), 0), iota((size, size), 1)
    upto = same & (order >= other)
    below = same & (order > other)
    carried = (col < first).astype(jnp.float32)
    last = (col == row[:, size - 1 :]).astype(jnp.float32)
    keep = (row[:, size - 1 :] < first).astype(jnp.float32)
    return upto, below, carried, last, keep


def invert_units(systems):
    size = systems[0].shape[0]
    order, other = iota((size, size), 0), iota((size, size), 1)
    identity = (order == other).astype(jnp.float32)
    span = 1
    found = None
    while span < size:
        pair = (order // (2 * span) == other // (2 * span)) & (order // span != other // span)
        parts = [jnp.where(pair, system, 0.0) for system in systems]
        if found is None:
            found = [identity - part for part in parts]
        else:
            right = [mul_nn(part, value) for part, value in zip(parts, found)]
            found = [value - mul_nn(value, part) for value, part in zip(found, right)]
        span *= 2
    return found


def conv_rows(ext, conv, col, offset, size, lane, taps):
    total = None
    moved = []
    position = iota((size, 1), 0) + offset
    for tap in range(taps):
        back = taps - 1 - tap
        values = ext[pl.ds(HALO + offset - back, size), lane : lane + LANES]
        values = jnp.where(position - back >= col, values, 0.0)
        moved.append(values)
        term = conv[tap : tap + 1, lane : lane + LANES] * values
        total = term if total is None else total + term
    return total, moved


def unit(values):
    return values * lax.rsqrt(jnp.sum(values * values, axis=-1, keepdims=True) + EPSILON)


def head_column(values, head):
    return jnp.sum(jnp.where(iota(values.shape, 1) == head, values, 0.0), axis=-1, keepdims=True)


def forward_kernel(taps, heads, first, pre, beta, bias, halo, conv, col_ref, row_ref, own, carry, final, inv, upd, states, ext):
    length = pre.shape[0]
    ext[:HALO] = halo[0]
    ext[HALO:] = pre[...]
    head = first + pl.program_id(1) * heads
    jobs = [(i, j) for j in range(length // CHUNK) for i in range(heads)]
    data = {}
    for j in range(length // CHUNK):
        rows = pl.ds(j * CHUNK, CHUNK)
        col, row = col_ref[0, rows], row_ref[0, :, rows]
        masks = chunk_masks(col, row, j * CHUNK)
        strengths = jax.nn.sigmoid(beta[rows] + bias[...])
        for i in range(heads):
            acts = []
            for kind in range(3):
                total, _ = conv_rows(ext, conv, col, j * CHUNK, CHUNK, (3 * i + kind) * LANES, taps)
                acts.append(total * jax.nn.sigmoid(total))
            query, key, value = unit(acts[0]), unit(acts[1]), acts[2]
            strength = head_column(strengths, head + i)
            grams = mul_nt(jnp.concatenate([low(key), low(query)], axis=0), key)
            system = jnp.where(masks[1], strength * grams[:CHUNK], 0.0)
            scores = low(jnp.where(masks[0], grams[CHUNK:], 0.0))
            data[i, j] = (low(query), low(key), value, strength, scores, masks, system)
    inverses = dict(zip(jobs, invert_units([data[job][6] for job in jobs])))
    for i in range(heads):
        state = jnp.concatenate(
            [
                jnp.zeros((LANES, LANES), jnp.float32),
                (iota((LANES, LANES), 0) == iota((LANES, LANES), 1)).astype(jnp.float32),
            ],
            axis=1,
        )
        final[0, i] = state
    for j in range(length // CHUNK):
        rows = pl.ds(j * CHUNK, CHUNK)
        for i in range(heads):
            query, key, value, strength, scores, masks, _ = data[i, j]
            _, _, carried, last, keep = masks
            inverse = low(inverses[i, j])
            state = final[0, i]
            state_low = low(state)
            read = mul_nn(jnp.concatenate([key, query], axis=0), state_low)
            wide = jnp.concatenate([value, jnp.zeros_like(value)], axis=1)
            targets = strength * (wide - carried * read[:CHUNK])
            update = low(mul_nn(inverse, targets))
            result = carried * read[CHUNK:] + mul_nn(scores, update)
            final[0, i] = keep * state + mul_tn(key * low(last), update)
            lanes = slice(i * LANES, (i + 1) * LANES)
            own[rows, lanes] = result[:, :LANES]
            carry[rows, lanes] = low(result[:, LANES:])
            inv[0, i, j] = inverse
            upd[0, i, j] = update
            states[0, i, j] = state_low


def mixer_forward(pre, logit, bias, halo, conv, col, row, taps, first, heads_here, group):
    seqs, length = col.shape[0], col.shape[1]
    steps = heads_here // group
    chunks = length // CHUNK
    wide = 3 * LANES * group
    rows = seqs * length

    def tile(*tail, kind):
        return jax.ShapeDtypeStruct((seqs, heads_here) + tail, kind)

    def spec(*tail):
        return pl.BlockSpec((1, group) + tail, lambda s, h: (s, h) + (0,) * len(tail))

    flat = pl.BlockSpec((length, LANES * group), lambda s, h: (s, h))
    last = logit.shape[1] // LANES - 1
    return pl.pallas_call(
        functools.partial(forward_kernel, taps, group, first),
        grid=(seqs, steps),
        in_specs=[
            pl.BlockSpec((length, wide), lambda s, h: (s, h)),
            pl.BlockSpec((length, LANES), lambda s, h: (s, last)),
            pl.BlockSpec((1, LANES), lambda s, h: (0, 0)),
            pl.BlockSpec((1, HALO, wide), lambda s, h: (s, 0, h)),
            pl.BlockSpec((conv.shape[0], wide), lambda s, h: (0, h)),
            pl.BlockSpec((1, length, 1), lambda s, h: (s, 0, 0)),
            pl.BlockSpec((1, 1, length), lambda s, h: (s, 0, 0)),
        ],
        out_specs=[
            flat,
            flat,
            spec(LANES, 2 * LANES),
            spec(chunks, CHUNK, CHUNK),
            spec(chunks, CHUNK, 2 * LANES),
            spec(chunks, LANES, 2 * LANES),
        ],
        out_shape=[
            jax.ShapeDtypeStruct((rows, heads_here * LANES), jnp.float32),
            jax.ShapeDtypeStruct((rows, heads_here * LANES), jnp.bfloat16),
            tile(LANES, 2 * LANES, kind=jnp.float32),
            tile(chunks, CHUNK, CHUNK, kind=jnp.bfloat16),
            tile(chunks, CHUNK, 2 * LANES, kind=jnp.bfloat16),
            tile(chunks, LANES, 2 * LANES, kind=jnp.bfloat16),
        ],
        scratch_shapes=[pltpu.VMEM((length + HALO, wide), jnp.float32)],
        compiler_params=pltpu.CompilerParams(vmem_limit_bytes=VMEM_BYTES),
        cost_estimate=pl.CostEstimate(
            flops=60 * rows * heads_here * CHUNK * LANES, bytes_accessed=40 * rows * heads_here * LANES, transcendentals=0
        ),
    )(pre, logit, bias, halo, conv, col, row)


def backward_kernel(
    taps, heads, first, pre, beta, bias, halo, conv, col_ref, row_ref, grad_ref, inv, upd, states, start, end,
    grad_pre, tail, before, conv_grad, logits, ext, grad_ext,
):
    length = pre.shape[0]
    step = pl.program_id(1)
    head = first + step * heads
    ext[:HALO] = halo[0]
    ext[HALO:] = pre[...]
    grad_ext[...] = jnp.zeros_like(grad_ext)

    @pl.when(step == 0)
    def _():
        logits[...] = jnp.zeros_like(logits)

    grad_states = [end[0, i] for i in range(heads)]
    entry = [low(start[0, i]) for i in range(heads)]
    tap_sums = {}
    for j in reversed(range(length // CHUNK)):
        offset = j * CHUNK
        rows = pl.ds(offset, CHUNK)
        col, row = col_ref[0, rows], row_ref[0, :, rows]
        upto, below, carried, last, keep = chunk_masks(col, row, offset)
        strengths = jax.nn.sigmoid(beta[rows] + bias[...])
        grad_logit = jnp.zeros((CHUNK, LANES), jnp.float32)
        for i in range(heads):
            raw, taps_in = [], []
            for kind in range(3):
                total, moved = conv_rows(ext, conv, col, offset, CHUNK, (3 * i + kind) * LANES, taps)
                raw.append(total)
                taps_in.append(moved)
            gates = [jax.nn.sigmoid(total) for total in raw]
            acts = [total * gate for total, gate in zip(raw, gates)]
            scales = [lax.rsqrt(jnp.sum(act * act, axis=-1, keepdims=True) + EPSILON) for act in acts[:2]]
            query, key, value = acts[0] * scales[0], acts[1] * scales[1], acts[2]
            strength = head_column(strengths, head + i)
            lanes = slice(i * LANES, (i + 1) * LANES)
            query_low, key_low = low(query), low(key)
            grams = mul_nt(jnp.concatenate([key_low, query_low], axis=0), key_low)
            gram = jnp.where(below, grams[:CHUNK], 0.0)
            scores = jnp.where(upto, grams[CHUNK:], 0.0)
            inverse = inv[0, i, j]
            update = upd[0, i, j]
            update = low(update[:, :LANES].astype(jnp.float32) + mul_nn(update[:, LANES:], entry[i]))
            state = states[0, i, j]
            state = low(state[:, :LANES].astype(jnp.float32) + mul_nn(state[:, LANES:], entry[i]))
            grad_out = grad_ref[rows, lanes]
            grad_state = grad_states[i]
            grad_state_low = low(grad_state)
            key_last = key_low * low(last)
            grad_update = mul_tn(scores, grad_out) + mul_nn(key_last, grad_state_low)
            grad_target = mul_tn(inverse, grad_update)
            weighted = strength * grad_target
            passed = carried * weighted
            out_carried = carried * grad_out.astype(jnp.float32)
            query_carried = query_low * low(carried)
            grad_states[i] = (
                keep * grad_state + mul_tn(query_carried, grad_out) - mul_tn(key_low, passed)
            )
            grad_scores = jnp.where(upto, mul_nt(grad_out, update), 0.0)
            grad_system = jnp.where(below, mul_nt(grad_target, update), 0.0)
            remainder = value - carried * mul_nn(key_low, state)
            grad_strength = jnp.sum(grad_target * remainder - grad_system * gram, axis=-1, keepdims=True)
            scaled = strength * grad_system
            from_state = mul_nt(jnp.concatenate([low(out_carried), low(passed)], axis=0), state)
            from_keys = mul_nn(jnp.concatenate([low(grad_scores), low(scaled + scaled.T)], axis=0), key_low)
            grad_query = from_state[:CHUNK] + from_keys[:CHUNK]
            grad_key = (
                mul_tn(grad_scores, query_low)
                + last * mul_nt(update, grad_state_low)
                - from_state[CHUNK:]
                - from_keys[CHUNK:]
            )
            grad_logit = grad_logit + jnp.where(
                iota((CHUNK, LANES), 1) == head + i, grad_strength * strength * (1.0 - strength), 0.0
            )
            grads = [
                scales[0] * (grad_query - query * jnp.sum(grad_query * query, axis=-1, keepdims=True)),
                scales[1] * (grad_key - key * jnp.sum(grad_key * key, axis=-1, keepdims=True)),
                weighted,
            ]
            position = iota((CHUNK, 1), 0) + offset
            for kind in range(3):
                gate, total = gates[kind], raw[kind]
                grad_conv = grads[kind] * gate * (1.0 + total * (1.0 - gate))
                lane = (3 * i + kind) * LANES
                for tap in range(taps):
                    back = taps - 1 - tap
                    part = jnp.sum(grad_conv * taps_in[kind][tap], axis=0, keepdims=True)
                    spot = (i, kind, tap)
                    tap_sums[spot] = part if spot not in tap_sums else tap_sums[spot] + part
                    back_part = jnp.where(
                        position - back >= col, grad_conv * conv[tap : tap + 1, lane : lane + LANES], 0.0
                    )
                    where = pl.ds(HALO + offset - back, CHUNK)
                    grad_ext[where, lane : lane + LANES] += back_part
        logits[rows] += grad_logit
    grad_pre[...] = low(grad_ext[HALO:])
    before[0] = grad_ext[:HALO]
    tail[0] = grad_ext[length:]
    for i in range(heads):
        for kind in range(3):
            lane = (3 * i + kind) * LANES
            for tap in range(taps):
                conv_grad[0, tap : tap + 1, lane : lane + LANES] = tap_sums[i, kind, tap]


def mixer_backward(
    pre, logit, bias, halo, conv, col, row, grad_mixed, inv, upd, states, start, end, taps, first, heads_here, group
):
    seqs, length = col.shape[0], col.shape[1]
    steps = heads_here // group
    chunks = length // CHUNK
    wide = 3 * LANES * group
    rows = seqs * length

    def spec(*tail):
        return pl.BlockSpec((1, group) + tail, lambda s, h: (s, h) + (0,) * len(tail))

    last = logit.shape[1] // LANES - 1
    part = pl.BlockSpec((1, HALO, wide), lambda s, h: (s, 0, h))
    edge = jax.ShapeDtypeStruct((seqs, HALO, 3 * LANES * heads_here), jnp.float32)
    return pl.pallas_call(
        functools.partial(backward_kernel, taps, group, first),
        grid=(seqs, steps),
        in_specs=[
            pl.BlockSpec((length, wide), lambda s, h: (s, h)),
            pl.BlockSpec((length, LANES), lambda s, h: (s, last)),
            pl.BlockSpec((1, LANES), lambda s, h: (0, 0)),
            part,
            pl.BlockSpec((conv.shape[0], wide), lambda s, h: (0, h)),
            pl.BlockSpec((1, length, 1), lambda s, h: (s, 0, 0)),
            pl.BlockSpec((1, 1, length), lambda s, h: (s, 0, 0)),
            pl.BlockSpec((length, LANES * group), lambda s, h: (s, h)),
            spec(chunks, CHUNK, CHUNK),
            spec(chunks, CHUNK, 2 * LANES),
            spec(chunks, LANES, 2 * LANES),
            spec(LANES, LANES),
            spec(LANES, LANES),
        ],
        out_specs=[
            pl.BlockSpec((length, wide), lambda s, h: (s, h)),
            part,
            part,
            part,
            pl.BlockSpec((length, LANES), lambda s, h: (s, 0)),
        ],
        out_shape=[
            jax.ShapeDtypeStruct((rows, 3 * LANES * heads_here), jnp.bfloat16),
            edge,
            edge,
            edge,
            jax.ShapeDtypeStruct((rows, LANES), jnp.float32),
        ],
        scratch_shapes=[
            pltpu.VMEM((length + HALO, wide), jnp.float32),
            pltpu.VMEM((length + HALO, wide), jnp.float32),
        ],
        compiler_params=pltpu.CompilerParams(vmem_limit_bytes=VMEM_BYTES),
        cost_estimate=pl.CostEstimate(
            flops=60 * rows * heads_here * CHUNK * LANES, bytes_accessed=40 * rows * heads_here * LANES, transcendentals=0
        ),
    )(pre, logit, bias, halo, conv, col, row, grad_mixed, inv, upd, states, start, end)


def mixed_rows_of(own, carry, start):
    return own + mul_nn(carry, start)


def output_kernel(heads, own, carry, start, gain, out):
    for i in range(heads):
        lanes = slice(i * LANES, (i + 1) * LANES)
        mixed = mixed_rows_of(own[:, lanes], carry[:, lanes], start[0, i])
        scale = lax.rsqrt(jnp.mean(mixed * mixed, axis=-1, keepdims=True) + HEAD_FLOOR)
        out[:, lanes] = low(mixed * scale * gain[...])


def output_backward_kernel(heads, own, carry, start, gain, grad, out, across, gain_grad):
    total = jnp.zeros((1, LANES), jnp.float32)
    for i in range(heads):
        lanes = slice(i * LANES, (i + 1) * LANES)
        carried = carry[:, lanes]
        mixed = mixed_rows_of(own[:, lanes], carried, start[0, i])
        scale = lax.rsqrt(jnp.mean(mixed * mixed, axis=-1, keepdims=True) + HEAD_FLOOR)
        normed = mixed * scale
        upper = grad[:, lanes].astype(jnp.float32)
        total = total + jnp.sum(upper * normed, axis=0, keepdims=True)
        weighted = upper * gain[...]
        back = scale * (weighted - normed * jnp.mean(weighted * normed, axis=-1, keepdims=True))
        out[:, lanes] = low(back)
        across[0, i] = mul_tn(carried, back)
    gain_grad[0, 0] = total


def mixer_output(own, carry, start, gain, group):
    seqs, heads_here = start.shape[:2]
    rows = own.shape[0]
    length = rows // seqs
    flat = pl.BlockSpec((length, LANES * group), lambda s, h: (s, h))
    square = pl.BlockSpec((1, group, LANES, LANES), lambda s, h: (s, h, 0, 0))
    return pl.pallas_call(
        functools.partial(output_kernel, group),
        grid=(seqs, heads_here // group),
        in_specs=[flat, flat, square, pl.BlockSpec((1, LANES), lambda s, h: (0, 0))],
        out_specs=flat,
        out_shape=jax.ShapeDtypeStruct(own.shape, jnp.bfloat16),
        compiler_params=pltpu.CompilerParams(vmem_limit_bytes=VMEM_BYTES),
        cost_estimate=pl.CostEstimate(
            flops=2 * own.size * LANES, bytes_accessed=8 * own.size, transcendentals=0
        ),
    )(own, carry, start, gain)


def mixer_output_backward(own, carry, start, gain, grad, first, group):
    seqs, heads_here = start.shape[:2]
    rows = own.shape[0]
    length = rows // seqs
    steps = heads_here // group
    flat = pl.BlockSpec((length, LANES * group), lambda s, h: (s, h))
    base = first // group
    shifted = pl.BlockSpec((length, LANES * group), lambda s, h: (s, base + h))
    square = pl.BlockSpec((1, group, LANES, LANES), lambda s, h: (s, h, 0, 0))
    return pl.pallas_call(
        functools.partial(output_backward_kernel, group),
        grid=(seqs, steps),
        in_specs=[flat, flat, square, pl.BlockSpec((1, LANES), lambda s, h: (0, 0)), shifted],
        out_specs=[flat, square, pl.BlockSpec((1, 1, 1, LANES), lambda s, h: (s, h, 0, 0))],
        out_shape=[
            jax.ShapeDtypeStruct(own.shape, jnp.bfloat16),
            jax.ShapeDtypeStruct(start.shape, jnp.float32),
            jax.ShapeDtypeStruct((seqs, steps, 1, LANES), jnp.float32),
        ],
        compiler_params=pltpu.CompilerParams(vmem_limit_bytes=VMEM_BYTES),
        cost_estimate=pl.CostEstimate(
            flops=4 * own.size * LANES, bytes_accessed=12 * own.size, transcendentals=0
        ),
    )(own, carry, start, gain, grad)


def ffn_kernel(mine, other, mine_grads, other_grads, gate_w, up_w, down_w, *outs):
    rows = jnp.concatenate([mine[...], other[...]], axis=0)
    grads = jnp.concatenate([mine_grads[...], other_grads[...]], axis=0)
    half = mine.shape[0]
    gate = mul_nt(rows, gate_w[...])
    up = mul_nt(rows, up_w[...])
    grad_hidden = mul_nt(grads, down_w[...])
    sigmoid = jax.nn.sigmoid(gate)
    active = gate * sigmoid
    kept = low(active * up)
    back_gate = low(grad_hidden * up * sigmoid * (1.0 + gate * (1.0 - sigmoid)))
    back_up = low(grad_hidden * active)
    grad_rows = low(mul_nn(back_gate, gate_w[...]) + mul_nn(back_up, up_w[...]))
    result = low(mul_nn(kept, down_w[...]))
    for side in range(2):
        here = slice(side * half, (side + 1) * half)
        acts, grad_out, result_out = outs[3 * side : 3 * side + 3]
        for kind, value in enumerate((back_gate, back_up, kept)):
            acts[kind] = value[here]
        grad_out[...] = grad_rows[here]
        result_out[...] = result[here]


def ffn_both(rows, grads, gate_up, down):
    count, width = rows[0].shape
    units = down.shape[0]
    tile = min(256, count)
    wide_rows = pl.BlockSpec((tile, width), lambda i: (i, 0))
    narrow = pl.BlockSpec((3, tile, units), lambda i: (0, i, 0))

    def third(index):
        return pl.BlockSpec((units, width), lambda i: (index, 0))

    flat = jax.ShapeDtypeStruct((count, width), jnp.bfloat16)
    outs = pl.pallas_call(
        ffn_kernel,
        grid=(count // tile,),
        in_specs=[wide_rows] * 4 + [third(0), third(1), third(0)],
        out_specs=[narrow, wide_rows, wide_rows] * 2,
        out_shape=[jax.ShapeDtypeStruct((3, count, units), jnp.bfloat16), flat, flat] * 2,
        compiler_params=pltpu.CompilerParams(vmem_limit_bytes=VMEM_BYTES),
        cost_estimate=pl.CostEstimate(
            flops=24 * count * width * units, bytes_accessed=16 * count * width + 6 * units * width, transcendentals=0
        ),
    )(*rows, *grads, gate_up, gate_up, down)
    return outs[:3], outs[3:]


def ffn_weights_kernel(count, lines, *refs):
    acts, rows, grads = refs[:count], refs[count : 2 * count], refs[2 * count : 3 * count]
    out, total = refs[-2:]
    part = out.shape[-1]

    def add(sources):
        for i in range(count):
            value = mul_tn(acts[i][0], sources[i][...])
            if i == 0:
                total[...] = value
            else:
                total[...] += value

    @pl.when(pl.program_id(0) < 2)
    def _():
        add(rows)

    @pl.when(pl.program_id(0) == 2)
    def _():
        add(grads)

    for line in range(lines):
        out[line, 0] = low(total[:, line * part : (line + 1) * part])


def ffn_weights(acts, rows, grads, lines, squares):
    count, width = len(acts), rows[0].shape[1]
    size, units = acts[0].shape[1:]
    block = width // squares
    part = block // lines
    act_spec = pl.BlockSpec((1, size, units), lambda k, c: (k, 0, 0))
    row_spec = pl.BlockSpec((size, block), lambda k, c: (0, jnp.where(k < 2, c, squares - 1)))
    grad_spec = pl.BlockSpec((size, block), lambda k, c: (0, jnp.where(k < 2, 0, c)))
    return pl.pallas_call(
        functools.partial(ffn_weights_kernel, count, lines),
        grid=(3, squares),
        in_specs=[act_spec] * count + [row_spec] * count + [grad_spec] * count,
        out_specs=pl.BlockSpec((lines, 1, units, part), lambda k, c: (0, k, 0, c)),
        out_shape=jax.ShapeDtypeStruct((lines, 3, units, squares * part), jnp.bfloat16),
        scratch_shapes=[pltpu.VMEM((units, block), jnp.float32)],
        compiler_params=pltpu.CompilerParams(vmem_limit_bytes=VMEM_BYTES),
        cost_estimate=pl.CostEstimate(
            flops=6 * count * size * width * units, bytes_accessed=8 * count * size * width, transcendentals=0
        ),
    )(*acts, *rows, *grads)


def block_columns(place, bit, size):
    return pl.multiple_of((place[0] ^ bit) * size, size)


def gathered_kernel(place, rows, *refs):
    out = refs[-1]
    own, beside, across, upper, lower = refs[:-1]
    size, half = own.shape[0], upper.shape[0]
    total = None
    for bit, skip, ref in ((0, 0, own), (1, 0, beside), (2, 0, across), (3, 0, upper), (3, half, lower)):
        start = pl.multiple_of(block_columns(place, bit, size) + skip, half)
        value = mul_nn(rows[:, pl.ds(start, ref.shape[0])], ref[...])
        total = value if total is None else total + value
    out[...] = total


def gathered_times(rows, place, pieces):
    count, width = rows.shape
    columns = pieces[0].shape[1]
    tile = min(256, count)
    whole = [pl.BlockSpec(piece.shape, lambda i, place: (0, 0)) for piece in pieces]
    return pl.pallas_call(
        gathered_kernel,
        grid_spec=pltpu.PrefetchScalarGridSpec(
            num_scalar_prefetch=1,
            grid=(count // tile,),
            in_specs=[pl.BlockSpec((tile, width), lambda i, place: (i, 0))] + whole,
            out_specs=pl.BlockSpec((tile, columns), lambda i, place: (i, 0)),
        ),
        out_shape=jax.ShapeDtypeStruct((count, columns), jnp.float32),
        compiler_params=pltpu.CompilerParams(vmem_limit_bytes=VMEM_BYTES),
        cost_estimate=pl.CostEstimate(
            flops=2 * count * width * columns, bytes_accessed=2 * (count + columns) * width, transcendentals=0
        ),
    )(jnp.reshape(place, (1,)).astype(jnp.int32), rows, *pieces)


def gathered_transposed_kernel(count, place, *refs):
    factors, pieces, out = refs[:count], refs[count:-1], refs[-1]
    size, half = pieces[0].shape[0], pieces[3].shape[0]
    for i, (bit, skip) in enumerate(((0, 0), (1, 0), (2, 0), (3, 0), (3, half))):
        start = pl.multiple_of(block_columns(place, bit, size) + skip, half)
        total = None
        for p in range(count):
            value = mul_nt(factors[p][...], pieces[5 * p + i][...])
            total = value if total is None else total + value
        out[:, pl.ds(start, pieces[i].shape[0])] = low(total)


def gathered_times_transposed(factors, place, pieces):
    count, rows = len(factors), factors[0].shape[0]
    width = 4 * pieces[0][0].shape[0]
    tile = min(256, rows)
    flat = [piece for some in pieces for piece in some]
    whole = [pl.BlockSpec(piece.shape, lambda i, place: (0, 0)) for piece in flat]
    wides = [pl.BlockSpec((tile, factor.shape[1]), lambda i, place: (i, 0)) for factor in factors]
    columns = sum(factor.shape[1] for factor in factors)
    return pl.pallas_call(
        functools.partial(gathered_transposed_kernel, count),
        grid_spec=pltpu.PrefetchScalarGridSpec(
            num_scalar_prefetch=1,
            grid=(rows // tile,),
            in_specs=wides + whole,
            out_specs=pl.BlockSpec((tile, width), lambda i, place: (i, 0)),
        ),
        out_shape=jax.ShapeDtypeStruct((rows, width), jnp.bfloat16),
        compiler_params=pltpu.CompilerParams(vmem_limit_bytes=VMEM_BYTES),
        cost_estimate=pl.CostEstimate(
            flops=2 * rows * width * columns, bytes_accessed=2 * (rows + columns) * width, transcendentals=0
        ),
    )(jnp.reshape(place, (1,)).astype(jnp.int32), *factors, *flat)


def join_kernel(source, target):
    target[...] = source[0]


def columns_join(parts, squares):
    lines, rows, columns = parts.shape
    part = columns // squares
    return pl.pallas_call(
        join_kernel,
        grid=(lines, squares),
        in_specs=[pl.BlockSpec((1, rows, part), lambda i, j: (i, 0, j))],
        out_specs=pl.BlockSpec((rows, part), lambda i, j: (0, j * lines + i)),
        out_shape=jax.ShapeDtypeStruct((rows, lines * columns), parts.dtype),
        compiler_params=pltpu.CompilerParams(vmem_limit_bytes=VMEM_BYTES),
        cost_estimate=pl.CostEstimate(flops=0, bytes_accessed=4 * parts.size, transcendentals=0),
    )(parts)


def flip(value, axis, bit):
    devices = range(lax.axis_size(axis))
    return lax.ppermute(value, axis, [(i, i ^ bit) for i in devices])


def shift(value, axis, distance):
    count = lax.axis_size(axis)
    return lax.ppermute(value, axis, [(i, (i + distance) % count) for i in range(count)])


def from_behind(block, axis, distance):
    devices = range(lax.axis_size(axis))
    route = [(i - distance, i) for i in devices if i - distance in devices]
    return lax.ppermute(block, axis, route)


def tie(value, *earlier):
    return lax.optimization_barrier((value,) + earlier)[0]


def put(buffer, piece, *start):
    return lax.dynamic_update_slice(buffer, piece, start)


def wide(value):
    return value.astype(jnp.float32)


def gather_line(shard):
    count, place = lax.axis_size("fsdp"), lax.axis_index("fsdp")
    pieces = [shard] + [shift(shard, "fsdp", d) for d in range(1, count)]
    order = [(place - i) % count for i in range(count)]
    return jnp.concatenate([lax.select_n(which, *pieces) for which in order], axis=0)


class Square:
    def __init__(self, own):
        self.own = own
        self.half = own.shape[0] // 2
        self.beside = flip(own, "ctx", 1)
        self.across = flip(own, "ctx", 2)

    def forward(self, *earlier):
        upper = self.beside[: self.half]
        lower = self.across[self.half :]
        if earlier:
            upper, lower = lax.optimization_barrier((upper, lower) + earlier)[:2]
        self.upper = flip(upper, "ctx", 2)
        self.lower = flip(lower, "ctx", 1)
        return self

    def done(self):
        return (self.upper, self.lower)

    def pieces(self):
        return [self.own, self.beside, self.across, self.upper, self.lower]

    def far(self):
        return jnp.concatenate([self.upper, self.lower], axis=0)


def both_sides(rows):
    if lax.axis_size("tp") == 2:
        return rows, flip(rows, "tp", 1)
    every = lax.all_gather(rows, "tp", axis=0, tiled=True)
    half = every.shape[0] // 2
    return every[:half], every[half:]


def core_sum(mine, other):
    if lax.axis_size("tp") == 2:
        return wide(mine) + wide(flip(other, "tp", 1))
    both = jnp.concatenate([mine, other], axis=0)
    return wide(lax.psum_scatter(both, "tp", scatter_dimension=0, tiled=True))


def neighbour_columns(rows):
    width = rows.shape[1] // 4
    place = lax.axis_index("ctx")
    return [lax.dynamic_slice_in_dim(rows, (place ^ bit) * width, width, 1) for bit in range(4)]


def line_sum(own):
    count, place = own.shape[0], lax.axis_index("fsdp")
    total = lax.dynamic_index_in_dim(own, place, 0, keepdims=False)
    for distance in range(1, count):
        piece = lax.dynamic_index_in_dim(own, (place + distance) % count, 0, keepdims=False)
        total = total + wide(shift(low(piece), "fsdp", distance))
    return total


class Scatter:
    def __init__(self, columns, grads):
        self.columns, self.grads = columns, grads
        self.half = columns[0].shape[1] // 2
        beside, across = (
            jnp.concatenate([self.side(3, 1), self.side(1, 1)], axis=1),
            jnp.concatenate([self.side(3, 0), self.side(2, 0)], axis=1),
        )
        self.sent = [low(outer_rows(beside, grads)), low(outer_rows(across, grads))]
        self.first = (flip(self.sent[0], "ctx", 1), flip(self.sent[1], "ctx", 2))

    def side(self, bit, lower):
        return self.columns[bit][:, lower * self.half : (lower + 1) * self.half]

    def second(self, *earlier):
        first = self.first
        if earlier:
            first = lax.optimization_barrier(first + earlier)[:2]
        beside, across = (wide(part) for part in first)
        beside_upper = flip(low(outer_rows(self.side(1, 0), self.grads) + across[: self.half]), "ctx", 1)
        across_lower = flip(low(outer_rows(self.side(2, 1), self.grads) + beside[: self.half]), "ctx", 2)
        self.last = (beside_upper, across_lower)
        self.kept = (beside, across)

    def finish(self, *earlier):
        beside_upper, across_lower = lax.optimization_barrier(self.last + earlier)[:2]
        beside, across = self.kept
        own = outer_rows(self.columns[0], self.grads)
        upper = own[: self.half] + wide(beside_upper) + across[self.half :]
        lower = own[self.half :] + beside[self.half :] + wide(across_lower)
        own = jnp.concatenate([upper, lower], axis=0)
        lines = lax.axis_size("fsdp")
        return line_sum(own.reshape(lines, own.shape[0] // lines, own.shape[1]))


def butterfly(value, axes):
    for axis in axes:
        count, bit = lax.axis_size(axis), 1
        while bit < count:
            value = value + flip(value, axis, bit)
            bit *= 2
    return value


def rms_scale(values, floor_value):
    return lax.rsqrt(jnp.mean(values * values, axis=-1, keepdims=True) + floor_value)


def norm_backward(grad_normed, inputs, scale, gain):
    normed = inputs * scale
    weighted = grad_normed * gain
    return (
        scale * (weighted - normed * jnp.mean(weighted * normed, axis=-1, keepdims=True)),
        normed,
    )


def times(left, right):
    return jnp.dot(left, right, preferred_element_type=jnp.float32)


def times_transposed(left, right):
    return lax.dot_general(
        left, right, (((1,), (1,)), ((), ())), preferred_element_type=jnp.float32
    )


def outer_rows(left, right):
    return lax.dot_general(
        left, right, (((0,), (0,)), ((), ())), preferred_element_type=jnp.float32
    )


def rows_mine(rows):
    count = rows.shape[1] // lax.axis_size("tp")
    return lax.dynamic_slice_in_dim(rows, lax.axis_index("tp") * count, count, 1)


def rows_scatter(partial):
    if lax.axis_size("tp") != 2:
        return wide(lax.psum_scatter(partial, "tp", scatter_dimension=1, tiled=True))
    count = partial.shape[1] // 2
    other = lax.dynamic_slice_in_dim(partial, (1 - lax.axis_index("tp")) * count, count, 1)
    return wide(rows_mine(partial)) + wide(flip(other, "tp", 1))


def rows_full(mine):
    if lax.axis_size("tp") != 2:
        return lax.all_gather(mine, "tp", axis=1, tiled=True)
    other = flip(mine, "tp", 1)
    lower = lax.axis_index("tp") == 0
    return jnp.concatenate([jnp.where(lower, mine, other), jnp.where(lower, other, mine)], axis=1)


def by_head(parts):
    heads = range(parts[0].shape[-1] // LANES)
    return jnp.concatenate([part[..., h * LANES : (h + 1) * LANES] for h in heads for part in parts], axis=-1)


def by_kind(joined):
    return [
        jnp.concatenate(
            [
                some[..., at : at + LANES]
                for some in joined
                for at in range(kind * LANES, some.shape[-1], 3 * LANES)
            ],
            axis=-1,
        )
        for kind in range(3)
    ]


def pass_states(own, transfer, forward):
    rule = "shij,shjk->shik" if forward == 1 else "shji,shjk->shik"
    leaving = own
    entered = low(jnp.zeros_like(own))
    for repeat in range(lax.axis_size("ctx") - 1):
        entered = from_behind(low(leaving), "ctx", forward)
        leaving = own + jnp.einsum(rule, transfer, entered, preferred_element_type=jnp.float32)
    return wide(entered)


def local(
    block_input,
    doc_start,
    gain_mix,
    query_weight,
    key_weight,
    value_weight,
    beta_weight,
    beta_bias,
    conv_weight,
    gain_o,
    out_weight,
    gain_ffn,
    gate_weight,
    up_weight,
    down_weight,
    out_grad,
):
    seq_count, local_len, width = block_input.shape
    row_count = seq_count * local_len
    heads_here = beta_weight.shape[1]
    taps = conv_weight.shape[1]
    parts = 2 if heads_here % 2 == 0 else 1
    part_heads = heads_here // parts
    group = 2 if part_heads % 2 == 0 else 1
    part_cols = 3 * part_heads * LANES
    spare = LANES - heads_here
    units_here = gate_weight.shape[1]
    shard_rows = gate_weight.shape[0]

    joined = by_head([low(query_weight), low(key_weight), low(value_weight)])
    shards = [joined[:, p * part_cols : (p + 1) * part_cols] for p in range(parts)]
    shards[0] = jnp.concatenate([shards[0], jnp.pad(low(beta_weight), ((0, 0), (0, spare)))], axis=1)
    shards.append(low(out_weight).T)
    lines = []
    for shard in shards:
        lines.append(gather_line(tie(shard, lines[-1]) if lines else shard))
    units = units_here // 4
    pieces = jnp.stack([low(gate_weight).T, low(up_weight).T, low(down_weight)])
    pieces = pieces.reshape(3, 4, units, shard_rows).transpose(1, 0, 2, 3)
    ffn_line = lax.all_to_all(pieces.reshape(4, 3 * units, shard_rows), "ctx", 0, 0)
    ffn_line = ffn_line.transpose(1, 0, 2).reshape(3 * units, 4 * shard_rows)
    gate_up_parts = lax.all_gather(ffn_line[: 2 * units], "fsdp", axis=0)
    down_parts = lax.all_gather(ffn_line[2 * units :], "fsdp", axis=0)
    line_count = lax.axis_size("fsdp")

    ctx_place = lax.axis_index("ctx")
    first_pos = ctx_place * local_len
    starts = doc_start - first_pos
    col, row = starts[:, :, None], starts[:, None, :]
    conv = by_head([conv_weight[0], conv_weight[1], conv_weight[2]])
    bias = jnp.pad(beta_bias, (0, spare))[None]
    gain_head = gain_o[None]
    tokens = block_input.reshape(row_count, width)
    inputs = wide(tokens)
    normed_mix = low(inputs * rms_scale(inputs, EPSILON) * gain_mix)
    inputs_mine = wide(rows_mine(block_input).reshape(-1, width))
    grads_mine = rows_mine(out_grad).reshape(-1, width)

    square = Square(tie(lines[0], ffn_line)).forward()
    mix_full, kept, pre = [], [], []
    for p in range(parts):
        mix_full.append(square.pieces())
        square = Square(tie(lines[p + 1], *square.done()))
        rows = tie(normed_mix, lines[-1]) if p == 0 else normed_mix
        ends = rows.reshape(seq_count, local_len, width)[:, local_len - HALO :].reshape(seq_count * HALO, width)
        ends = gathered_times(ends, ctx_place, mix_full[p])[:, :part_cols]
        halo = from_behind(ends.reshape(seq_count, HALO, part_cols), "ctx", 1)
        pre.append(gathered_times(tie(rows, ends), ctx_place, mix_full[p]))
        convs = conv[:, p * part_cols : (p + 1) * part_cols]
        held = pre[p]
        if p > 0:
            held = tie(held, grad_square.beside, grad_square.across)
        kept.append(
            [halo, convs]
            + list(
                mixer_forward(
                    held, pre[0], bias, halo, convs, col, row, taps, p * part_heads, part_heads, group
                )
            )
        )
        square.forward(kept[p][2])
        if p == 0:
            grad_square = Square(tie(grads_mine, kept[p][2]))
        if p == parts - 1:
            grad_square.forward()
    out_full = square.pieces()

    entered, transfers, mixed_rows = [], [], []
    for _, _, own, carry, final, _, _, _ in kept:
        transfers.append(low(final[..., LANES:]))
        first = final[..., :LANES]
        if len(entered) == parts - 1:
            first, gate_up_parts = lax.optimization_barrier((first, gate_up_parts) + grad_square.done())[:2]
        entered.append(pass_states(first, transfers[-1], 1))
        if len(entered) == parts:
            carry, down_parts = lax.optimization_barrier((carry, down_parts))
        mixed_rows.append(mixer_output(own, carry, entered[-1], gain_head, group))
    mixed_rows = jnp.concatenate(mixed_rows, axis=1)
    grad_rows = [
        both_sides(part) for part in (grad_square.own, grad_square.beside, grad_square.across, grad_square.far())
    ]
    mixed_rows = tie(mixed_rows, *(other for _, other in grad_rows))

    branch = gathered_times_transposed([mixed_rows], ctx_place, [out_full]).reshape(seq_count, local_len, width)
    residual = inputs_mine + rows_scatter(branch).reshape(-1, width)
    scale_ffn = rms_scale(residual, EPSILON)
    square = Square(low(residual * scale_ffn * gain_ffn))
    ffn_full = (columns_join(gate_up_parts, 4), columns_join(down_parts, 4))

    ffn_rows = [both_sides(square.own)]
    ffn_out = [ffn_both(ffn_rows[0], grad_rows[0], *ffn_full)]
    square.forward(ffn_out[0][0][0])
    ffn_rows.append(both_sides(tie(square.beside, ffn_out[0][0][0])))
    ffn_out.append(ffn_both(ffn_rows[1], grad_rows[1], *ffn_full))
    ffn_rows.append(both_sides(tie(square.across, ffn_out[0][0][0])))
    mine, other = ffn_rows[2]
    ffn_out.append(ffn_both((tie(mine, ffn_out[1][0][0], *square.done()), other), grad_rows[2], *ffn_full))
    beside_sums, across_sums = (low(core_sum(*(side[1] for side in ffn_out[bit]))) for bit in (1, 2))
    ffn_rows.append(both_sides(square.far()))
    mine, other = ffn_rows[3]
    ffn_out.append(ffn_both((tie(mine, beside_sums, across_sums), other), grad_rows[3], *ffn_full))
    near_sums = (flip(beside_sums, "ctx", 1), flip(across_sums, "ctx", 2))
    mine, other = (side[1] for side in ffn_out[3])
    far_sums = low(core_sum(mine, tie(other, *near_sums)))
    acts = [side[0] for outs in ffn_out for side in outs]
    acts[0] = tie(acts[0], far_sums)
    far_sums = flip(far_sums, "ctx", 3)
    sums = ffn_weights(
        acts,
        [side for sides in ffn_rows for side in sides],
        [side for sides in grad_rows for side in sides],
        line_count,
        4,
    ).reshape(line_count, 3 * units, 4 * shard_rows)

    far_sums, sums = lax.optimization_barrier((far_sums, sums))
    result_near = []
    for bit in (1, 2):
        mine, other = (side[2] for side in ffn_out[bit])
        result_near.append(flip(low(core_sum(mine, tie(other, far_sums))), "ctx", bit))
    grad_normed = core_sum(*(side[1] for side in ffn_out[0]))
    grad_normed = grad_normed + wide(near_sums[0]) + wide(near_sums[1]) + wide(far_sums)
    back_ffn, unit_ffn = norm_backward(grad_normed, residual, scale_ffn, gain_ffn)
    grad_residual = wide(grads_mine) + back_ffn
    gain_ffn_part = jnp.sum(grad_normed * unit_ffn, axis=0)
    grad_branch = rows_full(low(grad_residual).reshape(seq_count, -1, width)).reshape(row_count, width)
    grad_heads = gathered_times(grad_branch, ctx_place, out_full)
    backs, acrosses, gain_o_part = [], [], 0.0
    for p in range(parts):
        _, _, own, carry, _, _, _, _ = kept[p]
        back, across, gain_part = mixer_output_backward(
            own, carry, entered[p], gain_head, grad_heads, p * part_heads, group
        )
        backs.append(back)
        acrosses.append(across)
        gain_o_part = gain_o_part + jnp.sum(gain_part, axis=(0, 1, 2))
    acrosses[0] = tie(acrosses[0], *result_near)
    grad_end = pass_states(jnp.concatenate(acrosses, axis=1), jnp.concatenate(transfers, axis=1), -1)
    total = lax.psum_scatter(sums, "fsdp", scatter_dimension=0, tiled=True)

    out_grad_w = low(outer_rows(grad_branch, mixed_rows))
    out_grad_w = lax.psum_scatter(out_grad_w, ("ctx", "fsdp"), scatter_dimension=0, tiled=True)

    mine, other = (side[2] for side in ffn_out[0])
    result_own = core_sum(mine, tie(other, grad_branch))
    mine, other = (side[2] for side in ffn_out[3])
    result_far = flip(tie(low(core_sum(mine, tie(other, grad_branch))), grad_end), "ctx", 3)
    columns = neighbour_columns(normed_mix)
    grad_mixes, mix_grads, conv_parts = [None] * parts, [None] * parts, [None] * parts
    logits = 0.0
    scatter = None
    for p in reversed(range(parts)):
        halo, convs, own, carry, final, inverses, updates, states = kept[p]
        heads = slice(p * part_heads, (p + 1) * part_heads)
        back = backs[p] if scatter is None else tie(backs[p], total, *scatter.sent)
        grad_mix, tail, before, conv_parts[p], logit = mixer_backward(
            pre[p], pre[0], bias, halo, convs, col, row, back, inverses, updates, states,
            entered[p], grad_end[:, heads], taps, p * part_heads, part_heads, group,
        )
        logits = logits + logit
        tail = low(tail + from_behind(before, "ctx", -1))
        grad_mix = put(grad_mix.reshape(seq_count, local_len, -1), tail, 0, local_len - HALO, 0)
        grad_mix = grad_mix.reshape(row_count, -1)
        if scatter is not None:
            scatter.second(grad_mix)
            mix_grads[p + 1] = scatter.finish()
        else:
            grad_mix = tie(grad_mix, result_far)
        if p == 0:
            grad_mix = jnp.concatenate([grad_mix, low(logits)], axis=1)
        grad_mixes[p] = grad_mix
        scatter = Scatter(columns, grad_mix)
    grad_mixes[0] = tie(grad_mixes[0], *scatter.sent)
    mix_back = gathered_times_transposed(grad_mixes, ctx_place, mix_full)
    mix_back = rows_scatter(mix_back.reshape(seq_count, local_len, width)).reshape(-1, width)
    back_mix, unit_mix = norm_backward(mix_back, inputs_mine, rms_scale(inputs_mine, EPSILON), gain_mix)
    input_grad = rows_full(low(grad_residual + back_mix).reshape(seq_count, -1, width))
    gain_mix_part = jnp.sum(mix_back * unit_mix, axis=0)

    conv_cols = jnp.concatenate([jnp.sum(part, axis=0)[:taps] for part in conv_parts], axis=1)
    gains = butterfly(jnp.concatenate([gain_mix_part, gain_ffn_part, gain_o_part]), ("tp",))
    sums = jnp.concatenate([gains, conv_cols.reshape(-1), jnp.sum(logits, axis=0)])
    scatter.second()
    sums = butterfly(sums, ("ctx", "fsdp"))
    mix_grads[0] = scatter.finish(sums)
    ends = [width, 2 * width, 2 * width + LANES, sums.shape[0] - LANES]
    gain_mix_grad, gain_ffn_grad, gain_o_grad, conv_grad, bias_grad = jnp.split(sums, ends)
    conv_grad = jnp.stack(by_kind([conv_grad.reshape(taps, -1)]))
    bias_grad = bias_grad[:heads_here]
    out_grad_w = wide(tie(out_grad_w, *scatter.last)).T
    pieces = tie(total, *scatter.last).reshape(3 * units, 4, shard_rows).transpose(1, 0, 2)
    arrived = lax.all_to_all(pieces, "ctx", 0, 0).reshape(4, 3, units, shard_rows)
    gate_grad, up_grad, down_grad = (wide(arrived[:, i].reshape(units_here, shard_rows)) for i in range(3))
    result = result_own + wide(result_near[0]) + wide(result_near[1])
    result = result + wide(result_far)
    block_output = rows_full(low(residual + result).reshape(seq_count, -1, width))
    query_grad, key_grad, value_grad = by_kind([grad[:, :part_cols] for grad in mix_grads])
    beta_grad = mix_grads[0][:, part_cols : part_cols + heads_here]

    return (
        block_output,
        input_grad,
        gain_mix_grad,
        query_grad,
        key_grad,
        value_grad,
        beta_grad,
        bias_grad,
        conv_grad,
        gain_o_grad,
        out_grad_w,
        gain_ffn_grad,
        gate_grad.T,
        up_grad.T,
        down_grad,
    )


def solution(mesh):
    placed = (
        P("fsdp", "ctx", None),
        P("fsdp", "ctx"),
        P(),
        P(("ctx", "fsdp"), "tp"),
        P(("ctx", "fsdp"), "tp"),
        P(("ctx", "fsdp"), "tp"),
        P(("ctx", "fsdp"), "tp"),
        P("tp"),
        P(None, None, "tp"),
        P(),
        P("tp", ("ctx", "fsdp")),
        P(),
        P(("ctx", "fsdp"), "tp"),
        P(("ctx", "fsdp"), "tp"),
        P("tp", ("ctx", "fsdp")),
        P("fsdp", "ctx", None),
    )
    return jax.shard_map(
        local,
        mesh=mesh,
        in_specs=placed,
        out_specs=(
            P("fsdp", "ctx", None),
            P("fsdp", "ctx", None),
            P(),
            P(("ctx", "fsdp"), "tp"),
            P(("ctx", "fsdp"), "tp"),
            P(("ctx", "fsdp"), "tp"),
            P(("ctx", "fsdp"), "tp"),
            P("tp"),
            P(None, None, "tp"),
            P(),
            P("tp", ("ctx", "fsdp")),
            P(),
            P(("ctx", "fsdp"), "tp"),
            P(("ctx", "fsdp"), "tp"),
            P("tp", ("ctx", "fsdp")),
        ),
        check_vma=False,
    )
```

```python
import functools
import math
import jax
import jax.numpy as jnp
from jax import lax
from jax.experimental import pallas as pl
from jax.experimental.pallas import tpu as pltpu
from jax.sharding import PartitionSpec as P

LANES = 128
CHUNK = 128
HALO = 8
EPSILON = 1e-06
HEAD_FLOOR = 0.01
VMEM_BYTES = 60 * 1024 * 1024


def low(value):
    return value.astype(jnp.bfloat16)


def mul_nn(left, right):
    return lax.dot_general(low(left), low(right), (((1,), (0,)), ((), ())), preferred_element_type=jnp.float32)


def mul_nt(left, right):
    return lax.dot_general(low(left), low(right), (((1,), (1,)), ((), ())), preferred_element_type=jnp.float32)


def mul_tn(left, right):
    return lax.dot_general(low(left), low(right), (((0,), (0,)), ((), ())), preferred_element_type=jnp.float32)


def iota(shape, axis):
    return lax.broadcasted_iota(jnp.int32, shape, axis)


def chunk_masks(col, row, first):
    size = col.shape[0]
    same = col == row
    order, other = iota((size, size), 0), iota((size, size), 1)
    upto = same & (order >= other)
    below = same & (order > other)
    carried = (col < first).astype(jnp.float32)
    last = (col == row[:, size - 1 :]).astype(jnp.float32)
    keep = (row[:, size - 1 :] < first).astype(jnp.float32)
    return upto, below, carried, last, keep


def invert_units(systems):
    size = systems[0].shape[0]
    order, other = iota((size, size), 0), iota((size, size), 1)
    identity = (order == other).astype(jnp.float32)
    span = 1
    found = None
    while span < size:
        pair = (order // (2 * span) == other // (2 * span)) & (order // span != other // span)
        parts = [jnp.where(pair, system, 0.0) for system in systems]
        if found is None:
            found = [identity - part for part in parts]
        else:
            right = [mul_nn(part, value) for part, value in zip(parts, found)]
            found = [value - mul_nn(value, part) for value, part in zip(found, right)]
        span *= 2
    return found


def conv_rows(ext, conv, col, offset, size, lane, taps):
    total = None
    moved = []
    position = iota((size, 1), 0) + offset
    for tap in range(taps):
        back = taps - 1 - tap
        values = ext[pl.ds(HALO + offset - back, size), lane : lane + LANES]
        values = jnp.where(position - back >= col, values, 0.0)
        moved.append(values)
        term = conv[tap : tap + 1, lane : lane + LANES] * values
        total = term if total is None else total + term
    return total, moved


def unit(values):
    return values * lax.rsqrt(jnp.sum(values * values, axis=-1, keepdims=True) + EPSILON)


def head_column(values, head):
    return jnp.sum(jnp.where(iota(values.shape, 1) == head, values, 0.0), axis=-1, keepdims=True)


def forward_kernel(taps, heads, first, pre, beta, bias, halo, conv, col_ref, row_ref, own, carry, final, inv, upd, states, ext):
    length = pre.shape[0]
    ext[:HALO] = halo[0]
    ext[HALO:] = pre[...]
    head = first + pl.program_id(1) * heads
    jobs = [(i, j) for j in range(length // CHUNK) for i in range(heads)]
    data = {}
    for j in range(length // CHUNK):
        rows = pl.ds(j * CHUNK, CHUNK)
        col, row = col_ref[0, rows], row_ref[0, :, rows]
        masks = chunk_masks(col, row, j * CHUNK)
        strengths = jax.nn.sigmoid(beta[rows] + bias[...])
        for i in range(heads):
            acts = []
            for kind in range(3):
                total, _ = conv_rows(ext, conv, col, j * CHUNK, CHUNK, (3 * i + kind) * LANES, taps)
                acts.append(total * jax.nn.sigmoid(total))
            query, key, value = unit(acts[0]), unit(acts[1]), acts[2]
            strength = head_column(strengths, head + i)
            grams = mul_nt(jnp.concatenate([low(key), low(query)], axis=0), key)
            system = jnp.where(masks[1], strength * grams[:CHUNK], 0.0)
            scores = low(jnp.where(masks[0], grams[CHUNK:], 0.0))
            data[i, j] = (low(query), low(key), value, strength, scores, masks, system)
    inverses = dict(zip(jobs, invert_units([data[job][6] for job in jobs])))
    for i in range(heads):
        state = jnp.concatenate(
            [
                jnp.zeros((LANES, LANES), jnp.float32),
                (iota((LANES, LANES), 0) == iota((LANES, LANES), 1)).astype(jnp.float32),
            ],
            axis=1,
        )
        final[0, i] = state
    for j in range(length // CHUNK):
        rows = pl.ds(j * CHUNK, CHUNK)
        for i in range(heads):
            query, key, value, strength, scores, masks, _ = data[i, j]
            _, _, carried, last, keep = masks
            inverse = low(inverses[i, j])
            state = final[0, i]
            state_low = low(state)
            read = mul_nn(jnp.concatenate([key, query], axis=0), state_low)
            wide = jnp.concatenate([value, jnp.zeros_like(value)], axis=1)
            targets = strength * (wide - carried * read[:CHUNK])
            update = low(mul_nn(inverse, targets))
            result = carried * read[CHUNK:] + mul_nn(scores, update)
            final[0, i] = keep * state + mul_tn(key * low(last), update)
            lanes = slice(i * LANES, (i + 1) * LANES)
            own[rows, lanes] = result[:, :LANES]
            carry[rows, lanes] = low(result[:, LANES:])
            inv[0, i, j] = inverse
            upd[0, i, j] = update
            states[0, i, j] = state_low


def mixer_forward(pre, logit, bias, halo, conv, col, row, taps, first, heads_here, group):
    seqs, length = col.shape[0], col.shape[1]
    steps = heads_here // group
    chunks = length // CHUNK
    wide = 3 * LANES * group
    rows = seqs * length

    def tile(*tail, kind):
        return jax.ShapeDtypeStruct((seqs, heads_here) + tail, kind)

    def spec(*tail):
        return pl.BlockSpec((1, group) + tail, lambda s, h: (s, h) + (0,) * len(tail))

    flat = pl.BlockSpec((length, LANES * group), lambda s, h: (s, h))
    last = logit.shape[1] // LANES - 1
    return pl.pallas_call(
        functools.partial(forward_kernel, taps, group, first),
        grid=(seqs, steps),
        in_specs=[
            pl.BlockSpec((length, wide), lambda s, h: (s, h)),
            pl.BlockSpec((length, LANES), lambda s, h: (s, last)),
            pl.BlockSpec((1, LANES), lambda s, h: (0, 0)),
            pl.BlockSpec((1, HALO, wide), lambda s, h: (s, 0, h)),
            pl.BlockSpec((conv.shape[0], wide), lambda s, h: (0, h)),
            pl.BlockSpec((1, length, 1), lambda s, h: (s, 0, 0)),
            pl.BlockSpec((1, 1, length), lambda s, h: (s, 0, 0)),
        ],
        out_specs=[
            flat,
            flat,
            spec(LANES, 2 * LANES),
            spec(chunks, CHUNK, CHUNK),
            spec(chunks, CHUNK, 2 * LANES),
            spec(chunks, LANES, 2 * LANES),
        ],
        out_shape=[
            jax.ShapeDtypeStruct((rows, heads_here * LANES), jnp.float32),
            jax.ShapeDtypeStruct((rows, heads_here * LANES), jnp.bfloat16),
            tile(LANES, 2 * LANES, kind=jnp.float32),
            tile(chunks, CHUNK, CHUNK, kind=jnp.bfloat16),
            tile(chunks, CHUNK, 2 * LANES, kind=jnp.bfloat16),
            tile(chunks, LANES, 2 * LANES, kind=jnp.bfloat16),
        ],
        scratch_shapes=[pltpu.VMEM((length + HALO, wide), jnp.float32)],
        compiler_params=pltpu.CompilerParams(vmem_limit_bytes=VMEM_BYTES),
        cost_estimate=pl.CostEstimate(
            flops=60 * rows * heads_here * CHUNK * LANES, bytes_accessed=40 * rows * heads_here * LANES, transcendentals=0
        ),
    )(pre, logit, bias, halo, conv, col, row)


def backward_kernel(
    taps, heads, first, pre, beta, bias, halo, conv, col_ref, row_ref, grad_ref, inv, upd, states, start, end,
    grad_pre, tail, before, conv_grad, logits, ext, grad_ext,
):
    length = pre.shape[0]
    step = pl.program_id(1)
    head = first + step * heads
    ext[:HALO] = halo[0]
    ext[HALO:] = pre[...]
    grad_ext[...] = jnp.zeros_like(grad_ext)

    @pl.when(step == 0)
    def _():
        logits[...] = jnp.zeros_like(logits)

    grad_states = [end[0, i] for i in range(heads)]
    entry = [low(start[0, i]) for i in range(heads)]
    tap_sums = {}
    for j in reversed(range(length // CHUNK)):
        offset = j * CHUNK
        rows = pl.ds(offset, CHUNK)
        col, row = col_ref[0, rows], row_ref[0, :, rows]
        upto, below, carried, last, keep = chunk_masks(col, row, offset)
        strengths = jax.nn.sigmoid(beta[rows] + bias[...])
        grad_logit = jnp.zeros((CHUNK, LANES), jnp.float32)
        for i in range(heads):
            raw, taps_in = [], []
            for kind in range(3):
                total, moved = conv_rows(ext, conv, col, offset, CHUNK, (3 * i + kind) * LANES, taps)
                raw.append(total)
                taps_in.append(moved)
            gates = [jax.nn.sigmoid(total) for total in raw]
            acts = [total * gate for total, gate in zip(raw, gates)]
            scales = [lax.rsqrt(jnp.sum(act * act, axis=-1, keepdims=True) + EPSILON) for act in acts[:2]]
            query, key, value = acts[0] * scales[0], acts[1] * scales[1], acts[2]
            strength = head_column(strengths, head + i)
            lanes = slice(i * LANES, (i + 1) * LANES)
            query_low, key_low = low(query), low(key)
            grams = mul_nt(jnp.concatenate([key_low, query_low], axis=0), key_low)
            gram = jnp.where(below, grams[:CHUNK], 0.0)
            scores = jnp.where(upto, grams[CHUNK:], 0.0)
            inverse = inv[0, i, j]
            update = upd[0, i, j]
            update = low(update[:, :LANES].astype(jnp.float32) + mul_nn(update[:, LANES:], entry[i]))
            state = states[0, i, j]
            state = low(state[:, :LANES].astype(jnp.float32) + mul_nn(state[:, LANES:], entry[i]))
            grad_out = grad_ref[rows, lanes]
            grad_state = grad_states[i]
            grad_state_low = low(grad_state)
            key_last = key_low * low(last)
            grad_update = mul_tn(scores, grad_out) + mul_nn(key_last, grad_state_low)
            grad_target = mul_tn(inverse, grad_update)
            weighted = strength * grad_target
            passed = carried * weighted
            out_carried = carried * grad_out.astype(jnp.float32)
            query_carried = query_low * low(carried)
            grad_states[i] = (
                keep * grad_state + mul_tn(query_carried, grad_out) - mul_tn(key_low, passed)
            )
            grad_scores = jnp.where(upto, mul_nt(grad_out, update), 0.0)
            grad_system = jnp.where(below, mul_nt(grad_target, update), 0.0)
            remainder = value - carried * mul_nn(key_low, state)
            grad_strength = jnp.sum(grad_target * remainder - grad_system * gram, axis=-1, keepdims=True)
            scaled = strength * grad_system
            from_state = mul_nt(jnp.concatenate([low(out_carried), low(passed)], axis=0), state)
            from_keys = mul_nn(jnp.concatenate([low(grad_scores), low(scaled + scaled.T)], axis=0), key_low)
            grad_query = from_state[:CHUNK] + from_keys[:CHUNK]
            grad_key = (
                mul_tn(grad_scores, query_low)
                + last * mul_nt(update, grad_state_low)
                - from_state[CHUNK:]
                - from_keys[CHUNK:]
            )
            grad_logit = grad_logit + jnp.where(
                iota((CHUNK, LANES), 1) == head + i, grad_strength * strength * (1.0 - strength), 0.0
            )
            grads = [
                scales[0] * (grad_query - query * jnp.sum(grad_query * query, axis=-1, keepdims=True)),
                scales[1] * (grad_key - key * jnp.sum(grad_key * key, axis=-1, keepdims=True)),
                weighted,
            ]
            position = iota((CHUNK, 1), 0) + offset
            for kind in range(3):
                gate, total = gates[kind], raw[kind]
                grad_conv = grads[kind] * gate * (1.0 + total * (1.0 - gate))
                lane = (3 * i + kind) * LANES
                for tap in range(taps):
                    back = taps - 1 - tap
                    part = jnp.sum(grad_conv * taps_in[kind][tap], axis=0, keepdims=True)
                    spot = (i, kind, tap)
                    tap_sums[spot] = part if spot not in tap_sums else tap_sums[spot] + part
                    back_part = jnp.where(
                        position - back >= col, grad_conv * conv[tap : tap + 1, lane : lane + LANES], 0.0
                    )
                    where = pl.ds(HALO + offset - back, CHUNK)
                    grad_ext[where, lane : lane + LANES] += back_part
        logits[rows] += grad_logit
    grad_pre[...] = low(grad_ext[HALO:])
    before[0] = grad_ext[:HALO]
    tail[0] = grad_ext[length:]
    for i in range(heads):
        for kind in range(3):
            lane = (3 * i + kind) * LANES
            for tap in range(taps):
                conv_grad[0, tap : tap + 1, lane : lane + LANES] = tap_sums[i, kind, tap]


def mixer_backward(
    pre, logit, bias, halo, conv, col, row, grad_mixed, inv, upd, states, start, end, taps, first, heads_here, group
):
    seqs, length = col.shape[0], col.shape[1]
    steps = heads_here // group
    chunks = length // CHUNK
    wide = 3 * LANES * group
    rows = seqs * length

    def spec(*tail):
        return pl.BlockSpec((1, group) + tail, lambda s, h: (s, h) + (0,) * len(tail))

    last = logit.shape[1] // LANES - 1
    part = pl.BlockSpec((1, HALO, wide), lambda s, h: (s, 0, h))
    edge = jax.ShapeDtypeStruct((seqs, HALO, 3 * LANES * heads_here), jnp.float32)
    return pl.pallas_call(
        functools.partial(backward_kernel, taps, group, first),
        grid=(seqs, steps),
        in_specs=[
            pl.BlockSpec((length, wide), lambda s, h: (s, h)),
            pl.BlockSpec((length, LANES), lambda s, h: (s, last)),
            pl.BlockSpec((1, LANES), lambda s, h: (0, 0)),
            part,
            pl.BlockSpec((conv.shape[0], wide), lambda s, h: (0, h)),
            pl.BlockSpec((1, length, 1), lambda s, h: (s, 0, 0)),
            pl.BlockSpec((1, 1, length), lambda s, h: (s, 0, 0)),
            pl.BlockSpec((length, LANES * group), lambda s, h: (s, h)),
            spec(chunks, CHUNK, CHUNK),
            spec(chunks, CHUNK, 2 * LANES),
            spec(chunks, LANES, 2 * LANES),
            spec(LANES, LANES),
            spec(LANES, LANES),
        ],
        out_specs=[
            pl.BlockSpec((length, wide), lambda s, h: (s, h)),
            part,
            part,
            part,
            pl.BlockSpec((length, LANES), lambda s, h: (s, 0)),
        ],
        out_shape=[
            jax.ShapeDtypeStruct((rows, 3 * LANES * heads_here), jnp.bfloat16),
            edge,
            edge,
            edge,
            jax.ShapeDtypeStruct((rows, LANES), jnp.float32),
        ],
        scratch_shapes=[
            pltpu.VMEM((length + HALO, wide), jnp.float32),
            pltpu.VMEM((length + HALO, wide), jnp.float32),
        ],
        compiler_params=pltpu.CompilerParams(vmem_limit_bytes=VMEM_BYTES),
        cost_estimate=pl.CostEstimate(
            flops=60 * rows * heads_here * CHUNK * LANES, bytes_accessed=40 * rows * heads_here * LANES, transcendentals=0
        ),
    )(pre, logit, bias, halo, conv, col, row, grad_mixed, inv, upd, states, start, end)


def mixed_rows_of(own, carry, start):
    return own + mul_nn(carry, start)


def output_kernel(heads, own, carry, start, gain, out):
    for i in range(heads):
        lanes = slice(i * LANES, (i + 1) * LANES)
        mixed = mixed_rows_of(own[:, lanes], carry[:, lanes], start[0, i])
        scale = lax.rsqrt(jnp.mean(mixed * mixed, axis=-1, keepdims=True) + HEAD_FLOOR)
        out[:, lanes] = low(mixed * scale * gain[...])


def output_backward_kernel(heads, own, carry, start, gain, grad, out, across, gain_grad):
    total = jnp.zeros((1, LANES), jnp.float32)
    for i in range(heads):
        lanes = slice(i * LANES, (i + 1) * LANES)
        carried = carry[:, lanes]
        mixed = mixed_rows_of(own[:, lanes], carried, start[0, i])
        scale = lax.rsqrt(jnp.mean(mixed * mixed, axis=-1, keepdims=True) + HEAD_FLOOR)
        normed = mixed * scale
        upper = grad[:, lanes].astype(jnp.float32)
        total = total + jnp.sum(upper * normed, axis=0, keepdims=True)
        weighted = upper * gain[...]
        back = scale * (weighted - normed * jnp.mean(weighted * normed, axis=-1, keepdims=True))
        out[:, lanes] = low(back)
        across[0, i] = mul_tn(carried, back)
    gain_grad[0, 0] = total


def mixer_output(own, carry, start, gain, group):
    seqs, heads_here = start.shape[:2]
    rows = own.shape[0]
    length = rows // seqs
    flat = pl.BlockSpec((length, LANES * group), lambda s, h: (s, h))
    square = pl.BlockSpec((1, group, LANES, LANES), lambda s, h: (s, h, 0, 0))
    return pl.pallas_call(
        functools.partial(output_kernel, group),
        grid=(seqs, heads_here // group),
        in_specs=[flat, flat, square, pl.BlockSpec((1, LANES), lambda s, h: (0, 0))],
        out_specs=flat,
        out_shape=jax.ShapeDtypeStruct(own.shape, jnp.bfloat16),
        compiler_params=pltpu.CompilerParams(vmem_limit_bytes=VMEM_BYTES),
        cost_estimate=pl.CostEstimate(
            flops=2 * own.size * LANES, bytes_accessed=8 * own.size, transcendentals=0
        ),
    )(own, carry, start, gain)


def mixer_output_backward(own, carry, start, gain, grad, first, group):
    seqs, heads_here = start.shape[:2]
    rows = own.shape[0]
    length = rows // seqs
    steps = heads_here // group
    flat = pl.BlockSpec((length, LANES * group), lambda s, h: (s, h))
    base = first // group
    shifted = pl.BlockSpec((length, LANES * group), lambda s, h: (s, base + h))
    square = pl.BlockSpec((1, group, LANES, LANES), lambda s, h: (s, h, 0, 0))
    return pl.pallas_call(
        functools.partial(output_backward_kernel, group),
        grid=(seqs, steps),
        in_specs=[flat, flat, square, pl.BlockSpec((1, LANES), lambda s, h: (0, 0)), shifted],
        out_specs=[flat, square, pl.BlockSpec((1, 1, 1, LANES), lambda s, h: (s, h, 0, 0))],
        out_shape=[
            jax.ShapeDtypeStruct(own.shape, jnp.bfloat16),
            jax.ShapeDtypeStruct(start.shape, jnp.float32),
            jax.ShapeDtypeStruct((seqs, steps, 1, LANES), jnp.float32),
        ],
        compiler_params=pltpu.CompilerParams(vmem_limit_bytes=VMEM_BYTES),
        cost_estimate=pl.CostEstimate(
            flops=4 * own.size * LANES, bytes_accessed=12 * own.size, transcendentals=0
        ),
    )(own, carry, start, gain, grad)


def ffn_kernel(mine, other, mine_grads, other_grads, gate_w, up_w, down_w, *outs):
    rows = jnp.concatenate([mine[...], other[...]], axis=0)
    grads = jnp.concatenate([mine_grads[...], other_grads[...]], axis=0)
    half = mine.shape[0]
    gate = mul_nt(rows, gate_w[...])
    up = mul_nt(rows, up_w[...])
    grad_hidden = mul_nt(grads, down_w[...])
    sigmoid = jax.nn.sigmoid(gate)
    active = gate * sigmoid
    kept = low(active * up)
    back_gate = low(grad_hidden * up * sigmoid * (1.0 + gate * (1.0 - sigmoid)))
    back_up = low(grad_hidden * active)
    grad_rows = low(mul_nn(back_gate, gate_w[...]) + mul_nn(back_up, up_w[...]))
    result = low(mul_nn(kept, down_w[...]))
    for side in range(2):
        here = slice(side * half, (side + 1) * half)
        acts, grad_out, result_out = outs[3 * side : 3 * side + 3]
        for kind, value in enumerate((back_gate, back_up, kept)):
            acts[kind] = value[here]
        grad_out[...] = grad_rows[here]
        result_out[...] = result[here]


def ffn_both(rows, grads, gate_up, down):
    count, width = rows[0].shape
    units = down.shape[0]
    tile = min(256, count)
    wide_rows = pl.BlockSpec((tile, width), lambda i: (i, 0))
    narrow = pl.BlockSpec((3, tile, units), lambda i: (0, i, 0))

    def third(index):
        return pl.BlockSpec((units, width), lambda i: (index, 0))

    flat = jax.ShapeDtypeStruct((count, width), jnp.bfloat16)
    outs = pl.pallas_call(
        ffn_kernel,
        grid=(count // tile,),
        in_specs=[wide_rows] * 4 + [third(0), third(1), third(0)],
        out_specs=[narrow, wide_rows, wide_rows] * 2,
        out_shape=[jax.ShapeDtypeStruct((3, count, units), jnp.bfloat16), flat, flat] * 2,
        compiler_params=pltpu.CompilerParams(vmem_limit_bytes=VMEM_BYTES),
        cost_estimate=pl.CostEstimate(
            flops=24 * count * width * units, bytes_accessed=16 * count * width + 6 * units * width, transcendentals=0
        ),
    )(*rows, *grads, gate_up, gate_up, down)
    return outs[:3], outs[3:]


def ffn_weights_kernel(count, lines, *refs):
    acts, rows, grads = refs[:count], refs[count : 2 * count], refs[2 * count : 3 * count]
    out, total = refs[-2:]
    part = out.shape[-1]

    def add(sources):
        for i in range(count):
            value = mul_tn(acts[i][0], sources[i][...])
            if i == 0:
                total[...] = value
            else:
                total[...] += value

    @pl.when(pl.program_id(0) < 2)
    def _():
        add(rows)

    @pl.when(pl.program_id(0) == 2)
    def _():
        add(grads)

    for line in range(lines):
        out[line, 0] = low(total[:, line * part : (line + 1) * part])


def ffn_weights(acts, rows, grads, lines, squares):
    count, width = len(acts), rows[0].shape[1]
    size, units = acts[0].shape[1:]
    block = width // squares
    part = block // lines
    act_spec = pl.BlockSpec((1, size, units), lambda k, c: (k, 0, 0))
    row_spec = pl.BlockSpec((size, block), lambda k, c: (0, jnp.where(k < 2, c, squares - 1)))
    grad_spec = pl.BlockSpec((size, block), lambda k, c: (0, jnp.where(k < 2, 0, c)))
    return pl.pallas_call(
        functools.partial(ffn_weights_kernel, count, lines),
        grid=(3, squares),
        in_specs=[act_spec] * count + [row_spec] * count + [grad_spec] * count,
        out_specs=pl.BlockSpec((lines, 1, units, part), lambda k, c: (0, k, 0, c)),
        out_shape=jax.ShapeDtypeStruct((lines, 3, units, squares * part), jnp.bfloat16),
        scratch_shapes=[pltpu.VMEM((units, block), jnp.float32)],
        compiler_params=pltpu.CompilerParams(vmem_limit_bytes=VMEM_BYTES),
        cost_estimate=pl.CostEstimate(
            flops=6 * count * size * width * units, bytes_accessed=8 * count * size * width, transcendentals=0
        ),
    )(*acts, *rows, *grads)


def block_columns(place, bit, size):
    return pl.multiple_of((place[0] ^ bit) * size, size)


def gathered_kernel(place, rows, *refs):
    out = refs[-1]
    own, beside, across, upper, lower = refs[:-1]
    size, half = own.shape[0], upper.shape[0]
    total = None
    for bit, skip, ref in ((0, 0, own), (1, 0, beside), (2, 0, across), (3, 0, upper), (3, half, lower)):
        start = pl.multiple_of(block_columns(place, bit, size) + skip, half)
        value = mul_nn(rows[:, pl.ds(start, ref.shape[0])], ref[...])
        total = value if total is None else total + value
    out[...] = total


def gathered_times(rows, place, pieces):
    count, width = rows.shape
    columns = pieces[0].shape[1]
    tile = min(256, count)
    whole = [pl.BlockSpec(piece.shape, lambda i, place: (0, 0)) for piece in pieces]
    return pl.pallas_call(
        gathered_kernel,
        grid_spec=pltpu.PrefetchScalarGridSpec(
            num_scalar_prefetch=1,
            grid=(count // tile,),
            in_specs=[pl.BlockSpec((tile, width), lambda i, place: (i, 0))] + whole,
            out_specs=pl.BlockSpec((tile, columns), lambda i, place: (i, 0)),
        ),
        out_shape=jax.ShapeDtypeStruct((count, columns), jnp.float32),
        compiler_params=pltpu.CompilerParams(vmem_limit_bytes=VMEM_BYTES),
        cost_estimate=pl.CostEstimate(
            flops=2 * count * width * columns, bytes_accessed=2 * (count + columns) * width, transcendentals=0
        ),
    )(jnp.reshape(place, (1,)).astype(jnp.int32), rows, *pieces)


def gathered_transposed_kernel(count, place, *refs):
    factors, pieces, out = refs[:count], refs[count:-1], refs[-1]
    size, half = pieces[0].shape[0], pieces[3].shape[0]
    for i, (bit, skip) in enumerate(((0, 0), (1, 0), (2, 0), (3, 0), (3, half))):
        start = pl.multiple_of(block_columns(place, bit, size) + skip, half)
        total = None
        for p in range(count):
            value = mul_nt(factors[p][...], pieces[5 * p + i][...])
            total = value if total is None else total + value
        out[:, pl.ds(start, pieces[i].shape[0])] = low(total)


def gathered_times_transposed(factors, place, pieces):
    count, rows = len(factors), factors[0].shape[0]
    width = 4 * pieces[0][0].shape[0]
    tile = min(256, rows)
    flat = [piece for some in pieces for piece in some]
    whole = [pl.BlockSpec(piece.shape, lambda i, place: (0, 0)) for piece in flat]
    wides = [pl.BlockSpec((tile, factor.shape[1]), lambda i, place: (i, 0)) for factor in factors]
    columns = sum(factor.shape[1] for factor in factors)
    return pl.pallas_call(
        functools.partial(gathered_transposed_kernel, count),
        grid_spec=pltpu.PrefetchScalarGridSpec(
            num_scalar_prefetch=1,
            grid=(rows // tile,),
            in_specs=wides + whole,
            out_specs=pl.BlockSpec((tile, width), lambda i, place: (i, 0)),
        ),
        out_shape=jax.ShapeDtypeStruct((rows, width), jnp.bfloat16),
        compiler_params=pltpu.CompilerParams(vmem_limit_bytes=VMEM_BYTES),
        cost_estimate=pl.CostEstimate(
            flops=2 * rows * width * columns, bytes_accessed=2 * (rows + columns) * width, transcendentals=0
        ),
    )(jnp.reshape(place, (1,)).astype(jnp.int32), *factors, *flat)


def join_kernel(squares, source, target):
    lines, _, columns = source.shape
    part = columns // squares
    for i in range(lines):
        for j in range(squares):
            at = (j * lines + i) * part
            target[:, at : at + part] = source[i, :, j * part : (j + 1) * part]


def columns_join(parts, squares):
    lines, rows, columns = parts.shape
    tile = 176 if rows % 176 == 0 else rows
    return pl.pallas_call(
        functools.partial(join_kernel, squares),
        grid=(rows // tile,),
        in_specs=[pl.BlockSpec((lines, tile, columns), lambda i: (0, i, 0))],
        out_specs=pl.BlockSpec((tile, lines * columns), lambda i: (i, 0)),
        out_shape=jax.ShapeDtypeStruct((rows, lines * columns), parts.dtype),
        compiler_params=pltpu.CompilerParams(vmem_limit_bytes=VMEM_BYTES),
        cost_estimate=pl.CostEstimate(flops=0, bytes_accessed=4 * parts.size, transcendentals=0),
    )(parts)


def flip(value, axis, bit):
    devices = range(lax.axis_size(axis))
    return lax.ppermute(value, axis, [(i, i ^ bit) for i in devices])


def shift(value, axis, distance):
    count = lax.axis_size(axis)
    return lax.ppermute(value, axis, [(i, (i + distance) % count) for i in range(count)])


def from_behind(block, axis, distance):
    devices = range(lax.axis_size(axis))
    route = [(i - distance, i) for i in devices if i - distance in devices]
    return lax.ppermute(block, axis, route)


def tie(value, *earlier):
    return lax.optimization_barrier((value,) + earlier)[0]


def put(buffer, piece, *start):
    return lax.dynamic_update_slice(buffer, piece, start)


def wide(value):
    return value.astype(jnp.float32)


def gather_line(shard):
    count, place = lax.axis_size("fsdp"), lax.axis_index("fsdp")
    pieces = [shard] + [shift(shard, "fsdp", d) for d in range(1, count)]
    order = [(place - i) % count for i in range(count)]
    return jnp.concatenate([lax.select_n(which, *pieces) for which in order], axis=0)


class Square:
    def __init__(self, own):
        self.own = own
        self.half = own.shape[0] // 2
        self.beside = flip(own, "ctx", 1)
        self.across = flip(own, "ctx", 2)

    def forward(self, *earlier):
        upper = self.beside[: self.half]
        lower = self.across[self.half :]
        if earlier:
            upper, lower = lax.optimization_barrier((upper, lower) + earlier)[:2]
        self.upper = flip(upper, "ctx", 2)
        self.lower = flip(lower, "ctx", 1)
        return self

    def done(self):
        return (self.upper, self.lower)

    def pieces(self):
        return [self.own, self.beside, self.across, self.upper, self.lower]

    def far(self):
        return jnp.concatenate([self.upper, self.lower], axis=0)


def both_sides(rows):
    if lax.axis_size("tp") == 2:
        return rows, flip(rows, "tp", 1)
    every = lax.all_gather(rows, "tp", axis=0, tiled=True)
    half = every.shape[0] // 2
    return every[:half], every[half:]


def core_sum(mine, other):
    if lax.axis_size("tp") == 2:
        return wide(mine) + wide(flip(other, "tp", 1))
    both = jnp.concatenate([mine, other], axis=0)
    return wide(lax.psum_scatter(both, "tp", scatter_dimension=0, tiled=True))


def neighbour_columns(rows):
    width = rows.shape[1] // 4
    place = lax.axis_index("ctx")
    return [lax.dynamic_slice_in_dim(rows, (place ^ bit) * width, width, 1) for bit in range(4)]


def line_sum(own, *late):
    count, place = own.shape[0], lax.axis_index("fsdp")
    total = lax.dynamic_index_in_dim(own, place, 0, keepdims=False)
    arrived = []
    for distance in range(1, count):
        piece = lax.dynamic_index_in_dim(own, (place + distance) % count, 0, keepdims=False)
        arrived.append(shift(low(piece), "fsdp", distance))
    for part in lax.optimization_barrier(tuple(arrived) + late)[: len(arrived)]:
        total = total + wide(part)
    return total


class Scatter:
    def __init__(self, columns, grads):
        self.columns, self.grads = columns, grads
        self.half = columns[0].shape[1] // 2
        beside, across = (
            jnp.concatenate([self.side(3, 1), self.side(1, 1)], axis=1),
            jnp.concatenate([self.side(3, 0), self.side(2, 0)], axis=1),
        )
        self.sent = [low(outer_rows(beside, grads)), low(outer_rows(across, grads))]
        self.first = (flip(self.sent[0], "ctx", 1), flip(self.sent[1], "ctx", 2))

    def side(self, bit, lower):
        return self.columns[bit][:, lower * self.half : (lower + 1) * self.half]

    def second(self, *earlier):
        first = self.first
        if earlier:
            first = lax.optimization_barrier(first + earlier)[:2]
        beside, across = (wide(part) for part in first)
        upper = low(outer_rows(self.side(1, 0), self.grads) + across[: self.half])
        lower = low(outer_rows(self.side(2, 1), self.grads) + beside[: self.half])
        self.last = (flip(upper, "ctx", 1), flip(lower, "ctx", 2))
        self.kept = (beside, across)
        return upper, lower

    def finish(self, last, *ties):
        beside_upper, across_lower = self.last
        if not last:
            beside_upper, across_lower = lax.optimization_barrier(self.last + ties)[:2]
        beside, across = self.kept
        own = outer_rows(self.columns[0], self.grads)
        upper = own[: self.half] + wide(beside_upper) + across[self.half :]
        lower = own[self.half :] + beside[self.half :] + wide(across_lower)
        own = jnp.concatenate([upper, lower], axis=0)
        lines = lax.axis_size("fsdp")
        if not last:
            return wide(lax.psum_scatter(low(own), "fsdp", scatter_dimension=0, tiled=True))
        return line_sum(own.reshape(lines, own.shape[0] // lines, own.shape[1]), *ties)


def butterfly(value, axes):
    for axis in axes:
        count, bit = lax.axis_size(axis), 1
        while bit < count:
            value = value + flip(value, axis, bit)
            bit *= 2
    return value


def rms_scale(values, floor_value):
    return lax.rsqrt(jnp.mean(values * values, axis=-1, keepdims=True) + floor_value)


def norm_backward(grad_normed, inputs, scale, gain):
    normed = inputs * scale
    weighted = grad_normed * gain
    return (
        scale * (weighted - normed * jnp.mean(weighted * normed, axis=-1, keepdims=True)),
        normed,
    )


def times(left, right):
    return jnp.dot(left, right, preferred_element_type=jnp.float32)


def times_transposed(left, right):
    return lax.dot_general(
        left, right, (((1,), (1,)), ((), ())), preferred_element_type=jnp.float32
    )


def outer_rows(left, right):
    return lax.dot_general(
        left, right, (((0,), (0,)), ((), ())), preferred_element_type=jnp.float32
    )


def rows_mine(rows):
    count = rows.shape[1] // lax.axis_size("tp")
    return lax.dynamic_slice_in_dim(rows, lax.axis_index("tp") * count, count, 1)


def rows_scatter(partial):
    if lax.axis_size("tp") != 2:
        return wide(lax.psum_scatter(partial, "tp", scatter_dimension=1, tiled=True))
    count = partial.shape[1] // 2
    other = lax.dynamic_slice_in_dim(partial, (1 - lax.axis_index("tp")) * count, count, 1)
    return wide(rows_mine(partial)) + wide(flip(other, "tp", 1))


def rows_full(mine):
    if lax.axis_size("tp") != 2:
        return lax.all_gather(mine, "tp", axis=1, tiled=True)
    other = flip(mine, "tp", 1)
    lower = lax.axis_index("tp") == 0
    return jnp.concatenate([jnp.where(lower, mine, other), jnp.where(lower, other, mine)], axis=1)


def by_head(parts):
    heads = range(parts[0].shape[-1] // LANES)
    return jnp.concatenate([part[..., h * LANES : (h + 1) * LANES] for h in heads for part in parts], axis=-1)


def by_kind(joined):
    return [
        jnp.concatenate(
            [
                some[..., at : at + LANES]
                for some in joined
                for at in range(kind * LANES, some.shape[-1], 3 * LANES)
            ],
            axis=-1,
        )
        for kind in range(3)
    ]


def pass_states(own, transfer, forward, *beside):
    rule = "shij,shjk->shik" if forward == 1 else "shji,shjk->shik"
    leaving = own
    entered = low(jnp.zeros_like(own))
    for repeat in range(lax.axis_size("ctx") - 1):
        entered = from_behind(low(leaving), "ctx", forward)
        if repeat == 0 and beside:
            entered = tie(entered, *beside)
        leaving = own + jnp.einsum(rule, transfer, entered, preferred_element_type=jnp.float32)
    return wide(entered)


def local(
    block_input,
    doc_start,
    gain_mix,
    query_weight,
    key_weight,
    value_weight,
    beta_weight,
    beta_bias,
    conv_weight,
    gain_o,
    out_weight,
    gain_ffn,
    gate_weight,
    up_weight,
    down_weight,
    out_grad,
):
    seq_count, local_len, width = block_input.shape
    row_count = seq_count * local_len
    heads_here = beta_weight.shape[1]
    taps = conv_weight.shape[1]
    parts = 2 if heads_here % 2 == 0 else 1
    part_heads = heads_here // parts
    group = 2 if part_heads % 2 == 0 else 1
    part_cols = 3 * part_heads * LANES
    spare = LANES - heads_here
    units_here = gate_weight.shape[1]
    shard_rows = gate_weight.shape[0]

    joined = by_head([low(query_weight), low(key_weight), low(value_weight)])
    shards = [joined[:, p * part_cols : (p + 1) * part_cols] for p in range(parts)]
    shards[0] = jnp.concatenate([shards[0], jnp.pad(low(beta_weight), ((0, 0), (0, spare)))], axis=1)
    shards.append(low(out_weight).T)
    lines = []
    for shard in shards:
        lines.append(gather_line(tie(shard, lines[-1]) if lines else shard))
    units = units_here // 4
    pieces = jnp.stack([low(gate_weight).T, low(up_weight).T, low(down_weight)])
    pieces = pieces.reshape(3, 4, units, shard_rows).transpose(1, 0, 2, 3)
    ffn_line = lax.all_to_all(pieces.reshape(4, 3 * units, shard_rows), "ctx", 0, 0)
    ffn_line = ffn_line.transpose(1, 0, 2).reshape(3 * units, 4 * shard_rows)
    line_count = lax.axis_size("fsdp")

    ctx_place = lax.axis_index("ctx")
    first_pos = ctx_place * local_len
    starts = doc_start - first_pos
    col, row = starts[:, :, None], starts[:, None, :]
    conv = by_head([conv_weight[0], conv_weight[1], conv_weight[2]])
    bias = jnp.pad(beta_bias, (0, spare))[None]
    gain_head = gain_o[None]
    tokens = block_input.reshape(row_count, width)
    inputs = wide(tokens)
    normed_mix = low(inputs * rms_scale(inputs, EPSILON) * gain_mix)
    inputs_mine = wide(rows_mine(block_input).reshape(-1, width))
    grads_mine = rows_mine(out_grad).reshape(-1, width)

    square = Square(tie(lines[0], ffn_line)).forward()
    gate_up_parts = lax.all_gather(tie(ffn_line[: 2 * units], lines[parts - 1], *square.done()), "fsdp", axis=0)
    down_parts = lax.all_gather(ffn_line[2 * units :], "fsdp", axis=0)
    mix_full, kept, pre = [], [], []
    for p in range(parts):
        mix_full.append(square.pieces())
        square = Square(tie(lines[p + 1], *square.done()))
        rows = normed_mix
        ends = rows.reshape(seq_count, local_len, width)[:, local_len - HALO :].reshape(seq_count * HALO, width)
        ends = gathered_times(ends, ctx_place, mix_full[p])[:, :part_cols]
        halo = from_behind(ends.reshape(seq_count, HALO, part_cols), "ctx", 1)
        pre.append(gathered_times(tie(rows, ends), ctx_place, mix_full[p]))
        convs = conv[:, p * part_cols : (p + 1) * part_cols]
        held = pre[p]
        if p > 0:
            held = tie(held, grad_square.beside, grad_square.across)
        kept.append(
            [halo, convs]
            + list(
                mixer_forward(
                    held, pre[0], bias, halo, convs, col, row, taps, p * part_heads, part_heads, group
                )
            )
        )
        square.forward(kept[p][2], lines[-1])
        if p == 0:
            grad_square = Square(tie(grads_mine, kept[p][2], square.beside, square.across))
        if p == parts - 1:
            grad_square.forward()
    out_full = square.pieces()

    entered, transfers, mixed_rows = [], [], []
    for _, _, own, carry, final, _, _, _ in kept:
        transfers.append(low(final[..., LANES:]))
        first = final[..., :LANES]
        if len(entered) == parts - 1:
            first, gate_up_parts = lax.optimization_barrier((first, gate_up_parts) + grad_square.done())[:2]
            gate_up_full = columns_join(gate_up_parts, 4)
        entered.append(pass_states(first, transfers[-1], 1))
        if len(entered) == parts:
            carry = tie(carry, gate_up_full)
        mixed_rows.append(mixer_output(own, carry, entered[-1], gain_head, group))
    mixed_rows = jnp.concatenate(mixed_rows, axis=1)
    grad_rows = [
        both_sides(part) for part in (grad_square.own, grad_square.beside, grad_square.across, grad_square.far())
    ]
    mixed_rows = tie(mixed_rows, *(other for _, other in grad_rows))

    branch = gathered_times_transposed([mixed_rows], ctx_place, [out_full]).reshape(seq_count, local_len, width)
    branch, down_parts = lax.optimization_barrier((branch, down_parts))
    residual = inputs_mine + rows_scatter(branch).reshape(-1, width)
    scale_ffn = rms_scale(residual, EPSILON)
    square = Square(low(residual * scale_ffn * gain_ffn))
    ffn_full = (gate_up_full, columns_join(down_parts, 4))

    ffn_rows = [both_sides(square.own)]
    ffn_out = [ffn_both(ffn_rows[0], grad_rows[0], *ffn_full)]
    square.forward(ffn_out[0][0][0])
    ffn_rows.append(both_sides(tie(square.beside, ffn_out[0][0][0])))
    ffn_out.append(ffn_both(ffn_rows[1], grad_rows[1], *ffn_full))
    ffn_rows.append(both_sides(tie(square.across, ffn_out[0][0][0])))
    mine, other = ffn_rows[2]
    ffn_out.append(ffn_both((tie(mine, ffn_out[1][0][0], *square.done()), other), grad_rows[2], *ffn_full))
    beside_sums, across_sums = (low(core_sum(*(side[1] for side in ffn_out[bit]))) for bit in (1, 2))
    ffn_rows.append(both_sides(square.far()))
    mine, other = ffn_rows[3]
    ffn_out.append(ffn_both((tie(mine, beside_sums, across_sums), other), grad_rows[3], *ffn_full))
    near_sums = (flip(beside_sums, "ctx", 1), flip(across_sums, "ctx", 2))
    mine, other = (side[1] for side in ffn_out[3])
    far_sums = low(core_sum(mine, tie(other, *near_sums)))
    acts = [side[0] for outs in ffn_out for side in outs]
    acts[0] = tie(acts[0], far_sums)
    far_sums = flip(far_sums, "ctx", 3)
    sums = ffn_weights(
        acts,
        [side for sides in ffn_rows for side in sides],
        [side for sides in grad_rows for side in sides],
        line_count,
        4,
    ).reshape(line_count, 3 * units, 4 * shard_rows)

    far_sums, sums = lax.optimization_barrier((far_sums, sums))
    result_near = []
    for bit in (1, 2):
        mine, other = (side[2] for side in ffn_out[bit])
        result_near.append(flip(low(core_sum(mine, tie(other, far_sums))), "ctx", bit))
    grad_normed = core_sum(*(side[1] for side in ffn_out[0]))
    grad_normed = grad_normed + wide(near_sums[0]) + wide(near_sums[1]) + wide(far_sums)
    back_ffn, unit_ffn = norm_backward(grad_normed, residual, scale_ffn, gain_ffn)
    grad_residual = wide(grads_mine) + back_ffn
    gain_ffn_part = jnp.sum(grad_normed * unit_ffn, axis=0)
    grad_branch = rows_full(low(grad_residual).reshape(seq_count, -1, width)).reshape(row_count, width)
    grad_heads = gathered_times(grad_branch, ctx_place, out_full)
    backs, acrosses, gain_o_part = [], [], 0.0
    for p in range(parts):
        _, _, own, carry, _, _, _, _ = kept[p]
        back, across, gain_part = mixer_output_backward(
            own, carry, entered[p], gain_head, grad_heads, p * part_heads, group
        )
        backs.append(back)
        acrosses.append(across)
        gain_o_part = gain_o_part + jnp.sum(gain_part, axis=(0, 1, 2))
    grad_end = pass_states(jnp.concatenate(acrosses, axis=1), jnp.concatenate(transfers, axis=1), -1, *result_near)
    total = lax.psum_scatter(sums, "fsdp", scatter_dimension=0, tiled=True)

    out_grad_w = low(outer_rows(grad_branch, mixed_rows))
    out_grad_w = lax.psum_scatter(out_grad_w, ("ctx", "fsdp"), scatter_dimension=0, tiled=True)

    mine, other = (side[2] for side in ffn_out[0])
    result_own = core_sum(mine, tie(other, grad_branch))
    mine, other = (side[2] for side in ffn_out[3])
    result_far = flip(tie(low(core_sum(mine, tie(other, grad_branch))), grad_end), "ctx", 3)
    columns = neighbour_columns(normed_mix)
    grad_mixes, mix_grads, conv_parts = [None] * parts, [None] * parts, [None] * parts
    logits = 0.0
    scatter = None
    for p in reversed(range(parts)):
        halo, convs, own, carry, final, inverses, updates, states = kept[p]
        heads = slice(p * part_heads, (p + 1) * part_heads)
        back = backs[p] if scatter is None else tie(backs[p], total, *scatter.sent)
        grad_mix, tail, before, conv_parts[p], logit = mixer_backward(
            pre[p], pre[0], bias, halo, convs, col, row, back, inverses, updates, states,
            entered[p], grad_end[:, heads], taps, p * part_heads, part_heads, group,
        )
        logits = logits + logit
        tail = low(tail + from_behind(before, "ctx", -1))
        grad_mix = put(grad_mix.reshape(seq_count, local_len, -1), tail, 0, local_len - HALO, 0)
        grad_mix = grad_mix.reshape(row_count, -1)
        if scatter is not None:
            scatter.second(before)
            earlier_scatter = scatter
        else:
            grad_mix = tie(grad_mix, result_far)
        if p == 0:
            grad_mix = jnp.concatenate([grad_mix, low(logits)], axis=1)
        grad_mixes[p] = grad_mix
        scatter = Scatter(columns, grad_mix)
    ready = scatter.second()
    grad_mixes[0] = tie(grad_mixes[0], *ready)
    mix_back = gathered_times_transposed(grad_mixes, ctx_place, mix_full)
    mix_back = rows_scatter(mix_back.reshape(seq_count, local_len, width)).reshape(-1, width)
    back_mix, unit_mix = norm_backward(mix_back, inputs_mine, rms_scale(inputs_mine, EPSILON), gain_mix)
    input_grad = rows_full(low(grad_residual + back_mix).reshape(seq_count, -1, width))
    gain_mix_part = jnp.sum(mix_back * unit_mix, axis=0)

    conv_cols = jnp.concatenate([jnp.sum(part, axis=0)[:taps] for part in conv_parts], axis=1)
    gains = butterfly(jnp.concatenate([gain_mix_part, gain_ffn_part, gain_o_part]), ("tp",))
    sums = jnp.concatenate([gains, conv_cols.reshape(-1), jnp.sum(logits, axis=0)])
    for p in range(1, parts):
        mix_grads[p] = earlier_scatter.finish(False, *ready)
    sums = butterfly(sums, ("ctx", "fsdp"))
    mix_grads[0] = scatter.finish(True, sums)
    query_grad, key_grad, value_grad = by_kind([grad[:, :part_cols] for grad in mix_grads])
    beta_grad = mix_grads[0][:, part_cols : part_cols + heads_here]
    ends = [width, 2 * width, 2 * width + LANES, sums.shape[0] - LANES]
    gain_mix_grad, gain_ffn_grad, gain_o_grad, conv_grad, bias_grad = jnp.split(sums, ends)
    conv_grad = jnp.stack(by_kind([conv_grad.reshape(taps, -1)]))
    bias_grad = bias_grad[:heads_here]
    out_grad_w = wide(tie(out_grad_w, *scatter.last)).T
    pieces = tie(total, *scatter.last).reshape(3 * units, 4, shard_rows).transpose(1, 0, 2)
    arrived = lax.all_to_all(pieces, "ctx", 0, 0).reshape(4, 3, units, shard_rows)
    gate_grad, up_grad, down_grad = (wide(arrived[:, i].reshape(units_here, shard_rows)) for i in range(3))
    result = result_own + wide(result_near[0]) + wide(result_near[1])
    result = result + wide(result_far)
    block_output = rows_full(low(residual + result).reshape(seq_count, -1, width))

    return (
        block_output,
        input_grad,
        gain_mix_grad,
        query_grad,
        key_grad,
        value_grad,
        beta_grad,
        bias_grad,
        conv_grad,
        gain_o_grad,
        out_grad_w,
        gain_ffn_grad,
        gate_grad.T,
        up_grad.T,
        down_grad,
    )


def solution(mesh):
    placed = (
        P("fsdp", "ctx", None),
        P("fsdp", "ctx"),
        P(),
        P(("ctx", "fsdp"), "tp"),
        P(("ctx", "fsdp"), "tp"),
        P(("ctx", "fsdp"), "tp"),
        P(("ctx", "fsdp"), "tp"),
        P("tp"),
        P(None, None, "tp"),
        P(),
        P("tp", ("ctx", "fsdp")),
        P(),
        P(("ctx", "fsdp"), "tp"),
        P(("ctx", "fsdp"), "tp"),
        P("tp", ("ctx", "fsdp")),
        P("fsdp", "ctx", None),
    )
    return jax.shard_map(
        local,
        mesh=mesh,
        in_specs=placed,
        out_specs=(
            P("fsdp", "ctx", None),
            P("fsdp", "ctx", None),
            P(),
            P(("ctx", "fsdp"), "tp"),
            P(("ctx", "fsdp"), "tp"),
            P(("ctx", "fsdp"), "tp"),
            P(("ctx", "fsdp"), "tp"),
            P("tp"),
            P(None, None, "tp"),
            P(),
            P("tp", ("ctx", "fsdp")),
            P(),
            P(("ctx", "fsdp"), "tp"),
            P(("ctx", "fsdp"), "tp"),
            P("tp", ("ctx", "fsdp")),
        ),
        check_vma=False,
    )
```

```python
import functools
import math
import jax
import jax.numpy as jnp
from jax import lax
from jax.experimental import pallas as pl
from jax.experimental.pallas import tpu as pltpu
from jax.sharding import PartitionSpec as P

LANES = 128
CHUNK = 128
HALO = 8
EPSILON = 1e-06
HEAD_FLOOR = 0.01
VMEM_BYTES = 60 * 1024 * 1024


def low(value):
    return value.astype(jnp.bfloat16)


def mul_nn(left, right):
    return lax.dot_general(low(left), low(right), (((1,), (0,)), ((), ())), preferred_element_type=jnp.float32)


def mul_nt(left, right):
    return lax.dot_general(low(left), low(right), (((1,), (1,)), ((), ())), preferred_element_type=jnp.float32)


def mul_tn(left, right):
    return lax.dot_general(low(left), low(right), (((0,), (0,)), ((), ())), preferred_element_type=jnp.float32)


def iota(shape, axis):
    return lax.broadcasted_iota(jnp.int32, shape, axis)


def chunk_masks(col, row, first):
    size = col.shape[0]
    same = col == row
    order, other = iota((size, size), 0), iota((size, size), 1)
    upto = same & (order >= other)
    below = same & (order > other)
    carried = (col < first).astype(jnp.float32)
    last = (col == row[:, size - 1 :]).astype(jnp.float32)
    keep = (row[:, size - 1 :] < first).astype(jnp.float32)
    return upto, below, carried, last, keep


def invert_units(systems):
    size = systems[0].shape[0]
    order, other = iota((size, size), 0), iota((size, size), 1)
    identity = (order == other).astype(jnp.float32)
    span = 1
    found = None
    while span < size:
        pair = (order // (2 * span) == other // (2 * span)) & (order // span != other // span)
        parts = [jnp.where(pair, system, 0.0) for system in systems]
        if found is None:
            found = [identity - part for part in parts]
        else:
            right = [mul_nn(part, value) for part, value in zip(parts, found)]
            found = [value - mul_nn(value, part) for value, part in zip(found, right)]
        span *= 2
    return found


def conv_rows(ext, conv, col, offset, size, lane, taps):
    total = None
    moved = []
    position = iota((size, 1), 0) + offset
    for tap in range(taps):
        back = taps - 1 - tap
        values = ext[pl.ds(HALO + offset - back, size), lane : lane + LANES]
        values = jnp.where(position - back >= col, values, 0.0)
        moved.append(values)
        term = conv[tap : tap + 1, lane : lane + LANES] * values
        total = term if total is None else total + term
    return total, moved


def unit(values):
    return values * lax.rsqrt(jnp.sum(values * values, axis=-1, keepdims=True) + EPSILON)


def head_column(values, head):
    return jnp.sum(jnp.where(iota(values.shape, 1) == head, values, 0.0), axis=-1, keepdims=True)


def forward_kernel(taps, heads, first, pre, beta, bias, halo, conv, col_ref, row_ref, own, carry, final, inv, upd, states, ext):
    length = pre.shape[0]
    ext[:HALO] = halo[0]
    ext[HALO:] = pre[...]
    head = first + pl.program_id(1) * heads
    jobs = [(i, j) for j in range(length // CHUNK) for i in range(heads)]
    data = {}
    for j in range(length // CHUNK):
        rows = pl.ds(j * CHUNK, CHUNK)
        col, row = col_ref[0, rows], row_ref[0, :, rows]
        masks = chunk_masks(col, row, j * CHUNK)
        strengths = jax.nn.sigmoid(beta[rows] + bias[...])
        for i in range(heads):
            acts = []
            for kind in range(3):
                total, _ = conv_rows(ext, conv, col, j * CHUNK, CHUNK, (3 * i + kind) * LANES, taps)
                acts.append(total * jax.nn.sigmoid(total))
            query, key, value = unit(acts[0]), unit(acts[1]), acts[2]
            strength = head_column(strengths, head + i)
            grams = mul_nt(jnp.concatenate([low(key), low(query)], axis=0), key)
            system = jnp.where(masks[1], strength * grams[:CHUNK], 0.0)
            scores = low(jnp.where(masks[0], grams[CHUNK:], 0.0))
            data[i, j] = (low(query), low(key), value, strength, scores, masks, system)
    inverses = dict(zip(jobs, invert_units([data[job][6] for job in jobs])))
    for i in range(heads):
        state = jnp.concatenate(
            [
                jnp.zeros((LANES, LANES), jnp.float32),
                (iota((LANES, LANES), 0) == iota((LANES, LANES), 1)).astype(jnp.float32),
            ],
            axis=1,
        )
        final[0, i] = state
    for j in range(length // CHUNK):
        rows = pl.ds(j * CHUNK, CHUNK)
        for i in range(heads):
            query, key, value, strength, scores, masks, _ = data[i, j]
            _, _, carried, last, keep = masks
            inverse = low(inverses[i, j])
            state = final[0, i]
            state_low = low(state)
            read = mul_nn(jnp.concatenate([key, query], axis=0), state_low)
            wide = jnp.concatenate([value, jnp.zeros_like(value)], axis=1)
            targets = strength * (wide - carried * read[:CHUNK])
            update = low(mul_nn(inverse, targets))
            result = carried * read[CHUNK:] + mul_nn(scores, update)
            final[0, i] = keep * state + mul_tn(key * low(last), update)
            lanes = slice(i * LANES, (i + 1) * LANES)
            own[rows, lanes] = result[:, :LANES]
            carry[rows, lanes] = low(result[:, LANES:])
            inv[0, i, j] = inverse
            upd[0, i, j] = update
            states[0, i, j] = state_low


def mixer_forward(pre, logit, bias, halo, conv, col, row, taps, first, heads_here, group):
    seqs, length = col.shape[0], col.shape[1]
    steps = heads_here // group
    chunks = length // CHUNK
    wide = 3 * LANES * group
    rows = seqs * length

    def tile(*tail, kind):
        return jax.ShapeDtypeStruct((seqs, heads_here) + tail, kind)

    def spec(*tail):
        return pl.BlockSpec((1, group) + tail, lambda s, h: (s, h) + (0,) * len(tail))

    flat = pl.BlockSpec((length, LANES * group), lambda s, h: (s, h))
    last = logit.shape[1] // LANES - 1
    return pl.pallas_call(
        functools.partial(forward_kernel, taps, group, first),
        grid=(seqs, steps),
        in_specs=[
            pl.BlockSpec((length, wide), lambda s, h: (s, h)),
            pl.BlockSpec((length, LANES), lambda s, h: (s, last)),
            pl.BlockSpec((1, LANES), lambda s, h: (0, 0)),
            pl.BlockSpec((1, HALO, wide), lambda s, h: (s, 0, h)),
            pl.BlockSpec((conv.shape[0], wide), lambda s, h: (0, h)),
            pl.BlockSpec((1, length, 1), lambda s, h: (s, 0, 0)),
            pl.BlockSpec((1, 1, length), lambda s, h: (s, 0, 0)),
        ],
        out_specs=[
            flat,
            flat,
            spec(LANES, 2 * LANES),
            spec(chunks, CHUNK, CHUNK),
            spec(chunks, CHUNK, 2 * LANES),
            spec(chunks, LANES, 2 * LANES),
        ],
        out_shape=[
            jax.ShapeDtypeStruct((rows, heads_here * LANES), jnp.float32),
            jax.ShapeDtypeStruct((rows, heads_here * LANES), jnp.bfloat16),
            tile(LANES, 2 * LANES, kind=jnp.float32),
            tile(chunks, CHUNK, CHUNK, kind=jnp.bfloat16),
            tile(chunks, CHUNK, 2 * LANES, kind=jnp.bfloat16),
            tile(chunks, LANES, 2 * LANES, kind=jnp.bfloat16),
        ],
        scratch_shapes=[pltpu.VMEM((length + HALO, wide), jnp.float32)],
        compiler_params=pltpu.CompilerParams(vmem_limit_bytes=VMEM_BYTES),
        cost_estimate=pl.CostEstimate(
            flops=60 * rows * heads_here * CHUNK * LANES, bytes_accessed=40 * rows * heads_here * LANES, transcendentals=0
        ),
    )(pre, logit, bias, halo, conv, col, row)


def backward_kernel(
    taps, heads, first, pre, beta, bias, halo, conv, col_ref, row_ref, grad_ref, inv, upd, states, start, end,
    grad_pre, tail, before, conv_grad, logits, ext, grad_ext,
):
    length = pre.shape[0]
    step = pl.program_id(1)
    head = first + step * heads
    ext[:HALO] = halo[0]
    ext[HALO:] = pre[...]
    grad_ext[...] = jnp.zeros_like(grad_ext)

    @pl.when(step == 0)
    def _():
        logits[...] = jnp.zeros_like(logits)

    grad_states = [end[0, i] for i in range(heads)]
    entry = [low(start[0, i]) for i in range(heads)]
    tap_sums = {}
    for j in reversed(range(length // CHUNK)):
        offset = j * CHUNK
        rows = pl.ds(offset, CHUNK)
        col, row = col_ref[0, rows], row_ref[0, :, rows]
        upto, below, carried, last, keep = chunk_masks(col, row, offset)
        strengths = jax.nn.sigmoid(beta[rows] + bias[...])
        grad_logit = jnp.zeros((CHUNK, LANES), jnp.float32)
        for i in range(heads):
            raw, taps_in = [], []
            for kind in range(3):
                total, moved = conv_rows(ext, conv, col, offset, CHUNK, (3 * i + kind) * LANES, taps)
                raw.append(total)
                taps_in.append(moved)
            gates = [jax.nn.sigmoid(total) for total in raw]
            acts = [total * gate for total, gate in zip(raw, gates)]
            scales = [lax.rsqrt(jnp.sum(act * act, axis=-1, keepdims=True) + EPSILON) for act in acts[:2]]
            query, key, value = acts[0] * scales[0], acts[1] * scales[1], acts[2]
            strength = head_column(strengths, head + i)
            lanes = slice(i * LANES, (i + 1) * LANES)
            query_low, key_low = low(query), low(key)
            grams = mul_nt(jnp.concatenate([key_low, query_low], axis=0), key_low)
            gram = jnp.where(below, grams[:CHUNK], 0.0)
            scores = jnp.where(upto, grams[CHUNK:], 0.0)
            inverse = inv[0, i, j]
            update = upd[0, i, j]
            update = low(update[:, :LANES].astype(jnp.float32) + mul_nn(update[:, LANES:], entry[i]))
            state = states[0, i, j]
            state = low(state[:, :LANES].astype(jnp.float32) + mul_nn(state[:, LANES:], entry[i]))
            grad_out = grad_ref[rows, lanes]
            grad_state = grad_states[i]
            grad_state_low = low(grad_state)
            key_last = key_low * low(last)
            grad_update = mul_tn(scores, grad_out) + mul_nn(key_last, grad_state_low)
            grad_target = mul_tn(inverse, grad_update)
            weighted = strength * grad_target
            passed = carried * weighted
            out_carried = carried * grad_out.astype(jnp.float32)
            query_carried = query_low * low(carried)
            grad_states[i] = (
                keep * grad_state + mul_tn(query_carried, grad_out) - mul_tn(key_low, passed)
            )
            grad_scores = jnp.where(upto, mul_nt(grad_out, update), 0.0)
            grad_system = jnp.where(below, mul_nt(grad_target, update), 0.0)
            remainder = value - carried * mul_nn(key_low, state)
            grad_strength = jnp.sum(grad_target * remainder - grad_system * gram, axis=-1, keepdims=True)
            scaled = strength * grad_system
            from_state = mul_nt(jnp.concatenate([low(out_carried), low(passed)], axis=0), state)
            from_keys = mul_nn(jnp.concatenate([low(grad_scores), low(scaled + scaled.T)], axis=0), key_low)
            grad_query = from_state[:CHUNK] + from_keys[:CHUNK]
            grad_key = (
                mul_tn(grad_scores, query_low)
                + last * mul_nt(update, grad_state_low)
                - from_state[CHUNK:]
                - from_keys[CHUNK:]
            )
            grad_logit = grad_logit + jnp.where(
                iota((CHUNK, LANES), 1) == head + i, grad_strength * strength * (1.0 - strength), 0.0
            )
            grads = [
                scales[0] * (grad_query - query * jnp.sum(grad_query * query, axis=-1, keepdims=True)),
                scales[1] * (grad_key - key * jnp.sum(grad_key * key, axis=-1, keepdims=True)),
                weighted,
            ]
            position = iota((CHUNK, 1), 0) + offset
            for kind in range(3):
                gate, total = gates[kind], raw[kind]
                grad_conv = grads[kind] * gate * (1.0 + total * (1.0 - gate))
                lane = (3 * i + kind) * LANES
                for tap in range(taps):
                    back = taps - 1 - tap
                    part = jnp.sum(grad_conv * taps_in[kind][tap], axis=0, keepdims=True)
                    spot = (i, kind, tap)
                    tap_sums[spot] = part if spot not in tap_sums else tap_sums[spot] + part
                    back_part = jnp.where(
                        position - back >= col, grad_conv * conv[tap : tap + 1, lane : lane + LANES], 0.0
                    )
                    where = pl.ds(HALO + offset - back, CHUNK)
                    grad_ext[where, lane : lane + LANES] += back_part
        logits[rows] += grad_logit
    grad_pre[...] = low(grad_ext[HALO:])
    before[0] = grad_ext[:HALO]
    tail[0] = grad_ext[length:]
    for i in range(heads):
        for kind in range(3):
            lane = (3 * i + kind) * LANES
            for tap in range(taps):
                conv_grad[0, tap : tap + 1, lane : lane + LANES] = tap_sums[i, kind, tap]


def mixer_backward(
    pre, logit, bias, halo, conv, col, row, grad_mixed, inv, upd, states, start, end, taps, first, heads_here, group
):
    seqs, length = col.shape[0], col.shape[1]
    steps = heads_here // group
    chunks = length // CHUNK
    wide = 3 * LANES * group
    rows = seqs * length

    def spec(*tail):
        return pl.BlockSpec((1, group) + tail, lambda s, h: (s, h) + (0,) * len(tail))

    last = logit.shape[1] // LANES - 1
    part = pl.BlockSpec((1, HALO, wide), lambda s, h: (s, 0, h))
    edge = jax.ShapeDtypeStruct((seqs, HALO, 3 * LANES * heads_here), jnp.float32)
    return pl.pallas_call(
        functools.partial(backward_kernel, taps, group, first),
        grid=(seqs, steps),
        in_specs=[
            pl.BlockSpec((length, wide), lambda s, h: (s, h)),
            pl.BlockSpec((length, LANES), lambda s, h: (s, last)),
            pl.BlockSpec((1, LANES), lambda s, h: (0, 0)),
            part,
            pl.BlockSpec((conv.shape[0], wide), lambda s, h: (0, h)),
            pl.BlockSpec((1, length, 1), lambda s, h: (s, 0, 0)),
            pl.BlockSpec((1, 1, length), lambda s, h: (s, 0, 0)),
            pl.BlockSpec((length, LANES * group), lambda s, h: (s, h)),
            spec(chunks, CHUNK, CHUNK),
            spec(chunks, CHUNK, 2 * LANES),
            spec(chunks, LANES, 2 * LANES),
            spec(LANES, LANES),
            spec(LANES, LANES),
        ],
        out_specs=[
            pl.BlockSpec((length, wide), lambda s, h: (s, h)),
            part,
            part,
            part,
            pl.BlockSpec((length, LANES), lambda s, h: (s, 0)),
        ],
        out_shape=[
            jax.ShapeDtypeStruct((rows, 3 * LANES * heads_here), jnp.bfloat16),
            edge,
            edge,
            edge,
            jax.ShapeDtypeStruct((rows, LANES), jnp.float32),
        ],
        scratch_shapes=[
            pltpu.VMEM((length + HALO, wide), jnp.float32),
            pltpu.VMEM((length + HALO, wide), jnp.float32),
        ],
        compiler_params=pltpu.CompilerParams(vmem_limit_bytes=VMEM_BYTES),
        cost_estimate=pl.CostEstimate(
            flops=60 * rows * heads_here * CHUNK * LANES, bytes_accessed=40 * rows * heads_here * LANES, transcendentals=0
        ),
    )(pre, logit, bias, halo, conv, col, row, grad_mixed, inv, upd, states, start, end)


def mixed_rows_of(own, carry, start):
    return own + mul_nn(carry, start)


def output_kernel(heads, own, carry, start, gain, out):
    for i in range(heads):
        lanes = slice(i * LANES, (i + 1) * LANES)
        mixed = mixed_rows_of(own[:, lanes], carry[:, lanes], start[0, i])
        scale = lax.rsqrt(jnp.mean(mixed * mixed, axis=-1, keepdims=True) + HEAD_FLOOR)
        out[:, lanes] = low(mixed * scale * gain[...])


def output_backward_kernel(heads, own, carry, start, gain, grad, out, across, gain_grad):
    total = jnp.zeros((1, LANES), jnp.float32)
    for i in range(heads):
        lanes = slice(i * LANES, (i + 1) * LANES)
        carried = carry[:, lanes]
        mixed = mixed_rows_of(own[:, lanes], carried, start[0, i])
        scale = lax.rsqrt(jnp.mean(mixed * mixed, axis=-1, keepdims=True) + HEAD_FLOOR)
        normed = mixed * scale
        upper = grad[:, lanes].astype(jnp.float32)
        total = total + jnp.sum(upper * normed, axis=0, keepdims=True)
        weighted = upper * gain[...]
        back = scale * (weighted - normed * jnp.mean(weighted * normed, axis=-1, keepdims=True))
        out[:, lanes] = low(back)
        across[0, i] = mul_tn(carried, back)
    gain_grad[0, 0] = total


def mixer_output(own, carry, start, gain, group):
    seqs, heads_here = start.shape[:2]
    rows = own.shape[0]
    length = rows // seqs
    flat = pl.BlockSpec((length, LANES * group), lambda s, h: (s, h))
    square = pl.BlockSpec((1, group, LANES, LANES), lambda s, h: (s, h, 0, 0))
    return pl.pallas_call(
        functools.partial(output_kernel, group),
        grid=(seqs, heads_here // group),
        in_specs=[flat, flat, square, pl.BlockSpec((1, LANES), lambda s, h: (0, 0))],
        out_specs=flat,
        out_shape=jax.ShapeDtypeStruct(own.shape, jnp.bfloat16),
        compiler_params=pltpu.CompilerParams(vmem_limit_bytes=VMEM_BYTES),
        cost_estimate=pl.CostEstimate(
            flops=2 * own.size * LANES, bytes_accessed=8 * own.size, transcendentals=0
        ),
    )(own, carry, start, gain)


def mixer_output_backward(own, carry, start, gain, grad, first, group):
    seqs, heads_here = start.shape[:2]
    rows = own.shape[0]
    length = rows // seqs
    steps = heads_here // group
    flat = pl.BlockSpec((length, LANES * group), lambda s, h: (s, h))
    base = first // group
    shifted = pl.BlockSpec((length, LANES * group), lambda s, h: (s, base + h))
    square = pl.BlockSpec((1, group, LANES, LANES), lambda s, h: (s, h, 0, 0))
    return pl.pallas_call(
        functools.partial(output_backward_kernel, group),
        grid=(seqs, steps),
        in_specs=[flat, flat, square, pl.BlockSpec((1, LANES), lambda s, h: (0, 0)), shifted],
        out_specs=[flat, square, pl.BlockSpec((1, 1, 1, LANES), lambda s, h: (s, h, 0, 0))],
        out_shape=[
            jax.ShapeDtypeStruct(own.shape, jnp.bfloat16),
            jax.ShapeDtypeStruct(start.shape, jnp.float32),
            jax.ShapeDtypeStruct((seqs, steps, 1, LANES), jnp.float32),
        ],
        compiler_params=pltpu.CompilerParams(vmem_limit_bytes=VMEM_BYTES),
        cost_estimate=pl.CostEstimate(
            flops=4 * own.size * LANES, bytes_accessed=12 * own.size, transcendentals=0
        ),
    )(own, carry, start, gain, grad)


def ffn_kernel(mine, other, mine_grads, other_grads, gate_w, up_w, down_w, *outs):
    rows = jnp.concatenate([mine[...], other[...]], axis=0)
    grads = jnp.concatenate([mine_grads[...], other_grads[...]], axis=0)
    half = mine.shape[0]
    gate = mul_nt(rows, gate_w[...])
    up = mul_nt(rows, up_w[...])
    grad_hidden = mul_nt(grads, down_w[...])
    sigmoid = jax.nn.sigmoid(gate)
    active = gate * sigmoid
    kept = low(active * up)
    back_gate = low(grad_hidden * up * sigmoid * (1.0 + gate * (1.0 - sigmoid)))
    back_up = low(grad_hidden * active)
    grad_rows = low(mul_nn(back_gate, gate_w[...]) + mul_nn(back_up, up_w[...]))
    result = low(mul_nn(kept, down_w[...]))
    for side in range(2):
        here = slice(side * half, (side + 1) * half)
        acts, grad_out, result_out = outs[3 * side : 3 * side + 3]
        for kind, value in enumerate((back_gate, back_up, kept)):
            acts[kind] = value[here]
        grad_out[...] = grad_rows[here]
        result_out[...] = result[here]


def ffn_both(rows, grads, gate_up, down):
    count, width = rows[0].shape
    units = down.shape[0]
    tile = min(256, count)
    wide_rows = pl.BlockSpec((tile, width), lambda i: (i, 0))
    narrow = pl.BlockSpec((3, tile, units), lambda i: (0, i, 0))

    def third(index):
        return pl.BlockSpec((units, width), lambda i: (index, 0))

    flat = jax.ShapeDtypeStruct((count, width), jnp.bfloat16)
    outs = pl.pallas_call(
        ffn_kernel,
        grid=(count // tile,),
        in_specs=[wide_rows] * 4 + [third(0), third(1), third(0)],
        out_specs=[narrow, wide_rows, wide_rows] * 2,
        out_shape=[jax.ShapeDtypeStruct((3, count, units), jnp.bfloat16), flat, flat] * 2,
        compiler_params=pltpu.CompilerParams(vmem_limit_bytes=VMEM_BYTES),
        cost_estimate=pl.CostEstimate(
            flops=24 * count * width * units, bytes_accessed=16 * count * width + 6 * units * width, transcendentals=0
        ),
    )(*rows, *grads, gate_up, gate_up, down)
    return outs[:3], outs[3:]


def ffn_weights_kernel(count, lines, *refs):
    acts, rows, grads = refs[:count], refs[count : 2 * count], refs[2 * count : 3 * count]
    out, total = refs[-2:]
    part = out.shape[-1]

    def add(sources):
        for i in range(count):
            value = mul_tn(acts[i][0], sources[i][...])
            if i == 0:
                total[...] = value
            else:
                total[...] += value

    @pl.when(pl.program_id(0) < 2)
    def _():
        add(rows)

    @pl.when(pl.program_id(0) == 2)
    def _():
        add(grads)

    for line in range(lines):
        out[line, 0] = low(total[:, line * part : (line + 1) * part])


def ffn_weights(acts, rows, grads, lines, squares):
    count, width = len(acts), rows[0].shape[1]
    size, units = acts[0].shape[1:]
    block = width // squares
    part = block // lines
    act_spec = pl.BlockSpec((1, size, units), lambda k, c: (k, 0, 0))
    row_spec = pl.BlockSpec((size, block), lambda k, c: (0, jnp.where(k < 2, c, squares - 1)))
    grad_spec = pl.BlockSpec((size, block), lambda k, c: (0, jnp.where(k < 2, 0, c)))
    return pl.pallas_call(
        functools.partial(ffn_weights_kernel, count, lines),
        grid=(3, squares),
        in_specs=[act_spec] * count + [row_spec] * count + [grad_spec] * count,
        out_specs=pl.BlockSpec((lines, 1, units, part), lambda k, c: (0, k, 0, c)),
        out_shape=jax.ShapeDtypeStruct((lines, 3, units, squares * part), jnp.bfloat16),
        scratch_shapes=[pltpu.VMEM((units, block), jnp.float32)],
        compiler_params=pltpu.CompilerParams(vmem_limit_bytes=VMEM_BYTES),
        cost_estimate=pl.CostEstimate(
            flops=6 * count * size * width * units, bytes_accessed=8 * count * size * width, transcendentals=0
        ),
    )(*acts, *rows, *grads)


def block_columns(place, bit, size):
    return pl.multiple_of((place[0] ^ bit) * size, size)


def gathered_kernel(place, rows, *refs):
    out = refs[-1]
    own, beside, across, upper, lower = refs[:-1]
    size, half = own.shape[0], upper.shape[0]
    total = None
    for bit, skip, ref in ((0, 0, own), (1, 0, beside), (2, 0, across), (3, 0, upper), (3, half, lower)):
        start = pl.multiple_of(block_columns(place, bit, size) + skip, half)
        value = mul_nn(rows[:, pl.ds(start, ref.shape[0])], ref[...])
        total = value if total is None else total + value
    out[...] = total


def gathered_times(rows, place, pieces):
    count, width = rows.shape
    columns = pieces[0].shape[1]
    tile = min(256, count)
    whole = [pl.BlockSpec(piece.shape, lambda i, place: (0, 0)) for piece in pieces]
    return pl.pallas_call(
        gathered_kernel,
        grid_spec=pltpu.PrefetchScalarGridSpec(
            num_scalar_prefetch=1,
            grid=(count // tile,),
            in_specs=[pl.BlockSpec((tile, width), lambda i, place: (i, 0))] + whole,
            out_specs=pl.BlockSpec((tile, columns), lambda i, place: (i, 0)),
        ),
        out_shape=jax.ShapeDtypeStruct((count, columns), jnp.float32),
        compiler_params=pltpu.CompilerParams(vmem_limit_bytes=VMEM_BYTES),
        cost_estimate=pl.CostEstimate(
            flops=2 * count * width * columns, bytes_accessed=2 * (count + columns) * width, transcendentals=0
        ),
    )(jnp.reshape(place, (1,)).astype(jnp.int32), rows, *pieces)


def gathered_transposed_kernel(count, place, *refs):
    factors, pieces, out = refs[:count], refs[count:-1], refs[-1]
    size, half = pieces[0].shape[0], pieces[3].shape[0]
    for i, (bit, skip) in enumerate(((0, 0), (1, 0), (2, 0), (3, 0), (3, half))):
        start = pl.multiple_of(block_columns(place, bit, size) + skip, half)
        total = None
        for p in range(count):
            value = mul_nt(factors[p][...], pieces[5 * p + i][...])
            total = value if total is None else total + value
        out[:, pl.ds(start, pieces[i].shape[0])] = low(total)


def gathered_times_transposed(factors, place, pieces):
    count, rows = len(factors), factors[0].shape[0]
    width = 4 * pieces[0][0].shape[0]
    tile = min(256, rows)
    flat = [piece for some in pieces for piece in some]
    whole = [pl.BlockSpec(piece.shape, lambda i, place: (0, 0)) for piece in flat]
    wides = [pl.BlockSpec((tile, factor.shape[1]), lambda i, place: (i, 0)) for factor in factors]
    columns = sum(factor.shape[1] for factor in factors)
    return pl.pallas_call(
        functools.partial(gathered_transposed_kernel, count),
        grid_spec=pltpu.PrefetchScalarGridSpec(
            num_scalar_prefetch=1,
            grid=(rows // tile,),
            in_specs=wides + whole,
            out_specs=pl.BlockSpec((tile, width), lambda i, place: (i, 0)),
        ),
        out_shape=jax.ShapeDtypeStruct((rows, width), jnp.bfloat16),
        compiler_params=pltpu.CompilerParams(vmem_limit_bytes=VMEM_BYTES),
        cost_estimate=pl.CostEstimate(
            flops=2 * rows * width * columns, bytes_accessed=2 * (rows + columns) * width, transcendentals=0
        ),
    )(jnp.reshape(place, (1,)).astype(jnp.int32), *factors, *flat)


def join_kernel(squares, source, target):
    lines, _, columns = source.shape
    part = columns // squares
    for i in range(lines):
        for j in range(squares):
            at = (j * lines + i) * part
            target[:, at : at + part] = source[i, :, j * part : (j + 1) * part]


def columns_join(parts, squares):
    lines, rows, columns = parts.shape
    tile = 176 if rows % 176 == 0 else rows
    return pl.pallas_call(
        functools.partial(join_kernel, squares),
        grid=(rows // tile,),
        in_specs=[pl.BlockSpec((lines, tile, columns), lambda i: (0, i, 0))],
        out_specs=pl.BlockSpec((tile, lines * columns), lambda i: (i, 0)),
        out_shape=jax.ShapeDtypeStruct((rows, lines * columns), parts.dtype),
        compiler_params=pltpu.CompilerParams(vmem_limit_bytes=VMEM_BYTES),
        cost_estimate=pl.CostEstimate(flops=0, bytes_accessed=4 * parts.size, transcendentals=0),
    )(parts)


def flip(value, axis, bit):
    devices = range(lax.axis_size(axis))
    return lax.ppermute(value, axis, [(i, i ^ bit) for i in devices])


def shift(value, axis, distance):
    count = lax.axis_size(axis)
    return lax.ppermute(value, axis, [(i, (i + distance) % count) for i in range(count)])


def from_behind(block, axis, distance):
    devices = range(lax.axis_size(axis))
    route = [(i - distance, i) for i in devices if i - distance in devices]
    return lax.ppermute(block, axis, route)


def tie(value, *earlier):
    return lax.optimization_barrier((value,) + earlier)[0]


def put(buffer, piece, *start):
    return lax.dynamic_update_slice(buffer, piece, start)


def wide(value):
    return value.astype(jnp.float32)


def gather_line(shard):
    count, place = lax.axis_size("fsdp"), lax.axis_index("fsdp")
    pieces = [shard] + [shift(shard, "fsdp", d) for d in range(1, count)]
    order = [(place - i) % count for i in range(count)]
    return jnp.concatenate([lax.select_n(which, *pieces) for which in order], axis=0)


class Square:
    def __init__(self, own):
        self.own = own
        self.half = own.shape[0] // 2
        self.beside = flip(own, "ctx", 1)
        self.across = flip(own, "ctx", 2)

    def forward(self, *earlier):
        upper = self.beside[: self.half]
        lower = self.across[self.half :]
        if earlier:
            upper, lower = lax.optimization_barrier((upper, lower) + earlier)[:2]
        self.upper = flip(upper, "ctx", 2)
        self.lower = flip(lower, "ctx", 1)
        return self

    def done(self):
        return (self.upper, self.lower)

    def pieces(self):
        return [self.own, self.beside, self.across, self.upper, self.lower]

    def far(self):
        return jnp.concatenate([self.upper, self.lower], axis=0)


def both_sides(rows):
    if lax.axis_size("tp") == 2:
        return rows, flip(rows, "tp", 1)
    every = lax.all_gather(rows, "tp", axis=0, tiled=True)
    half = every.shape[0] // 2
    return every[:half], every[half:]


def core_sum(mine, other):
    if lax.axis_size("tp") == 2:
        return wide(mine) + wide(flip(other, "tp", 1))
    both = jnp.concatenate([mine, other], axis=0)
    return wide(lax.psum_scatter(both, "tp", scatter_dimension=0, tiled=True))


def neighbour_columns(rows):
    width = rows.shape[1] // 4
    place = lax.axis_index("ctx")
    return [lax.dynamic_slice_in_dim(rows, (place ^ bit) * width, width, 1) for bit in range(4)]


class Line:
    def __init__(self, own):
        count, place = lax.axis_size("fsdp"), lax.axis_index("fsdp")
        own = own.reshape(count, own.shape[0] // count, own.shape[1])

        def part(distance):
            return lax.dynamic_index_in_dim(own, (place + distance) % count, 0, keepdims=False)

        self.kept = part(0)
        self.sent = [low(part(distance)) for distance in range(1, count)]
        self.arrived = [shift(piece, "fsdp", distance + 1) for distance, piece in enumerate(self.sent)]

    def total(self, *late):
        total = self.kept
        for part in lax.optimization_barrier(tuple(self.arrived) + late)[: len(self.arrived)]:
            total = total + wide(part)
        return total


class Scatter:
    def __init__(self, columns, grads):
        self.columns, self.grads = columns, grads
        self.half = columns[0].shape[1] // 2
        beside, across = (
            jnp.concatenate([self.side(3, 1), self.side(1, 1)], axis=1),
            jnp.concatenate([self.side(3, 0), self.side(2, 0)], axis=1),
        )
        self.sent = [low(outer_rows(beside, grads)), low(outer_rows(across, grads))]
        self.first = (flip(self.sent[0], "ctx", 1), flip(self.sent[1], "ctx", 2))

    def side(self, bit, lower):
        return self.columns[bit][:, lower * self.half : (lower + 1) * self.half]

    def second(self, *earlier):
        first = self.first
        if earlier:
            first = lax.optimization_barrier(first + earlier)[:2]
        beside, across = (wide(part) for part in first)
        upper = low(outer_rows(self.side(1, 0), self.grads) + across[: self.half])
        lower = low(outer_rows(self.side(2, 1), self.grads) + beside[: self.half])
        self.last = (flip(upper, "ctx", 1), flip(lower, "ctx", 2))
        self.kept = (beside, across)
        return upper, lower

    def own(self, *ties):
        beside_upper, across_lower = self.last
        if ties:
            beside_upper, across_lower = lax.optimization_barrier(self.last + ties)[:2]
        beside, across = self.kept
        own = outer_rows(self.columns[0], self.grads)
        upper = own[: self.half] + wide(beside_upper) + across[self.half :]
        lower = own[self.half :] + beside[self.half :] + wide(across_lower)
        return jnp.concatenate([upper, lower], axis=0)


def butterfly(value, axes):
    for axis in axes:
        count, bit = lax.axis_size(axis), 1
        while bit < count:
            value = value + flip(value, axis, bit)
            bit *= 2
    return value


def rms_scale(values, floor_value):
    return lax.rsqrt(jnp.mean(values * values, axis=-1, keepdims=True) + floor_value)


def norm_backward(grad_normed, inputs, scale, gain):
    normed = inputs * scale
    weighted = grad_normed * gain
    return (
        scale * (weighted - normed * jnp.mean(weighted * normed, axis=-1, keepdims=True)),
        normed,
    )


def times(left, right):
    return jnp.dot(left, right, preferred_element_type=jnp.float32)


def times_transposed(left, right):
    return lax.dot_general(
        left, right, (((1,), (1,)), ((), ())), preferred_element_type=jnp.float32
    )


def outer_rows(left, right):
    return lax.dot_general(
        left, right, (((0,), (0,)), ((), ())), preferred_element_type=jnp.float32
    )


def rows_mine(rows):
    count = rows.shape[1] // lax.axis_size("tp")
    return lax.dynamic_slice_in_dim(rows, lax.axis_index("tp") * count, count, 1)


def rows_scatter(partial):
    if lax.axis_size("tp") != 2:
        return wide(lax.psum_scatter(partial, "tp", scatter_dimension=1, tiled=True))
    count = partial.shape[1] // 2
    other = lax.dynamic_slice_in_dim(partial, (1 - lax.axis_index("tp")) * count, count, 1)
    return wide(rows_mine(partial)) + wide(flip(other, "tp", 1))


def rows_full(mine):
    if lax.axis_size("tp") != 2:
        return lax.all_gather(mine, "tp", axis=1, tiled=True)
    other = flip(mine, "tp", 1)
    lower = lax.axis_index("tp") == 0
    return jnp.concatenate([jnp.where(lower, mine, other), jnp.where(lower, other, mine)], axis=1)


def by_head(parts):
    heads = range(parts[0].shape[-1] // LANES)
    return jnp.concatenate([part[..., h * LANES : (h + 1) * LANES] for h in heads for part in parts], axis=-1)


def by_kind(joined):
    return [
        jnp.concatenate(
            [
                some[..., at : at + LANES]
                for some in joined
                for at in range(kind * LANES, some.shape[-1], 3 * LANES)
            ],
            axis=-1,
        )
        for kind in range(3)
    ]


def pass_states(own, transfer, forward, *beside):
    rule = "shij,shjk->shik" if forward == 1 else "shji,shjk->shik"
    leaving = own
    entered = low(jnp.zeros_like(own))
    for repeat in range(lax.axis_size("ctx") - 1):
        entered = from_behind(low(leaving), "ctx", forward)
        if repeat == 0 and beside:
            entered = tie(entered, *beside)
        leaving = own + jnp.einsum(rule, transfer, entered, preferred_element_type=jnp.float32)
    return wide(entered)


def local(
    block_input,
    doc_start,
    gain_mix,
    query_weight,
    key_weight,
    value_weight,
    beta_weight,
    beta_bias,
    conv_weight,
    gain_o,
    out_weight,
    gain_ffn,
    gate_weight,
    up_weight,
    down_weight,
    out_grad,
):
    seq_count, local_len, width = block_input.shape
    row_count = seq_count * local_len
    heads_here = beta_weight.shape[1]
    taps = conv_weight.shape[1]
    parts = 2 if heads_here % 2 == 0 else 1
    part_heads = heads_here // parts
    group = 2 if part_heads % 2 == 0 else 1
    part_cols = 3 * part_heads * LANES
    spare = LANES - heads_here
    units_here = gate_weight.shape[1]
    shard_rows = gate_weight.shape[0]

    joined = by_head([low(query_weight), low(key_weight), low(value_weight)])
    shards = [joined[:, p * part_cols : (p + 1) * part_cols] for p in range(parts)]
    shards[0] = jnp.concatenate([shards[0], jnp.pad(low(beta_weight), ((0, 0), (0, spare)))], axis=1)
    shards.append(low(out_weight).T)
    lines = []
    for shard in shards[:parts]:
        lines.append(gather_line(tie(shard, lines[-1]) if lines else shard))
    units = units_here // 4
    pieces = jnp.stack([low(gate_weight).T, low(up_weight).T, low(down_weight)])
    pieces = pieces.reshape(3, 4, units, shard_rows).transpose(1, 0, 2, 3)
    ffn_swapped = lax.all_to_all(pieces.reshape(4, 3 * units, shard_rows), "ctx", 0, 0)
    ffn_line = ffn_swapped.transpose(1, 0, 2).reshape(3 * units, 4 * shard_rows)
    line_count = lax.axis_size("fsdp")

    ctx_place = lax.axis_index("ctx")
    first_pos = ctx_place * local_len
    starts = doc_start - first_pos
    col, row = starts[:, :, None], starts[:, None, :]
    conv = by_head([conv_weight[0], conv_weight[1], conv_weight[2]])
    bias = jnp.pad(beta_bias, (0, spare))[None]
    gain_head = gain_o[None]
    tokens = block_input.reshape(row_count, width)
    inputs = wide(tokens)
    normed_mix = low(inputs * rms_scale(inputs, EPSILON) * gain_mix)
    inputs_mine = wide(rows_mine(block_input).reshape(-1, width))
    grads_mine = rows_mine(out_grad).reshape(-1, width)

    square = Square(tie(lines[0], ffn_swapped)).forward()
    gate_up_parts = lax.all_gather(tie(ffn_line[: 2 * units], lines[parts - 1], *square.done()), "fsdp", axis=0)
    down_parts = lax.all_gather(ffn_line[2 * units :], "fsdp", axis=0)
    mix_full, kept, pre = [], [], []
    for p in range(parts):
        mix_full.append(square.pieces())
        square = Square(tie(lines[p + 1], *square.done()))
        ends = normed_mix.reshape(seq_count, local_len, width)[:, local_len - HALO :].reshape(seq_count * HALO, width)
        ends = gathered_times(ends, ctx_place, mix_full[p])
        halo = from_behind(ends[:, :part_cols].reshape(seq_count, HALO, part_cols), "ctx", 1)
        pre.append(gathered_times(tie(normed_mix, ends), ctx_place, mix_full[p]))
        convs = conv[:, p * part_cols : (p + 1) * part_cols]
        kept.append(
            [halo, convs]
            + list(
                mixer_forward(
                    pre[p], pre[0], bias, halo, convs, col, row, taps, p * part_heads, part_heads, group
                )
            )
        )
        square.forward(kept[p][2])
        if p == 0:
            lines.append(gather_line(tie(shards[-1], kept[p][2], square.beside)))
            grad_square = Square(tie(grads_mine, kept[p][2], *square.done()))
    out_full = square.pieces()

    gate_up_full = columns_join(gate_up_parts, 4)
    finals = jnp.concatenate([some[4] for some in kept], axis=1)
    transfer = low(finals[..., LANES:])
    first = tie(finals[..., :LANES], gate_up_parts, grad_square.beside, grad_square.across)
    entering = pass_states(first, transfer, 1)
    entered = [entering[:, p * part_heads : (p + 1) * part_heads] for p in range(parts)]
    grad_square.forward(entering)
    grad_rows = [both_sides(part) for part in (grad_square.own, grad_square.beside, grad_square.across)]
    mixed_rows = []
    for p in range(parts):
        own, carry = kept[p][2:4]
        if p == parts - 1:
            own = tie(own, gate_up_full)
        mixed_rows.append(mixer_output(own, carry, entered[p], gain_head, group))
    mixed_rows = jnp.concatenate(mixed_rows, axis=1)
    mixed_rows = tie(mixed_rows, *(other for _, other in grad_rows))
    grad_rows.append(both_sides(grad_square.far()))

    branch = gathered_times_transposed([mixed_rows], ctx_place, [out_full]).reshape(seq_count, local_len, width)
    branch = tie(branch, down_parts)
    residual = inputs_mine + rows_scatter(branch).reshape(-1, width)
    scale_ffn = rms_scale(residual, EPSILON)
    square = Square(low(residual * scale_ffn * gain_ffn))
    ffn_full = (gate_up_full, columns_join(down_parts, 4))

    ffn_rows = [both_sides(square.own)]
    ffn_out = [ffn_both(ffn_rows[0], grad_rows[0], *ffn_full)]
    square.forward(ffn_out[0][0][0])
    ffn_rows.append(both_sides(tie(square.beside, ffn_out[0][0][0])))
    ffn_out.append(ffn_both(ffn_rows[1], grad_rows[1], *ffn_full))
    ffn_rows.append(both_sides(tie(square.across, ffn_out[0][0][0])))
    mine, other = ffn_rows[2]
    ffn_out.append(ffn_both((tie(mine, ffn_out[1][0][0], *square.done()), other), grad_rows[2], *ffn_full))
    beside_sums, across_sums = (low(core_sum(*(side[1] for side in ffn_out[bit]))) for bit in (1, 2))
    ffn_rows.append(both_sides(square.far()))
    mine, other = ffn_rows[3]
    ffn_out.append(ffn_both((tie(mine, beside_sums, across_sums), other), grad_rows[3], *ffn_full))
    near_sums = (flip(beside_sums, "ctx", 1), flip(across_sums, "ctx", 2))
    mine, other = (side[1] for side in ffn_out[3])
    far_sums = low(core_sum(mine, tie(other, *near_sums)))
    acts = [side[0] for outs in ffn_out for side in outs]
    acts[0] = tie(acts[0], far_sums)
    far_sums = flip(far_sums, "ctx", 3)
    sums = ffn_weights(
        acts,
        [side for sides in ffn_rows for side in sides],
        [side for sides in grad_rows for side in sides],
        line_count,
        4,
    ).reshape(line_count, 3 * units, 4 * shard_rows)

    far_sums, sums = lax.optimization_barrier((far_sums, sums))
    result_near = []
    for bit in (1, 2):
        mine, other = (side[2] for side in ffn_out[bit])
        result_near.append(flip(low(core_sum(mine, tie(other, far_sums))), "ctx", bit))
    grad_normed = core_sum(*(side[1] for side in ffn_out[0]))
    grad_normed = grad_normed + wide(near_sums[0]) + wide(near_sums[1]) + wide(far_sums)
    back_ffn, unit_ffn = norm_backward(grad_normed, residual, scale_ffn, gain_ffn)
    grad_residual = wide(grads_mine) + back_ffn
    gain_ffn_part = jnp.sum(grad_normed * unit_ffn, axis=0)
    grad_branch = rows_full(low(grad_residual).reshape(seq_count, -1, width)).reshape(row_count, width)
    grad_heads = gathered_times(grad_branch, ctx_place, out_full)
    backs, acrosses, gain_o_part = [], [], 0.0
    for p in range(parts):
        _, _, own, carry, _, _, _, _ = kept[p]
        back, across, gain_part = mixer_output_backward(
            own, carry, entered[p], gain_head, grad_heads, p * part_heads, group
        )
        backs.append(back)
        acrosses.append(across)
        gain_o_part = gain_o_part + jnp.sum(gain_part, axis=(0, 1, 2))
    grad_end = pass_states(jnp.concatenate(acrosses, axis=1), transfer, -1, *result_near)
    total = lax.psum_scatter(sums, "fsdp", scatter_dimension=0, tiled=True)

    out_grad_w = low(outer_rows(grad_branch, mixed_rows))
    out_grad_w = lax.psum_scatter(out_grad_w, ("ctx", "fsdp"), scatter_dimension=0, tiled=True)

    mine, other = (side[2] for side in ffn_out[0])
    result_own = core_sum(mine, tie(other, grad_branch))
    mine, other = (side[2] for side in ffn_out[3])
    result_far = flip(tie(low(core_sum(mine, tie(other, grad_branch))), grad_end), "ctx", 3)
    columns = neighbour_columns(normed_mix)
    grad_mixes, mix_grads, conv_parts = [None] * parts, [None] * parts, [None] * parts
    logits = 0.0
    scatter = None
    for p in reversed(range(parts)):
        halo, convs, own, carry, final, inverses, updates, states = kept[p]
        heads = slice(p * part_heads, (p + 1) * part_heads)
        back = backs[p] if scatter is None else tie(backs[p], total, *scatter.sent)
        grad_mix, tail, before, conv_parts[p], logit = mixer_backward(
            pre[p], pre[0], bias, halo, convs, col, row, back, inverses, updates, states,
            entered[p], grad_end[:, heads], taps, p * part_heads, part_heads, group,
        )
        logits = logits + logit
        tail = low(tail + from_behind(before, "ctx", -1))
        grad_mix = put(grad_mix.reshape(seq_count, local_len, -1), tail, 0, local_len - HALO, 0)
        grad_mix = grad_mix.reshape(row_count, -1)
        if scatter is not None:
            scatter.second(before)
            earlier_scatter = scatter
        else:
            grad_mix = tie(grad_mix, result_far)
        if p == 0:
            grad_mix = jnp.concatenate([grad_mix, low(logits)], axis=1)
        grad_mixes[p] = grad_mix
        scatter = Scatter(columns, grad_mix)
    ready = scatter.second()
    grad_mixes[0] = tie(grad_mixes[0], *ready)
    mix_back = tie(gathered_times_transposed(grad_mixes, ctx_place, mix_full), *scatter.last)
    mix_back = rows_scatter(mix_back.reshape(seq_count, local_len, width)).reshape(-1, width)
    back_mix, unit_mix = norm_backward(mix_back, inputs_mine, rms_scale(inputs_mine, EPSILON), gain_mix)
    input_grad = rows_full(low(grad_residual + back_mix).reshape(seq_count, -1, width))
    gain_mix_part = jnp.sum(mix_back * unit_mix, axis=0)

    conv_cols = jnp.concatenate([jnp.sum(part, axis=0)[:taps] for part in conv_parts], axis=1)
    gains = butterfly(jnp.concatenate([gain_mix_part, gain_ffn_part, gain_o_part]), ("tp",))
    sums = jnp.concatenate([gains, conv_cols.reshape(-1), jnp.sum(logits, axis=0)])
    for p in range(1, parts):
        own = low(earlier_scatter.own(*ready))
        mix_grads[p] = wide(lax.psum_scatter(own, "fsdp", scatter_dimension=0, tiled=True))
    last_line = Line(scatter.own())
    sums = butterfly(tie(sums, *last_line.sent), ("ctx", "fsdp"))
    mix_grads[0] = last_line.total(sums)
    query_grad, key_grad, value_grad = by_kind([grad[:, :part_cols] for grad in mix_grads])
    beta_grad = mix_grads[0][:, part_cols : part_cols + heads_here]
    ends = [width, 2 * width, 2 * width + LANES, sums.shape[0] - LANES]
    gain_mix_grad, gain_ffn_grad, gain_o_grad, conv_grad, bias_grad = jnp.split(sums, ends)
    conv_grad = jnp.stack(by_kind([conv_grad.reshape(taps, -1)]))
    bias_grad = bias_grad[:heads_here]
    out_grad_w = wide(tie(out_grad_w, *scatter.last)).T
    pieces = tie(total, *scatter.last).reshape(3 * units, 4, shard_rows).transpose(1, 0, 2)
    arrived = lax.all_to_all(pieces, "ctx", 0, 0).reshape(4, 3, units, shard_rows)
    gate_grad, up_grad, down_grad = (wide(arrived[:, i].reshape(units_here, shard_rows)) for i in range(3))
    result = result_own + wide(result_near[0]) + wide(result_near[1])
    result = result + wide(result_far)
    block_output = rows_full(low(residual + result).reshape(seq_count, -1, width))

    return (
        block_output,
        input_grad,
        gain_mix_grad,
        query_grad,
        key_grad,
        value_grad,
        beta_grad,
        bias_grad,
        conv_grad,
        gain_o_grad,
        out_grad_w,
        gain_ffn_grad,
        gate_grad.T,
        up_grad.T,
        down_grad,
    )


def solution(mesh):
    placed = (
        P("fsdp", "ctx", None),
        P("fsdp", "ctx"),
        P(),
        P(("ctx", "fsdp"), "tp"),
        P(("ctx", "fsdp"), "tp"),
        P(("ctx", "fsdp"), "tp"),
        P(("ctx", "fsdp"), "tp"),
        P("tp"),
        P(None, None, "tp"),
        P(),
        P("tp", ("ctx", "fsdp")),
        P(),
        P(("ctx", "fsdp"), "tp"),
        P(("ctx", "fsdp"), "tp"),
        P("tp", ("ctx", "fsdp")),
        P("fsdp", "ctx", None),
    )
    return jax.shard_map(
        local,
        mesh=mesh,
        in_specs=placed,
        out_specs=(
            P("fsdp", "ctx", None),
            P("fsdp", "ctx", None),
            P(),
            P(("ctx", "fsdp"), "tp"),
            P(("ctx", "fsdp"), "tp"),
            P(("ctx", "fsdp"), "tp"),
            P(("ctx", "fsdp"), "tp"),
            P("tp"),
            P(None, None, "tp"),
            P(),
            P("tp", ("ctx", "fsdp")),
            P(),
            P(("ctx", "fsdp"), "tp"),
            P(("ctx", "fsdp"), "tp"),
            P("tp", ("ctx", "fsdp")),
        ),
        check_vma=False,
    )
```

```python
import functools
import math
import jax
import jax.numpy as jnp
from jax import lax
from jax.experimental import pallas as pl
from jax.experimental.pallas import tpu as pltpu
from jax.sharding import PartitionSpec as P

LANES = 128
CHUNK = 128
HALO = 8
EPSILON = 1e-06
HEAD_FLOOR = 0.01
VMEM_BYTES = 60 * 1024 * 1024


def low(value):
    return value.astype(jnp.bfloat16)


def mul_nn(left, right):
    return lax.dot_general(low(left), low(right), (((1,), (0,)), ((), ())), preferred_element_type=jnp.float32)


def mul_nt(left, right):
    return lax.dot_general(low(left), low(right), (((1,), (1,)), ((), ())), preferred_element_type=jnp.float32)


def mul_tn(left, right):
    return lax.dot_general(low(left), low(right), (((0,), (0,)), ((), ())), preferred_element_type=jnp.float32)


def iota(shape, axis):
    return lax.broadcasted_iota(jnp.int32, shape, axis)


def chunk_masks(col, row, first):
    size = col.shape[0]
    same = col == row
    order, other = iota((size, size), 0), iota((size, size), 1)
    upto = same & (order >= other)
    below = same & (order > other)
    carried = (col < first).astype(jnp.float32)
    last = (col == row[:, size - 1 :]).astype(jnp.float32)
    keep = (row[:, size - 1 :] < first).astype(jnp.float32)
    return upto, below, carried, last, keep


def invert_units(systems):
    size = systems[0].shape[0]
    order, other = iota((size, size), 0), iota((size, size), 1)
    identity = (order == other).astype(jnp.float32)
    span = 1
    found = None
    while span < size:
        pair = (order // (2 * span) == other // (2 * span)) & (order // span != other // span)
        parts = [jnp.where(pair, system, 0.0) for system in systems]
        if found is None:
            found = [identity - part for part in parts]
        else:
            right = [mul_nn(part, value) for part, value in zip(parts, found)]
            found = [value - mul_nn(value, part) for value, part in zip(found, right)]
        span *= 2
    return found


def conv_rows(ext, conv, col, offset, size, lane, taps):
    total = None
    moved = []
    position = iota((size, 1), 0) + offset
    for tap in range(taps):
        back = taps - 1 - tap
        values = ext[pl.ds(HALO + offset - back, size), lane : lane + LANES]
        values = jnp.where(position - back >= col, values, 0.0)
        moved.append(values)
        term = conv[tap : tap + 1, lane : lane + LANES] * values
        total = term if total is None else total + term
    return total, moved


def unit(values):
    return values * lax.rsqrt(jnp.sum(values * values, axis=-1, keepdims=True) + EPSILON)


def head_column(values, head):
    return jnp.sum(jnp.where(iota(values.shape, 1) == head, values, 0.0), axis=-1, keepdims=True)


def forward_kernel(taps, heads, first, pre, beta, bias, halo, conv, col_ref, row_ref, own, carry, final, inv, upd, states, ext):
    length = pre.shape[0]
    ext[:HALO] = halo[0]
    ext[HALO:] = pre[...]
    head = first + pl.program_id(1) * heads
    jobs = [(i, j) for j in range(length // CHUNK) for i in range(heads)]
    data = {}
    for j in range(length // CHUNK):
        rows = pl.ds(j * CHUNK, CHUNK)
        col, row = col_ref[0, rows], row_ref[0, :, rows]
        masks = chunk_masks(col, row, j * CHUNK)
        strengths = jax.nn.sigmoid(beta[rows] + bias[...])
        for i in range(heads):
            acts = []
            for kind in range(3):
                total, _ = conv_rows(ext, conv, col, j * CHUNK, CHUNK, (3 * i + kind) * LANES, taps)
                acts.append(total * jax.nn.sigmoid(total))
            query, key, value = unit(acts[0]), unit(acts[1]), acts[2]
            strength = head_column(strengths, head + i)
            grams = mul_nt(jnp.concatenate([low(key), low(query)], axis=0), key)
            system = jnp.where(masks[1], strength * grams[:CHUNK], 0.0)
            scores = low(jnp.where(masks[0], grams[CHUNK:], 0.0))
            data[i, j] = (low(query), low(key), value, strength, scores, masks, system)
    inverses = dict(zip(jobs, invert_units([data[job][6] for job in jobs])))
    for i in range(heads):
        state = jnp.concatenate(
            [
                jnp.zeros((LANES, LANES), jnp.float32),
                (iota((LANES, LANES), 0) == iota((LANES, LANES), 1)).astype(jnp.float32),
            ],
            axis=1,
        )
        final[0, i] = state
    for j in range(length // CHUNK):
        rows = pl.ds(j * CHUNK, CHUNK)
        for i in range(heads):
            query, key, value, strength, scores, masks, _ = data[i, j]
            _, _, carried, last, keep = masks
            inverse = low(inverses[i, j])
            state = final[0, i]
            state_low = low(state)
            read = mul_nn(jnp.concatenate([key, query], axis=0), state_low)
            wide = jnp.concatenate([value, jnp.zeros_like(value)], axis=1)
            targets = strength * (wide - carried * read[:CHUNK])
            update = low(mul_nn(inverse, targets))
            result = carried * read[CHUNK:] + mul_nn(scores, update)
            final[0, i] = keep * state + mul_tn(key * low(last), update)
            lanes = slice(i * LANES, (i + 1) * LANES)
            own[rows, lanes] = result[:, :LANES]
            carry[rows, lanes] = low(result[:, LANES:])
            inv[0, i, j] = inverse
            upd[0, i, j] = update
            states[0, i, j] = state_low


def mixer_forward(pre, logit, bias, halo, conv, col, row, taps, first, heads_here, group):
    seqs, length = col.shape[0], col.shape[1]
    steps = heads_here // group
    chunks = length // CHUNK
    wide = 3 * LANES * group
    rows = seqs * length

    def tile(*tail, kind):
        return jax.ShapeDtypeStruct((seqs, heads_here) + tail, kind)

    def spec(*tail):
        return pl.BlockSpec((1, group) + tail, lambda s, h: (s, h) + (0,) * len(tail))

    flat = pl.BlockSpec((length, LANES * group), lambda s, h: (s, h))
    last = logit.shape[1] // LANES - 1
    return pl.pallas_call(
        functools.partial(forward_kernel, taps, group, first),
        grid=(seqs, steps),
        in_specs=[
            pl.BlockSpec((length, wide), lambda s, h: (s, h)),
            pl.BlockSpec((length, LANES), lambda s, h: (s, last)),
            pl.BlockSpec((1, LANES), lambda s, h: (0, 0)),
            pl.BlockSpec((1, HALO, wide), lambda s, h: (s, 0, h)),
            pl.BlockSpec((conv.shape[0], wide), lambda s, h: (0, h)),
            pl.BlockSpec((1, length, 1), lambda s, h: (s, 0, 0)),
            pl.BlockSpec((1, 1, length), lambda s, h: (s, 0, 0)),
        ],
        out_specs=[
            flat,
            flat,
            spec(LANES, 2 * LANES),
            spec(chunks, CHUNK, CHUNK),
            spec(chunks, CHUNK, 2 * LANES),
            spec(chunks, LANES, 2 * LANES),
        ],
        out_shape=[
            jax.ShapeDtypeStruct((rows, heads_here * LANES), jnp.float32),
            jax.ShapeDtypeStruct((rows, heads_here * LANES), jnp.bfloat16),
            tile(LANES, 2 * LANES, kind=jnp.float32),
            tile(chunks, CHUNK, CHUNK, kind=jnp.bfloat16),
            tile(chunks, CHUNK, 2 * LANES, kind=jnp.bfloat16),
            tile(chunks, LANES, 2 * LANES, kind=jnp.bfloat16),
        ],
        scratch_shapes=[pltpu.VMEM((length + HALO, wide), jnp.float32)],
        compiler_params=pltpu.CompilerParams(vmem_limit_bytes=VMEM_BYTES),
        cost_estimate=pl.CostEstimate(
            flops=60 * rows * heads_here * CHUNK * LANES, bytes_accessed=40 * rows * heads_here * LANES, transcendentals=0
        ),
    )(pre, logit, bias, halo, conv, col, row)


def backward_kernel(
    taps, heads, first, pre, beta, bias, halo, conv, col_ref, row_ref, grad_ref, inv, upd, states, start, end,
    grad_pre, tail, before, conv_grad, logits, ext, grad_ext,
):
    length = pre.shape[0]
    step = pl.program_id(1)
    head = first + step * heads
    ext[:HALO] = halo[0]
    ext[HALO:] = pre[...]
    grad_ext[...] = jnp.zeros_like(grad_ext)

    @pl.when(step == 0)
    def _():
        logits[...] = jnp.zeros_like(logits)

    grad_states = [end[0, i] for i in range(heads)]
    entry = [low(start[0, i]) for i in range(heads)]
    tap_sums = {}
    for j in reversed(range(length // CHUNK)):
        offset = j * CHUNK
        rows = pl.ds(offset, CHUNK)
        col, row = col_ref[0, rows], row_ref[0, :, rows]
        upto, below, carried, last, keep = chunk_masks(col, row, offset)
        strengths = jax.nn.sigmoid(beta[rows] + bias[...])
        grad_logit = jnp.zeros((CHUNK, LANES), jnp.float32)
        for i in range(heads):
            raw, taps_in = [], []
            for kind in range(3):
                total, moved = conv_rows(ext, conv, col, offset, CHUNK, (3 * i + kind) * LANES, taps)
                raw.append(total)
                taps_in.append(moved)
            gates = [jax.nn.sigmoid(total) for total in raw]
            acts = [total * gate for total, gate in zip(raw, gates)]
            scales = [lax.rsqrt(jnp.sum(act * act, axis=-1, keepdims=True) + EPSILON) for act in acts[:2]]
            query, key, value = acts[0] * scales[0], acts[1] * scales[1], acts[2]
            strength = head_column(strengths, head + i)
            lanes = slice(i * LANES, (i + 1) * LANES)
            query_low, key_low = low(query), low(key)
            grams = mul_nt(jnp.concatenate([key_low, query_low], axis=0), key_low)
            gram = jnp.where(below, grams[:CHUNK], 0.0)
            scores = jnp.where(upto, grams[CHUNK:], 0.0)
            inverse = inv[0, i, j]
            update = upd[0, i, j]
            update = low(update[:, :LANES].astype(jnp.float32) + mul_nn(update[:, LANES:], entry[i]))
            state = states[0, i, j]
            state = low(state[:, :LANES].astype(jnp.float32) + mul_nn(state[:, LANES:], entry[i]))
            grad_out = grad_ref[rows, lanes]
            grad_state = grad_states[i]
            grad_state_low = low(grad_state)
            key_last = key_low * low(last)
            grad_update = mul_tn(scores, grad_out) + mul_nn(key_last, grad_state_low)
            grad_target = mul_tn(inverse, grad_update)
            weighted = strength * grad_target
            passed = carried * weighted
            out_carried = carried * grad_out.astype(jnp.float32)
            query_carried = query_low * low(carried)
            grad_states[i] = (
                keep * grad_state + mul_tn(query_carried, grad_out) - mul_tn(key_low, passed)
            )
            grad_scores = jnp.where(upto, mul_nt(grad_out, update), 0.0)
            grad_system = jnp.where(below, mul_nt(grad_target, update), 0.0)
            remainder = value - carried * mul_nn(key_low, state)
            grad_strength = jnp.sum(grad_target * remainder - grad_system * gram, axis=-1, keepdims=True)
            scaled = strength * grad_system
            from_state = mul_nt(jnp.concatenate([low(out_carried), low(passed)], axis=0), state)
            from_keys = mul_nn(jnp.concatenate([low(grad_scores), low(scaled + scaled.T)], axis=0), key_low)
            grad_query = from_state[:CHUNK] + from_keys[:CHUNK]
            grad_key = (
                mul_tn(grad_scores, query_low)
                + last * mul_nt(update, grad_state_low)
                - from_state[CHUNK:]
                - from_keys[CHUNK:]
            )
            grad_logit = grad_logit + jnp.where(
                iota((CHUNK, LANES), 1) == head + i, grad_strength * strength * (1.0 - strength), 0.0
            )
            grads = [
                scales[0] * (grad_query - query * jnp.sum(grad_query * query, axis=-1, keepdims=True)),
                scales[1] * (grad_key - key * jnp.sum(grad_key * key, axis=-1, keepdims=True)),
                weighted,
            ]
            position = iota((CHUNK, 1), 0) + offset
            for kind in range(3):
                gate, total = gates[kind], raw[kind]
                grad_conv = grads[kind] * gate * (1.0 + total * (1.0 - gate))
                lane = (3 * i + kind) * LANES
                for tap in range(taps):
                    back = taps - 1 - tap
                    part = jnp.sum(grad_conv * taps_in[kind][tap], axis=0, keepdims=True)
                    spot = (i, kind, tap)
                    tap_sums[spot] = part if spot not in tap_sums else tap_sums[spot] + part
                    back_part = jnp.where(
                        position - back >= col, grad_conv * conv[tap : tap + 1, lane : lane + LANES], 0.0
                    )
                    where = pl.ds(HALO + offset - back, CHUNK)
                    grad_ext[where, lane : lane + LANES] += back_part
        logits[rows] += grad_logit
    grad_pre[...] = low(grad_ext[HALO:])
    before[0] = grad_ext[:HALO]
    tail[0] = grad_ext[length:]
    for i in range(heads):
        for kind in range(3):
            lane = (3 * i + kind) * LANES
            for tap in range(taps):
                conv_grad[0, tap : tap + 1, lane : lane + LANES] = tap_sums[i, kind, tap]


def mixer_backward(
    pre, logit, bias, halo, conv, col, row, grad_mixed, inv, upd, states, start, end, taps, first, heads_here, group
):
    seqs, length = col.shape[0], col.shape[1]
    steps = heads_here // group
    chunks = length // CHUNK
    wide = 3 * LANES * group
    rows = seqs * length

    def spec(*tail):
        return pl.BlockSpec((1, group) + tail, lambda s, h: (s, h) + (0,) * len(tail))

    last = logit.shape[1] // LANES - 1
    part = pl.BlockSpec((1, HALO, wide), lambda s, h: (s, 0, h))
    edge = jax.ShapeDtypeStruct((seqs, HALO, 3 * LANES * heads_here), jnp.float32)
    return pl.pallas_call(
        functools.partial(backward_kernel, taps, group, first),
        grid=(seqs, steps),
        in_specs=[
            pl.BlockSpec((length, wide), lambda s, h: (s, h)),
            pl.BlockSpec((length, LANES), lambda s, h: (s, last)),
            pl.BlockSpec((1, LANES), lambda s, h: (0, 0)),
            part,
            pl.BlockSpec((conv.shape[0], wide), lambda s, h: (0, h)),
            pl.BlockSpec((1, length, 1), lambda s, h: (s, 0, 0)),
            pl.BlockSpec((1, 1, length), lambda s, h: (s, 0, 0)),
            pl.BlockSpec((length, LANES * group), lambda s, h: (s, h)),
            spec(chunks, CHUNK, CHUNK),
            spec(chunks, CHUNK, 2 * LANES),
            spec(chunks, LANES, 2 * LANES),
            spec(LANES, LANES),
            spec(LANES, LANES),
        ],
        out_specs=[
            pl.BlockSpec((length, wide), lambda s, h: (s, h)),
            part,
            part,
            part,
            pl.BlockSpec((length, LANES), lambda s, h: (s, 0)),
        ],
        out_shape=[
            jax.ShapeDtypeStruct((rows, 3 * LANES * heads_here), jnp.bfloat16),
            edge,
            edge,
            edge,
            jax.ShapeDtypeStruct((rows, LANES), jnp.float32),
        ],
        scratch_shapes=[
            pltpu.VMEM((length + HALO, wide), jnp.float32),
            pltpu.VMEM((length + HALO, wide), jnp.float32),
        ],
        compiler_params=pltpu.CompilerParams(vmem_limit_bytes=VMEM_BYTES),
        cost_estimate=pl.CostEstimate(
            flops=60 * rows * heads_here * CHUNK * LANES, bytes_accessed=40 * rows * heads_here * LANES, transcendentals=0
        ),
    )(pre, logit, bias, halo, conv, col, row, grad_mixed, inv, upd, states, start, end)


def mixed_rows_of(own, carry, start):
    return own + mul_nn(carry, start)


def output_kernel(heads, own, carry, start, gain, out):
    for i in range(heads):
        lanes = slice(i * LANES, (i + 1) * LANES)
        mixed = mixed_rows_of(own[:, lanes], carry[:, lanes], start[0, i])
        scale = lax.rsqrt(jnp.mean(mixed * mixed, axis=-1, keepdims=True) + HEAD_FLOOR)
        out[:, lanes] = low(mixed * scale * gain[...])


def output_backward_kernel(heads, own, carry, start, gain, grad, out, across, gain_grad):
    total = jnp.zeros((1, LANES), jnp.float32)
    for i in range(heads):
        lanes = slice(i * LANES, (i + 1) * LANES)
        carried = carry[:, lanes]
        mixed = mixed_rows_of(own[:, lanes], carried, start[0, i])
        scale = lax.rsqrt(jnp.mean(mixed * mixed, axis=-1, keepdims=True) + HEAD_FLOOR)
        normed = mixed * scale
        upper = grad[:, lanes].astype(jnp.float32)
        total = total + jnp.sum(upper * normed, axis=0, keepdims=True)
        weighted = upper * gain[...]
        back = scale * (weighted - normed * jnp.mean(weighted * normed, axis=-1, keepdims=True))
        out[:, lanes] = low(back)
        across[0, i] = mul_tn(carried, back)
    gain_grad[0, 0] = total


def mixer_output(own, carry, start, gain, group):
    seqs, heads_here = start.shape[:2]
    rows = own.shape[0]
    length = rows // seqs
    flat = pl.BlockSpec((length, LANES * group), lambda s, h: (s, h))
    square = pl.BlockSpec((1, group, LANES, LANES), lambda s, h: (s, h, 0, 0))
    return pl.pallas_call(
        functools.partial(output_kernel, group),
        grid=(seqs, heads_here // group),
        in_specs=[flat, flat, square, pl.BlockSpec((1, LANES), lambda s, h: (0, 0))],
        out_specs=flat,
        out_shape=jax.ShapeDtypeStruct(own.shape, jnp.bfloat16),
        compiler_params=pltpu.CompilerParams(vmem_limit_bytes=VMEM_BYTES),
        cost_estimate=pl.CostEstimate(
            flops=2 * own.size * LANES, bytes_accessed=8 * own.size, transcendentals=0
        ),
    )(own, carry, start, gain)


def mixer_output_backward(own, carry, start, gain, grad, first, group):
    seqs, heads_here = start.shape[:2]
    rows = own.shape[0]
    length = rows // seqs
    steps = heads_here // group
    flat = pl.BlockSpec((length, LANES * group), lambda s, h: (s, h))
    base = first // group
    shifted = pl.BlockSpec((length, LANES * group), lambda s, h: (s, base + h))
    square = pl.BlockSpec((1, group, LANES, LANES), lambda s, h: (s, h, 0, 0))
    return pl.pallas_call(
        functools.partial(output_backward_kernel, group),
        grid=(seqs, steps),
        in_specs=[flat, flat, square, pl.BlockSpec((1, LANES), lambda s, h: (0, 0)), shifted],
        out_specs=[flat, square, pl.BlockSpec((1, 1, 1, LANES), lambda s, h: (s, h, 0, 0))],
        out_shape=[
            jax.ShapeDtypeStruct(own.shape, jnp.bfloat16),
            jax.ShapeDtypeStruct(start.shape, jnp.float32),
            jax.ShapeDtypeStruct((seqs, steps, 1, LANES), jnp.float32),
        ],
        compiler_params=pltpu.CompilerParams(vmem_limit_bytes=VMEM_BYTES),
        cost_estimate=pl.CostEstimate(
            flops=4 * own.size * LANES, bytes_accessed=12 * own.size, transcendentals=0
        ),
    )(own, carry, start, gain, grad)


def ffn_kernel(mine, other, mine_grads, other_grads, gate_w, up_w, down_w, *outs):
    rows = jnp.concatenate([mine[...], other[...]], axis=0)
    grads = jnp.concatenate([mine_grads[...], other_grads[...]], axis=0)
    half = mine.shape[0]
    gate = mul_nt(rows, gate_w[...])
    up = mul_nt(rows, up_w[...])
    grad_hidden = mul_nt(grads, down_w[...])
    sigmoid = jax.nn.sigmoid(gate)
    active = gate * sigmoid
    kept = low(active * up)
    back_gate = low(grad_hidden * up * sigmoid * (1.0 + gate * (1.0 - sigmoid)))
    back_up = low(grad_hidden * active)
    grad_rows = low(mul_nn(back_gate, gate_w[...]) + mul_nn(back_up, up_w[...]))
    result = low(mul_nn(kept, down_w[...]))
    for side in range(2):
        here = slice(side * half, (side + 1) * half)
        acts, grad_out, result_out = outs[3 * side : 3 * side + 3]
        for kind, value in enumerate((back_gate, back_up, kept)):
            acts[kind] = value[here]
        grad_out[...] = grad_rows[here]
        result_out[...] = result[here]


def ffn_both(rows, grads, gate_up, down):
    count, width = rows[0].shape
    units = down.shape[0]
    tile = min(256, count)
    wide_rows = pl.BlockSpec((tile, width), lambda i: (i, 0))
    narrow = pl.BlockSpec((3, tile, units), lambda i: (0, i, 0))

    def third(index):
        return pl.BlockSpec((units, width), lambda i: (index, 0))

    flat = jax.ShapeDtypeStruct((count, width), jnp.bfloat16)
    outs = pl.pallas_call(
        ffn_kernel,
        grid=(count // tile,),
        in_specs=[wide_rows] * 4 + [third(0), third(1), third(0)],
        out_specs=[narrow, wide_rows, wide_rows] * 2,
        out_shape=[jax.ShapeDtypeStruct((3, count, units), jnp.bfloat16), flat, flat] * 2,
        compiler_params=pltpu.CompilerParams(vmem_limit_bytes=VMEM_BYTES),
        cost_estimate=pl.CostEstimate(
            flops=24 * count * width * units, bytes_accessed=16 * count * width + 6 * units * width, transcendentals=0
        ),
    )(*rows, *grads, gate_up, gate_up, down)
    return outs[:3], outs[3:]


def ffn_weights_kernel(count, lines, *refs):
    acts, rows, grads = refs[:count], refs[count : 2 * count], refs[2 * count : 3 * count]
    out, total = refs[-2:]
    part = out.shape[-1]

    def add(sources):
        for i in range(count):
            value = mul_tn(acts[i][0], sources[i][...])
            if i == 0:
                total[...] = value
            else:
                total[...] += value

    @pl.when(pl.program_id(0) < 2)
    def _():
        add(rows)

    @pl.when(pl.program_id(0) == 2)
    def _():
        add(grads)

    for line in range(lines):
        out[line, 0] = low(total[:, line * part : (line + 1) * part])


def ffn_weights(acts, rows, grads, lines, squares):
    count, width = len(acts), rows[0].shape[1]
    size, units = acts[0].shape[1:]
    block = width // squares
    part = block // lines
    act_spec = pl.BlockSpec((1, size, units), lambda k, c: (k, 0, 0))
    row_spec = pl.BlockSpec((size, block), lambda k, c: (0, jnp.where(k < 2, c, squares - 1)))
    grad_spec = pl.BlockSpec((size, block), lambda k, c: (0, jnp.where(k < 2, 0, c)))
    return pl.pallas_call(
        functools.partial(ffn_weights_kernel, count, lines),
        grid=(3, squares),
        in_specs=[act_spec] * count + [row_spec] * count + [grad_spec] * count,
        out_specs=pl.BlockSpec((lines, 1, units, part), lambda k, c: (0, k, 0, c)),
        out_shape=jax.ShapeDtypeStruct((lines, 3, units, squares * part), jnp.bfloat16),
        scratch_shapes=[pltpu.VMEM((units, block), jnp.float32)],
        compiler_params=pltpu.CompilerParams(vmem_limit_bytes=VMEM_BYTES),
        cost_estimate=pl.CostEstimate(
            flops=6 * count * size * width * units, bytes_accessed=8 * count * size * width, transcendentals=0
        ),
    )(*acts, *rows, *grads)


def block_columns(place, bit, size):
    return pl.multiple_of((place[0] ^ bit) * size, size)


def gathered_kernel(place, rows, *refs):
    out = refs[-1]
    own, beside, across, upper, lower = refs[:-1]
    size, half = own.shape[0], upper.shape[0]
    total = None
    for bit, skip, ref in ((0, 0, own), (1, 0, beside), (2, 0, across), (3, 0, upper), (3, half, lower)):
        start = pl.multiple_of(block_columns(place, bit, size) + skip, half)
        value = mul_nn(rows[:, pl.ds(start, ref.shape[0])], ref[...])
        total = value if total is None else total + value
    out[...] = total


def gathered_times(rows, place, pieces):
    count, width = rows.shape
    columns = pieces[0].shape[1]
    tile = min(256, count)
    whole = [pl.BlockSpec(piece.shape, lambda i, place: (0, 0)) for piece in pieces]
    return pl.pallas_call(
        gathered_kernel,
        grid_spec=pltpu.PrefetchScalarGridSpec(
            num_scalar_prefetch=1,
            grid=(count // tile,),
            in_specs=[pl.BlockSpec((tile, width), lambda i, place: (i, 0))] + whole,
            out_specs=pl.BlockSpec((tile, columns), lambda i, place: (i, 0)),
        ),
        out_shape=jax.ShapeDtypeStruct((count, columns), jnp.float32),
        compiler_params=pltpu.CompilerParams(vmem_limit_bytes=VMEM_BYTES),
        cost_estimate=pl.CostEstimate(
            flops=2 * count * width * columns, bytes_accessed=2 * (count + columns) * width, transcendentals=0
        ),
    )(jnp.reshape(place, (1,)).astype(jnp.int32), rows, *pieces)


def gathered_transposed_kernel(count, place, *refs):
    factors, pieces, out = refs[:count], refs[count:-1], refs[-1]
    size, half = pieces[0].shape[0], pieces[3].shape[0]
    for i, (bit, skip) in enumerate(((0, 0), (1, 0), (2, 0), (3, 0), (3, half))):
        start = pl.multiple_of(block_columns(place, bit, size) + skip, half)
        total = None
        for p in range(count):
            value = mul_nt(factors[p][...], pieces[5 * p + i][...])
            total = value if total is None else total + value
        out[:, pl.ds(start, pieces[i].shape[0])] = low(total)


def gathered_times_transposed(factors, place, pieces):
    count, rows = len(factors), factors[0].shape[0]
    width = 4 * pieces[0][0].shape[0]
    tile = min(256, rows)
    flat = [piece for some in pieces for piece in some]
    whole = [pl.BlockSpec(piece.shape, lambda i, place: (0, 0)) for piece in flat]
    wides = [pl.BlockSpec((tile, factor.shape[1]), lambda i, place: (i, 0)) for factor in factors]
    columns = sum(factor.shape[1] for factor in factors)
    return pl.pallas_call(
        functools.partial(gathered_transposed_kernel, count),
        grid_spec=pltpu.PrefetchScalarGridSpec(
            num_scalar_prefetch=1,
            grid=(rows // tile,),
            in_specs=wides + whole,
            out_specs=pl.BlockSpec((tile, width), lambda i, place: (i, 0)),
        ),
        out_shape=jax.ShapeDtypeStruct((rows, width), jnp.bfloat16),
        compiler_params=pltpu.CompilerParams(vmem_limit_bytes=VMEM_BYTES),
        cost_estimate=pl.CostEstimate(
            flops=2 * rows * width * columns, bytes_accessed=2 * (rows + columns) * width, transcendentals=0
        ),
    )(jnp.reshape(place, (1,)).astype(jnp.int32), *factors, *flat)


def join_kernel(squares, source, target):
    lines, _, columns = source.shape
    part = columns // squares
    for i in range(lines):
        for j in range(squares):
            at = (j * lines + i) * part
            target[:, at : at + part] = source[i, :, j * part : (j + 1) * part]


def columns_join(parts, squares):
    lines, rows, columns = parts.shape
    tile = 176 if rows % 176 == 0 else rows
    return pl.pallas_call(
        functools.partial(join_kernel, squares),
        grid=(rows // tile,),
        in_specs=[pl.BlockSpec((lines, tile, columns), lambda i: (0, i, 0))],
        out_specs=pl.BlockSpec((tile, lines * columns), lambda i: (i, 0)),
        out_shape=jax.ShapeDtypeStruct((rows, lines * columns), parts.dtype),
        compiler_params=pltpu.CompilerParams(vmem_limit_bytes=VMEM_BYTES),
        cost_estimate=pl.CostEstimate(flops=0, bytes_accessed=4 * parts.size, transcendentals=0),
    )(parts)


def flip(value, axis, bit):
    devices = range(lax.axis_size(axis))
    return lax.ppermute(value, axis, [(i, i ^ bit) for i in devices])


def shift(value, axis, distance):
    count = lax.axis_size(axis)
    return lax.ppermute(value, axis, [(i, (i + distance) % count) for i in range(count)])


def from_behind(block, axis, distance):
    devices = range(lax.axis_size(axis))
    route = [(i - distance, i) for i in devices if i - distance in devices]
    return lax.ppermute(block, axis, route)


def tie(value, *earlier):
    return lax.optimization_barrier((value,) + earlier)[0]


def put(buffer, piece, *start):
    return lax.dynamic_update_slice(buffer, piece, start)


def wide(value):
    return value.astype(jnp.float32)


def gather_line(shard):
    count, place = lax.axis_size("fsdp"), lax.axis_index("fsdp")
    pieces = [shard] + [shift(shard, "fsdp", d) for d in range(1, count)]
    order = [(place - i) % count for i in range(count)]
    return jnp.concatenate([lax.select_n(which, *pieces) for which in order], axis=0)


class Square:
    def __init__(self, own):
        self.own = own
        self.half = own.shape[0] // 2
        self.beside = flip(own, "ctx", 1)
        self.across = flip(own, "ctx", 2)

    def forward(self, *earlier):
        upper = self.beside[: self.half]
        lower = self.across[self.half :]
        if earlier:
            upper, lower = lax.optimization_barrier((upper, lower) + earlier)[:2]
        self.upper = flip(upper, "ctx", 2)
        self.lower = flip(lower, "ctx", 1)
        return self

    def done(self):
        return (self.upper, self.lower)

    def pieces(self):
        return [self.own, self.beside, self.across, self.upper, self.lower]

    def far(self):
        return jnp.concatenate([self.upper, self.lower], axis=0)


def both_sides(rows):
    if lax.axis_size("tp") == 2:
        return rows, flip(rows, "tp", 1)
    every = lax.all_gather(rows, "tp", axis=0, tiled=True)
    half = every.shape[0] // 2
    return every[:half], every[half:]


def core_sum(mine, other):
    if lax.axis_size("tp") == 2:
        return wide(mine) + wide(flip(other, "tp", 1))
    both = jnp.concatenate([mine, other], axis=0)
    return wide(lax.psum_scatter(both, "tp", scatter_dimension=0, tiled=True))


def neighbour_columns(rows):
    width = rows.shape[1] // 4
    place = lax.axis_index("ctx")
    return [lax.dynamic_slice_in_dim(rows, (place ^ bit) * width, width, 1) for bit in range(4)]


class Line:
    def __init__(self, own):
        count, place = lax.axis_size("fsdp"), lax.axis_index("fsdp")
        own = own.reshape(count, own.shape[0] // count, own.shape[1])

        def part(distance):
            return lax.dynamic_index_in_dim(own, (place + distance) % count, 0, keepdims=False)

        self.kept = part(0)
        self.sent = [low(part(distance)) for distance in range(1, count)]
        self.arrived = [shift(piece, "fsdp", distance + 1) for distance, piece in enumerate(self.sent)]

    def total(self, *late):
        total = self.kept
        for part in lax.optimization_barrier(tuple(self.arrived) + late)[: len(self.arrived)]:
            total = total + wide(part)
        return total


class Scatter:
    def __init__(self, columns, grads):
        self.columns, self.grads = columns, grads
        self.half = columns[0].shape[1] // 2
        beside, across = (
            jnp.concatenate([self.side(3, 1), self.side(1, 1)], axis=1),
            jnp.concatenate([self.side(3, 0), self.side(2, 0)], axis=1),
        )
        self.sent = [low(outer_rows(beside, grads)), low(outer_rows(across, grads))]
        self.first = (flip(self.sent[0], "ctx", 1), flip(self.sent[1], "ctx", 2))

    def side(self, bit, lower):
        return self.columns[bit][:, lower * self.half : (lower + 1) * self.half]

    def second(self, *earlier):
        first = self.first
        if earlier:
            first = lax.optimization_barrier(first + earlier)[:2]
        beside, across = (wide(part) for part in first)
        upper = low(outer_rows(self.side(1, 0), self.grads) + across[: self.half])
        lower = low(outer_rows(self.side(2, 1), self.grads) + beside[: self.half])
        self.last = (flip(upper, "ctx", 1), flip(lower, "ctx", 2))
        self.kept = (beside, across)
        return upper, lower

    def own(self, *ties):
        beside_upper, across_lower = self.last
        if ties:
            beside_upper, across_lower = lax.optimization_barrier(self.last + ties)[:2]
        beside, across = self.kept
        own = outer_rows(self.columns[0], self.grads)
        upper = own[: self.half] + wide(beside_upper) + across[self.half :]
        lower = own[self.half :] + beside[self.half :] + wide(across_lower)
        return jnp.concatenate([upper, lower], axis=0)


def butterfly(value, axes):
    for axis in axes:
        count, bit = lax.axis_size(axis), 1
        while bit < count:
            value = value + flip(value, axis, bit)
            bit *= 2
    return value


def rms_scale(values, floor_value):
    return lax.rsqrt(jnp.mean(values * values, axis=-1, keepdims=True) + floor_value)


def norm_backward(grad_normed, inputs, scale, gain):
    normed = inputs * scale
    weighted = grad_normed * gain
    return (
        scale * (weighted - normed * jnp.mean(weighted * normed, axis=-1, keepdims=True)),
        normed,
    )


def times(left, right):
    return jnp.dot(left, right, preferred_element_type=jnp.float32)


def times_transposed(left, right):
    return lax.dot_general(
        left, right, (((1,), (1,)), ((), ())), preferred_element_type=jnp.float32
    )


def outer_rows(left, right):
    return lax.dot_general(
        left, right, (((0,), (0,)), ((), ())), preferred_element_type=jnp.float32
    )


def rows_mine(rows):
    count = rows.shape[1] // lax.axis_size("tp")
    return lax.dynamic_slice_in_dim(rows, lax.axis_index("tp") * count, count, 1)


def rows_scatter(partial):
    if lax.axis_size("tp") != 2:
        return wide(lax.psum_scatter(partial, "tp", scatter_dimension=1, tiled=True))
    count = partial.shape[1] // 2
    other = lax.dynamic_slice_in_dim(partial, (1 - lax.axis_index("tp")) * count, count, 1)
    return wide(rows_mine(partial)) + wide(flip(other, "tp", 1))


def rows_full(mine):
    if lax.axis_size("tp") != 2:
        return lax.all_gather(mine, "tp", axis=1, tiled=True)
    other = flip(mine, "tp", 1)
    lower = lax.axis_index("tp") == 0
    return jnp.concatenate([jnp.where(lower, mine, other), jnp.where(lower, other, mine)], axis=1)


def by_head(parts):
    heads = range(parts[0].shape[-1] // LANES)
    return jnp.concatenate([part[..., h * LANES : (h + 1) * LANES] for h in heads for part in parts], axis=-1)


def by_kind(joined):
    return [
        jnp.concatenate(
            [
                some[..., at : at + LANES]
                for some in joined
                for at in range(kind * LANES, some.shape[-1], 3 * LANES)
            ],
            axis=-1,
        )
        for kind in range(3)
    ]


def pass_states(own, transfer, forward, *beside):
    rule = "shij,shjk->shik" if forward == 1 else "shji,shjk->shik"
    leaving = own
    entered = low(jnp.zeros_like(own))
    for repeat in range(lax.axis_size("ctx") - 1):
        entered = from_behind(low(leaving), "ctx", forward)
        if repeat == 0 and beside:
            entered = tie(entered, *beside)
        leaving = own + jnp.einsum(rule, transfer, entered, preferred_element_type=jnp.float32)
    return wide(entered)


def local(
    block_input,
    doc_start,
    gain_mix,
    query_weight,
    key_weight,
    value_weight,
    beta_weight,
    beta_bias,
    conv_weight,
    gain_o,
    out_weight,
    gain_ffn,
    gate_weight,
    up_weight,
    down_weight,
    out_grad,
):
    seq_count, local_len, width = block_input.shape
    row_count = seq_count * local_len
    heads_here = beta_weight.shape[1]
    taps = conv_weight.shape[1]
    parts = 2 if heads_here % 2 == 0 else 1
    part_heads = heads_here // parts
    group = 2 if part_heads % 2 == 0 else 1
    part_cols = 3 * part_heads * LANES
    spare = LANES - heads_here
    units_here = gate_weight.shape[1]
    shard_rows = gate_weight.shape[0]

    joined = by_head([low(query_weight), low(key_weight), low(value_weight)])
    shards = [joined[:, p * part_cols : (p + 1) * part_cols] for p in range(parts)]
    shards[0] = jnp.concatenate([shards[0], jnp.pad(low(beta_weight), ((0, 0), (0, spare)))], axis=1)
    shards.append(low(out_weight).T)
    lines = []
    for shard in shards[:parts]:
        lines.append(gather_line(tie(shard, lines[-1]) if lines else shard))
    units = units_here // 4
    pieces = jnp.stack([low(gate_weight).T, low(up_weight).T, low(down_weight)])
    pieces = pieces.reshape(3, 4, units, shard_rows).transpose(1, 0, 2, 3)
    ffn_swapped = lax.all_to_all(pieces.reshape(4, 3 * units, shard_rows), "ctx", 0, 0)
    ffn_line = ffn_swapped.transpose(1, 0, 2).reshape(3 * units, 4 * shard_rows)
    line_count = lax.axis_size("fsdp")

    ctx_place = lax.axis_index("ctx")
    first_pos = ctx_place * local_len
    starts = doc_start - first_pos
    col, row = starts[:, :, None], starts[:, None, :]
    conv = by_head([conv_weight[0], conv_weight[1], conv_weight[2]])
    bias = jnp.pad(beta_bias, (0, spare))[None]
    gain_head = gain_o[None]
    tokens = block_input.reshape(row_count, width)
    inputs = wide(tokens)
    normed_mix = low(inputs * rms_scale(inputs, EPSILON) * gain_mix)
    inputs_mine = wide(rows_mine(block_input).reshape(-1, width))
    grads_mine = rows_mine(out_grad).reshape(-1, width)

    square = Square(tie(lines[0], ffn_swapped)).forward(normed_mix)
    gate_up_parts = lax.all_gather(tie(ffn_line[: 2 * units], lines[parts - 1], *square.done()), "fsdp", axis=0)
    down_parts = lax.all_gather(ffn_line[2 * units :], "fsdp", axis=0)
    mix_full, kept, pre = [], [], []
    for p in range(parts):
        mix_full.append(square.pieces())
        arrived = square.done()
        ends = normed_mix.reshape(seq_count, local_len, width)[:, local_len - HALO :].reshape(seq_count * HALO, width)
        ends = gathered_times(ends, ctx_place, mix_full[p])
        ends = low(ends)
        square = Square(tie(lines[p + 1], ends, *arrived))
        halo = wide(from_behind(ends[:, :part_cols].reshape(seq_count, HALO, part_cols), "ctx", 1))
        pre.append(gathered_times(tie(normed_mix, ends), ctx_place, mix_full[p]))
        convs = conv[:, p * part_cols : (p + 1) * part_cols]
        kept.append(
            [halo, convs]
            + list(
                mixer_forward(
                    pre[p], pre[0], bias, halo, convs, col, row, taps, p * part_heads, part_heads, group
                )
            )
        )
        square.forward(kept[p][2])
        if p == 0:
            lines.append(gather_line(tie(shards[-1], kept[p][2], square.beside)))
            grad_square = Square(tie(grads_mine, kept[p][2], *square.done()))
    out_full = square.pieces()

    gate_up_full = columns_join(gate_up_parts, 4)
    finals = jnp.concatenate([some[4] for some in kept], axis=1)
    transfer = low(finals[..., LANES:])
    first = tie(finals[..., :LANES], gate_up_full, grad_square.beside, grad_square.across)
    entering = pass_states(first, transfer, 1)
    entered = [entering[:, p * part_heads : (p + 1) * part_heads] for p in range(parts)]
    grad_square.forward(entering)
    grad_rows = [both_sides(part) for part in (grad_square.own, grad_square.beside, grad_square.across)]
    mixed_rows = []
    for p in range(parts):
        own, carry = kept[p][2:4]
        mixed_rows.append(mixer_output(own, carry, entered[p], gain_head, group))
    mixed_rows = jnp.concatenate(mixed_rows, axis=1)
    mixed_rows = tie(mixed_rows, *(other for _, other in grad_rows))
    grad_rows.append(both_sides(grad_square.far()))

    branch = gathered_times_transposed([mixed_rows], ctx_place, [out_full]).reshape(seq_count, local_len, width)
    branch = tie(branch, down_parts)
    residual = inputs_mine + rows_scatter(branch).reshape(-1, width)
    scale_ffn = rms_scale(residual, EPSILON)
    square = Square(low(residual * scale_ffn * gain_ffn))
    ffn_full = (gate_up_full, columns_join(down_parts, 4))

    ffn_rows = [both_sides(square.own)]
    ffn_out = [ffn_both(ffn_rows[0], grad_rows[0], *ffn_full)]
    square.forward(ffn_out[0][0][0])
    ffn_rows.append(both_sides(tie(square.beside, ffn_out[0][0][0])))
    ffn_out.append(ffn_both(ffn_rows[1], grad_rows[1], *ffn_full))
    ffn_rows.append(both_sides(tie(square.across, ffn_out[0][0][0])))
    mine, other = ffn_rows[2]
    ffn_out.append(ffn_both((tie(mine, ffn_out[1][0][0], *square.done()), other), grad_rows[2], *ffn_full))
    beside_sums, across_sums = (low(core_sum(*(side[1] for side in ffn_out[bit]))) for bit in (1, 2))
    ffn_rows.append(both_sides(square.far()))
    mine, other = ffn_rows[3]
    ffn_out.append(ffn_both((tie(mine, beside_sums, across_sums), other), grad_rows[3], *ffn_full))
    near_sums = (flip(beside_sums, "ctx", 1), flip(across_sums, "ctx", 2))
    mine, other = (side[1] for side in ffn_out[3])
    far_sums = low(core_sum(mine, tie(other, *near_sums)))
    acts = [side[0] for outs in ffn_out for side in outs]
    own_sums = core_sum(*(side[1] for side in ffn_out[0]))
    result_low = [low(core_sum(*(side[2] for side in ffn_out[bit]))) for bit in (1, 2)]
    acts[0] = tie(acts[0], far_sums, own_sums, *result_low)
    far_sums = flip(far_sums, "ctx", 3)
    sums = ffn_weights(
        acts,
        [side for sides in ffn_rows for side in sides],
        [side for sides in grad_rows for side in sides],
        line_count,
        4,
    ).reshape(line_count, 3 * units, 4 * shard_rows)

    far_sums, sums = lax.optimization_barrier((far_sums, sums))
    result_near = [flip(tie(part, far_sums), "ctx", bit) for part, bit in zip(result_low, (1, 2))]
    grad_normed = own_sums + wide(near_sums[0]) + wide(near_sums[1]) + wide(far_sums)
    back_ffn, unit_ffn = norm_backward(grad_normed, residual, scale_ffn, gain_ffn)
    grad_residual = wide(grads_mine) + back_ffn
    gain_ffn_part = jnp.sum(grad_normed * unit_ffn, axis=0)
    grad_branch = rows_full(low(grad_residual).reshape(seq_count, -1, width)).reshape(row_count, width)
    grad_heads = gathered_times(grad_branch, ctx_place, out_full)
    backs, acrosses, gain_o_part = [], [], 0.0
    for p in range(parts):
        _, _, own, carry, _, _, _, _ = kept[p]
        back, across, gain_part = mixer_output_backward(
            own, carry, entered[p], gain_head, grad_heads, p * part_heads, group
        )
        backs.append(back)
        acrosses.append(across)
        gain_o_part = gain_o_part + jnp.sum(gain_part, axis=(0, 1, 2))
    grad_end = pass_states(jnp.concatenate(acrosses, axis=1), transfer, -1, *result_near)
    total = lax.psum_scatter(sums, "fsdp", scatter_dimension=0, tiled=True)

    out_grad_w = low(outer_rows(grad_branch, mixed_rows))
    out_part = out_grad_w
    out_grad_w = lax.psum_scatter(out_grad_w, ("ctx", "fsdp"), scatter_dimension=0, tiled=True)

    mine, other = (side[2] for side in ffn_out[0])
    result_own = core_sum(mine, tie(other, grad_branch))
    mine, other = (side[2] for side in ffn_out[3])
    result_far = flip(tie(low(core_sum(mine, tie(other, grad_branch))), grad_end), "ctx", 3)
    columns = neighbour_columns(normed_mix)
    grad_mixes, mix_grads, conv_parts = [None] * parts, [None] * parts, [None] * parts
    logits = 0.0
    scatter = None
    for p in reversed(range(parts)):
        halo, convs, own, carry, final, inverses, updates, states = kept[p]
        heads = slice(p * part_heads, (p + 1) * part_heads)
        back = tie(backs[p], out_part) if scatter is None else tie(backs[p], total, *scatter.sent)
        grad_mix, tail, before, conv_parts[p], logit = mixer_backward(
            pre[p], pre[0], bias, halo, convs, col, row, back, inverses, updates, states,
            entered[p], grad_end[:, heads], taps, p * part_heads, part_heads, group,
        )
        logits = logits + logit
        if scatter is None:
            result_far = tie(result_far, before)
        tail = low(tail + from_behind(before, "ctx", -1))
        grad_mix = put(grad_mix.reshape(seq_count, local_len, -1), tail, 0, local_len - HALO, 0)
        grad_mix = grad_mix.reshape(row_count, -1)
        if scatter is not None:
            scatter.second(before)
            earlier_scatter = scatter
        else:
            grad_mix = tie(grad_mix, result_far)
        if p == 0:
            grad_mix = jnp.concatenate([grad_mix, low(logits)], axis=1)
        grad_mixes[p] = grad_mix
        scatter = Scatter(columns, grad_mix)
    result = result_own + wide(result_near[0]) + wide(result_near[1])
    result = result + wide(result_far)
    block_output = rows_full(low(residual + result).reshape(seq_count, -1, width))
    ready = scatter.second(block_output)
    grad_mixes[0] = tie(grad_mixes[0], *ready)
    mix_back = tie(gathered_times_transposed(grad_mixes, ctx_place, mix_full), *scatter.last)
    mix_back = rows_scatter(mix_back.reshape(seq_count, local_len, width)).reshape(-1, width)
    back_mix, unit_mix = norm_backward(mix_back, inputs_mine, rms_scale(inputs_mine, EPSILON), gain_mix)
    input_grad = rows_full(low(grad_residual + back_mix).reshape(seq_count, -1, width))
    gain_mix_part = jnp.sum(mix_back * unit_mix, axis=0)

    conv_cols = jnp.concatenate([jnp.sum(part, axis=0)[:taps] for part in conv_parts], axis=1)
    gains = butterfly(jnp.concatenate([gain_mix_part, gain_ffn_part, gain_o_part]), ("tp",))
    sums = jnp.concatenate([gains, conv_cols.reshape(-1), jnp.sum(logits, axis=0)])
    for p in range(1, parts):
        own = low(earlier_scatter.own(*ready))
        mix_grads[p] = wide(lax.psum_scatter(own, "fsdp", scatter_dimension=0, tiled=True))
    last_line = Line(scatter.own())
    sums = butterfly(tie(sums, *last_line.sent), ("ctx", "fsdp"))
    mix_grads[0] = last_line.total(sums)
    query_grad, key_grad, value_grad = by_kind([grad[:, :part_cols] for grad in mix_grads])
    beta_grad = mix_grads[0][:, part_cols : part_cols + heads_here]
    ends = [width, 2 * width, 2 * width + LANES, sums.shape[0] - LANES]
    gain_mix_grad, gain_ffn_grad, gain_o_grad, conv_grad, bias_grad = jnp.split(sums, ends)
    conv_grad = jnp.stack(by_kind([conv_grad.reshape(taps, -1)]))
    bias_grad = bias_grad[:heads_here]
    out_grad_w = wide(tie(out_grad_w, *scatter.last)).T
    pieces = tie(total, *scatter.last).reshape(3 * units, 4, shard_rows).transpose(1, 0, 2)
    arrived = lax.all_to_all(pieces, "ctx", 0, 0).reshape(4, 3, units, shard_rows)
    gate_grad, up_grad, down_grad = (wide(arrived[:, i].reshape(units_here, shard_rows)) for i in range(3))

    return (
        block_output,
        input_grad,
        gain_mix_grad,
        query_grad,
        key_grad,
        value_grad,
        beta_grad,
        bias_grad,
        conv_grad,
        gain_o_grad,
        out_grad_w,
        gain_ffn_grad,
        gate_grad.T,
        up_grad.T,
        down_grad,
    )


def solution(mesh):
    placed = (
        P("fsdp", "ctx", None),
        P("fsdp", "ctx"),
        P(),
        P(("ctx", "fsdp"), "tp"),
        P(("ctx", "fsdp"), "tp"),
        P(("ctx", "fsdp"), "tp"),
        P(("ctx", "fsdp"), "tp"),
        P("tp"),
        P(None, None, "tp"),
        P(),
        P("tp", ("ctx", "fsdp")),
        P(),
        P(("ctx", "fsdp"), "tp"),
        P(("ctx", "fsdp"), "tp"),
        P("tp", ("ctx", "fsdp")),
        P("fsdp", "ctx", None),
    )
    return jax.shard_map(
        local,
        mesh=mesh,
        in_specs=placed,
        out_specs=(
            P("fsdp", "ctx", None),
            P("fsdp", "ctx", None),
            P(),
            P(("ctx", "fsdp"), "tp"),
            P(("ctx", "fsdp"), "tp"),
            P(("ctx", "fsdp"), "tp"),
            P(("ctx", "fsdp"), "tp"),
            P("tp"),
            P(None, None, "tp"),
            P(),
            P("tp", ("ctx", "fsdp")),
            P(),
            P(("ctx", "fsdp"), "tp"),
            P(("ctx", "fsdp"), "tp"),
            P("tp", ("ctx", "fsdp")),
        ),
        check_vma=False,
    )
```

```python
import functools
import math
import jax
import jax.numpy as jnp
from jax import lax
from jax.experimental import pallas as pl
from jax.experimental.pallas import tpu as pltpu
from jax.sharding import PartitionSpec as P

LANES = 128
CHUNK = 128
HALO = 8
EPSILON = 1e-06
HEAD_FLOOR = 0.01
VMEM_BYTES = 60 * 1024 * 1024


def low(value):
    return value.astype(jnp.bfloat16)


def mul_nn(left, right):
    return lax.dot_general(low(left), low(right), (((1,), (0,)), ((), ())), preferred_element_type=jnp.float32)


def mul_nt(left, right):
    return lax.dot_general(low(left), low(right), (((1,), (1,)), ((), ())), preferred_element_type=jnp.float32)


def mul_tn(left, right):
    return lax.dot_general(low(left), low(right), (((0,), (0,)), ((), ())), preferred_element_type=jnp.float32)


def iota(shape, axis):
    return lax.broadcasted_iota(jnp.int32, shape, axis)


def chunk_masks(col, row, first):
    size = col.shape[0]
    same = col == row
    order, other = iota((size, size), 0), iota((size, size), 1)
    upto = same & (order >= other)
    below = same & (order > other)
    carried = (col < first).astype(jnp.float32)
    last = (col == row[:, size - 1 :]).astype(jnp.float32)
    keep = (row[:, size - 1 :] < first).astype(jnp.float32)
    return upto, below, carried, last, keep


def invert_units(systems):
    size = systems[0].shape[0]
    order, other = iota((size, size), 0), iota((size, size), 1)
    identity = (order == other).astype(jnp.float32)
    span = 1
    found = None
    while span < size:
        pair = (order // (2 * span) == other // (2 * span)) & (order // span != other // span)
        parts = [jnp.where(pair, system, 0.0) for system in systems]
        if found is None:
            found = [identity - part for part in parts]
        else:
            right = [mul_nn(part, value) for part, value in zip(parts, found)]
            found = [value - mul_nn(value, part) for value, part in zip(found, right)]
        span *= 2
    return found


def conv_rows(ext, conv, col, offset, size, lane, taps):
    total = None
    moved = []
    position = iota((size, 1), 0) + offset
    for tap in range(taps):
        back = taps - 1 - tap
        values = ext[pl.ds(HALO + offset - back, size), lane : lane + LANES]
        values = jnp.where(position - back >= col, values, 0.0)
        moved.append(values)
        term = conv[tap : tap + 1, lane : lane + LANES] * values
        total = term if total is None else total + term
    return total, moved


def unit(values):
    return values * lax.rsqrt(jnp.sum(values * values, axis=-1, keepdims=True) + EPSILON)


def head_column(values, head):
    return jnp.sum(jnp.where(iota(values.shape, 1) == head, values, 0.0), axis=-1, keepdims=True)


def forward_kernel(taps, heads, first, pre, beta, bias, halo, conv, col_ref, row_ref, own, carry, final, inv, upd, states, ext):
    length = pre.shape[0]
    ext[:HALO] = halo[0]
    ext[HALO:] = pre[...]
    head = first + pl.program_id(1) * heads
    jobs = [(i, j) for j in range(length // CHUNK) for i in range(heads)]
    data = {}
    for j in range(length // CHUNK):
        rows = pl.ds(j * CHUNK, CHUNK)
        col, row = col_ref[0, rows], row_ref[0, :, rows]
        masks = chunk_masks(col, row, j * CHUNK)
        strengths = jax.nn.sigmoid(beta[rows] + bias[...])
        for i in range(heads):
            acts = []
            for kind in range(3):
                total, _ = conv_rows(ext, conv, col, j * CHUNK, CHUNK, (3 * i + kind) * LANES, taps)
                acts.append(total * jax.nn.sigmoid(total))
            query, key, value = unit(acts[0]), unit(acts[1]), acts[2]
            strength = head_column(strengths, head + i)
            grams = mul_nt(jnp.concatenate([low(key), low(query)], axis=0), key)
            system = jnp.where(masks[1], strength * grams[:CHUNK], 0.0)
            scores = low(jnp.where(masks[0], grams[CHUNK:], 0.0))
            data[i, j] = (low(query), low(key), value, strength, scores, masks, system)
    inverses = dict(zip(jobs, invert_units([data[job][6] for job in jobs])))
    for i in range(heads):
        state = jnp.concatenate(
            [
                jnp.zeros((LANES, LANES), jnp.float32),
                (iota((LANES, LANES), 0) == iota((LANES, LANES), 1)).astype(jnp.float32),
            ],
            axis=1,
        )
        final[0, i] = state
    for j in range(length // CHUNK):
        rows = pl.ds(j * CHUNK, CHUNK)
        for i in range(heads):
            query, key, value, strength, scores, masks, _ = data[i, j]
            _, _, carried, last, keep = masks
            inverse = low(inverses[i, j])
            state = final[0, i]
            state_low = low(state)
            read = mul_nn(jnp.concatenate([key, query], axis=0), state_low)
            wide = jnp.concatenate([value, jnp.zeros_like(value)], axis=1)
            targets = strength * (wide - carried * read[:CHUNK])
            update = low(mul_nn(inverse, targets))
            result = carried * read[CHUNK:] + mul_nn(scores, update)
            final[0, i] = keep * state + mul_tn(key * low(last), update)
            lanes = slice(i * LANES, (i + 1) * LANES)
            own[rows, lanes] = result[:, :LANES]
            carry[rows, lanes] = low(result[:, LANES:])
            inv[0, i, j] = inverse
            upd[0, i, j] = update
            states[0, i, j] = state_low


def mixer_forward(pre, logit, bias, halo, conv, col, row, taps, first, heads_here, group):
    seqs, length = col.shape[0], col.shape[1]
    steps = heads_here // group
    chunks = length // CHUNK
    wide = 3 * LANES * group
    rows = seqs * length

    def tile(*tail, kind):
        return jax.ShapeDtypeStruct((seqs, heads_here) + tail, kind)

    def spec(*tail):
        return pl.BlockSpec((1, group) + tail, lambda s, h: (s, h) + (0,) * len(tail))

    flat = pl.BlockSpec((length, LANES * group), lambda s, h: (s, h))
    last = logit.shape[1] // LANES - 1
    return pl.pallas_call(
        functools.partial(forward_kernel, taps, group, first),
        grid=(seqs, steps),
        in_specs=[
            pl.BlockSpec((length, wide), lambda s, h: (s, h)),
            pl.BlockSpec((length, LANES), lambda s, h: (s, last)),
            pl.BlockSpec((1, LANES), lambda s, h: (0, 0)),
            pl.BlockSpec((1, HALO, wide), lambda s, h: (s, 0, h)),
            pl.BlockSpec((conv.shape[0], wide), lambda s, h: (0, h)),
            pl.BlockSpec((1, length, 1), lambda s, h: (s, 0, 0)),
            pl.BlockSpec((1, 1, length), lambda s, h: (s, 0, 0)),
        ],
        out_specs=[
            flat,
            flat,
            spec(LANES, 2 * LANES),
            spec(chunks, CHUNK, CHUNK),
            spec(chunks, CHUNK, 2 * LANES),
            spec(chunks, LANES, 2 * LANES),
        ],
        out_shape=[
            jax.ShapeDtypeStruct((rows, heads_here * LANES), jnp.float32),
            jax.ShapeDtypeStruct((rows, heads_here * LANES), jnp.bfloat16),
            tile(LANES, 2 * LANES, kind=jnp.float32),
            tile(chunks, CHUNK, CHUNK, kind=jnp.bfloat16),
            tile(chunks, CHUNK, 2 * LANES, kind=jnp.bfloat16),
            tile(chunks, LANES, 2 * LANES, kind=jnp.bfloat16),
        ],
        scratch_shapes=[pltpu.VMEM((length + HALO, wide), jnp.float32)],
        compiler_params=pltpu.CompilerParams(vmem_limit_bytes=VMEM_BYTES),
        cost_estimate=pl.CostEstimate(
            flops=60 * rows * heads_here * CHUNK * LANES, bytes_accessed=40 * rows * heads_here * LANES, transcendentals=0
        ),
    )(pre, logit, bias, halo, conv, col, row)


def backward_kernel(
    taps, heads, first, pre, beta, bias, halo, conv, col_ref, row_ref, grad_ref, inv, upd, states, start, end,
    grad_pre, tail, before, conv_grad, logits, ext, grad_ext,
):
    length = pre.shape[0]
    step = pl.program_id(1)
    head = first + step * heads
    ext[:HALO] = halo[0]
    ext[HALO:] = pre[...]
    grad_ext[...] = jnp.zeros_like(grad_ext)

    @pl.when(step == 0)
    def _():
        logits[...] = jnp.zeros_like(logits)

    grad_states = [end[0, i] for i in range(heads)]
    entry = [low(start[0, i]) for i in range(heads)]
    tap_sums = {}
    for j in reversed(range(length // CHUNK)):
        offset = j * CHUNK
        rows = pl.ds(offset, CHUNK)
        col, row = col_ref[0, rows], row_ref[0, :, rows]
        upto, below, carried, last, keep = chunk_masks(col, row, offset)
        strengths = jax.nn.sigmoid(beta[rows] + bias[...])
        grad_logit = jnp.zeros((CHUNK, LANES), jnp.float32)
        for i in range(heads):
            raw, taps_in = [], []
            for kind in range(3):
                total, moved = conv_rows(ext, conv, col, offset, CHUNK, (3 * i + kind) * LANES, taps)
                raw.append(total)
                taps_in.append(moved)
            gates = [jax.nn.sigmoid(total) for total in raw]
            acts = [total * gate for total, gate in zip(raw, gates)]
            scales = [lax.rsqrt(jnp.sum(act * act, axis=-1, keepdims=True) + EPSILON) for act in acts[:2]]
            query, key, value = acts[0] * scales[0], acts[1] * scales[1], acts[2]
            strength = head_column(strengths, head + i)
            lanes = slice(i * LANES, (i + 1) * LANES)
            query_low, key_low = low(query), low(key)
            grams = mul_nt(jnp.concatenate([key_low, query_low], axis=0), key_low)
            gram = jnp.where(below, grams[:CHUNK], 0.0)
            scores = jnp.where(upto, grams[CHUNK:], 0.0)
            inverse = inv[0, i, j]
            update = upd[0, i, j]
            update = low(update[:, :LANES].astype(jnp.float32) + mul_nn(update[:, LANES:], entry[i]))
            state = states[0, i, j]
            state = low(state[:, :LANES].astype(jnp.float32) + mul_nn(state[:, LANES:], entry[i]))
            grad_out = grad_ref[rows, lanes]
            grad_state = grad_states[i]
            grad_state_low = low(grad_state)
            key_last = key_low * low(last)
            grad_update = mul_tn(scores, grad_out) + mul_nn(key_last, grad_state_low)
            grad_target = mul_tn(inverse, grad_update)
            weighted = strength * grad_target
            passed = carried * weighted
            out_carried = carried * grad_out.astype(jnp.float32)
            query_carried = query_low * low(carried)
            grad_states[i] = (
                keep * grad_state + mul_tn(query_carried, grad_out) - mul_tn(key_low, passed)
            )
            grad_scores = jnp.where(upto, mul_nt(grad_out, update), 0.0)
            grad_system = jnp.where(below, mul_nt(grad_target, update), 0.0)
            remainder = value - carried * mul_nn(key_low, state)
            grad_strength = jnp.sum(grad_target * remainder - grad_system * gram, axis=-1, keepdims=True)
            scaled = strength * grad_system
            from_state = mul_nt(jnp.concatenate([low(out_carried), low(passed)], axis=0), state)
            from_keys = mul_nn(jnp.concatenate([low(grad_scores), low(scaled + scaled.T)], axis=0), key_low)
            grad_query = from_state[:CHUNK] + from_keys[:CHUNK]
            grad_key = (
                mul_tn(grad_scores, query_low)
                + last * mul_nt(update, grad_state_low)
                - from_state[CHUNK:]
                - from_keys[CHUNK:]
            )
            grad_logit = grad_logit + jnp.where(
                iota((CHUNK, LANES), 1) == head + i, grad_strength * strength * (1.0 - strength), 0.0
            )
            grads = [
                scales[0] * (grad_query - query * jnp.sum(grad_query * query, axis=-1, keepdims=True)),
                scales[1] * (grad_key - key * jnp.sum(grad_key * key, axis=-1, keepdims=True)),
                weighted,
            ]
            position = iota((CHUNK, 1), 0) + offset
            for kind in range(3):
                gate, total = gates[kind], raw[kind]
                grad_conv = grads[kind] * gate * (1.0 + total * (1.0 - gate))
                lane = (3 * i + kind) * LANES
                for tap in range(taps):
                    back = taps - 1 - tap
                    part = jnp.sum(grad_conv * taps_in[kind][tap], axis=0, keepdims=True)
                    spot = (i, kind, tap)
                    tap_sums[spot] = part if spot not in tap_sums else tap_sums[spot] + part
                    back_part = jnp.where(
                        position - back >= col, grad_conv * conv[tap : tap + 1, lane : lane + LANES], 0.0
                    )
                    where = pl.ds(HALO + offset - back, CHUNK)
                    grad_ext[where, lane : lane + LANES] += back_part
        logits[rows] += grad_logit
    grad_pre[...] = low(grad_ext[HALO:])
    before[0] = grad_ext[:HALO]
    tail[0] = grad_ext[length:]
    for i in range(heads):
        for kind in range(3):
            lane = (3 * i + kind) * LANES
            for tap in range(taps):
                conv_grad[0, tap : tap + 1, lane : lane + LANES] = tap_sums[i, kind, tap]


def mixer_backward(
    pre, logit, bias, halo, conv, col, row, grad_mixed, inv, upd, states, start, end, taps, first, heads_here, group
):
    seqs, length = col.shape[0], col.shape[1]
    steps = heads_here // group
    chunks = length // CHUNK
    wide = 3 * LANES * group
    rows = seqs * length

    def spec(*tail):
        return pl.BlockSpec((1, group) + tail, lambda s, h: (s, h) + (0,) * len(tail))

    last = logit.shape[1] // LANES - 1
    part = pl.BlockSpec((1, HALO, wide), lambda s, h: (s, 0, h))
    edge = jax.ShapeDtypeStruct((seqs, HALO, 3 * LANES * heads_here), jnp.float32)
    return pl.pallas_call(
        functools.partial(backward_kernel, taps, group, first),
        grid=(seqs, steps),
        in_specs=[
            pl.BlockSpec((length, wide), lambda s, h: (s, h)),
            pl.BlockSpec((length, LANES), lambda s, h: (s, last)),
            pl.BlockSpec((1, LANES), lambda s, h: (0, 0)),
            part,
            pl.BlockSpec((conv.shape[0], wide), lambda s, h: (0, h)),
            pl.BlockSpec((1, length, 1), lambda s, h: (s, 0, 0)),
            pl.BlockSpec((1, 1, length), lambda s, h: (s, 0, 0)),
            pl.BlockSpec((length, LANES * group), lambda s, h: (s, h)),
            spec(chunks, CHUNK, CHUNK),
            spec(chunks, CHUNK, 2 * LANES),
            spec(chunks, LANES, 2 * LANES),
            spec(LANES, LANES),
            spec(LANES, LANES),
        ],
        out_specs=[
            pl.BlockSpec((length, wide), lambda s, h: (s, h)),
            part,
            part,
            part,
            pl.BlockSpec((length, LANES), lambda s, h: (s, 0)),
        ],
        out_shape=[
            jax.ShapeDtypeStruct((rows, 3 * LANES * heads_here), jnp.bfloat16),
            edge,
            edge,
            edge,
            jax.ShapeDtypeStruct((rows, LANES), jnp.float32),
        ],
        scratch_shapes=[
            pltpu.VMEM((length + HALO, wide), jnp.float32),
            pltpu.VMEM((length + HALO, wide), jnp.float32),
        ],
        compiler_params=pltpu.CompilerParams(vmem_limit_bytes=VMEM_BYTES),
        cost_estimate=pl.CostEstimate(
            flops=60 * rows * heads_here * CHUNK * LANES, bytes_accessed=40 * rows * heads_here * LANES, transcendentals=0
        ),
    )(pre, logit, bias, halo, conv, col, row, grad_mixed, inv, upd, states, start, end)


def mixed_rows_of(own, carry, start):
    return own + mul_nn(carry, start)


def output_kernel(heads, own, carry, start, gain, out):
    for i in range(heads):
        lanes = slice(i * LANES, (i + 1) * LANES)
        mixed = mixed_rows_of(own[:, lanes], carry[:, lanes], start[0, i])
        scale = lax.rsqrt(jnp.mean(mixed * mixed, axis=-1, keepdims=True) + HEAD_FLOOR)
        out[:, lanes] = low(mixed * scale * gain[...])


def output_backward_kernel(heads, own, carry, start, gain, grad, out, across, gain_grad):
    total = jnp.zeros((1, LANES), jnp.float32)
    for i in range(heads):
        lanes = slice(i * LANES, (i + 1) * LANES)
        carried = carry[:, lanes]
        mixed = mixed_rows_of(own[:, lanes], carried, start[0, i])
        scale = lax.rsqrt(jnp.mean(mixed * mixed, axis=-1, keepdims=True) + HEAD_FLOOR)
        normed = mixed * scale
        upper = grad[:, lanes].astype(jnp.float32)
        total = total + jnp.sum(upper * normed, axis=0, keepdims=True)
        weighted = upper * gain[...]
        back = scale * (weighted - normed * jnp.mean(weighted * normed, axis=-1, keepdims=True))
        out[:, lanes] = low(back)
        across[0, i] = mul_tn(carried, back)
    gain_grad[0, 0] = total


def mixer_output(own, carry, start, gain, group):
    seqs, heads_here = start.shape[:2]
    rows = own.shape[0]
    length = rows // seqs
    flat = pl.BlockSpec((length, LANES * group), lambda s, h: (s, h))
    square = pl.BlockSpec((1, group, LANES, LANES), lambda s, h: (s, h, 0, 0))
    return pl.pallas_call(
        functools.partial(output_kernel, group),
        grid=(seqs, heads_here // group),
        in_specs=[flat, flat, square, pl.BlockSpec((1, LANES), lambda s, h: (0, 0))],
        out_specs=flat,
        out_shape=jax.ShapeDtypeStruct(own.shape, jnp.bfloat16),
        compiler_params=pltpu.CompilerParams(vmem_limit_bytes=VMEM_BYTES),
        cost_estimate=pl.CostEstimate(
            flops=2 * own.size * LANES, bytes_accessed=8 * own.size, transcendentals=0
        ),
    )(own, carry, start, gain)


def mixer_output_backward(own, carry, start, gain, grad, first, group):
    seqs, heads_here = start.shape[:2]
    rows = own.shape[0]
    length = rows // seqs
    steps = heads_here // group
    flat = pl.BlockSpec((length, LANES * group), lambda s, h: (s, h))
    base = first // group
    shifted = pl.BlockSpec((length, LANES * group), lambda s, h: (s, base + h))
    square = pl.BlockSpec((1, group, LANES, LANES), lambda s, h: (s, h, 0, 0))
    return pl.pallas_call(
        functools.partial(output_backward_kernel, group),
        grid=(seqs, steps),
        in_specs=[flat, flat, square, pl.BlockSpec((1, LANES), lambda s, h: (0, 0)), shifted],
        out_specs=[flat, square, pl.BlockSpec((1, 1, 1, LANES), lambda s, h: (s, h, 0, 0))],
        out_shape=[
            jax.ShapeDtypeStruct(own.shape, jnp.bfloat16),
            jax.ShapeDtypeStruct(start.shape, jnp.float32),
            jax.ShapeDtypeStruct((seqs, steps, 1, LANES), jnp.float32),
        ],
        compiler_params=pltpu.CompilerParams(vmem_limit_bytes=VMEM_BYTES),
        cost_estimate=pl.CostEstimate(
            flops=4 * own.size * LANES, bytes_accessed=12 * own.size, transcendentals=0
        ),
    )(own, carry, start, gain, grad)


def ffn_kernel(mine, other, mine_grads, other_grads, gate_w, up_w, down_w, *outs):
    rows = jnp.concatenate([mine[...], other[...]], axis=0)
    grads = jnp.concatenate([mine_grads[...], other_grads[...]], axis=0)
    half = mine.shape[0]
    gate = mul_nt(rows, gate_w[...])
    up = mul_nt(rows, up_w[...])
    grad_hidden = mul_nt(grads, down_w[...])
    sigmoid = jax.nn.sigmoid(gate)
    active = gate * sigmoid
    kept = low(active * up)
    back_gate = low(grad_hidden * up * sigmoid * (1.0 + gate * (1.0 - sigmoid)))
    back_up = low(grad_hidden * active)
    grad_rows = low(mul_nn(back_gate, gate_w[...]) + mul_nn(back_up, up_w[...]))
    result = low(mul_nn(kept, down_w[...]))
    for side in range(2):
        here = slice(side * half, (side + 1) * half)
        acts, grad_out, result_out = outs[3 * side : 3 * side + 3]
        for kind, value in enumerate((back_gate, back_up, kept)):
            acts[kind] = value[here]
        grad_out[...] = grad_rows[here]
        result_out[...] = result[here]


def ffn_both(rows, grads, gate_up, down):
    count, width = rows[0].shape
    units = down.shape[0]
    tile = min(256, count)
    wide_rows = pl.BlockSpec((tile, width), lambda i: (i, 0))
    narrow = pl.BlockSpec((3, tile, units), lambda i: (0, i, 0))

    def third(index):
        return pl.BlockSpec((units, width), lambda i: (index, 0))

    flat = jax.ShapeDtypeStruct((count, width), jnp.bfloat16)
    outs = pl.pallas_call(
        ffn_kernel,
        grid=(count // tile,),
        in_specs=[wide_rows] * 4 + [third(0), third(1), third(0)],
        out_specs=[narrow, wide_rows, wide_rows] * 2,
        out_shape=[jax.ShapeDtypeStruct((3, count, units), jnp.bfloat16), flat, flat] * 2,
        compiler_params=pltpu.CompilerParams(vmem_limit_bytes=VMEM_BYTES),
        cost_estimate=pl.CostEstimate(
            flops=24 * count * width * units, bytes_accessed=16 * count * width + 6 * units * width, transcendentals=0
        ),
    )(*rows, *grads, gate_up, gate_up, down)
    return outs[:3], outs[3:]


def ffn_weights_kernel(count, lines, *refs):
    acts, rows, grads = refs[:count], refs[count : 2 * count], refs[2 * count : 3 * count]
    out, total = refs[-2:]
    part = out.shape[-1]

    def add(sources):
        for i in range(count):
            value = mul_tn(acts[i][0], sources[i][...])
            if i == 0:
                total[...] = value
            else:
                total[...] += value

    @pl.when(pl.program_id(0) < 2)
    def _():
        add(rows)

    @pl.when(pl.program_id(0) == 2)
    def _():
        add(grads)

    for line in range(lines):
        out[line, 0] = low(total[:, line * part : (line + 1) * part])


def ffn_weights(acts, rows, grads, lines, squares):
    count, width = len(acts), rows[0].shape[1]
    size, units = acts[0].shape[1:]
    block = width // squares
    part = block // lines
    act_spec = pl.BlockSpec((1, size, units), lambda k, c: (k, 0, 0))
    row_spec = pl.BlockSpec((size, block), lambda k, c: (0, jnp.where(k < 2, c, squares - 1)))
    grad_spec = pl.BlockSpec((size, block), lambda k, c: (0, jnp.where(k < 2, 0, c)))
    return pl.pallas_call(
        functools.partial(ffn_weights_kernel, count, lines),
        grid=(3, squares),
        in_specs=[act_spec] * count + [row_spec] * count + [grad_spec] * count,
        out_specs=pl.BlockSpec((lines, 1, units, part), lambda k, c: (0, k, 0, c)),
        out_shape=jax.ShapeDtypeStruct((lines, 3, units, squares * part), jnp.bfloat16),
        scratch_shapes=[pltpu.VMEM((units, block), jnp.float32)],
        compiler_params=pltpu.CompilerParams(vmem_limit_bytes=VMEM_BYTES),
        cost_estimate=pl.CostEstimate(
            flops=6 * count * size * width * units, bytes_accessed=8 * count * size * width, transcendentals=0
        ),
    )(*acts, *rows, *grads)


def block_columns(place, bit, size):
    return pl.multiple_of((place[0] ^ bit) * size, size)


def gathered_kernel(place, rows, *refs):
    out = refs[-1]
    own, beside, across, upper, lower = refs[:-1]
    size, half = own.shape[0], upper.shape[0]
    total = None
    for bit, skip, ref in ((0, 0, own), (1, 0, beside), (2, 0, across), (3, 0, upper), (3, half, lower)):
        start = pl.multiple_of(block_columns(place, bit, size) + skip, half)
        value = mul_nn(rows[:, pl.ds(start, ref.shape[0])], ref[...])
        total = value if total is None else total + value
    out[...] = total


def gathered_times(rows, place, pieces):
    count, width = rows.shape
    columns = pieces[0].shape[1]
    tile = min(256, count)
    whole = [pl.BlockSpec(piece.shape, lambda i, place: (0, 0)) for piece in pieces]
    return pl.pallas_call(
        gathered_kernel,
        grid_spec=pltpu.PrefetchScalarGridSpec(
            num_scalar_prefetch=1,
            grid=(count // tile,),
            in_specs=[pl.BlockSpec((tile, width), lambda i, place: (i, 0))] + whole,
            out_specs=pl.BlockSpec((tile, columns), lambda i, place: (i, 0)),
        ),
        out_shape=jax.ShapeDtypeStruct((count, columns), jnp.float32),
        compiler_params=pltpu.CompilerParams(vmem_limit_bytes=VMEM_BYTES),
        cost_estimate=pl.CostEstimate(
            flops=2 * count * width * columns, bytes_accessed=2 * (count + columns) * width, transcendentals=0
        ),
    )(jnp.reshape(place, (1,)).astype(jnp.int32), rows, *pieces)


def gathered_transposed_kernel(count, place, *refs):
    factors, pieces, out = refs[:count], refs[count:-1], refs[-1]
    size, half = pieces[0].shape[0], pieces[3].shape[0]
    for i, (bit, skip) in enumerate(((0, 0), (1, 0), (2, 0), (3, 0), (3, half))):
        start = pl.multiple_of(block_columns(place, bit, size) + skip, half)
        total = None
        for p in range(count):
            value = mul_nt(factors[p][...], pieces[5 * p + i][...])
            total = value if total is None else total + value
        out[:, pl.ds(start, pieces[i].shape[0])] = low(total)


def gathered_times_transposed(factors, place, pieces):
    count, rows = len(factors), factors[0].shape[0]
    width = 4 * pieces[0][0].shape[0]
    tile = min(256, rows)
    flat = [piece for some in pieces for piece in some]
    whole = [pl.BlockSpec(piece.shape, lambda i, place: (0, 0)) for piece in flat]
    wides = [pl.BlockSpec((tile, factor.shape[1]), lambda i, place: (i, 0)) for factor in factors]
    columns = sum(factor.shape[1] for factor in factors)
    return pl.pallas_call(
        functools.partial(gathered_transposed_kernel, count),
        grid_spec=pltpu.PrefetchScalarGridSpec(
            num_scalar_prefetch=1,
            grid=(rows // tile,),
            in_specs=wides + whole,
            out_specs=pl.BlockSpec((tile, width), lambda i, place: (i, 0)),
        ),
        out_shape=jax.ShapeDtypeStruct((rows, width), jnp.bfloat16),
        compiler_params=pltpu.CompilerParams(vmem_limit_bytes=VMEM_BYTES),
        cost_estimate=pl.CostEstimate(
            flops=2 * rows * width * columns, bytes_accessed=2 * (rows + columns) * width, transcendentals=0
        ),
    )(jnp.reshape(place, (1,)).astype(jnp.int32), *factors, *flat)


def join_kernel(squares, source, target):
    lines, _, columns = source.shape
    part = columns // squares
    for i in range(lines):
        for j in range(squares):
            at = (j * lines + i) * part
            target[:, at : at + part] = source[i, :, j * part : (j + 1) * part]


def columns_join(parts, squares):
    lines, rows, columns = parts.shape
    tile = 176 if rows % 176 == 0 else rows
    return pl.pallas_call(
        functools.partial(join_kernel, squares),
        grid=(rows // tile,),
        in_specs=[pl.BlockSpec((lines, tile, columns), lambda i: (0, i, 0))],
        out_specs=pl.BlockSpec((tile, lines * columns), lambda i: (i, 0)),
        out_shape=jax.ShapeDtypeStruct((rows, lines * columns), parts.dtype),
        compiler_params=pltpu.CompilerParams(vmem_limit_bytes=VMEM_BYTES),
        cost_estimate=pl.CostEstimate(flops=0, bytes_accessed=4 * parts.size, transcendentals=0),
    )(parts)


def flip(value, axis, bit):
    devices = range(lax.axis_size(axis))
    return lax.ppermute(value, axis, [(i, i ^ bit) for i in devices])


def shift(value, axis, distance):
    count = lax.axis_size(axis)
    return lax.ppermute(value, axis, [(i, (i + distance) % count) for i in range(count)])


def from_behind(block, axis, distance):
    devices = range(lax.axis_size(axis))
    route = [(i - distance, i) for i in devices if i - distance in devices]
    return lax.ppermute(block, axis, route)


def tie(value, *earlier):
    return lax.optimization_barrier((value,) + earlier)[0]


def put(buffer, piece, *start):
    return lax.dynamic_update_slice(buffer, piece, start)


def wide(value):
    return value.astype(jnp.float32)


def gather_line(shard):
    count, place = lax.axis_size("fsdp"), lax.axis_index("fsdp")
    pieces = [shard] + [shift(shard, "fsdp", d) for d in range(1, count)]
    order = [(place - i) % count for i in range(count)]
    return jnp.concatenate([lax.select_n(which, *pieces) for which in order], axis=0)


class Square:
    def __init__(self, own):
        self.own = own
        self.half = own.shape[0] // 2
        self.beside = flip(own, "ctx", 1)
        self.across = flip(own, "ctx", 2)

    def forward(self, *earlier):
        upper = self.beside[: self.half]
        lower = self.across[self.half :]
        if earlier:
            upper, lower = lax.optimization_barrier((upper, lower) + earlier)[:2]
        self.upper = flip(upper, "ctx", 2)
        self.lower = flip(lower, "ctx", 1)
        return self

    def done(self):
        return (self.upper, self.lower)

    def pieces(self):
        return [self.own, self.beside, self.across, self.upper, self.lower]

    def far(self):
        return jnp.concatenate([self.upper, self.lower], axis=0)


def both_sides(rows):
    if lax.axis_size("tp") == 2:
        return rows, flip(rows, "tp", 1)
    every = lax.all_gather(rows, "tp", axis=0, tiled=True)
    half = every.shape[0] // 2
    return every[:half], every[half:]


def core_sum(mine, other):
    if lax.axis_size("tp") == 2:
        return wide(mine) + wide(flip(other, "tp", 1))
    both = jnp.concatenate([mine, other], axis=0)
    return wide(lax.psum_scatter(both, "tp", scatter_dimension=0, tiled=True))


def neighbour_columns(rows):
    width = rows.shape[1] // 4
    place = lax.axis_index("ctx")
    return [lax.dynamic_slice_in_dim(rows, (place ^ bit) * width, width, 1) for bit in range(4)]


class Line:
    def __init__(self, own):
        count, place = lax.axis_size("fsdp"), lax.axis_index("fsdp")
        own = own.reshape(count, own.shape[0] // count, own.shape[1])

        def part(distance):
            return lax.dynamic_index_in_dim(own, (place + distance) % count, 0, keepdims=False)

        self.kept = part(0)
        self.sent = [low(part(distance)) for distance in range(1, count)]
        self.arrived = [shift(piece, "fsdp", distance + 1) for distance, piece in enumerate(self.sent)]

    def total(self, *late):
        total = self.kept
        for part in lax.optimization_barrier(tuple(self.arrived) + late)[: len(self.arrived)]:
            total = total + wide(part)
        return total


class Scatter:
    def __init__(self, columns, grads):
        self.columns, self.grads = columns, grads
        self.half = columns[0].shape[1] // 2
        beside, across = (
            jnp.concatenate([self.side(3, 1), self.side(1, 1)], axis=1),
            jnp.concatenate([self.side(3, 0), self.side(2, 0)], axis=1),
        )
        self.sent = [low(outer_rows(beside, grads)), low(outer_rows(across, grads))]
        self.first = (flip(self.sent[0], "ctx", 1), flip(self.sent[1], "ctx", 2))

    def side(self, bit, lower):
        return self.columns[bit][:, lower * self.half : (lower + 1) * self.half]

    def second(self, *earlier):
        first = self.first
        if earlier:
            first = lax.optimization_barrier(first + earlier)[:2]
        beside, across = (wide(part) for part in first)
        upper = low(outer_rows(self.side(1, 0), self.grads) + across[: self.half])
        lower = low(outer_rows(self.side(2, 1), self.grads) + beside[: self.half])
        self.last = (flip(upper, "ctx", 1), flip(lower, "ctx", 2))
        self.kept = (beside, across)
        return upper, lower

    def own(self, *ties):
        beside_upper, across_lower = self.last
        if ties:
            beside_upper, across_lower = lax.optimization_barrier(self.last + ties)[:2]
        beside, across = self.kept
        own = outer_rows(self.columns[0], self.grads)
        upper = own[: self.half] + wide(beside_upper) + across[self.half :]
        lower = own[self.half :] + beside[self.half :] + wide(across_lower)
        return jnp.concatenate([upper, lower], axis=0)


def butterfly(value, axes):
    for axis in axes:
        count, bit = lax.axis_size(axis), 1
        while bit < count:
            value = value + flip(value, axis, bit)
            bit *= 2
    return value


def rms_scale(values, floor_value):
    return lax.rsqrt(jnp.mean(values * values, axis=-1, keepdims=True) + floor_value)


def norm_backward(grad_normed, inputs, scale, gain):
    normed = inputs * scale
    weighted = grad_normed * gain
    return (
        scale * (weighted - normed * jnp.mean(weighted * normed, axis=-1, keepdims=True)),
        normed,
    )


def times(left, right):
    return jnp.dot(left, right, preferred_element_type=jnp.float32)


def times_transposed(left, right):
    return lax.dot_general(
        left, right, (((1,), (1,)), ((), ())), preferred_element_type=jnp.float32
    )


def outer_rows(left, right):
    return lax.dot_general(
        left, right, (((0,), (0,)), ((), ())), preferred_element_type=jnp.float32
    )


def rows_mine(rows):
    count = rows.shape[1] // lax.axis_size("tp")
    return lax.dynamic_slice_in_dim(rows, lax.axis_index("tp") * count, count, 1)


def rows_scatter(partial):
    if lax.axis_size("tp") != 2:
        return wide(lax.psum_scatter(partial, "tp", scatter_dimension=1, tiled=True))
    count = partial.shape[1] // 2
    other = lax.dynamic_slice_in_dim(partial, (1 - lax.axis_index("tp")) * count, count, 1)
    return wide(rows_mine(partial)) + wide(flip(other, "tp", 1))


def rows_full(mine):
    if lax.axis_size("tp") != 2:
        return lax.all_gather(mine, "tp", axis=1, tiled=True)
    other = flip(mine, "tp", 1)
    lower = lax.axis_index("tp") == 0
    return jnp.concatenate([jnp.where(lower, mine, other), jnp.where(lower, other, mine)], axis=1)


def by_head(parts):
    heads = range(parts[0].shape[-1] // LANES)
    return jnp.concatenate([part[..., h * LANES : (h + 1) * LANES] for h in heads for part in parts], axis=-1)


def by_kind(joined):
    return [
        jnp.concatenate(
            [
                some[..., at : at + LANES]
                for some in joined
                for at in range(kind * LANES, some.shape[-1], 3 * LANES)
            ],
            axis=-1,
        )
        for kind in range(3)
    ]


def pass_states(own, transfer, forward, *beside):
    rule = "shij,shjk->shik" if forward == 1 else "shji,shjk->shik"
    leaving = own
    entered = low(jnp.zeros_like(own))
    for repeat in range(lax.axis_size("ctx") - 1):
        entered = from_behind(low(leaving), "ctx", forward)
        if repeat == 0 and beside:
            entered = tie(entered, *beside)
        leaving = own + jnp.einsum(rule, transfer, entered, preferred_element_type=jnp.float32)
    return wide(entered)


def local(
    block_input,
    doc_start,
    gain_mix,
    query_weight,
    key_weight,
    value_weight,
    beta_weight,
    beta_bias,
    conv_weight,
    gain_o,
    out_weight,
    gain_ffn,
    gate_weight,
    up_weight,
    down_weight,
    out_grad,
):
    seq_count, local_len, width = block_input.shape
    row_count = seq_count * local_len
    heads_here = beta_weight.shape[1]
    taps = conv_weight.shape[1]
    parts = 2 if heads_here % 2 == 0 else 1
    part_heads = heads_here // parts
    group = 2 if part_heads % 2 == 0 else 1
    part_cols = 3 * part_heads * LANES
    spare = LANES - heads_here
    units_here = gate_weight.shape[1]
    shard_rows = gate_weight.shape[0]

    joined = by_head([low(query_weight), low(key_weight), low(value_weight)])
    shards = [joined[:, p * part_cols : (p + 1) * part_cols] for p in range(parts)]
    shards[0] = jnp.concatenate([shards[0], jnp.pad(low(beta_weight), ((0, 0), (0, spare)))], axis=1)
    shards.append(low(out_weight).T)
    lines = []
    for shard in shards[:parts]:
        lines.append(gather_line(tie(shard, lines[-1]) if lines else shard))
    units = units_here // 4
    pieces = jnp.stack([low(gate_weight).T, low(up_weight).T, low(down_weight)])
    pieces = pieces.reshape(3, 4, units, shard_rows).transpose(1, 0, 2, 3)
    ffn_swapped = lax.all_to_all(pieces.reshape(4, 3 * units, shard_rows), "ctx", 0, 0)
    ffn_line = ffn_swapped.transpose(1, 0, 2).reshape(3 * units, 4 * shard_rows)
    line_count = lax.axis_size("fsdp")

    ctx_place = lax.axis_index("ctx")
    first_pos = ctx_place * local_len
    starts = doc_start - first_pos
    col, row = starts[:, :, None], starts[:, None, :]
    conv = by_head([conv_weight[0], conv_weight[1], conv_weight[2]])
    bias = jnp.pad(beta_bias, (0, spare))[None]
    gain_head = gain_o[None]
    tokens = block_input.reshape(row_count, width)
    inputs = wide(tokens)
    normed_mix = low(inputs * rms_scale(inputs, EPSILON) * gain_mix)
    grads_mine = rows_mine(out_grad).reshape(-1, width)

    square = Square(tie(lines[0], ffn_swapped)).forward(normed_mix)
    gate_up_parts = tie(ffn_line[None, : 2 * units], lines[parts - 1], *square.done())
    gate_up_parts = lax.all_gather(gate_up_parts, "fsdp", axis=0, tiled=True)
    down_parts = lax.all_gather(ffn_line[None, 2 * units :], "fsdp", axis=0, tiled=True)
    mix_full, kept, pre = [], [], []
    for p in range(parts):
        mix_full.append(square.pieces())
        arrived = square.done()
        ends = normed_mix.reshape(seq_count, local_len, width)[:, local_len - HALO :].reshape(seq_count * HALO, width)
        ends = gathered_times(ends, ctx_place, mix_full[p])
        ends = low(ends)
        halo = from_behind(ends[:, :part_cols].reshape(seq_count, HALO, part_cols), "ctx", 1)
        pre.append(gathered_times(tie(normed_mix, ends), ctx_place, mix_full[p]))
        square = Square(tie(lines[p + 1], halo, pre[p], *arrived))
        halo = wide(halo)
        convs = conv[:, p * part_cols : (p + 1) * part_cols]
        kept.append(
            [halo, convs]
            + list(
                mixer_forward(
                    pre[p], pre[0], bias, halo, convs, col, row, taps, p * part_heads, part_heads, group
                )
            )
        )
        square.forward(kept[p][2])
        if p == 0:
            lines.append(gather_line(tie(shards[-1], kept[p][2], square.beside)))
            grad_square = Square(tie(grads_mine, kept[p][2], *square.done()))
    out_full = square.pieces()

    inputs_mine = wide(rows_mine(tie(block_input, kept[0][2])).reshape(-1, width))
    gate_up_full = columns_join(gate_up_parts, 4)
    finals = jnp.concatenate([some[4] for some in kept], axis=1)
    transfer = low(finals[..., LANES:])
    first = tie(finals[..., :LANES], gate_up_full, grad_square.beside, grad_square.across)
    entering = pass_states(first, transfer, 1)
    entered = [entering[:, p * part_heads : (p + 1) * part_heads] for p in range(parts)]
    grad_square.forward(entering)
    grad_rows = [both_sides(part) for part in (grad_square.own, grad_square.beside, grad_square.across)]
    mixed_rows = []
    for p in range(parts):
        own, carry = kept[p][2:4]
        mixed_rows.append(mixer_output(own, carry, entered[p], gain_head, group))
    mixed_rows = jnp.concatenate(mixed_rows, axis=1)
    mixed_rows = tie(mixed_rows, *(other for _, other in grad_rows))
    grad_rows.append(both_sides(grad_square.far()))

    branch = gathered_times_transposed([mixed_rows], ctx_place, [out_full]).reshape(seq_count, local_len, width)
    branch = tie(branch, down_parts)
    residual = inputs_mine + rows_scatter(branch).reshape(-1, width)
    scale_ffn = rms_scale(residual, EPSILON)
    square = Square(low(residual * scale_ffn * gain_ffn))
    ffn_full = (gate_up_full, columns_join(down_parts, 4))

    ffn_rows = [both_sides(square.own)]
    ffn_out = [ffn_both(ffn_rows[0], grad_rows[0], *ffn_full)]
    square.forward(ffn_out[0][0][0])
    ffn_rows.append(both_sides(tie(square.beside, ffn_out[0][0][0])))
    ffn_out.append(ffn_both(ffn_rows[1], grad_rows[1], *ffn_full))
    ffn_rows.append(both_sides(tie(square.across, ffn_out[0][0][0])))
    mine, other = ffn_rows[2]
    ffn_out.append(ffn_both((tie(mine, ffn_out[1][0][0], *square.done()), other), grad_rows[2], *ffn_full))
    beside_sums, across_sums = (low(core_sum(*(side[1] for side in ffn_out[bit]))) for bit in (1, 2))
    ffn_rows.append(both_sides(square.far()))
    mine, other = ffn_rows[3]
    ffn_out.append(ffn_both((tie(mine, beside_sums, across_sums), other), grad_rows[3], *ffn_full))
    near_sums = (flip(beside_sums, "ctx", 1), flip(across_sums, "ctx", 2))
    mine, other = (side[1] for side in ffn_out[3])
    far_sums = low(core_sum(mine, tie(other, *near_sums)))
    acts = [side[0] for outs in ffn_out for side in outs]
    own_sums = core_sum(*(side[1] for side in ffn_out[0]))
    result_low = [low(core_sum(*(side[2] for side in ffn_out[bit]))) for bit in (1, 2)]
    acts[0] = tie(acts[0], far_sums, own_sums, *result_low)
    far_sums = flip(far_sums, "ctx", 3)
    sums = ffn_weights(
        acts,
        [side for sides in ffn_rows for side in sides],
        [side for sides in grad_rows for side in sides],
        line_count,
        4,
    )

    far_sums, sums = lax.optimization_barrier((far_sums, sums))
    result_near = [flip(tie(part, far_sums), "ctx", bit) for part, bit in zip(result_low, (1, 2))]
    grad_normed = own_sums + wide(near_sums[0]) + wide(near_sums[1]) + wide(far_sums)
    back_ffn, unit_ffn = norm_backward(grad_normed, residual, scale_ffn, gain_ffn)
    grad_residual = wide(grads_mine) + back_ffn
    gain_ffn_part = jnp.sum(grad_normed * unit_ffn, axis=0)
    grad_branch = rows_full(low(grad_residual).reshape(seq_count, -1, width)).reshape(row_count, width)
    grad_heads = gathered_times(grad_branch, ctx_place, out_full)
    backs, acrosses, gain_o_part = [], [], 0.0
    for p in range(parts):
        _, _, own, carry, _, _, _, _ = kept[p]
        back, across, gain_part = mixer_output_backward(
            own, carry, entered[p], gain_head, grad_heads, p * part_heads, group
        )
        backs.append(back)
        acrosses.append(across)
        gain_o_part = gain_o_part + jnp.sum(gain_part, axis=(0, 1, 2))
    grad_end = pass_states(jnp.concatenate(acrosses, axis=1), transfer, -1, *result_near)
    total = lax.psum_scatter(sums, "fsdp", scatter_dimension=0, tiled=True)

    out_grad_w = low(outer_rows(grad_branch, mixed_rows))
    out_part = out_grad_w
    out_grad_w = lax.psum_scatter(out_grad_w, ("ctx", "fsdp"), scatter_dimension=0, tiled=True)

    mine, other = (side[2] for side in ffn_out[0])
    result_own = core_sum(mine, tie(other, grad_branch))
    mine, other = (side[2] for side in ffn_out[3])
    result_far = flip(tie(low(core_sum(mine, tie(other, grad_branch))), grad_end), "ctx", 3)
    columns = neighbour_columns(normed_mix)
    grad_mixes, mix_grads, conv_parts = [None] * parts, [None] * parts, [None] * parts
    logits = 0.0
    scatter = None
    for p in reversed(range(parts)):
        halo, convs, own, carry, final, inverses, updates, states = kept[p]
        heads = slice(p * part_heads, (p + 1) * part_heads)
        back = tie(backs[p], out_part) if scatter is None else tie(backs[p], total, *scatter.sent)
        grad_mix, tail, before, conv_parts[p], logit = mixer_backward(
            pre[p], pre[0], bias, halo, convs, col, row, back, inverses, updates, states,
            entered[p], grad_end[:, heads], taps, p * part_heads, part_heads, group,
        )
        logits = logits + logit
        tail = low(tail + from_behind(before, "ctx", -1))
        grad_mix = put(grad_mix.reshape(seq_count, local_len, -1), tail, 0, local_len - HALO, 0)
        grad_mix = grad_mix.reshape(row_count, -1)
        if scatter is not None:
            scatter.second(before)
            earlier_scatter = scatter
        else:
            grad_mix = tie(grad_mix, result_far)
        if p == 0:
            grad_mix = jnp.concatenate([grad_mix, low(logits)], axis=1)
        grad_mixes[p] = grad_mix
        scatter = Scatter(columns, grad_mix)
        if p > 0:
            result_far = tie(result_far, *scatter.sent)
    result = result_own + wide(result_near[0]) + wide(result_near[1])
    result = result + wide(result_far)
    block_output = rows_full(low(residual + result).reshape(seq_count, -1, width))
    ready = scatter.second(block_output)
    grad_mixes[0] = tie(grad_mixes[0], *ready)
    mix_back = tie(gathered_times_transposed(grad_mixes, ctx_place, mix_full), *scatter.last)
    mix_back = rows_scatter(mix_back.reshape(seq_count, local_len, width)).reshape(-1, width)
    back_mix, unit_mix = norm_backward(mix_back, inputs_mine, rms_scale(inputs_mine, EPSILON), gain_mix)
    input_grad = rows_full(low(grad_residual + back_mix).reshape(seq_count, -1, width))
    gain_mix_part = jnp.sum(mix_back * unit_mix, axis=0)

    conv_cols = jnp.concatenate([jnp.sum(part, axis=0)[:taps] for part in conv_parts], axis=1)
    gains = butterfly(jnp.concatenate([gain_mix_part, gain_ffn_part, gain_o_part]), ("tp",))
    sums = jnp.concatenate([gains, conv_cols.reshape(-1), jnp.sum(logits, axis=0)])
    for p in range(1, parts):
        own = low(earlier_scatter.own(*ready))
        mix_grads[p] = wide(lax.psum_scatter(own, "fsdp", scatter_dimension=0, tiled=True))
    last_line = Line(scatter.own())
    sums = butterfly(tie(sums, input_grad, *last_line.sent), ("ctx", "fsdp"))
    mix_grads[0] = last_line.total(sums)
    query_grad, key_grad, value_grad = by_kind([grad[:, :part_cols] for grad in mix_grads])
    beta_grad = mix_grads[0][:, part_cols : part_cols + heads_here]
    ends = [width, 2 * width, 2 * width + LANES, sums.shape[0] - LANES]
    gain_mix_grad, gain_ffn_grad, gain_o_grad, conv_grad, bias_grad = jnp.split(sums, ends)
    conv_grad = jnp.stack(by_kind([conv_grad.reshape(taps, -1)]))
    bias_grad = bias_grad[:heads_here]
    out_grad_w = wide(tie(out_grad_w, *scatter.last)).T
    pieces = tie(total, *scatter.last).reshape(3 * units, 4, shard_rows).transpose(1, 0, 2)
    arrived = lax.all_to_all(pieces, "ctx", 0, 0).reshape(4, 3, units, shard_rows)
    gate_grad, up_grad, down_grad = (wide(arrived[:, i].reshape(units_here, shard_rows)) for i in range(3))

    return (
        block_output,
        input_grad,
        gain_mix_grad,
        query_grad,
        key_grad,
        value_grad,
        beta_grad,
        bias_grad,
        conv_grad,
        gain_o_grad,
        out_grad_w,
        gain_ffn_grad,
        gate_grad.T,
        up_grad.T,
        down_grad,
    )


def solution(mesh):
    placed = (
        P("fsdp", "ctx", None),
        P("fsdp", "ctx"),
        P(),
        P(("ctx", "fsdp"), "tp"),
        P(("ctx", "fsdp"), "tp"),
        P(("ctx", "fsdp"), "tp"),
        P(("ctx", "fsdp"), "tp"),
        P("tp"),
        P(None, None, "tp"),
        P(),
        P("tp", ("ctx", "fsdp")),
        P(),
        P(("ctx", "fsdp"), "tp"),
        P(("ctx", "fsdp"), "tp"),
        P("tp", ("ctx", "fsdp")),
        P("fsdp", "ctx", None),
    )
    return jax.shard_map(
        local,
        mesh=mesh,
        in_specs=placed,
        out_specs=(
            P("fsdp", "ctx", None),
            P("fsdp", "ctx", None),
            P(),
            P(("ctx", "fsdp"), "tp"),
            P(("ctx", "fsdp"), "tp"),
            P(("ctx", "fsdp"), "tp"),
            P(("ctx", "fsdp"), "tp"),
            P("tp"),
            P(None, None, "tp"),
            P(),
            P("tp", ("ctx", "fsdp")),
            P(),
            P(("ctx", "fsdp"), "tp"),
            P(("ctx", "fsdp"), "tp"),
            P("tp", ("ctx", "fsdp")),
        ),
        check_vma=False,
    )
```

```python
import functools
import math
import jax
import jax.numpy as jnp
from jax import lax
from jax.experimental import pallas as pl
from jax.experimental.pallas import tpu as pltpu
from jax.sharding import PartitionSpec as P

LANES = 128
CHUNK = 128
HALO = 8
EPSILON = 1e-06
HEAD_FLOOR = 0.01
VMEM_BYTES = 60 * 1024 * 1024


def low(value):
    return value.astype(jnp.bfloat16)


def mul_nn(left, right):
    return lax.dot_general(low(left), low(right), (((1,), (0,)), ((), ())), preferred_element_type=jnp.float32)


def mul_nt(left, right):
    return lax.dot_general(low(left), low(right), (((1,), (1,)), ((), ())), preferred_element_type=jnp.float32)


def mul_tn(left, right):
    return lax.dot_general(low(left), low(right), (((0,), (0,)), ((), ())), preferred_element_type=jnp.float32)


def iota(shape, axis):
    return lax.broadcasted_iota(jnp.int32, shape, axis)


def chunk_masks(col, row, first):
    size = col.shape[0]
    same = col == row
    order, other = iota((size, size), 0), iota((size, size), 1)
    upto = same & (order >= other)
    below = same & (order > other)
    carried = (col < first).astype(jnp.float32)
    last = (col == row[:, size - 1 :]).astype(jnp.float32)
    keep = (row[:, size - 1 :] < first).astype(jnp.float32)
    return upto, below, carried, last, keep


def invert_units(systems):
    size = systems[0].shape[0]
    order, other = iota((size, size), 0), iota((size, size), 1)
    identity = (order == other).astype(jnp.float32)
    span = 1
    found = None
    while span < size:
        pair = (order // (2 * span) == other // (2 * span)) & (order // span != other // span)
        parts = [jnp.where(pair, system, 0.0) for system in systems]
        if found is None:
            found = [identity - part for part in parts]
        else:
            right = [mul_nn(part, value) for part, value in zip(parts, found)]
            found = [value - mul_nn(value, part) for value, part in zip(found, right)]
        span *= 2
    return found


def conv_rows(ext, conv, col, offset, size, lane, taps):
    total = None
    moved = []
    position = iota((size, 1), 0) + offset
    for tap in range(taps):
        back = taps - 1 - tap
        values = ext[pl.ds(HALO + offset - back, size), lane : lane + LANES]
        values = jnp.where(position - back >= col, values, 0.0)
        moved.append(values)
        term = conv[tap : tap + 1, lane : lane + LANES] * values
        total = term if total is None else total + term
    return total, moved


def unit(values):
    return values * lax.rsqrt(jnp.sum(values * values, axis=-1, keepdims=True) + EPSILON)


def head_column(values, head):
    return jnp.sum(jnp.where(iota(values.shape, 1) == head, values, 0.0), axis=-1, keepdims=True)


def forward_kernel(taps, heads, first, pre, beta, bias, halo, conv, col_ref, row_ref, own, carry, final, inv, upd, states, ext):
    length = pre.shape[0]
    ext[:HALO] = halo[0]
    ext[HALO:] = pre[...]
    head = first + pl.program_id(1) * heads
    jobs = [(i, j) for j in range(length // CHUNK) for i in range(heads)]
    data = {}
    for j in range(length // CHUNK):
        rows = pl.ds(j * CHUNK, CHUNK)
        col, row = col_ref[0, rows], row_ref[0, :, rows]
        masks = chunk_masks(col, row, j * CHUNK)
        strengths = jax.nn.sigmoid(beta[rows] + bias[...])
        for i in range(heads):
            acts = []
            for kind in range(3):
                total, _ = conv_rows(ext, conv, col, j * CHUNK, CHUNK, (3 * i + kind) * LANES, taps)
                acts.append(total * jax.nn.sigmoid(total))
            query, key, value = unit(acts[0]), unit(acts[1]), acts[2]
            strength = head_column(strengths, head + i)
            grams = mul_nt(jnp.concatenate([low(key), low(query)], axis=0), key)
            system = jnp.where(masks[1], strength * grams[:CHUNK], 0.0)
            scores = low(jnp.where(masks[0], grams[CHUNK:], 0.0))
            data[i, j] = (low(query), low(key), value, strength, scores, masks, system)
    inverses = dict(zip(jobs, invert_units([data[job][6] for job in jobs])))
    for i in range(heads):
        state = jnp.concatenate(
            [
                jnp.zeros((LANES, LANES), jnp.float32),
                (iota((LANES, LANES), 0) == iota((LANES, LANES), 1)).astype(jnp.float32),
            ],
            axis=1,
        )
        final[0, i] = state
    for j in range(length // CHUNK):
        rows = pl.ds(j * CHUNK, CHUNK)
        for i in range(heads):
            query, key, value, strength, scores, masks, _ = data[i, j]
            _, _, carried, last, keep = masks
            inverse = low(inverses[i, j])
            state = final[0, i]
            state_low = low(state)
            read = mul_nn(jnp.concatenate([key, query], axis=0), state_low)
            wide = jnp.concatenate([value, jnp.zeros_like(value)], axis=1)
            targets = strength * (wide - carried * read[:CHUNK])
            update = low(mul_nn(inverse, targets))
            result = carried * read[CHUNK:] + mul_nn(scores, update)
            final[0, i] = keep * state + mul_tn(key * low(last), update)
            lanes = slice(i * LANES, (i + 1) * LANES)
            own[rows, lanes] = result[:, :LANES]
            carry[rows, lanes] = low(result[:, LANES:])
            inv[0, i, j] = inverse
            upd[0, i, j] = update
            states[0, i, j] = state_low


def mixer_forward(pre, logit, bias, halo, conv, col, row, taps, first, heads_here, group):
    seqs, length = col.shape[0], col.shape[1]
    steps = heads_here // group
    chunks = length // CHUNK
    wide = 3 * LANES * group
    rows = seqs * length

    def tile(*tail, kind):
        return jax.ShapeDtypeStruct((seqs, heads_here) + tail, kind)

    def spec(*tail):
        return pl.BlockSpec((1, group) + tail, lambda s, h: (s, h) + (0,) * len(tail))

    flat = pl.BlockSpec((length, LANES * group), lambda s, h: (s, h))
    last = logit.shape[1] // LANES - 1
    return pl.pallas_call(
        functools.partial(forward_kernel, taps, group, first),
        grid=(seqs, steps),
        in_specs=[
            pl.BlockSpec((length, wide), lambda s, h: (s, h)),
            pl.BlockSpec((length, LANES), lambda s, h: (s, last)),
            pl.BlockSpec((1, LANES), lambda s, h: (0, 0)),
            pl.BlockSpec((1, HALO, wide), lambda s, h: (s, 0, h)),
            pl.BlockSpec((conv.shape[0], wide), lambda s, h: (0, h)),
            pl.BlockSpec((1, length, 1), lambda s, h: (s, 0, 0)),
            pl.BlockSpec((1, 1, length), lambda s, h: (s, 0, 0)),
        ],
        out_specs=[
            flat,
            flat,
            spec(LANES, 2 * LANES),
            spec(chunks, CHUNK, CHUNK),
            spec(chunks, CHUNK, 2 * LANES),
            spec(chunks, LANES, 2 * LANES),
        ],
        out_shape=[
            jax.ShapeDtypeStruct((rows, heads_here * LANES), jnp.float32),
            jax.ShapeDtypeStruct((rows, heads_here * LANES), jnp.bfloat16),
            tile(LANES, 2 * LANES, kind=jnp.float32),
            tile(chunks, CHUNK, CHUNK, kind=jnp.bfloat16),
            tile(chunks, CHUNK, 2 * LANES, kind=jnp.bfloat16),
            tile(chunks, LANES, 2 * LANES, kind=jnp.bfloat16),
        ],
        scratch_shapes=[pltpu.VMEM((length + HALO, wide), jnp.float32)],
        compiler_params=pltpu.CompilerParams(vmem_limit_bytes=VMEM_BYTES),
        cost_estimate=pl.CostEstimate(
            flops=60 * rows * heads_here * CHUNK * LANES, bytes_accessed=40 * rows * heads_here * LANES, transcendentals=0
        ),
    )(pre, logit, bias, halo, conv, col, row)


def backward_kernel(
    taps, heads, first, pre, beta, bias, halo, conv, col_ref, row_ref, grad_ref, inv, upd, states, start, end,
    grad_pre, tail, before, conv_grad, logits, ext, grad_ext,
):
    length = pre.shape[0]
    step = pl.program_id(1)
    head = first + step * heads
    ext[:HALO] = halo[0]
    ext[HALO:] = pre[...]
    grad_ext[...] = jnp.zeros_like(grad_ext)

    @pl.when(step == 0)
    def _():
        logits[...] = jnp.zeros_like(logits)

    grad_states = [end[0, i] for i in range(heads)]
    entry = [low(start[0, i]) for i in range(heads)]
    tap_sums = {}
    for j in reversed(range(length // CHUNK)):
        offset = j * CHUNK
        rows = pl.ds(offset, CHUNK)
        col, row = col_ref[0, rows], row_ref[0, :, rows]
        upto, below, carried, last, keep = chunk_masks(col, row, offset)
        strengths = jax.nn.sigmoid(beta[rows] + bias[...])
        grad_logit = jnp.zeros((CHUNK, LANES), jnp.float32)
        for i in range(heads):
            raw, taps_in = [], []
            for kind in range(3):
                total, moved = conv_rows(ext, conv, col, offset, CHUNK, (3 * i + kind) * LANES, taps)
                raw.append(total)
                taps_in.append(moved)
            gates = [jax.nn.sigmoid(total) for total in raw]
            acts = [total * gate for total, gate in zip(raw, gates)]
            scales = [lax.rsqrt(jnp.sum(act * act, axis=-1, keepdims=True) + EPSILON) for act in acts[:2]]
            query, key, value = acts[0] * scales[0], acts[1] * scales[1], acts[2]
            strength = head_column(strengths, head + i)
            lanes = slice(i * LANES, (i + 1) * LANES)
            query_low, key_low = low(query), low(key)
            grams = mul_nt(jnp.concatenate([key_low, query_low], axis=0), key_low)
            gram = jnp.where(below, grams[:CHUNK], 0.0)
            scores = jnp.where(upto, grams[CHUNK:], 0.0)
            inverse = inv[0, i, j]
            update = upd[0, i, j]
            update = low(update[:, :LANES].astype(jnp.float32) + mul_nn(update[:, LANES:], entry[i]))
            state = states[0, i, j]
            state = low(state[:, :LANES].astype(jnp.float32) + mul_nn(state[:, LANES:], entry[i]))
            grad_out = grad_ref[rows, lanes]
            grad_state = grad_states[i]
            grad_state_low = low(grad_state)
            key_last = key_low * low(last)
            grad_update = mul_tn(scores, grad_out) + mul_nn(key_last, grad_state_low)
            grad_target = mul_tn(inverse, grad_update)
            weighted = strength * grad_target
            passed = carried * weighted
            out_carried = carried * grad_out.astype(jnp.float32)
            query_carried = query_low * low(carried)
            grad_states[i] = (
                keep * grad_state + mul_tn(query_carried, grad_out) - mul_tn(key_low, passed)
            )
            grad_scores = jnp.where(upto, mul_nt(grad_out, update), 0.0)
            grad_system = jnp.where(below, mul_nt(grad_target, update), 0.0)
            remainder = value - carried * mul_nn(key_low, state)
            grad_strength = jnp.sum(grad_target * remainder - grad_system * gram, axis=-1, keepdims=True)
            scaled = strength * grad_system
            from_state = mul_nt(jnp.concatenate([low(out_carried), low(passed)], axis=0), state)
            from_keys = mul_nn(jnp.concatenate([low(grad_scores), low(scaled + scaled.T)], axis=0), key_low)
            grad_query = from_state[:CHUNK] + from_keys[:CHUNK]
            grad_key = (
                mul_tn(grad_scores, query_low)
                + last * mul_nt(update, grad_state_low)
                - from_state[CHUNK:]
                - from_keys[CHUNK:]
            )
            grad_logit = grad_logit + jnp.where(
                iota((CHUNK, LANES), 1) == head + i, grad_strength * strength * (1.0 - strength), 0.0
            )
            grads = [
                scales[0] * (grad_query - query * jnp.sum(grad_query * query, axis=-1, keepdims=True)),
                scales[1] * (grad_key - key * jnp.sum(grad_key * key, axis=-1, keepdims=True)),
                weighted,
            ]
            position = iota((CHUNK, 1), 0) + offset
            for kind in range(3):
                gate, total = gates[kind], raw[kind]
                grad_conv = grads[kind] * gate * (1.0 + total * (1.0 - gate))
                lane = (3 * i + kind) * LANES
                for tap in range(taps):
                    back = taps - 1 - tap
                    part = jnp.sum(grad_conv * taps_in[kind][tap], axis=0, keepdims=True)
                    spot = (i, kind, tap)
                    tap_sums[spot] = part if spot not in tap_sums else tap_sums[spot] + part
                    back_part = jnp.where(
                        position - back >= col, grad_conv * conv[tap : tap + 1, lane : lane + LANES], 0.0
                    )
                    where = pl.ds(HALO + offset - back, CHUNK)
                    grad_ext[where, lane : lane + LANES] += back_part
        logits[rows] += grad_logit
    grad_pre[...] = low(grad_ext[HALO:])
    before[0] = grad_ext[:HALO]
    tail[0] = grad_ext[length:]
    for i in range(heads):
        for kind in range(3):
            lane = (3 * i + kind) * LANES
            for tap in range(taps):
                conv_grad[0, tap : tap + 1, lane : lane + LANES] = tap_sums[i, kind, tap]


def mixer_backward(
    pre, logit, bias, halo, conv, col, row, grad_mixed, inv, upd, states, start, end, taps, first, heads_here, group
):
    seqs, length = col.shape[0], col.shape[1]
    steps = heads_here // group
    chunks = length // CHUNK
    wide = 3 * LANES * group
    rows = seqs * length

    def spec(*tail):
        return pl.BlockSpec((1, group) + tail, lambda s, h: (s, h) + (0,) * len(tail))

    last = logit.shape[1] // LANES - 1
    part = pl.BlockSpec((1, HALO, wide), lambda s, h: (s, 0, h))
    edge = jax.ShapeDtypeStruct((seqs, HALO, 3 * LANES * heads_here), jnp.float32)
    return pl.pallas_call(
        functools.partial(backward_kernel, taps, group, first),
        grid=(seqs, steps),
        in_specs=[
            pl.BlockSpec((length, wide), lambda s, h: (s, h)),
            pl.BlockSpec((length, LANES), lambda s, h: (s, last)),
            pl.BlockSpec((1, LANES), lambda s, h: (0, 0)),
            part,
            pl.BlockSpec((conv.shape[0], wide), lambda s, h: (0, h)),
            pl.BlockSpec((1, length, 1), lambda s, h: (s, 0, 0)),
            pl.BlockSpec((1, 1, length), lambda s, h: (s, 0, 0)),
            pl.BlockSpec((length, LANES * group), lambda s, h: (s, h)),
            spec(chunks, CHUNK, CHUNK),
            spec(chunks, CHUNK, 2 * LANES),
            spec(chunks, LANES, 2 * LANES),
            spec(LANES, LANES),
            spec(LANES, LANES),
        ],
        out_specs=[
            pl.BlockSpec((length, wide), lambda s, h: (s, h)),
            part,
            part,
            part,
            pl.BlockSpec((length, LANES), lambda s, h: (s, 0)),
        ],
        out_shape=[
            jax.ShapeDtypeStruct((rows, 3 * LANES * heads_here), jnp.bfloat16),
            edge,
            edge,
            edge,
            jax.ShapeDtypeStruct((rows, LANES), jnp.float32),
        ],
        scratch_shapes=[
            pltpu.VMEM((length + HALO, wide), jnp.float32),
            pltpu.VMEM((length + HALO, wide), jnp.float32),
        ],
        compiler_params=pltpu.CompilerParams(vmem_limit_bytes=VMEM_BYTES),
        cost_estimate=pl.CostEstimate(
            flops=60 * rows * heads_here * CHUNK * LANES, bytes_accessed=40 * rows * heads_here * LANES, transcendentals=0
        ),
    )(pre, logit, bias, halo, conv, col, row, grad_mixed, inv, upd, states, start, end)


def mixed_rows_of(own, carry, start):
    return own + mul_nn(carry, start)


def output_kernel(heads, own, carry, start, gain, out):
    for i in range(heads):
        lanes = slice(i * LANES, (i + 1) * LANES)
        mixed = mixed_rows_of(own[:, lanes], carry[:, lanes], start[0, i])
        scale = lax.rsqrt(jnp.mean(mixed * mixed, axis=-1, keepdims=True) + HEAD_FLOOR)
        out[:, lanes] = low(mixed * scale * gain[...])


def output_backward_kernel(heads, own, carry, start, gain, grad, out, across, gain_grad):
    total = jnp.zeros((1, LANES), jnp.float32)
    for i in range(heads):
        lanes = slice(i * LANES, (i + 1) * LANES)
        carried = carry[:, lanes]
        mixed = mixed_rows_of(own[:, lanes], carried, start[0, i])
        scale = lax.rsqrt(jnp.mean(mixed * mixed, axis=-1, keepdims=True) + HEAD_FLOOR)
        normed = mixed * scale
        upper = grad[:, lanes].astype(jnp.float32)
        total = total + jnp.sum(upper * normed, axis=0, keepdims=True)
        weighted = upper * gain[...]
        back = scale * (weighted - normed * jnp.mean(weighted * normed, axis=-1, keepdims=True))
        out[:, lanes] = low(back)
        across[0, i] = mul_tn(carried, back)
    gain_grad[0, 0] = total


def mixer_output(own, carry, start, gain, group):
    seqs, heads_here = start.shape[:2]
    rows = own.shape[0]
    length = rows // seqs
    flat = pl.BlockSpec((length, LANES * group), lambda s, h: (s, h))
    square = pl.BlockSpec((1, group, LANES, LANES), lambda s, h: (s, h, 0, 0))
    return pl.pallas_call(
        functools.partial(output_kernel, group),
        grid=(seqs, heads_here // group),
        in_specs=[flat, flat, square, pl.BlockSpec((1, LANES), lambda s, h: (0, 0))],
        out_specs=flat,
        out_shape=jax.ShapeDtypeStruct(own.shape, jnp.bfloat16),
        compiler_params=pltpu.CompilerParams(vmem_limit_bytes=VMEM_BYTES),
        cost_estimate=pl.CostEstimate(
            flops=2 * own.size * LANES, bytes_accessed=8 * own.size, transcendentals=0
        ),
    )(own, carry, start, gain)


def mixer_output_backward(own, carry, start, gain, grad, first, group):
    seqs, heads_here = start.shape[:2]
    rows = own.shape[0]
    length = rows // seqs
    steps = heads_here // group
    flat = pl.BlockSpec((length, LANES * group), lambda s, h: (s, h))
    base = first // group
    shifted = pl.BlockSpec((length, LANES * group), lambda s, h: (s, base + h))
    square = pl.BlockSpec((1, group, LANES, LANES), lambda s, h: (s, h, 0, 0))
    return pl.pallas_call(
        functools.partial(output_backward_kernel, group),
        grid=(seqs, steps),
        in_specs=[flat, flat, square, pl.BlockSpec((1, LANES), lambda s, h: (0, 0)), shifted],
        out_specs=[flat, square, pl.BlockSpec((1, 1, 1, LANES), lambda s, h: (s, h, 0, 0))],
        out_shape=[
            jax.ShapeDtypeStruct(own.shape, jnp.bfloat16),
            jax.ShapeDtypeStruct(start.shape, jnp.float32),
            jax.ShapeDtypeStruct((seqs, steps, 1, LANES), jnp.float32),
        ],
        compiler_params=pltpu.CompilerParams(vmem_limit_bytes=VMEM_BYTES),
        cost_estimate=pl.CostEstimate(
            flops=4 * own.size * LANES, bytes_accessed=12 * own.size, transcendentals=0
        ),
    )(own, carry, start, gain, grad)


def ffn_kernel(mine, other, mine_grads, other_grads, gate_w, up_w, down_w, *outs):
    rows = jnp.concatenate([mine[...], other[...]], axis=0)
    grads = jnp.concatenate([mine_grads[...], other_grads[...]], axis=0)
    half = mine.shape[0]
    gate = mul_nt(rows, gate_w[...])
    up = mul_nt(rows, up_w[...])
    grad_hidden = mul_nt(grads, down_w[...])
    sigmoid = jax.nn.sigmoid(gate)
    active = gate * sigmoid
    kept = low(active * up)
    back_gate = low(grad_hidden * up * sigmoid * (1.0 + gate * (1.0 - sigmoid)))
    back_up = low(grad_hidden * active)
    grad_rows = low(mul_nn(back_gate, gate_w[...]) + mul_nn(back_up, up_w[...]))
    result = low(mul_nn(kept, down_w[...]))
    for side in range(2):
        here = slice(side * half, (side + 1) * half)
        acts, grad_out, result_out = outs[3 * side : 3 * side + 3]
        for kind, value in enumerate((back_gate, back_up, kept)):
            acts[kind] = value[here]
        grad_out[...] = grad_rows[here]
        result_out[...] = result[here]


def ffn_both(rows, grads, gate_up, down):
    count, width = rows[0].shape
    units = down.shape[0]
    tile = min(256, count)
    wide_rows = pl.BlockSpec((tile, width), lambda i: (i, 0))
    narrow = pl.BlockSpec((3, tile, units), lambda i: (0, i, 0))

    def third(index):
        return pl.BlockSpec((units, width), lambda i: (index, 0))

    flat = jax.ShapeDtypeStruct((count, width), jnp.bfloat16)
    outs = pl.pallas_call(
        ffn_kernel,
        grid=(count // tile,),
        in_specs=[wide_rows] * 4 + [third(0), third(1), third(0)],
        out_specs=[narrow, wide_rows, wide_rows] * 2,
        out_shape=[jax.ShapeDtypeStruct((3, count, units), jnp.bfloat16), flat, flat] * 2,
        compiler_params=pltpu.CompilerParams(vmem_limit_bytes=VMEM_BYTES),
        cost_estimate=pl.CostEstimate(
            flops=24 * count * width * units, bytes_accessed=16 * count * width + 6 * units * width, transcendentals=0
        ),
    )(*rows, *grads, gate_up, gate_up, down)
    return outs[:3], outs[3:]


def ffn_weights_kernel(count, lines, *refs):
    acts, rows, grads = refs[:count], refs[count : 2 * count], refs[2 * count : 3 * count]
    out, total = refs[-2:]
    part = out.shape[-1]

    def add(sources):
        for i in range(count):
            value = mul_tn(acts[i][0], sources[i][...])
            if i == 0:
                total[...] = value
            else:
                total[...] += value

    @pl.when(pl.program_id(0) < 2)
    def _():
        add(rows)

    @pl.when(pl.program_id(0) == 2)
    def _():
        add(grads)

    for line in range(lines):
        out[line, 0] = low(total[:, line * part : (line + 1) * part])


def ffn_weights(acts, rows, grads, lines, squares):
    count, width = len(acts), rows[0].shape[1]
    size, units = acts[0].shape[1:]
    block = width // squares
    part = block // lines
    act_spec = pl.BlockSpec((1, size, units), lambda k, c: (k, 0, 0))
    row_spec = pl.BlockSpec((size, block), lambda k, c: (0, jnp.where(k < 2, c, squares - 1)))
    grad_spec = pl.BlockSpec((size, block), lambda k, c: (0, jnp.where(k < 2, 0, c)))
    return pl.pallas_call(
        functools.partial(ffn_weights_kernel, count, lines),
        grid=(3, squares),
        in_specs=[act_spec] * count + [row_spec] * count + [grad_spec] * count,
        out_specs=pl.BlockSpec((lines, 1, units, part), lambda k, c: (0, k, 0, c)),
        out_shape=jax.ShapeDtypeStruct((lines, 3, units, squares * part), jnp.bfloat16),
        scratch_shapes=[pltpu.VMEM((units, block), jnp.float32)],
        compiler_params=pltpu.CompilerParams(vmem_limit_bytes=VMEM_BYTES),
        cost_estimate=pl.CostEstimate(
            flops=6 * count * size * width * units, bytes_accessed=8 * count * size * width, transcendentals=0
        ),
    )(*acts, *rows, *grads)


def block_columns(place, bit, size):
    return pl.multiple_of((place[0] ^ bit) * size, size)


def gathered_kernel(place, rows, *refs):
    out = refs[-1]
    own, beside, across, upper, lower = refs[:-1]
    size, half = own.shape[0], upper.shape[0]
    total = None
    for bit, skip, ref in ((0, 0, own), (1, 0, beside), (2, 0, across), (3, 0, upper), (3, half, lower)):
        start = pl.multiple_of(block_columns(place, bit, size) + skip, half)
        value = mul_nn(rows[:, pl.ds(start, ref.shape[0])], ref[...])
        total = value if total is None else total + value
    out[...] = total


def gathered_times(rows, place, pieces):
    count, width = rows.shape
    columns = pieces[0].shape[1]
    tile = min(256, count)
    whole = [pl.BlockSpec(piece.shape, lambda i, place: (0, 0)) for piece in pieces]
    return pl.pallas_call(
        gathered_kernel,
        grid_spec=pltpu.PrefetchScalarGridSpec(
            num_scalar_prefetch=1,
            grid=(count // tile,),
            in_specs=[pl.BlockSpec((tile, width), lambda i, place: (i, 0))] + whole,
            out_specs=pl.BlockSpec((tile, columns), lambda i, place: (i, 0)),
        ),
        out_shape=jax.ShapeDtypeStruct((count, columns), jnp.float32),
        compiler_params=pltpu.CompilerParams(vmem_limit_bytes=VMEM_BYTES),
        cost_estimate=pl.CostEstimate(
            flops=2 * count * width * columns, bytes_accessed=2 * (count + columns) * width, transcendentals=0
        ),
    )(jnp.reshape(place, (1,)).astype(jnp.int32), rows, *pieces)


def gathered_transposed_kernel(count, place, *refs):
    factors, pieces, out = refs[:count], refs[count:-1], refs[-1]
    size, half = pieces[0].shape[0], pieces[3].shape[0]
    for i, (bit, skip) in enumerate(((0, 0), (1, 0), (2, 0), (3, 0), (3, half))):
        start = pl.multiple_of(block_columns(place, bit, size) + skip, half)
        total = None
        for p in range(count):
            value = mul_nt(factors[p][...], pieces[5 * p + i][...])
            total = value if total is None else total + value
        out[:, pl.ds(start, pieces[i].shape[0])] = low(total)


def gathered_times_transposed(factors, place, pieces):
    count, rows = len(factors), factors[0].shape[0]
    width = 4 * pieces[0][0].shape[0]
    tile = min(256, rows)
    flat = [piece for some in pieces for piece in some]
    whole = [pl.BlockSpec(piece.shape, lambda i, place: (0, 0)) for piece in flat]
    wides = [pl.BlockSpec((tile, factor.shape[1]), lambda i, place: (i, 0)) for factor in factors]
    columns = sum(factor.shape[1] for factor in factors)
    return pl.pallas_call(
        functools.partial(gathered_transposed_kernel, count),
        grid_spec=pltpu.PrefetchScalarGridSpec(
            num_scalar_prefetch=1,
            grid=(rows // tile,),
            in_specs=wides + whole,
            out_specs=pl.BlockSpec((tile, width), lambda i, place: (i, 0)),
        ),
        out_shape=jax.ShapeDtypeStruct((rows, width), jnp.bfloat16),
        compiler_params=pltpu.CompilerParams(vmem_limit_bytes=VMEM_BYTES),
        cost_estimate=pl.CostEstimate(
            flops=2 * rows * width * columns, bytes_accessed=2 * (rows + columns) * width, transcendentals=0
        ),
    )(jnp.reshape(place, (1,)).astype(jnp.int32), *factors, *flat)


def join_kernel(squares, source, target):
    lines, _, columns = source.shape
    part = columns // squares
    for i in range(lines):
        for j in range(squares):
            at = (j * lines + i) * part
            target[:, at : at + part] = source[i, :, j * part : (j + 1) * part]


def columns_join(parts, squares):
    lines, rows, columns = parts.shape
    tile = 176 if rows % 176 == 0 else rows
    return pl.pallas_call(
        functools.partial(join_kernel, squares),
        grid=(rows // tile,),
        in_specs=[pl.BlockSpec((lines, tile, columns), lambda i: (0, i, 0))],
        out_specs=pl.BlockSpec((tile, lines * columns), lambda i: (i, 0)),
        out_shape=jax.ShapeDtypeStruct((rows, lines * columns), parts.dtype),
        compiler_params=pltpu.CompilerParams(vmem_limit_bytes=VMEM_BYTES),
        cost_estimate=pl.CostEstimate(flops=0, bytes_accessed=4 * parts.size, transcendentals=0),
    )(parts)


def flip(value, axis, bit):
    devices = range(lax.axis_size(axis))
    return lax.ppermute(value, axis, [(i, i ^ bit) for i in devices])


def shift(value, axis, distance):
    count = lax.axis_size(axis)
    return lax.ppermute(value, axis, [(i, (i + distance) % count) for i in range(count)])


def from_behind(block, axis, distance):
    devices = range(lax.axis_size(axis))
    route = [(i - distance, i) for i in devices if i - distance in devices]
    return lax.ppermute(block, axis, route)


def tie(value, *earlier):
    return lax.optimization_barrier((value,) + earlier)[0]


def put(buffer, piece, *start):
    return lax.dynamic_update_slice(buffer, piece, start)


def wide(value):
    return value.astype(jnp.float32)


def gather_line(shard):
    count, place = lax.axis_size("fsdp"), lax.axis_index("fsdp")
    pieces = [shard] + [shift(shard, "fsdp", d) for d in range(1, count)]
    order = [(place - i) % count for i in range(count)]
    return jnp.concatenate([lax.select_n(which, *pieces) for which in order], axis=0)


class Square:
    def __init__(self, own):
        self.own = own
        self.half = own.shape[0] // 2
        self.beside = flip(own, "ctx", 1)
        self.across = flip(own, "ctx", 2)

    def forward(self, *earlier):
        upper = self.beside[: self.half]
        lower = self.across[self.half :]
        if earlier:
            upper, lower = lax.optimization_barrier((upper, lower) + earlier)[:2]
        self.upper = flip(upper, "ctx", 2)
        self.lower = flip(lower, "ctx", 1)
        return self

    def done(self):
        return (self.upper, self.lower)

    def pieces(self):
        return [self.own, self.beside, self.across, self.upper, self.lower]

    def far(self):
        return jnp.concatenate([self.upper, self.lower], axis=0)


def both_sides(rows):
    if lax.axis_size("tp") == 2:
        return rows, flip(rows, "tp", 1)
    every = lax.all_gather(rows, "tp", axis=0, tiled=True)
    half = every.shape[0] // 2
    return every[:half], every[half:]


def core_sum(mine, other):
    if lax.axis_size("tp") == 2:
        return wide(mine) + wide(flip(other, "tp", 1))
    both = jnp.concatenate([mine, other], axis=0)
    return wide(lax.psum_scatter(both, "tp", scatter_dimension=0, tiled=True))


def neighbour_columns(rows):
    width = rows.shape[1] // 4
    place = lax.axis_index("ctx")
    return [lax.dynamic_slice_in_dim(rows, (place ^ bit) * width, width, 1) for bit in range(4)]


class Line:
    def __init__(self, own):
        count, place = lax.axis_size("fsdp"), lax.axis_index("fsdp")
        own = own.reshape(count, own.shape[0] // count, own.shape[1])

        def part(distance):
            return lax.dynamic_index_in_dim(own, (place + distance) % count, 0, keepdims=False)

        self.kept = part(0)
        self.sent = [low(part(distance)) for distance in range(1, count)]
        self.arrived = [shift(piece, "fsdp", distance + 1) for distance, piece in enumerate(self.sent)]

    def total(self, *late):
        total = self.kept
        for part in lax.optimization_barrier(tuple(self.arrived) + late)[: len(self.arrived)]:
            total = total + wide(part)
        return total


class Scatter:
    def __init__(self, columns, grads):
        self.columns, self.grads = columns, grads
        self.half = columns[0].shape[1] // 2
        self.mine = outer_rows(columns[0], grads)
        beside, across = (
            jnp.concatenate([self.side(3, 1), self.side(1, 1)], axis=1),
            jnp.concatenate([self.side(3, 0), self.side(2, 0)], axis=1),
        )
        self.sent = [low(outer_rows(beside, grads)), low(outer_rows(across, grads))]
        self.first = (flip(self.sent[0], "ctx", 1), flip(self.sent[1], "ctx", 2))

    def side(self, bit, lower):
        return self.columns[bit][:, lower * self.half : (lower + 1) * self.half]

    def second(self, *earlier):
        first = self.first
        if earlier:
            first = lax.optimization_barrier(first + earlier)[:2]
        beside, across = (wide(part) for part in first)
        upper = low(outer_rows(self.side(1, 0), self.grads) + across[: self.half])
        lower = low(outer_rows(self.side(2, 1), self.grads) + beside[: self.half])
        self.last = (flip(upper, "ctx", 1), flip(lower, "ctx", 2))
        self.kept = (beside, across)
        return upper, lower

    def own(self, *ties):
        beside_upper, across_lower = self.last
        if ties:
            beside_upper, across_lower = lax.optimization_barrier(self.last + ties)[:2]
        beside, across = self.kept
        own = self.mine
        upper = own[: self.half] + wide(beside_upper) + across[self.half :]
        lower = own[self.half :] + beside[self.half :] + wide(across_lower)
        return jnp.concatenate([upper, lower], axis=0)


def butterfly(value, axes):
    for axis in axes:
        count, bit = lax.axis_size(axis), 1
        while bit < count:
            value = value + flip(value, axis, bit)
            bit *= 2
    return value


def rms_scale(values, floor_value):
    return lax.rsqrt(jnp.mean(values * values, axis=-1, keepdims=True) + floor_value)


def norm_backward(grad_normed, inputs, scale, gain):
    normed = inputs * scale
    weighted = grad_normed * gain
    return (
        scale * (weighted - normed * jnp.mean(weighted * normed, axis=-1, keepdims=True)),
        normed,
    )


def times(left, right):
    return jnp.dot(left, right, preferred_element_type=jnp.float32)


def times_transposed(left, right):
    return lax.dot_general(
        left, right, (((1,), (1,)), ((), ())), preferred_element_type=jnp.float32
    )


def outer_rows(left, right):
    return lax.dot_general(
        left, right, (((0,), (0,)), ((), ())), preferred_element_type=jnp.float32
    )


def rows_mine(rows):
    count = rows.shape[1] // lax.axis_size("tp")
    return lax.dynamic_slice_in_dim(rows, lax.axis_index("tp") * count, count, 1)


def rows_scatter(partial):
    if lax.axis_size("tp") != 2:
        return wide(lax.psum_scatter(partial, "tp", scatter_dimension=1, tiled=True))
    count = partial.shape[1] // 2
    other = lax.dynamic_slice_in_dim(partial, (1 - lax.axis_index("tp")) * count, count, 1)
    return wide(rows_mine(partial)) + wide(flip(other, "tp", 1))


def rows_full(mine):
    if lax.axis_size("tp") != 2:
        return lax.all_gather(mine, "tp", axis=1, tiled=True)
    other = flip(mine, "tp", 1)
    lower = lax.axis_index("tp") == 0
    return jnp.concatenate([jnp.where(lower, mine, other), jnp.where(lower, other, mine)], axis=1)


def by_head(parts):
    heads = range(parts[0].shape[-1] // LANES)
    return jnp.concatenate([part[..., h * LANES : (h + 1) * LANES] for h in heads for part in parts], axis=-1)


def by_kind(joined):
    return [
        jnp.concatenate(
            [
                some[..., at : at + LANES]
                for some in joined
                for at in range(kind * LANES, some.shape[-1], 3 * LANES)
            ],
            axis=-1,
        )
        for kind in range(3)
    ]


def pass_states(own, transfer, forward, *beside):
    rule = "shij,shjk->shik" if forward == 1 else "shji,shjk->shik"
    leaving = own
    entered = low(jnp.zeros_like(own))
    for repeat in range(lax.axis_size("ctx") - 1):
        entered = from_behind(low(leaving), "ctx", forward)
        if repeat == 1 and beside:
            entered = tie(entered, *beside)
        leaving = own + jnp.einsum(rule, transfer, entered, preferred_element_type=jnp.float32)
    return wide(entered)


def local(
    block_input,
    doc_start,
    gain_mix,
    query_weight,
    key_weight,
    value_weight,
    beta_weight,
    beta_bias,
    conv_weight,
    gain_o,
    out_weight,
    gain_ffn,
    gate_weight,
    up_weight,
    down_weight,
    out_grad,
):
    seq_count, local_len, width = block_input.shape
    row_count = seq_count * local_len
    heads_here = beta_weight.shape[1]
    taps = conv_weight.shape[1]
    parts = 2 if heads_here % 2 == 0 else 1
    part_heads = heads_here // parts
    group = 2 if part_heads % 2 == 0 else 1
    part_cols = 3 * part_heads * LANES
    spare = LANES - heads_here
    units_here = gate_weight.shape[1]
    shard_rows = gate_weight.shape[0]

    joined = by_head([low(query_weight), low(key_weight), low(value_weight)])
    shards = [joined[:, p * part_cols : (p + 1) * part_cols] for p in range(parts)]
    shards[0] = jnp.concatenate([shards[0], jnp.pad(low(beta_weight), ((0, 0), (0, spare)))], axis=1)
    shards.append(low(out_weight).T)
    lines = []
    for shard in shards[:parts]:
        lines.append(gather_line(tie(shard, lines[-1]) if lines else shard))
    units = units_here // 4
    pieces = jnp.stack([low(gate_weight).T, low(up_weight).T, low(down_weight)])
    pieces = pieces.reshape(3, 4, units, shard_rows).transpose(1, 0, 2, 3)
    ffn_swapped = lax.all_to_all(pieces.reshape(4, 3 * units, shard_rows), "ctx", 0, 0)
    ffn_line = ffn_swapped.transpose(1, 0, 2).reshape(3 * units, 4 * shard_rows)
    line_count = lax.axis_size("fsdp")

    ctx_place = lax.axis_index("ctx")
    first_pos = ctx_place * local_len
    starts = doc_start - first_pos
    col, row = starts[:, :, None], starts[:, None, :]
    conv = by_head([conv_weight[0], conv_weight[1], conv_weight[2]])
    bias = jnp.pad(beta_bias, (0, spare))[None]
    gain_head = gain_o[None]
    tokens = block_input.reshape(row_count, width)
    inputs = wide(tokens)
    normed_mix = low(inputs * rms_scale(inputs, EPSILON) * gain_mix)
    grads_mine = rows_mine(out_grad).reshape(-1, width)

    square = Square(tie(lines[0], ffn_swapped)).forward(normed_mix)
    gate_up_parts = tie(ffn_line[None, : 2 * units], lines[parts - 1], *square.done())
    gate_up_parts = lax.all_gather(gate_up_parts, "fsdp", axis=0, tiled=True)
    down_parts = lax.all_gather(ffn_line[None, 2 * units :], "fsdp", axis=0, tiled=True)
    mix_full, kept, pre = [], [], []
    for p in range(parts):
        mix_full.append(square.pieces())
        arrived = square.done()
        ends = normed_mix.reshape(seq_count, local_len, width)[:, local_len - HALO :].reshape(seq_count * HALO, width)
        ends = gathered_times(ends, ctx_place, mix_full[p])
        ends = low(ends)
        halo = from_behind(ends[:, :part_cols].reshape(seq_count, HALO, part_cols), "ctx", 1)
        pre.append(gathered_times(tie(normed_mix, ends), ctx_place, mix_full[p]))
        if p == parts - 1:
            lines.append(gather_line(tie(shards[-1], pre[p])))
        square = Square(tie(lines[p + 1], halo, pre[p], *arrived))
        halo = wide(halo)
        convs = conv[:, p * part_cols : (p + 1) * part_cols]
        kept.append(
            [halo, convs]
            + list(
                mixer_forward(
                    pre[p], pre[0], bias, halo, convs, col, row, taps, p * part_heads, part_heads, group
                )
            )
        )
        square.forward(kept[p][2])
        if p == 0:
            grad_square = Square(tie(grads_mine, kept[p][2], *square.done()))
    out_full = square.pieces()

    inputs_mine = wide(tie(rows_mine(block_input).reshape(-1, width), kept[0][2]))
    gate_up_full = columns_join(gate_up_parts, 4)
    finals = jnp.concatenate([some[4] for some in kept], axis=1)
    transfer = low(finals[..., LANES:])
    first = tie(finals[..., :LANES], gate_up_full, grad_square.beside, grad_square.across)
    entering = pass_states(first, transfer, 1)
    entered = [entering[:, p * part_heads : (p + 1) * part_heads] for p in range(parts)]
    grad_square.forward(entering)
    grad_rows = [both_sides(part) for part in (grad_square.own, grad_square.beside, grad_square.across)]
    mixed_rows = []
    for p in range(parts):
        own, carry = kept[p][2:4]
        mixed_rows.append(mixer_output(own, carry, entered[p], gain_head, group))
    mixed_rows = jnp.concatenate(mixed_rows, axis=1)
    mixed_rows = tie(mixed_rows, *(other for _, other in grad_rows))
    grad_rows.append(both_sides(grad_square.far()))

    branch = gathered_times_transposed([mixed_rows], ctx_place, [out_full]).reshape(seq_count, local_len, width)
    branch = tie(branch, down_parts)
    residual = inputs_mine + rows_scatter(branch).reshape(-1, width)
    scale_ffn = rms_scale(residual, EPSILON)
    square = Square(low(residual * scale_ffn * gain_ffn))
    ffn_full = (gate_up_full, columns_join(down_parts, 4))

    ffn_rows = [both_sides(square.own)]
    ffn_out = [ffn_both(ffn_rows[0], grad_rows[0], *ffn_full)]
    square.forward(ffn_out[0][0][0])
    ffn_rows.append(both_sides(tie(square.beside, ffn_out[0][0][0])))
    ffn_out.append(ffn_both(ffn_rows[1], grad_rows[1], *ffn_full))
    ffn_rows.append(both_sides(tie(square.across, ffn_out[0][0][0])))
    mine, other = ffn_rows[2]
    ffn_out.append(ffn_both((tie(mine, ffn_out[1][0][0], *square.done()), other), grad_rows[2], *ffn_full))
    beside_sums, across_sums = (low(core_sum(*(side[1] for side in ffn_out[bit]))) for bit in (1, 2))
    ffn_rows.append(both_sides(square.far()))
    mine, other = ffn_rows[3]
    ffn_out.append(ffn_both((tie(mine, beside_sums, across_sums), other), grad_rows[3], *ffn_full))
    near_sums = (flip(beside_sums, "ctx", 1), flip(across_sums, "ctx", 2))
    mine, other = (side[1] for side in ffn_out[3])
    far_sums = low(core_sum(mine, tie(other, *near_sums)))
    acts = [side[0] for outs in ffn_out for side in outs]
    own_sums = core_sum(*(side[1] for side in ffn_out[0]))
    result_low = []
    for bit in (1, 2):
        mine, other = (side[2] for side in ffn_out[bit])
        result_low.append(low(core_sum(tie(mine, far_sums), other)))
    acts[0] = tie(acts[0], far_sums, own_sums, *result_low)
    far_sums = flip(far_sums, "ctx", 3)
    sums = ffn_weights(
        acts,
        [side for sides in ffn_rows for side in sides],
        [side for sides in grad_rows for side in sides],
        line_count,
        4,
    )

    far_sums, sums = lax.optimization_barrier((far_sums, sums))
    result_near = [flip(tie(part, far_sums), "ctx", bit) for part, bit in zip(result_low, (1, 2))]
    grad_normed = own_sums + wide(near_sums[0]) + wide(near_sums[1]) + wide(far_sums)
    back_ffn, unit_ffn = norm_backward(grad_normed, residual, scale_ffn, gain_ffn)
    grad_residual = wide(grads_mine) + back_ffn
    gain_ffn_part = jnp.sum(grad_normed * unit_ffn, axis=0)
    grad_branch = rows_full(low(grad_residual).reshape(seq_count, -1, width)).reshape(row_count, width)
    grad_heads = gathered_times(grad_branch, ctx_place, out_full)
    backs, acrosses, gain_o_part = [], [], 0.0
    for p in range(parts):
        _, _, own, carry, _, _, _, _ = kept[p]
        back, across, gain_part = mixer_output_backward(
            own, carry, entered[p], gain_head, grad_heads, p * part_heads, group
        )
        backs.append(back)
        acrosses.append(across)
        gain_o_part = gain_o_part + jnp.sum(gain_part, axis=(0, 1, 2))
    grad_end = pass_states(jnp.concatenate(acrosses, axis=1), transfer, -1, *result_near)
    total = lax.psum_scatter(sums, "fsdp", scatter_dimension=0, tiled=True)

    out_grad_w = low(outer_rows(grad_branch, mixed_rows))
    out_part = out_grad_w
    out_grad_w = lax.psum_scatter(out_grad_w, ("ctx", "fsdp"), scatter_dimension=0, tiled=True)

    mine, other = (side[2] for side in ffn_out[0])
    result_own = core_sum(mine, tie(other, grad_branch))
    mine, other = (side[2] for side in ffn_out[3])
    result_far = flip(tie(low(core_sum(mine, tie(other, grad_branch))), grad_end), "ctx", 3)
    columns = neighbour_columns(normed_mix)
    grad_mixes, mix_grads, conv_parts = [None] * parts, [None] * parts, [None] * parts
    logits = 0.0
    scatter = None
    for p in reversed(range(parts)):
        halo, convs, own, carry, final, inverses, updates, states = kept[p]
        heads = slice(p * part_heads, (p + 1) * part_heads)
        back = tie(backs[p], out_part) if scatter is None else tie(backs[p], total, *scatter.sent)
        grad_mix, tail, before, conv_parts[p], logit = mixer_backward(
            pre[p], pre[0], bias, halo, convs, col, row, back, inverses, updates, states,
            entered[p], grad_end[:, heads], taps, p * part_heads, part_heads, group,
        )
        logits = logits + logit
        tail = low(tail + from_behind(before, "ctx", -1))
        grad_mix = put(grad_mix.reshape(seq_count, local_len, -1), tail, 0, local_len - HALO, 0)
        grad_mix = grad_mix.reshape(row_count, -1)
        if scatter is not None:
            earlier_ready = scatter.second(before)
            earlier_scatter = scatter
        else:
            grad_mix = tie(grad_mix, result_far)
        if p == 0:
            grad_mix = jnp.concatenate([grad_mix, low(logits)], axis=1)
        grad_mixes[p] = grad_mix
        scatter = Scatter(columns, grad_mix)
        if p > 0:
            result_far = tie(result_far, *scatter.sent)
    result = result_own + wide(result_near[0]) + wide(result_near[1])
    result = result + wide(result_far)
    block_output = rows_full(low(residual + result).reshape(seq_count, -1, width))
    ready = (block_output, scatter.mine)
    if parts > 1:
        ready = ready + tuple(earlier_ready) + (earlier_scatter.mine,)
    ready = scatter.second(*ready)
    grad_mixes[0] = tie(grad_mixes[0], *ready)
    mix_back = tie(gathered_times_transposed(grad_mixes, ctx_place, mix_full), *scatter.last)
    mix_back = rows_scatter(mix_back.reshape(seq_count, local_len, width)).reshape(-1, width)
    back_mix, unit_mix = norm_backward(mix_back, inputs_mine, rms_scale(inputs_mine, EPSILON), gain_mix)
    input_grad = rows_full(low(grad_residual + back_mix).reshape(seq_count, -1, width))
    gain_mix_part = jnp.sum(mix_back * unit_mix, axis=0)

    conv_cols = jnp.concatenate([jnp.sum(part, axis=0)[:taps] for part in conv_parts], axis=1)
    gains = butterfly(jnp.concatenate([gain_mix_part, gain_ffn_part, gain_o_part]), ("tp",))
    sums = jnp.concatenate([gains, conv_cols.reshape(-1), jnp.sum(logits, axis=0)])
    last_line = Line(scatter.own())
    for p in range(1, parts):
        own = low(earlier_scatter.own(*last_line.sent))
        mix_grads[p] = wide(lax.psum_scatter(own, "fsdp", scatter_dimension=0, tiled=True))
    sums = butterfly(tie(sums, input_grad, *last_line.sent), ("ctx", "fsdp"))
    mix_grads[0] = last_line.total(sums)
    query_grad, key_grad, value_grad = by_kind([grad[:, :part_cols] for grad in mix_grads])
    beta_grad = mix_grads[0][:, part_cols : part_cols + heads_here]
    ends = [width, 2 * width, 2 * width + LANES, sums.shape[0] - LANES]
    gain_mix_grad, gain_ffn_grad, gain_o_grad, conv_grad, bias_grad = jnp.split(sums, ends)
    conv_grad = jnp.stack(by_kind([conv_grad.reshape(taps, -1)]))
    bias_grad = bias_grad[:heads_here]
    out_grad_w = wide(tie(out_grad_w, *scatter.last)).T
    pieces = tie(total, *scatter.last).reshape(3 * units, 4, shard_rows).transpose(1, 0, 2)
    arrived = lax.all_to_all(pieces, "ctx", 0, 0).reshape(4, 3, units, shard_rows)
    gate_grad, up_grad, down_grad = (wide(arrived[:, i].reshape(units_here, shard_rows)) for i in range(3))

    return (
        block_output,
        input_grad,
        gain_mix_grad,
        query_grad,
        key_grad,
        value_grad,
        beta_grad,
        bias_grad,
        conv_grad,
        gain_o_grad,
        out_grad_w,
        gain_ffn_grad,
        gate_grad.T,
        up_grad.T,
        down_grad,
    )


def solution(mesh):
    placed = (
        P("fsdp", "ctx", None),
        P("fsdp", "ctx"),
        P(),
        P(("ctx", "fsdp"), "tp"),
        P(("ctx", "fsdp"), "tp"),
        P(("ctx", "fsdp"), "tp"),
        P(("ctx", "fsdp"), "tp"),
        P("tp"),
        P(None, None, "tp"),
        P(),
        P("tp", ("ctx", "fsdp")),
        P(),
        P(("ctx", "fsdp"), "tp"),
        P(("ctx", "fsdp"), "tp"),
        P("tp", ("ctx", "fsdp")),
        P("fsdp", "ctx", None),
    )
    return jax.shard_map(
        local,
        mesh=mesh,
        in_specs=placed,
        out_specs=(
            P("fsdp", "ctx", None),
            P("fsdp", "ctx", None),
            P(),
            P(("ctx", "fsdp"), "tp"),
            P(("ctx", "fsdp"), "tp"),
            P(("ctx", "fsdp"), "tp"),
            P(("ctx", "fsdp"), "tp"),
            P("tp"),
            P(None, None, "tp"),
            P(),
            P("tp", ("ctx", "fsdp")),
            P(),
            P(("ctx", "fsdp"), "tp"),
            P(("ctx", "fsdp"), "tp"),
            P("tp", ("ctx", "fsdp")),
        ),
        check_vma=False,
    )
```

```python
import functools
import math
import jax
import jax.numpy as jnp
from jax import lax
from jax.experimental import pallas as pl
from jax.experimental.pallas import tpu as pltpu
from jax.sharding import PartitionSpec as P

LANES = 128
CHUNK = 128
HALO = 8
EPSILON = 1e-06
HEAD_FLOOR = 0.01
VMEM_BYTES = 60 * 1024 * 1024


def low(value):
    return value.astype(jnp.bfloat16)


def mul_nn(left, right):
    return lax.dot_general(low(left), low(right), (((1,), (0,)), ((), ())), preferred_element_type=jnp.float32)


def mul_nt(left, right):
    return lax.dot_general(low(left), low(right), (((1,), (1,)), ((), ())), preferred_element_type=jnp.float32)


def mul_tn(left, right):
    return lax.dot_general(low(left), low(right), (((0,), (0,)), ((), ())), preferred_element_type=jnp.float32)


def iota(shape, axis):
    return lax.broadcasted_iota(jnp.int32, shape, axis)


def chunk_masks(col, row, first):
    size = col.shape[0]
    same = col == row
    order, other = iota((size, size), 0), iota((size, size), 1)
    upto = same & (order >= other)
    below = same & (order > other)
    carried = (col < first).astype(jnp.float32)
    last = (col == row[:, size - 1 :]).astype(jnp.float32)
    keep = (row[:, size - 1 :] < first).astype(jnp.float32)
    return upto, below, carried, last, keep


def invert_units(systems):
    size = systems[0].shape[0]
    order, other = iota((size, size), 0), iota((size, size), 1)
    identity = (order == other).astype(jnp.float32)
    span = 1
    found = None
    while span < size:
        pair = (order // (2 * span) == other // (2 * span)) & (order // span != other // span)
        parts = [jnp.where(pair, system, 0.0) for system in systems]
        if found is None:
            found = [identity - part for part in parts]
        else:
            right = [mul_nn(part, value) for part, value in zip(parts, found)]
            found = [value - mul_nn(value, part) for value, part in zip(found, right)]
        span *= 2
    return found


def conv_rows(ext, conv, col, offset, size, lane, taps):
    total = None
    moved = []
    position = iota((size, 1), 0) + offset
    for tap in range(taps):
        back = taps - 1 - tap
        values = ext[pl.ds(HALO + offset - back, size), lane : lane + LANES]
        values = jnp.where(position - back >= col, values, 0.0)
        moved.append(values)
        term = conv[tap : tap + 1, lane : lane + LANES] * values
        total = term if total is None else total + term
    return total, moved


def unit(values):
    return values * lax.rsqrt(jnp.sum(values * values, axis=-1, keepdims=True) + EPSILON)


def head_column(values, head):
    return jnp.sum(jnp.where(iota(values.shape, 1) == head, values, 0.0), axis=-1, keepdims=True)


def forward_kernel(taps, heads, first, pre, beta, bias, halo, conv, col_ref, row_ref, own, carry, final, inv, upd, states, ext):
    length = pre.shape[0]
    ext[:HALO] = halo[0]
    ext[HALO:] = pre[...]
    head = first + pl.program_id(1) * heads
    jobs = [(i, j) for j in range(length // CHUNK) for i in range(heads)]
    data = {}
    for j in range(length // CHUNK):
        rows = pl.ds(j * CHUNK, CHUNK)
        col, row = col_ref[0, rows], row_ref[0, :, rows]
        masks = chunk_masks(col, row, j * CHUNK)
        strengths = jax.nn.sigmoid(beta[rows] + bias[...])
        for i in range(heads):
            acts = []
            for kind in range(3):
                total, _ = conv_rows(ext, conv, col, j * CHUNK, CHUNK, (3 * i + kind) * LANES, taps)
                acts.append(total * jax.nn.sigmoid(total))
            query, key, value = unit(acts[0]), unit(acts[1]), acts[2]
            strength = head_column(strengths, head + i)
            grams = mul_nt(jnp.concatenate([low(key), low(query)], axis=0), key)
            system = jnp.where(masks[1], strength * grams[:CHUNK], 0.0)
            scores = low(jnp.where(masks[0], grams[CHUNK:], 0.0))
            data[i, j] = (low(query), low(key), value, strength, scores, masks, system)
    inverses = dict(zip(jobs, invert_units([data[job][6] for job in jobs])))
    for i in range(heads):
        state = jnp.concatenate(
            [
                jnp.zeros((LANES, LANES), jnp.float32),
                (iota((LANES, LANES), 0) == iota((LANES, LANES), 1)).astype(jnp.float32),
            ],
            axis=1,
        )
        final[0, i] = state
    for j in range(length // CHUNK):
        rows = pl.ds(j * CHUNK, CHUNK)
        for i in range(heads):
            query, key, value, strength, scores, masks, _ = data[i, j]
            _, _, carried, last, keep = masks
            inverse = low(inverses[i, j])
            state = final[0, i]
            state_low = low(state)
            read = mul_nn(jnp.concatenate([key, query], axis=0), state_low)
            wide = jnp.concatenate([value, jnp.zeros_like(value)], axis=1)
            targets = strength * (wide - carried * read[:CHUNK])
            update = low(mul_nn(inverse, targets))
            result = carried * read[CHUNK:] + mul_nn(scores, update)
            final[0, i] = keep * state + mul_tn(key * low(last), update)
            lanes = slice(i * LANES, (i + 1) * LANES)
            own[rows, lanes] = result[:, :LANES]
            carry[rows, lanes] = low(result[:, LANES:])
            inv[0, i, j] = inverse
            upd[0, i, j] = update
            states[0, i, j] = state_low


def mixer_forward(pre, logit, bias, halo, conv, col, row, taps, first, heads_here, group):
    seqs, length = col.shape[0], col.shape[1]
    steps = heads_here // group
    chunks = length // CHUNK
    wide = 3 * LANES * group
    rows = seqs * length

    def tile(*tail, kind):
        return jax.ShapeDtypeStruct((seqs, heads_here) + tail, kind)

    def spec(*tail):
        return pl.BlockSpec((1, group) + tail, lambda s, h: (s, h) + (0,) * len(tail))

    flat = pl.BlockSpec((length, LANES * group), lambda s, h: (s, h))
    last = logit.shape[1] // LANES - 1
    return pl.pallas_call(
        functools.partial(forward_kernel, taps, group, first),
        grid=(seqs, steps),
        in_specs=[
            pl.BlockSpec((length, wide), lambda s, h: (s, h)),
            pl.BlockSpec((length, LANES), lambda s, h: (s, last)),
            pl.BlockSpec((1, LANES), lambda s, h: (0, 0)),
            pl.BlockSpec((1, HALO, wide), lambda s, h: (s, 0, h)),
            pl.BlockSpec((conv.shape[0], wide), lambda s, h: (0, h)),
            pl.BlockSpec((1, length, 1), lambda s, h: (s, 0, 0)),
            pl.BlockSpec((1, 1, length), lambda s, h: (s, 0, 0)),
        ],
        out_specs=[
            flat,
            flat,
            spec(LANES, 2 * LANES),
            spec(chunks, CHUNK, CHUNK),
            spec(chunks, CHUNK, 2 * LANES),
            spec(chunks, LANES, 2 * LANES),
        ],
        out_shape=[
            jax.ShapeDtypeStruct((rows, heads_here * LANES), jnp.float32),
            jax.ShapeDtypeStruct((rows, heads_here * LANES), jnp.bfloat16),
            tile(LANES, 2 * LANES, kind=jnp.float32),
            tile(chunks, CHUNK, CHUNK, kind=jnp.bfloat16),
            tile(chunks, CHUNK, 2 * LANES, kind=jnp.bfloat16),
            tile(chunks, LANES, 2 * LANES, kind=jnp.bfloat16),
        ],
        scratch_shapes=[pltpu.VMEM((length + HALO, wide), jnp.float32)],
        compiler_params=pltpu.CompilerParams(vmem_limit_bytes=VMEM_BYTES),
        cost_estimate=pl.CostEstimate(
            flops=60 * rows * heads_here * CHUNK * LANES, bytes_accessed=40 * rows * heads_here * LANES, transcendentals=0
        ),
    )(pre, logit, bias, halo, conv, col, row)


def backward_kernel(
    taps, heads, first, pre, beta, bias, halo, conv, col_ref, row_ref, grad_ref, inv, upd, states, start, end,
    grad_pre, tail, before, conv_grad, logits, ext, grad_ext,
):
    length = pre.shape[0]
    step = pl.program_id(1)
    head = first + step * heads
    ext[:HALO] = halo[0]
    ext[HALO:] = pre[...]
    grad_ext[...] = jnp.zeros_like(grad_ext)

    @pl.when(step == 0)
    def _():
        logits[...] = jnp.zeros_like(logits)

    grad_states = [end[0, i] for i in range(heads)]
    entry = [low(start[0, i]) for i in range(heads)]
    tap_sums = {}
    for j in reversed(range(length // CHUNK)):
        offset = j * CHUNK
        rows = pl.ds(offset, CHUNK)
        col, row = col_ref[0, rows], row_ref[0, :, rows]
        upto, below, carried, last, keep = chunk_masks(col, row, offset)
        strengths = jax.nn.sigmoid(beta[rows] + bias[...])
        grad_logit = jnp.zeros((CHUNK, LANES), jnp.float32)
        for i in range(heads):
            raw, taps_in = [], []
            for kind in range(3):
                total, moved = conv_rows(ext, conv, col, offset, CHUNK, (3 * i + kind) * LANES, taps)
                raw.append(total)
                taps_in.append(moved)
            gates = [jax.nn.sigmoid(total) for total in raw]
            acts = [total * gate for total, gate in zip(raw, gates)]
            scales = [lax.rsqrt(jnp.sum(act * act, axis=-1, keepdims=True) + EPSILON) for act in acts[:2]]
            query, key, value = acts[0] * scales[0], acts[1] * scales[1], acts[2]
            strength = head_column(strengths, head + i)
            lanes = slice(i * LANES, (i + 1) * LANES)
            query_low, key_low = low(query), low(key)
            grams = mul_nt(jnp.concatenate([key_low, query_low], axis=0), key_low)
            gram = jnp.where(below, grams[:CHUNK], 0.0)
            scores = jnp.where(upto, grams[CHUNK:], 0.0)
            inverse = inv[0, i, j]
            update = upd[0, i, j]
            update = low(update[:, :LANES].astype(jnp.float32) + mul_nn(update[:, LANES:], entry[i]))
            state = states[0, i, j]
            state = low(state[:, :LANES].astype(jnp.float32) + mul_nn(state[:, LANES:], entry[i]))
            grad_out = grad_ref[rows, lanes]
            grad_state = grad_states[i]
            grad_state_low = low(grad_state)
            key_last = key_low * low(last)
            grad_update = mul_tn(scores, grad_out) + mul_nn(key_last, grad_state_low)
            grad_target = mul_tn(inverse, grad_update)
            weighted = strength * grad_target
            passed = carried * weighted
            out_carried = carried * grad_out.astype(jnp.float32)
            query_carried = query_low * low(carried)
            grad_states[i] = (
                keep * grad_state + mul_tn(query_carried, grad_out) - mul_tn(key_low, passed)
            )
            grad_scores = jnp.where(upto, mul_nt(grad_out, update), 0.0)
            grad_system = jnp.where(below, mul_nt(grad_target, update), 0.0)
            remainder = value - carried * mul_nn(key_low, state)
            grad_strength = jnp.sum(grad_target * remainder - grad_system * gram, axis=-1, keepdims=True)
            scaled = strength * grad_system
            from_state = mul_nt(jnp.concatenate([low(out_carried), low(passed)], axis=0), state)
            from_keys = mul_nn(jnp.concatenate([low(grad_scores), low(scaled + scaled.T)], axis=0), key_low)
            grad_query = from_state[:CHUNK] + from_keys[:CHUNK]
            grad_key = (
                mul_tn(grad_scores, query_low)
                + last * mul_nt(update, grad_state_low)
                - from_state[CHUNK:]
                - from_keys[CHUNK:]
            )
            grad_logit = grad_logit + jnp.where(
                iota((CHUNK, LANES), 1) == head + i, grad_strength * strength * (1.0 - strength), 0.0
            )
            grads = [
                scales[0] * (grad_query - query * jnp.sum(grad_query * query, axis=-1, keepdims=True)),
                scales[1] * (grad_key - key * jnp.sum(grad_key * key, axis=-1, keepdims=True)),
                weighted,
            ]
            position = iota((CHUNK, 1), 0) + offset
            for kind in range(3):
                gate, total = gates[kind], raw[kind]
                grad_conv = grads[kind] * gate * (1.0 + total * (1.0 - gate))
                lane = (3 * i + kind) * LANES
                for tap in range(taps):
                    back = taps - 1 - tap
                    part = jnp.sum(grad_conv * taps_in[kind][tap], axis=0, keepdims=True)
                    spot = (i, kind, tap)
                    tap_sums[spot] = part if spot not in tap_sums else tap_sums[spot] + part
                    back_part = jnp.where(
                        position - back >= col, grad_conv * conv[tap : tap + 1, lane : lane + LANES], 0.0
                    )
                    where = pl.ds(HALO + offset - back, CHUNK)
                    grad_ext[where, lane : lane + LANES] += back_part
        logits[rows] += grad_logit
    grad_pre[...] = low(grad_ext[HALO:])
    before[0] = grad_ext[:HALO]
    tail[0] = grad_ext[length:]
    for i in range(heads):
        for kind in range(3):
            lane = (3 * i + kind) * LANES
            for tap in range(taps):
                conv_grad[0, tap : tap + 1, lane : lane + LANES] = tap_sums[i, kind, tap]


def mixer_backward(
    pre, logit, bias, halo, conv, col, row, grad_mixed, inv, upd, states, start, end, taps, first, heads_here, group
):
    seqs, length = col.shape[0], col.shape[1]
    steps = heads_here // group
    chunks = length // CHUNK
    wide = 3 * LANES * group
    rows = seqs * length

    def spec(*tail):
        return pl.BlockSpec((1, group) + tail, lambda s, h: (s, h) + (0,) * len(tail))

    last = logit.shape[1] // LANES - 1
    part = pl.BlockSpec((1, HALO, wide), lambda s, h: (s, 0, h))
    edge = jax.ShapeDtypeStruct((seqs, HALO, 3 * LANES * heads_here), jnp.float32)
    return pl.pallas_call(
        functools.partial(backward_kernel, taps, group, first),
        grid=(seqs, steps),
        in_specs=[
            pl.BlockSpec((length, wide), lambda s, h: (s, h)),
            pl.BlockSpec((length, LANES), lambda s, h: (s, last)),
            pl.BlockSpec((1, LANES), lambda s, h: (0, 0)),
            part,
            pl.BlockSpec((conv.shape[0], wide), lambda s, h: (0, h)),
            pl.BlockSpec((1, length, 1), lambda s, h: (s, 0, 0)),
            pl.BlockSpec((1, 1, length), lambda s, h: (s, 0, 0)),
            pl.BlockSpec((length, LANES * group), lambda s, h: (s, h)),
            spec(chunks, CHUNK, CHUNK),
            spec(chunks, CHUNK, 2 * LANES),
            spec(chunks, LANES, 2 * LANES),
            spec(LANES, LANES),
            spec(LANES, LANES),
        ],
        out_specs=[
            pl.BlockSpec((length, wide), lambda s, h: (s, h)),
            part,
            part,
            part,
            pl.BlockSpec((length, LANES), lambda s, h: (s, 0)),
        ],
        out_shape=[
            jax.ShapeDtypeStruct((rows, 3 * LANES * heads_here), jnp.bfloat16),
            edge,
            edge,
            edge,
            jax.ShapeDtypeStruct((rows, LANES), jnp.float32),
        ],
        scratch_shapes=[
            pltpu.VMEM((length + HALO, wide), jnp.float32),
            pltpu.VMEM((length + HALO, wide), jnp.float32),
        ],
        compiler_params=pltpu.CompilerParams(vmem_limit_bytes=VMEM_BYTES),
        cost_estimate=pl.CostEstimate(
            flops=60 * rows * heads_here * CHUNK * LANES, bytes_accessed=40 * rows * heads_here * LANES, transcendentals=0
        ),
    )(pre, logit, bias, halo, conv, col, row, grad_mixed, inv, upd, states, start, end)


def mixed_rows_of(own, carry, start):
    return own + mul_nn(carry, start)


def output_kernel(heads, own, carry, start, gain, out):
    for i in range(heads):
        lanes = slice(i * LANES, (i + 1) * LANES)
        mixed = mixed_rows_of(own[:, lanes], carry[:, lanes], start[0, i])
        scale = lax.rsqrt(jnp.mean(mixed * mixed, axis=-1, keepdims=True) + HEAD_FLOOR)
        out[:, lanes] = low(mixed * scale * gain[...])


def output_backward_kernel(heads, own, carry, start, gain, grad, out, across, gain_grad):
    total = jnp.zeros((1, LANES), jnp.float32)
    for i in range(heads):
        lanes = slice(i * LANES, (i + 1) * LANES)
        carried = carry[:, lanes]
        mixed = mixed_rows_of(own[:, lanes], carried, start[0, i])
        scale = lax.rsqrt(jnp.mean(mixed * mixed, axis=-1, keepdims=True) + HEAD_FLOOR)
        normed = mixed * scale
        upper = grad[:, lanes].astype(jnp.float32)
        total = total + jnp.sum(upper * normed, axis=0, keepdims=True)
        weighted = upper * gain[...]
        back = scale * (weighted - normed * jnp.mean(weighted * normed, axis=-1, keepdims=True))
        out[:, lanes] = low(back)
        across[0, i] = mul_tn(carried, back)
    gain_grad[0, 0] = total


def mixer_output(own, carry, start, gain, group):
    seqs, heads_here = start.shape[:2]
    rows = own.shape[0]
    length = rows // seqs
    flat = pl.BlockSpec((length, LANES * group), lambda s, h: (s, h))
    square = pl.BlockSpec((1, group, LANES, LANES), lambda s, h: (s, h, 0, 0))
    return pl.pallas_call(
        functools.partial(output_kernel, group),
        grid=(seqs, heads_here // group),
        in_specs=[flat, flat, square, pl.BlockSpec((1, LANES), lambda s, h: (0, 0))],
        out_specs=flat,
        out_shape=jax.ShapeDtypeStruct(own.shape, jnp.bfloat16),
        compiler_params=pltpu.CompilerParams(vmem_limit_bytes=VMEM_BYTES),
        cost_estimate=pl.CostEstimate(
            flops=2 * own.size * LANES, bytes_accessed=8 * own.size, transcendentals=0
        ),
    )(own, carry, start, gain)


def mixer_output_backward(own, carry, start, gain, grad, first, group):
    seqs, heads_here = start.shape[:2]
    rows = own.shape[0]
    length = rows // seqs
    steps = heads_here // group
    flat = pl.BlockSpec((length, LANES * group), lambda s, h: (s, h))
    base = first // group
    shifted = pl.BlockSpec((length, LANES * group), lambda s, h: (s, base + h))
    square = pl.BlockSpec((1, group, LANES, LANES), lambda s, h: (s, h, 0, 0))
    return pl.pallas_call(
        functools.partial(output_backward_kernel, group),
        grid=(seqs, steps),
        in_specs=[flat, flat, square, pl.BlockSpec((1, LANES), lambda s, h: (0, 0)), shifted],
        out_specs=[flat, square, pl.BlockSpec((1, 1, 1, LANES), lambda s, h: (s, h, 0, 0))],
        out_shape=[
            jax.ShapeDtypeStruct(own.shape, jnp.bfloat16),
            jax.ShapeDtypeStruct(start.shape, jnp.float32),
            jax.ShapeDtypeStruct((seqs, steps, 1, LANES), jnp.float32),
        ],
        compiler_params=pltpu.CompilerParams(vmem_limit_bytes=VMEM_BYTES),
        cost_estimate=pl.CostEstimate(
            flops=4 * own.size * LANES, bytes_accessed=12 * own.size, transcendentals=0
        ),
    )(own, carry, start, gain, grad)


def ffn_kernel(mine, other, mine_grads, other_grads, gate_w, up_w, down_w, *outs):
    rows = jnp.concatenate([mine[...], other[...]], axis=0)
    grads = jnp.concatenate([mine_grads[...], other_grads[...]], axis=0)
    half = mine.shape[0]
    gate = mul_nt(rows, gate_w[...])
    up = mul_nt(rows, up_w[...])
    grad_hidden = mul_nt(grads, down_w[...])
    sigmoid = jax.nn.sigmoid(gate)
    active = gate * sigmoid
    kept = low(active * up)
    back_gate = low(grad_hidden * up * sigmoid * (1.0 + gate * (1.0 - sigmoid)))
    back_up = low(grad_hidden * active)
    grad_rows = low(mul_nn(back_gate, gate_w[...]) + mul_nn(back_up, up_w[...]))
    result = low(mul_nn(kept, down_w[...]))
    for side in range(2):
        here = slice(side * half, (side + 1) * half)
        acts, grad_out, result_out = outs[3 * side : 3 * side + 3]
        for kind, value in enumerate((back_gate, back_up, kept)):
            acts[kind] = value[here]
        grad_out[...] = grad_rows[here]
        result_out[...] = result[here]


def ffn_both(rows, grads, gate_up, down):
    count, width = rows[0].shape
    units = down.shape[0]
    tile = min(256, count)
    wide_rows = pl.BlockSpec((tile, width), lambda i: (i, 0))
    narrow = pl.BlockSpec((3, tile, units), lambda i: (0, i, 0))

    def third(index):
        return pl.BlockSpec((units, width), lambda i: (index, 0))

    flat = jax.ShapeDtypeStruct((count, width), jnp.bfloat16)
    outs = pl.pallas_call(
        ffn_kernel,
        grid=(count // tile,),
        in_specs=[wide_rows] * 4 + [third(0), third(1), third(0)],
        out_specs=[narrow, wide_rows, wide_rows] * 2,
        out_shape=[jax.ShapeDtypeStruct((3, count, units), jnp.bfloat16), flat, flat] * 2,
        compiler_params=pltpu.CompilerParams(vmem_limit_bytes=VMEM_BYTES),
        cost_estimate=pl.CostEstimate(
            flops=24 * count * width * units, bytes_accessed=16 * count * width + 6 * units * width, transcendentals=0
        ),
    )(*rows, *grads, gate_up, gate_up, down)
    return outs[:3], outs[3:]


def ffn_weights_kernel(count, lines, *refs):
    acts, rows, grads = refs[:count], refs[count : 2 * count], refs[2 * count : 3 * count]
    out, total = refs[-2:]
    part = out.shape[-1]

    def add(sources):
        for i in range(count):
            value = mul_tn(acts[i][0], sources[i][...])
            if i == 0:
                total[...] = value
            else:
                total[...] += value

    @pl.when(pl.program_id(0) < 2)
    def _():
        add(rows)

    @pl.when(pl.program_id(0) == 2)
    def _():
        add(grads)

    for line in range(lines):
        out[line, 0] = low(total[:, line * part : (line + 1) * part])


def ffn_weights(acts, rows, grads, lines, squares):
    count, width = len(acts), rows[0].shape[1]
    size, units = acts[0].shape[1:]
    block = width // squares
    part = block // lines
    act_spec = pl.BlockSpec((1, size, units), lambda k, c: (k, 0, 0))
    row_spec = pl.BlockSpec((size, block), lambda k, c: (0, jnp.where(k < 2, c, squares - 1)))
    grad_spec = pl.BlockSpec((size, block), lambda k, c: (0, jnp.where(k < 2, 0, c)))
    return pl.pallas_call(
        functools.partial(ffn_weights_kernel, count, lines),
        grid=(3, squares),
        in_specs=[act_spec] * count + [row_spec] * count + [grad_spec] * count,
        out_specs=pl.BlockSpec((lines, 1, units, part), lambda k, c: (0, k, 0, c)),
        out_shape=jax.ShapeDtypeStruct((lines, 3, units, squares * part), jnp.bfloat16),
        scratch_shapes=[pltpu.VMEM((units, block), jnp.float32)],
        compiler_params=pltpu.CompilerParams(vmem_limit_bytes=VMEM_BYTES),
        cost_estimate=pl.CostEstimate(
            flops=6 * count * size * width * units, bytes_accessed=8 * count * size * width, transcendentals=0
        ),
    )(*acts, *rows, *grads)


def block_columns(place, bit, size):
    return pl.multiple_of((place[0] ^ bit) * size, size)


def gathered_kernel(place, rows, *refs):
    out = refs[-1]
    own, beside, across, upper, lower = refs[:-1]
    size, half = own.shape[0], upper.shape[0]
    total = None
    for bit, skip, ref in ((0, 0, own), (1, 0, beside), (2, 0, across), (3, 0, upper), (3, half, lower)):
        start = pl.multiple_of(block_columns(place, bit, size) + skip, half)
        value = mul_nn(rows[:, pl.ds(start, ref.shape[0])], ref[...])
        total = value if total is None else total + value
    out[...] = total


def gathered_times(rows, place, pieces):
    count, width = rows.shape
    columns = pieces[0].shape[1]
    tile = min(256, count)
    whole = [pl.BlockSpec(piece.shape, lambda i, place: (0, 0)) for piece in pieces]
    return pl.pallas_call(
        gathered_kernel,
        grid_spec=pltpu.PrefetchScalarGridSpec(
            num_scalar_prefetch=1,
            grid=(count // tile,),
            in_specs=[pl.BlockSpec((tile, width), lambda i, place: (i, 0))] + whole,
            out_specs=pl.BlockSpec((tile, columns), lambda i, place: (i, 0)),
        ),
        out_shape=jax.ShapeDtypeStruct((count, columns), jnp.float32),
        compiler_params=pltpu.CompilerParams(vmem_limit_bytes=VMEM_BYTES),
        cost_estimate=pl.CostEstimate(
            flops=2 * count * width * columns, bytes_accessed=2 * (count + columns) * width, transcendentals=0
        ),
    )(jnp.reshape(place, (1,)).astype(jnp.int32), rows, *pieces)


def gathered_transposed_kernel(count, place, *refs):
    factors, pieces, out = refs[:count], refs[count:-1], refs[-1]
    size, half = pieces[0].shape[0], pieces[3].shape[0]
    for i, (bit, skip) in enumerate(((0, 0), (1, 0), (2, 0), (3, 0), (3, half))):
        start = pl.multiple_of(block_columns(place, bit, size) + skip, half)
        total = None
        for p in range(count):
            value = mul_nt(factors[p][...], pieces[5 * p + i][...])
            total = value if total is None else total + value
        out[:, pl.ds(start, pieces[i].shape[0])] = low(total)


def gathered_times_transposed(factors, place, pieces):
    count, rows = len(factors), factors[0].shape[0]
    width = 4 * pieces[0][0].shape[0]
    tile = min(256, rows)
    flat = [piece for some in pieces for piece in some]
    whole = [pl.BlockSpec(piece.shape, lambda i, place: (0, 0)) for piece in flat]
    wides = [pl.BlockSpec((tile, factor.shape[1]), lambda i, place: (i, 0)) for factor in factors]
    columns = sum(factor.shape[1] for factor in factors)
    return pl.pallas_call(
        functools.partial(gathered_transposed_kernel, count),
        grid_spec=pltpu.PrefetchScalarGridSpec(
            num_scalar_prefetch=1,
            grid=(rows // tile,),
            in_specs=wides + whole,
            out_specs=pl.BlockSpec((tile, width), lambda i, place: (i, 0)),
        ),
        out_shape=jax.ShapeDtypeStruct((rows, width), jnp.bfloat16),
        compiler_params=pltpu.CompilerParams(vmem_limit_bytes=VMEM_BYTES),
        cost_estimate=pl.CostEstimate(
            flops=2 * rows * width * columns, bytes_accessed=2 * (rows + columns) * width, transcendentals=0
        ),
    )(jnp.reshape(place, (1,)).astype(jnp.int32), *factors, *flat)


def join_kernel(squares, source, target):
    lines, _, columns = source.shape
    part = columns // squares
    for i in range(lines):
        for j in range(squares):
            at = (j * lines + i) * part
            target[:, at : at + part] = source[i, :, j * part : (j + 1) * part]


def columns_join(parts, squares):
    lines, rows, columns = parts.shape
    tile = 176 if rows % 176 == 0 else rows
    return pl.pallas_call(
        functools.partial(join_kernel, squares),
        grid=(rows // tile,),
        in_specs=[pl.BlockSpec((lines, tile, columns), lambda i: (0, i, 0))],
        out_specs=pl.BlockSpec((tile, lines * columns), lambda i: (i, 0)),
        out_shape=jax.ShapeDtypeStruct((rows, lines * columns), parts.dtype),
        compiler_params=pltpu.CompilerParams(vmem_limit_bytes=VMEM_BYTES),
        cost_estimate=pl.CostEstimate(flops=0, bytes_accessed=4 * parts.size, transcendentals=0),
    )(parts)


def flip(value, axis, bit):
    devices = range(lax.axis_size(axis))
    return lax.ppermute(value, axis, [(i, i ^ bit) for i in devices])


def shift(value, axis, distance):
    count = lax.axis_size(axis)
    return lax.ppermute(value, axis, [(i, (i + distance) % count) for i in range(count)])


def from_behind(block, axis, distance):
    devices = range(lax.axis_size(axis))
    route = [(i - distance, i) for i in devices if i - distance in devices]
    return lax.ppermute(block, axis, route)


def tie(value, *earlier):
    return lax.optimization_barrier((value,) + earlier)[0]


def put(buffer, piece, *start):
    return lax.dynamic_update_slice(buffer, piece, start)


def wide(value):
    return value.astype(jnp.float32)


def gather_line(shard):
    count, place = lax.axis_size("fsdp"), lax.axis_index("fsdp")
    pieces = [shard] + [shift(shard, "fsdp", d) for d in range(1, count)]
    order = [(place - i) % count for i in range(count)]
    return jnp.concatenate([lax.select_n(which, *pieces) for which in order], axis=0)


class Square:
    def __init__(self, own):
        self.own = own
        self.half = own.shape[0] // 2
        self.beside = flip(own, "ctx", 1)
        self.across = flip(own, "ctx", 2)

    def forward(self, *earlier):
        upper = self.beside[: self.half]
        lower = self.across[self.half :]
        if earlier:
            upper, lower = lax.optimization_barrier((upper, lower) + earlier)[:2]
        self.upper = flip(upper, "ctx", 2)
        self.lower = flip(lower, "ctx", 1)
        return self

    def done(self):
        return (self.upper, self.lower)

    def pieces(self):
        return [self.own, self.beside, self.across, self.upper, self.lower]

    def far(self):
        return jnp.concatenate([self.upper, self.lower], axis=0)


def both_sides(rows):
    if lax.axis_size("tp") == 2:
        return rows, flip(rows, "tp", 1)
    every = lax.all_gather(rows, "tp", axis=0, tiled=True)
    half = every.shape[0] // 2
    return every[:half], every[half:]


def core_sum(mine, other):
    if lax.axis_size("tp") == 2:
        return wide(mine) + wide(flip(other, "tp", 1))
    both = jnp.concatenate([mine, other], axis=0)
    return wide(lax.psum_scatter(both, "tp", scatter_dimension=0, tiled=True))


def neighbour_columns(rows):
    width = rows.shape[1] // 4
    place = lax.axis_index("ctx")
    return [lax.dynamic_slice_in_dim(rows, (place ^ bit) * width, width, 1) for bit in range(4)]


class Line:
    def __init__(self, own):
        count, place = lax.axis_size("fsdp"), lax.axis_index("fsdp")
        own = own.reshape(count, own.shape[0] // count, own.shape[1])

        def part(distance):
            return lax.dynamic_index_in_dim(own, (place + distance) % count, 0, keepdims=False)

        self.kept = part(0)
        self.sent = [low(part(distance)) for distance in range(1, count)]
        self.arrived = [shift(piece, "fsdp", distance + 1) for distance, piece in enumerate(self.sent)]

    def total(self, *late):
        total = self.kept
        for part in lax.optimization_barrier(tuple(self.arrived) + late)[: len(self.arrived)]:
            total = total + wide(part)
        return total


class Scatter:
    def __init__(self, columns, grads):
        self.columns, self.grads = columns, grads
        self.half = columns[0].shape[1] // 2
        self.mine = outer_rows(columns[0], grads)
        beside, across = (
            jnp.concatenate([self.side(3, 1), self.side(1, 1)], axis=1),
            jnp.concatenate([self.side(3, 0), self.side(2, 0)], axis=1),
        )
        self.sent = [low(outer_rows(beside, grads)), low(outer_rows(across, grads))]
        self.first = (flip(self.sent[0], "ctx", 1), flip(self.sent[1], "ctx", 2))

    def side(self, bit, lower):
        return self.columns[bit][:, lower * self.half : (lower + 1) * self.half]

    def second(self, *earlier):
        first = self.first
        if earlier:
            first = lax.optimization_barrier(first + earlier)[:2]
        beside, across = (wide(part) for part in first)
        upper = low(outer_rows(self.side(1, 0), self.grads) + across[: self.half])
        lower = low(outer_rows(self.side(2, 1), self.grads) + beside[: self.half])
        self.last = (flip(upper, "ctx", 1), flip(lower, "ctx", 2))
        self.kept = (beside, across)
        return upper, lower

    def own(self, *ties):
        beside_upper, across_lower = self.last
        if ties:
            beside_upper, across_lower = lax.optimization_barrier(self.last + ties)[:2]
        beside, across = self.kept
        own = self.mine
        upper = own[: self.half] + wide(beside_upper) + across[self.half :]
        lower = own[self.half :] + beside[self.half :] + wide(across_lower)
        return jnp.concatenate([upper, lower], axis=0)


def butterfly(value, axes):
    for axis in axes:
        count, bit = lax.axis_size(axis), 1
        while bit < count:
            value = value + flip(value, axis, bit)
            bit *= 2
    return value


def rms_scale(values, floor_value):
    return lax.rsqrt(jnp.mean(values * values, axis=-1, keepdims=True) + floor_value)


def norm_backward(grad_normed, inputs, scale, gain):
    normed = inputs * scale
    weighted = grad_normed * gain
    return (
        scale * (weighted - normed * jnp.mean(weighted * normed, axis=-1, keepdims=True)),
        normed,
    )


def times(left, right):
    return jnp.dot(left, right, preferred_element_type=jnp.float32)


def times_transposed(left, right):
    return lax.dot_general(
        left, right, (((1,), (1,)), ((), ())), preferred_element_type=jnp.float32
    )


def outer_rows(left, right):
    return lax.dot_general(
        left, right, (((0,), (0,)), ((), ())), preferred_element_type=jnp.float32
    )


def rows_mine(rows):
    count = rows.shape[1] // lax.axis_size("tp")
    return lax.dynamic_slice_in_dim(rows, lax.axis_index("tp") * count, count, 1)


def rows_scatter(partial):
    if lax.axis_size("tp") != 2:
        return wide(lax.psum_scatter(partial, "tp", scatter_dimension=1, tiled=True))
    count = partial.shape[1] // 2
    other = lax.dynamic_slice_in_dim(partial, (1 - lax.axis_index("tp")) * count, count, 1)
    return wide(rows_mine(partial)) + wide(flip(other, "tp", 1))


def rows_full(mine):
    if lax.axis_size("tp") != 2:
        return lax.all_gather(mine, "tp", axis=1, tiled=True)
    other = flip(mine, "tp", 1)
    lower = lax.axis_index("tp") == 0
    return jnp.concatenate([jnp.where(lower, mine, other), jnp.where(lower, other, mine)], axis=1)


def by_head(parts):
    heads = range(parts[0].shape[-1] // LANES)
    return jnp.concatenate([part[..., h * LANES : (h + 1) * LANES] for h in heads for part in parts], axis=-1)


def by_kind(joined):
    return [
        jnp.concatenate(
            [
                some[..., at : at + LANES]
                for some in joined
                for at in range(kind * LANES, some.shape[-1], 3 * LANES)
            ],
            axis=-1,
        )
        for kind in range(3)
    ]


def pass_states(own, transfer, forward, *beside):
    rule = "shij,shjk->shik" if forward == 1 else "shji,shjk->shik"
    leaving = own
    entered = low(jnp.zeros_like(own))
    for repeat in range(lax.axis_size("ctx") - 1):
        entered = from_behind(low(leaving), "ctx", forward)
        if repeat == 1 and beside:
            entered = tie(entered, *beside)
        leaving = own + jnp.einsum(rule, transfer, entered, preferred_element_type=jnp.float32)
    return wide(entered)


def local(
    block_input,
    doc_start,
    gain_mix,
    query_weight,
    key_weight,
    value_weight,
    beta_weight,
    beta_bias,
    conv_weight,
    gain_o,
    out_weight,
    gain_ffn,
    gate_weight,
    up_weight,
    down_weight,
    out_grad,
):
    seq_count, local_len, width = block_input.shape
    row_count = seq_count * local_len
    heads_here = beta_weight.shape[1]
    taps = conv_weight.shape[1]
    parts = 2 if heads_here % 2 == 0 else 1
    part_heads = heads_here // parts
    group = 2 if part_heads % 2 == 0 else 1
    part_cols = 3 * part_heads * LANES
    spare = LANES - heads_here
    units_here = gate_weight.shape[1]
    shard_rows = gate_weight.shape[0]

    joined = by_head([low(query_weight), low(key_weight), low(value_weight)])
    shards = [joined[:, p * part_cols : (p + 1) * part_cols] for p in range(parts)]
    shards[0] = jnp.concatenate([shards[0], jnp.pad(low(beta_weight), ((0, 0), (0, spare)))], axis=1)
    shards.append(low(out_weight).T)
    lines = []
    for shard in shards[:parts]:
        lines.append(gather_line(tie(shard, lines[-1]) if lines else shard))
    units = units_here // 4
    pieces = jnp.stack([low(gate_weight).T, low(up_weight).T, low(down_weight)])
    pieces = pieces.reshape(3, 4, units, shard_rows).transpose(1, 0, 2, 3)
    ffn_swapped = lax.all_to_all(pieces.reshape(4, 3 * units, shard_rows), "ctx", 0, 0)
    ffn_line = ffn_swapped.transpose(1, 0, 2).reshape(3 * units, 4 * shard_rows)
    line_count = lax.axis_size("fsdp")

    ctx_place = lax.axis_index("ctx")
    first_pos = ctx_place * local_len
    starts = doc_start - first_pos
    col, row = starts[:, :, None], starts[:, None, :]
    conv = by_head([conv_weight[0], conv_weight[1], conv_weight[2]])
    bias = jnp.pad(beta_bias, (0, spare))[None]
    gain_head = gain_o[None]
    tokens = block_input.reshape(row_count, width)
    inputs = wide(tokens)
    normed_mix = low(inputs * rms_scale(inputs, EPSILON) * gain_mix)
    grads_mine = rows_mine(out_grad).reshape(-1, width)

    square = Square(tie(lines[0], ffn_swapped)).forward(normed_mix)
    gate_up_parts = tie(ffn_line[None, : 2 * units], lines[parts - 1], *square.done())
    gate_up_parts = lax.all_gather(gate_up_parts, "fsdp", axis=0, tiled=True)
    down_parts = lax.all_gather(ffn_line[None, 2 * units :], "fsdp", axis=0, tiled=True)
    mix_full, kept, pre = [], [], []
    for p in range(parts):
        mix_full.append(square.pieces())
        arrived = square.done()
        ends = normed_mix.reshape(seq_count, local_len, width)[:, local_len - HALO :].reshape(seq_count * HALO, width)
        ends = gathered_times(ends, ctx_place, mix_full[p])
        ends = low(ends)
        halo = from_behind(ends[:, :part_cols].reshape(seq_count, HALO, part_cols), "ctx", 1)
        pre.append(gathered_times(tie(normed_mix, ends), ctx_place, mix_full[p]))
        if p == parts - 1:
            lines.append(gather_line(tie(shards[-1], pre[p])))
        square = Square(tie(lines[p + 1], halo, pre[p], *arrived))
        halo = wide(halo)
        convs = conv[:, p * part_cols : (p + 1) * part_cols]
        kept.append(
            [halo, convs]
            + list(
                mixer_forward(
                    pre[p], pre[0], bias, halo, convs, col, row, taps, p * part_heads, part_heads, group
                )
            )
        )
        square.forward(kept[p][2])
        if p == 0:
            grad_square = Square(tie(grads_mine, kept[p][2], *square.done()))
    out_full = square.pieces()

    inputs_mine = wide(tie(rows_mine(block_input).reshape(-1, width), kept[0][2]))
    gate_up_full = columns_join(gate_up_parts, 4)
    finals = jnp.concatenate([some[4] for some in kept], axis=1)
    transfer = low(finals[..., LANES:])
    first = tie(finals[..., :LANES], gate_up_full, grad_square.beside, grad_square.across)
    entering = pass_states(first, transfer, 1)
    entered = [entering[:, p * part_heads : (p + 1) * part_heads] for p in range(parts)]
    grad_square.forward(entering)
    grad_rows = [both_sides(part) for part in (grad_square.own, grad_square.beside, grad_square.across)]
    mixed_rows = []
    for p in range(parts):
        own, carry = kept[p][2:4]
        mixed_rows.append(mixer_output(own, carry, entered[p], gain_head, group))
    mixed_rows = jnp.concatenate(mixed_rows, axis=1)
    mixed_rows = tie(mixed_rows, *(other for _, other in grad_rows))
    grad_rows.append(both_sides(grad_square.far()))

    branch = gathered_times_transposed([mixed_rows], ctx_place, [out_full]).reshape(seq_count, local_len, width)
    branch = tie(branch, down_parts)
    residual = inputs_mine + rows_scatter(branch).reshape(-1, width)
    scale_ffn = rms_scale(residual, EPSILON)
    square = Square(low(residual * scale_ffn * gain_ffn))
    ffn_full = (gate_up_full, columns_join(down_parts, 4))

    ffn_rows = [both_sides(square.own)]
    ffn_out = [ffn_both(ffn_rows[0], grad_rows[0], *ffn_full)]
    square.forward(ffn_out[0][0][0])
    ffn_rows.append(both_sides(tie(square.beside, ffn_out[0][0][0])))
    ffn_out.append(ffn_both(ffn_rows[1], grad_rows[1], *ffn_full))
    ffn_rows.append(both_sides(tie(square.across, ffn_out[0][0][0])))
    mine, other = ffn_rows[2]
    ffn_out.append(ffn_both((tie(mine, ffn_out[1][0][0], *square.done()), other), grad_rows[2], *ffn_full))
    beside_sums, across_sums = (low(core_sum(*(side[1] for side in ffn_out[bit]))) for bit in (1, 2))
    ffn_rows.append(both_sides(square.far()))
    mine, other = ffn_rows[3]
    ffn_out.append(ffn_both((tie(mine, beside_sums, across_sums), other), grad_rows[3], *ffn_full))
    near_sums = (flip(beside_sums, "ctx", 1), flip(across_sums, "ctx", 2))
    mine, other = (side[1] for side in ffn_out[3])
    far_sums = low(core_sum(mine, tie(other, *near_sums)))
    acts = [side[0] for outs in ffn_out for side in outs]
    own_sums = core_sum(*(side[1] for side in ffn_out[0]))
    result_low = []
    for bit in (1, 2):
        mine, other = (side[2] for side in ffn_out[bit])
        result_low.append(low(core_sum(tie(mine, far_sums), other)))
    acts[0] = tie(acts[0], far_sums, own_sums, *result_low)
    far_sums = flip(far_sums, "ctx", 3)
    sums = ffn_weights(
        acts,
        [side for sides in ffn_rows for side in sides],
        [side for sides in grad_rows for side in sides],
        line_count,
        4,
    )

    far_sums, sums = lax.optimization_barrier((far_sums, sums))
    result_near = [flip(tie(part, far_sums), "ctx", bit) for part, bit in zip(result_low, (1, 2))]
    grad_normed = own_sums + wide(near_sums[0]) + wide(near_sums[1]) + wide(far_sums)
    back_ffn, unit_ffn = norm_backward(grad_normed, residual, scale_ffn, gain_ffn)
    grad_residual = wide(grads_mine) + back_ffn
    gain_ffn_part = jnp.sum(grad_normed * unit_ffn, axis=0)
    grad_branch = rows_full(low(grad_residual).reshape(seq_count, -1, width)).reshape(row_count, width)
    grad_heads = gathered_times(grad_branch, ctx_place, out_full)
    backs, acrosses, gain_o_part = [], [], 0.0
    for p in range(parts):
        _, _, own, carry, _, _, _, _ = kept[p]
        back, across, gain_part = mixer_output_backward(
            own, carry, entered[p], gain_head, grad_heads, p * part_heads, group
        )
        backs.append(back)
        acrosses.append(across)
        gain_o_part = gain_o_part + jnp.sum(gain_part, axis=(0, 1, 2))
    grad_end = pass_states(jnp.concatenate(acrosses, axis=1), transfer, -1, *result_near)
    total = lax.psum_scatter(sums, "fsdp", scatter_dimension=0, tiled=True)

    out_grad_w = low(outer_rows(grad_branch, mixed_rows))
    out_part = out_grad_w
    out_grad_w = lax.psum_scatter(out_grad_w, ("ctx", "fsdp"), scatter_dimension=0, tiled=True)

    mine, other = (side[2] for side in ffn_out[0])
    result_own = core_sum(mine, tie(other, grad_branch))
    mine, other = (side[2] for side in ffn_out[3])
    result_far = flip(tie(low(core_sum(mine, tie(other, grad_branch))), grad_end), "ctx", 3)
    columns = neighbour_columns(normed_mix)
    grad_mixes, mix_grads, conv_parts = [None] * parts, [None] * parts, [None] * parts
    logits = 0.0
    scatter = None
    for p in reversed(range(parts)):
        halo, convs, own, carry, final, inverses, updates, states = kept[p]
        heads = slice(p * part_heads, (p + 1) * part_heads)
        back = tie(backs[p], out_part) if scatter is None else tie(backs[p], total, *scatter.sent)
        grad_mix, tail, before, conv_parts[p], logit = mixer_backward(
            pre[p], pre[0], bias, halo, convs, col, row, back, inverses, updates, states,
            entered[p], grad_end[:, heads], taps, p * part_heads, part_heads, group,
        )
        logits = logits + logit
        tail = low(tail + from_behind(before, "ctx", -1))
        grad_mix = put(grad_mix.reshape(seq_count, local_len, -1), tail, 0, local_len - HALO, 0)
        grad_mix = grad_mix.reshape(row_count, -1)
        if scatter is not None:
            earlier_ready = scatter.second(before)
            earlier_scatter = scatter
        else:
            grad_mix = tie(grad_mix, result_far)
        if p == 0:
            grad_mix = jnp.concatenate([grad_mix, low(logits)], axis=1)
        grad_mixes[p] = grad_mix
        scatter = Scatter(columns, grad_mix)
        if p > 0:
            result_far = tie(result_far, *scatter.sent)
    result = result_own + wide(result_near[0]) + wide(result_near[1])
    result = result + wide(result_far)
    block_output = rows_full(low(residual + result).reshape(seq_count, -1, width))
    ready = (block_output, scatter.mine)
    if parts > 1:
        ready = ready + tuple(earlier_ready) + (earlier_scatter.mine,)
    ready = scatter.second(*ready)
    grad_mixes[0] = tie(grad_mixes[0], *ready)
    mix_back = tie(gathered_times_transposed(grad_mixes, ctx_place, mix_full), *scatter.last)
    mix_back = rows_scatter(mix_back.reshape(seq_count, local_len, width)).reshape(-1, width)
    back_mix, unit_mix = norm_backward(mix_back, inputs_mine, rms_scale(inputs_mine, EPSILON), gain_mix)
    input_grad = rows_full(low(grad_residual + back_mix).reshape(seq_count, -1, width))
    gain_mix_part = jnp.sum(mix_back * unit_mix, axis=0)

    conv_cols = jnp.concatenate([jnp.sum(part, axis=0)[:taps] for part in conv_parts], axis=1)
    gains = butterfly(jnp.concatenate([gain_mix_part, gain_ffn_part, gain_o_part]), ("tp",))
    conv_kinds = jnp.stack(by_kind([conv_cols]))
    sums = jnp.concatenate([gains, conv_kinds.reshape(-1), jnp.sum(logits, axis=0)])
    last_line = Line(scatter.own())
    for p in range(1, parts):
        own = low(earlier_scatter.own(*last_line.sent))
        mix_grads[p] = wide(lax.psum_scatter(own, "fsdp", scatter_dimension=0, tiled=True))
    sums = butterfly(tie(sums, input_grad, *last_line.sent), ("ctx", "fsdp"))
    mix_grads[0] = last_line.total(sums)
    query_grad, key_grad, value_grad = by_kind([grad[:, :part_cols] for grad in mix_grads])
    beta_grad = mix_grads[0][:, part_cols : part_cols + heads_here]
    ends = [width, 2 * width, 2 * width + LANES, sums.shape[0] - LANES]
    gain_mix_grad, gain_ffn_grad, gain_o_grad, conv_grad, bias_grad = jnp.split(sums, ends)
    conv_grad = conv_grad.reshape(conv_kinds.shape)
    bias_grad = bias_grad[:heads_here]
    out_grad_w = wide(tie(out_grad_w, *scatter.last)).T
    pieces = tie(total, *scatter.last).reshape(3 * units, 4, shard_rows).transpose(1, 0, 2)
    arrived = lax.all_to_all(pieces, "ctx", 0, 0).reshape(4, 3, units, shard_rows)
    gate_grad, up_grad, down_grad = (wide(arrived[:, i].reshape(units_here, shard_rows)) for i in range(3))

    return (
        block_output,
        input_grad,
        gain_mix_grad,
        query_grad,
        key_grad,
        value_grad,
        beta_grad,
        bias_grad,
        conv_grad,
        gain_o_grad,
        out_grad_w,
        gain_ffn_grad,
        gate_grad.T,
        up_grad.T,
        down_grad,
    )


def solution(mesh):
    placed = (
        P("fsdp", "ctx", None),
        P("fsdp", "ctx"),
        P(),
        P(("ctx", "fsdp"), "tp"),
        P(("ctx", "fsdp"), "tp"),
        P(("ctx", "fsdp"), "tp"),
        P(("ctx", "fsdp"), "tp"),
        P("tp"),
        P(None, None, "tp"),
        P(),
        P("tp", ("ctx", "fsdp")),
        P(),
        P(("ctx", "fsdp"), "tp"),
        P(("ctx", "fsdp"), "tp"),
        P("tp", ("ctx", "fsdp")),
        P("fsdp", "ctx", None),
    )
    return jax.shard_map(
        local,
        mesh=mesh,
        in_specs=placed,
        out_specs=(
            P("fsdp", "ctx", None),
            P("fsdp", "ctx", None),
            P(),
            P(("ctx", "fsdp"), "tp"),
            P(("ctx", "fsdp"), "tp"),
            P(("ctx", "fsdp"), "tp"),
            P(("ctx", "fsdp"), "tp"),
            P("tp"),
            P(None, None, "tp"),
            P(),
            P("tp", ("ctx", "fsdp")),
            P(),
            P(("ctx", "fsdp"), "tp"),
            P(("ctx", "fsdp"), "tp"),
            P("tp", ("ctx", "fsdp")),
        ),
        check_vma=False,
    )
```

```python
import functools
import math
import jax
import jax.numpy as jnp
from jax import lax
from jax.experimental import pallas as pl
from jax.experimental.pallas import tpu as pltpu
from jax.sharding import PartitionSpec as P

LANES = 128
CHUNK = 128
HALO = 8
EPSILON = 1e-06
HEAD_FLOOR = 0.01
VMEM_BYTES = 60 * 1024 * 1024


def low(value):
    return value.astype(jnp.bfloat16)


def mul_nn(left, right):
    return lax.dot_general(low(left), low(right), (((1,), (0,)), ((), ())), preferred_element_type=jnp.float32)


def mul_nt(left, right):
    return lax.dot_general(low(left), low(right), (((1,), (1,)), ((), ())), preferred_element_type=jnp.float32)


def mul_tn(left, right):
    return lax.dot_general(low(left), low(right), (((0,), (0,)), ((), ())), preferred_element_type=jnp.float32)


def iota(shape, axis):
    return lax.broadcasted_iota(jnp.int32, shape, axis)


def chunk_masks(col, row, first):
    size = col.shape[0]
    same = col == row
    order, other = iota((size, size), 0), iota((size, size), 1)
    upto = same & (order >= other)
    below = same & (order > other)
    carried = (col < first).astype(jnp.float32)
    last = (col == row[:, size - 1 :]).astype(jnp.float32)
    keep = (row[:, size - 1 :] < first).astype(jnp.float32)
    return upto, below, carried, last, keep


def invert_units(systems):
    size = systems[0].shape[0]
    order, other = iota((size, size), 0), iota((size, size), 1)
    identity = (order == other).astype(jnp.float32)
    span = 1
    found = None
    while span < size:
        pair = (order // (2 * span) == other // (2 * span)) & (order // span != other // span)
        parts = [jnp.where(pair, system, 0.0) for system in systems]
        if found is None:
            found = [identity - part for part in parts]
        else:
            right = [mul_nn(part, value) for part, value in zip(parts, found)]
            found = [value - mul_nn(value, part) for value, part in zip(found, right)]
        span *= 2
    return found


def conv_rows(ext, conv, col, offset, size, lane, taps):
    total = None
    moved = []
    position = iota((size, 1), 0) + offset
    for tap in range(taps):
        back = taps - 1 - tap
        values = ext[pl.ds(HALO + offset - back, size), lane : lane + LANES]
        values = jnp.where(position - back >= col, values, 0.0)
        moved.append(values)
        term = conv[tap : tap + 1, lane : lane + LANES] * values
        total = term if total is None else total + term
    return total, moved


def unit(values):
    return values * lax.rsqrt(jnp.sum(values * values, axis=-1, keepdims=True) + EPSILON)


def head_column(values, head):
    return jnp.sum(jnp.where(iota(values.shape, 1) == head, values, 0.0), axis=-1, keepdims=True)


def forward_kernel(taps, heads, first, pre, beta, bias, halo, conv, col_ref, row_ref, own, carry, final, inv, upd, states, ext):
    length = pre.shape[0]
    ext[:HALO] = halo[0]
    ext[HALO:] = pre[...]
    head = first + pl.program_id(1) * heads
    jobs = [(i, j) for j in range(length // CHUNK) for i in range(heads)]
    data = {}
    for j in range(length // CHUNK):
        rows = pl.ds(j * CHUNK, CHUNK)
        col, row = col_ref[0, rows], row_ref[0, :, rows]
        masks = chunk_masks(col, row, j * CHUNK)
        strengths = jax.nn.sigmoid(beta[rows] + bias[...])
        for i in range(heads):
            acts = []
            for kind in range(3):
                total, _ = conv_rows(ext, conv, col, j * CHUNK, CHUNK, (3 * i + kind) * LANES, taps)
                acts.append(total * jax.nn.sigmoid(total))
            query, key, value = unit(acts[0]), unit(acts[1]), acts[2]
            strength = head_column(strengths, head + i)
            grams = mul_nt(jnp.concatenate([low(key), low(query)], axis=0), key)
            system = jnp.where(masks[1], strength * grams[:CHUNK], 0.0)
            scores = low(jnp.where(masks[0], grams[CHUNK:], 0.0))
            data[i, j] = (low(query), low(key), value, strength, scores, masks, system)
    inverses = dict(zip(jobs, invert_units([data[job][6] for job in jobs])))
    for i in range(heads):
        state = jnp.concatenate(
            [
                jnp.zeros((LANES, LANES), jnp.float32),
                (iota((LANES, LANES), 0) == iota((LANES, LANES), 1)).astype(jnp.float32),
            ],
            axis=1,
        )
        final[0, i] = state
    for j in range(length // CHUNK):
        rows = pl.ds(j * CHUNK, CHUNK)
        for i in range(heads):
            query, key, value, strength, scores, masks, _ = data[i, j]
            _, _, carried, last, keep = masks
            inverse = low(inverses[i, j])
            state = final[0, i]
            state_low = low(state)
            read = mul_nn(jnp.concatenate([key, query], axis=0), state_low)
            wide = jnp.concatenate([value, jnp.zeros_like(value)], axis=1)
            targets = strength * (wide - carried * read[:CHUNK])
            update = low(mul_nn(inverse, targets))
            result = carried * read[CHUNK:] + mul_nn(scores, update)
            final[0, i] = keep * state + mul_tn(key * low(last), update)
            lanes = slice(i * LANES, (i + 1) * LANES)
            own[rows, lanes] = result[:, :LANES]
            carry[rows, lanes] = low(result[:, LANES:])
            inv[0, i, j] = inverse
            upd[0, i, j] = update
            states[0, i, j] = state_low


def mixer_forward(pre, logit, bias, halo, conv, col, row, taps, first, heads_here, group):
    seqs, length = col.shape[0], col.shape[1]
    steps = heads_here // group
    chunks = length // CHUNK
    wide = 3 * LANES * group
    rows = seqs * length

    def tile(*tail, kind):
        return jax.ShapeDtypeStruct((seqs, heads_here) + tail, kind)

    def spec(*tail):
        return pl.BlockSpec((1, group) + tail, lambda s, h: (s, h) + (0,) * len(tail))

    flat = pl.BlockSpec((length, LANES * group), lambda s, h: (s, h))
    last = logit.shape[1] // LANES - 1
    return pl.pallas_call(
        functools.partial(forward_kernel, taps, group, first),
        grid=(seqs, steps),
        in_specs=[
            pl.BlockSpec((length, wide), lambda s, h: (s, h)),
            pl.BlockSpec((length, LANES), lambda s, h: (s, last)),
            pl.BlockSpec((1, LANES), lambda s, h: (0, 0)),
            pl.BlockSpec((1, HALO, wide), lambda s, h: (s, 0, h)),
            pl.BlockSpec((conv.shape[0], wide), lambda s, h: (0, h)),
            pl.BlockSpec((1, length, 1), lambda s, h: (s, 0, 0)),
            pl.BlockSpec((1, 1, length), lambda s, h: (s, 0, 0)),
        ],
        out_specs=[
            flat,
            flat,
            spec(LANES, 2 * LANES),
            spec(chunks, CHUNK, CHUNK),
            spec(chunks, CHUNK, 2 * LANES),
            spec(chunks, LANES, 2 * LANES),
        ],
        out_shape=[
            jax.ShapeDtypeStruct((rows, heads_here * LANES), jnp.float32),
            jax.ShapeDtypeStruct((rows, heads_here * LANES), jnp.bfloat16),
            tile(LANES, 2 * LANES, kind=jnp.float32),
            tile(chunks, CHUNK, CHUNK, kind=jnp.bfloat16),
            tile(chunks, CHUNK, 2 * LANES, kind=jnp.bfloat16),
            tile(chunks, LANES, 2 * LANES, kind=jnp.bfloat16),
        ],
        scratch_shapes=[pltpu.VMEM((length + HALO, wide), jnp.float32)],
        compiler_params=pltpu.CompilerParams(vmem_limit_bytes=VMEM_BYTES),
        cost_estimate=pl.CostEstimate(
            flops=60 * rows * heads_here * CHUNK * LANES, bytes_accessed=40 * rows * heads_here * LANES, transcendentals=0
        ),
    )(pre, logit, bias, halo, conv, col, row)


def backward_kernel(
    taps, heads, first, pre, beta, bias, halo, conv, col_ref, row_ref, grad_ref, inv, upd, states, start, end,
    grad_pre, tail, before, conv_grad, logits, ext, grad_ext,
):
    length = pre.shape[0]
    step = pl.program_id(1)
    head = first + step * heads
    ext[:HALO] = halo[0]
    ext[HALO:] = pre[...]
    grad_ext[...] = jnp.zeros_like(grad_ext)

    @pl.when(step == 0)
    def _():
        logits[...] = jnp.zeros_like(logits)

    grad_states = [end[0, i] for i in range(heads)]
    entry = [low(start[0, i]) for i in range(heads)]
    tap_sums = {}
    for j in reversed(range(length // CHUNK)):
        offset = j * CHUNK
        rows = pl.ds(offset, CHUNK)
        col, row = col_ref[0, rows], row_ref[0, :, rows]
        upto, below, carried, last, keep = chunk_masks(col, row, offset)
        strengths = jax.nn.sigmoid(beta[rows] + bias[...])
        grad_logit = jnp.zeros((CHUNK, LANES), jnp.float32)
        for i in range(heads):
            raw, taps_in = [], []
            for kind in range(3):
                total, moved = conv_rows(ext, conv, col, offset, CHUNK, (3 * i + kind) * LANES, taps)
                raw.append(total)
                taps_in.append(moved)
            gates = [jax.nn.sigmoid(total) for total in raw]
            acts = [total * gate for total, gate in zip(raw, gates)]
            scales = [lax.rsqrt(jnp.sum(act * act, axis=-1, keepdims=True) + EPSILON) for act in acts[:2]]
            query, key, value = acts[0] * scales[0], acts[1] * scales[1], acts[2]
            strength = head_column(strengths, head + i)
            lanes = slice(i * LANES, (i + 1) * LANES)
            query_low, key_low = low(query), low(key)
            grams = mul_nt(jnp.concatenate([key_low, query_low], axis=0), key_low)
            gram = jnp.where(below, grams[:CHUNK], 0.0)
            scores = jnp.where(upto, grams[CHUNK:], 0.0)
            inverse = inv[0, i, j]
            update = upd[0, i, j]
            update = low(update[:, :LANES].astype(jnp.float32) + mul_nn(update[:, LANES:], entry[i]))
            state = states[0, i, j]
            state = low(state[:, :LANES].astype(jnp.float32) + mul_nn(state[:, LANES:], entry[i]))
            grad_out = grad_ref[rows, lanes]
            grad_state = grad_states[i]
            grad_state_low = low(grad_state)
            key_last = key_low * low(last)
            grad_update = mul_tn(scores, grad_out) + mul_nn(key_last, grad_state_low)
            grad_target = mul_tn(inverse, grad_update)
            weighted = strength * grad_target
            passed = carried * weighted
            out_carried = carried * grad_out.astype(jnp.float32)
            query_carried = query_low * low(carried)
            grad_states[i] = (
                keep * grad_state + mul_tn(query_carried, grad_out) - mul_tn(key_low, passed)
            )
            grad_scores = jnp.where(upto, mul_nt(grad_out, update), 0.0)
            grad_system = jnp.where(below, mul_nt(grad_target, update), 0.0)
            remainder = value - carried * mul_nn(key_low, state)
            grad_strength = jnp.sum(grad_target * remainder - grad_system * gram, axis=-1, keepdims=True)
            scaled = strength * grad_system
            from_state = mul_nt(jnp.concatenate([low(out_carried), low(passed)], axis=0), state)
            from_keys = mul_nn(jnp.concatenate([low(grad_scores), low(scaled + scaled.T)], axis=0), key_low)
            grad_query = from_state[:CHUNK] + from_keys[:CHUNK]
            grad_key = (
                mul_tn(grad_scores, query_low)
                + last * mul_nt(update, grad_state_low)
                - from_state[CHUNK:]
                - from_keys[CHUNK:]
            )
            grad_logit = grad_logit + jnp.where(
                iota((CHUNK, LANES), 1) == head + i, grad_strength * strength * (1.0 - strength), 0.0
            )
            grads = [
                scales[0] * (grad_query - query * jnp.sum(grad_query * query, axis=-1, keepdims=True)),
                scales[1] * (grad_key - key * jnp.sum(grad_key * key, axis=-1, keepdims=True)),
                weighted,
            ]
            position = iota((CHUNK, 1), 0) + offset
            for kind in range(3):
                gate, total = gates[kind], raw[kind]
                grad_conv = grads[kind] * gate * (1.0 + total * (1.0 - gate))
                lane = (3 * i + kind) * LANES
                for tap in range(taps):
                    back = taps - 1 - tap
                    part = jnp.sum(grad_conv * taps_in[kind][tap], axis=0, keepdims=True)
                    spot = (i, kind, tap)
                    tap_sums[spot] = part if spot not in tap_sums else tap_sums[spot] + part
                    back_part = jnp.where(
                        position - back >= col, grad_conv * conv[tap : tap + 1, lane : lane + LANES], 0.0
                    )
                    where = pl.ds(HALO + offset - back, CHUNK)
                    grad_ext[where, lane : lane + LANES] += back_part
        logits[rows] += grad_logit
    grad_pre[...] = low(grad_ext[HALO:])
    before[0] = grad_ext[:HALO]
    tail[0] = grad_ext[length:]
    for i in range(heads):
        for kind in range(3):
            lane = (3 * i + kind) * LANES
            for tap in range(taps):
                conv_grad[0, tap : tap + 1, lane : lane + LANES] = tap_sums[i, kind, tap]


def mixer_backward(
    pre, logit, bias, halo, conv, col, row, grad_mixed, inv, upd, states, start, end, taps, first, heads_here, group
):
    seqs, length = col.shape[0], col.shape[1]
    steps = heads_here // group
    chunks = length // CHUNK
    wide = 3 * LANES * group
    rows = seqs * length

    def spec(*tail):
        return pl.BlockSpec((1, group) + tail, lambda s, h: (s, h) + (0,) * len(tail))

    last = logit.shape[1] // LANES - 1
    part = pl.BlockSpec((1, HALO, wide), lambda s, h: (s, 0, h))
    edge = jax.ShapeDtypeStruct((seqs, HALO, 3 * LANES * heads_here), jnp.float32)
    return pl.pallas_call(
        functools.partial(backward_kernel, taps, group, first),
        grid=(seqs, steps),
        in_specs=[
            pl.BlockSpec((length, wide), lambda s, h: (s, h)),
            pl.BlockSpec((length, LANES), lambda s, h: (s, last)),
            pl.BlockSpec((1, LANES), lambda s, h: (0, 0)),
            part,
            pl.BlockSpec((conv.shape[0], wide), lambda s, h: (0, h)),
            pl.BlockSpec((1, length, 1), lambda s, h: (s, 0, 0)),
            pl.BlockSpec((1, 1, length), lambda s, h: (s, 0, 0)),
            pl.BlockSpec((length, LANES * group), lambda s, h: (s, h)),
            spec(chunks, CHUNK, CHUNK),
            spec(chunks, CHUNK, 2 * LANES),
            spec(chunks, LANES, 2 * LANES),
            spec(LANES, LANES),
            spec(LANES, LANES),
        ],
        out_specs=[
            pl.BlockSpec((length, wide), lambda s, h: (s, h)),
            part,
            part,
            part,
            pl.BlockSpec((length, LANES), lambda s, h: (s, 0)),
        ],
        out_shape=[
            jax.ShapeDtypeStruct((rows, 3 * LANES * heads_here), jnp.bfloat16),
            edge,
            edge,
            edge,
            jax.ShapeDtypeStruct((rows, LANES), jnp.float32),
        ],
        scratch_shapes=[
            pltpu.VMEM((length + HALO, wide), jnp.float32),
            pltpu.VMEM((length + HALO, wide), jnp.float32),
        ],
        compiler_params=pltpu.CompilerParams(vmem_limit_bytes=VMEM_BYTES),
        cost_estimate=pl.CostEstimate(
            flops=60 * rows * heads_here * CHUNK * LANES, bytes_accessed=40 * rows * heads_here * LANES, transcendentals=0
        ),
    )(pre, logit, bias, halo, conv, col, row, grad_mixed, inv, upd, states, start, end)


def mixed_rows_of(own, carry, start):
    return own + mul_nn(carry, start)


def output_kernel(heads, own, carry, start, gain, out):
    for i in range(heads):
        lanes = slice(i * LANES, (i + 1) * LANES)
        mixed = mixed_rows_of(own[:, lanes], carry[:, lanes], start[0, i])
        scale = lax.rsqrt(jnp.mean(mixed * mixed, axis=-1, keepdims=True) + HEAD_FLOOR)
        out[:, lanes] = low(mixed * scale * gain[...])


def output_backward_kernel(heads, own, carry, start, gain, grad, out, across, gain_grad):
    total = jnp.zeros((1, LANES), jnp.float32)
    for i in range(heads):
        lanes = slice(i * LANES, (i + 1) * LANES)
        carried = carry[:, lanes]
        mixed = mixed_rows_of(own[:, lanes], carried, start[0, i])
        scale = lax.rsqrt(jnp.mean(mixed * mixed, axis=-1, keepdims=True) + HEAD_FLOOR)
        normed = mixed * scale
        upper = grad[:, lanes].astype(jnp.float32)
        total = total + jnp.sum(upper * normed, axis=0, keepdims=True)
        weighted = upper * gain[...]
        back = scale * (weighted - normed * jnp.mean(weighted * normed, axis=-1, keepdims=True))
        out[:, lanes] = low(back)
        across[0, i] = mul_tn(carried, back)
    gain_grad[0, 0] = total


def mixer_output(own, carry, start, gain, group):
    seqs, heads_here = start.shape[:2]
    rows = own.shape[0]
    length = rows // seqs
    flat = pl.BlockSpec((length, LANES * group), lambda s, h: (s, h))
    square = pl.BlockSpec((1, group, LANES, LANES), lambda s, h: (s, h, 0, 0))
    return pl.pallas_call(
        functools.partial(output_kernel, group),
        grid=(seqs, heads_here // group),
        in_specs=[flat, flat, square, pl.BlockSpec((1, LANES), lambda s, h: (0, 0))],
        out_specs=flat,
        out_shape=jax.ShapeDtypeStruct(own.shape, jnp.bfloat16),
        compiler_params=pltpu.CompilerParams(vmem_limit_bytes=VMEM_BYTES),
        cost_estimate=pl.CostEstimate(
            flops=2 * own.size * LANES, bytes_accessed=8 * own.size, transcendentals=0
        ),
    )(own, carry, start, gain)


def mixer_output_backward(own, carry, start, gain, grad, first, group):
    seqs, heads_here = start.shape[:2]
    rows = own.shape[0]
    length = rows // seqs
    steps = heads_here // group
    flat = pl.BlockSpec((length, LANES * group), lambda s, h: (s, h))
    base = first // group
    shifted = pl.BlockSpec((length, LANES * group), lambda s, h: (s, base + h))
    square = pl.BlockSpec((1, group, LANES, LANES), lambda s, h: (s, h, 0, 0))
    return pl.pallas_call(
        functools.partial(output_backward_kernel, group),
        grid=(seqs, steps),
        in_specs=[flat, flat, square, pl.BlockSpec((1, LANES), lambda s, h: (0, 0)), shifted],
        out_specs=[flat, square, pl.BlockSpec((1, 1, 1, LANES), lambda s, h: (s, h, 0, 0))],
        out_shape=[
            jax.ShapeDtypeStruct(own.shape, jnp.bfloat16),
            jax.ShapeDtypeStruct(start.shape, jnp.float32),
            jax.ShapeDtypeStruct((seqs, steps, 1, LANES), jnp.float32),
        ],
        compiler_params=pltpu.CompilerParams(vmem_limit_bytes=VMEM_BYTES),
        cost_estimate=pl.CostEstimate(
            flops=4 * own.size * LANES, bytes_accessed=12 * own.size, transcendentals=0
        ),
    )(own, carry, start, gain, grad)


def ffn_kernel(mine, other, mine_grads, other_grads, gate_w, up_w, down_w, *outs):
    rows = jnp.concatenate([mine[...], other[...]], axis=0)
    grads = jnp.concatenate([mine_grads[...], other_grads[...]], axis=0)
    half = mine.shape[0]
    gate = mul_nt(rows, gate_w[...])
    up = mul_nt(rows, up_w[...])
    grad_hidden = mul_nt(grads, down_w[...])
    sigmoid = jax.nn.sigmoid(gate)
    active = gate * sigmoid
    kept = low(active * up)
    back_gate = low(grad_hidden * up * sigmoid * (1.0 + gate * (1.0 - sigmoid)))
    back_up = low(grad_hidden * active)
    grad_rows = low(mul_nn(back_gate, gate_w[...]) + mul_nn(back_up, up_w[...]))
    result = low(mul_nn(kept, down_w[...]))
    for side in range(2):
        here = slice(side * half, (side + 1) * half)
        acts, grad_out, result_out = outs[3 * side : 3 * side + 3]
        for kind, value in enumerate((back_gate, back_up, kept)):
            acts[kind] = value[here]
        grad_out[...] = grad_rows[here]
        result_out[...] = result[here]


def ffn_both(rows, grads, gate_up, down):
    count, width = rows[0].shape
    units = down.shape[0]
    tile = min(256, count)
    wide_rows = pl.BlockSpec((tile, width), lambda i: (i, 0))
    narrow = pl.BlockSpec((3, tile, units), lambda i: (0, i, 0))

    def third(index):
        return pl.BlockSpec((units, width), lambda i: (index, 0))

    flat = jax.ShapeDtypeStruct((count, width), jnp.bfloat16)
    outs = pl.pallas_call(
        ffn_kernel,
        grid=(count // tile,),
        in_specs=[wide_rows] * 4 + [third(0), third(1), third(0)],
        out_specs=[narrow, wide_rows, wide_rows] * 2,
        out_shape=[jax.ShapeDtypeStruct((3, count, units), jnp.bfloat16), flat, flat] * 2,
        compiler_params=pltpu.CompilerParams(vmem_limit_bytes=VMEM_BYTES),
        cost_estimate=pl.CostEstimate(
            flops=24 * count * width * units, bytes_accessed=16 * count * width + 6 * units * width, transcendentals=0
        ),
    )(*rows, *grads, gate_up, gate_up, down)
    return outs[:3], outs[3:]


def ffn_weights_kernel(count, lines, *refs):
    acts, rows, grads = refs[:count], refs[count : 2 * count], refs[2 * count : 3 * count]
    out, total = refs[-2:]
    part = out.shape[-1]

    def add(sources):
        for i in range(count):
            value = mul_tn(acts[i][0], sources[i][...])
            if i == 0:
                total[...] = value
            else:
                total[...] += value

    @pl.when(pl.program_id(0) < 2)
    def _():
        add(rows)

    @pl.when(pl.program_id(0) == 2)
    def _():
        add(grads)

    for line in range(lines):
        out[line, 0] = low(total[:, line * part : (line + 1) * part])


def ffn_weights(acts, rows, grads, lines, squares):
    count, width = len(acts), rows[0].shape[1]
    size, units = acts[0].shape[1:]
    block = width // squares
    part = block // lines
    act_spec = pl.BlockSpec((1, size, units), lambda k, c: (k, 0, 0))
    row_spec = pl.BlockSpec((size, block), lambda k, c: (0, jnp.where(k < 2, c, squares - 1)))
    grad_spec = pl.BlockSpec((size, block), lambda k, c: (0, jnp.where(k < 2, 0, c)))
    return pl.pallas_call(
        functools.partial(ffn_weights_kernel, count, lines),
        grid=(3, squares),
        in_specs=[act_spec] * count + [row_spec] * count + [grad_spec] * count,
        out_specs=pl.BlockSpec((lines, 1, units, part), lambda k, c: (0, k, 0, c)),
        out_shape=jax.ShapeDtypeStruct((lines, 3, units, squares * part), jnp.bfloat16),
        scratch_shapes=[pltpu.VMEM((units, block), jnp.float32)],
        compiler_params=pltpu.CompilerParams(vmem_limit_bytes=VMEM_BYTES),
        cost_estimate=pl.CostEstimate(
            flops=6 * count * size * width * units, bytes_accessed=8 * count * size * width, transcendentals=0
        ),
    )(*acts, *rows, *grads)


def block_columns(place, bit, size):
    return pl.multiple_of((place[0] ^ bit) * size, size)


def gathered_kernel(place, rows, *refs):
    out = refs[-1]
    own, beside, across, upper, lower = refs[:-1]
    size, half = own.shape[0], upper.shape[0]
    total = None
    for bit, skip, ref in ((0, 0, own), (1, 0, beside), (2, 0, across), (3, 0, upper), (3, half, lower)):
        start = pl.multiple_of(block_columns(place, bit, size) + skip, half)
        value = mul_nn(rows[:, pl.ds(start, ref.shape[0])], ref[...])
        total = value if total is None else total + value
    out[...] = total


def gathered_times(rows, place, pieces):
    count, width = rows.shape
    columns = pieces[0].shape[1]
    tile = min(256, count)
    whole = [pl.BlockSpec(piece.shape, lambda i, place: (0, 0)) for piece in pieces]
    return pl.pallas_call(
        gathered_kernel,
        grid_spec=pltpu.PrefetchScalarGridSpec(
            num_scalar_prefetch=1,
            grid=(count // tile,),
            in_specs=[pl.BlockSpec((tile, width), lambda i, place: (i, 0))] + whole,
            out_specs=pl.BlockSpec((tile, columns), lambda i, place: (i, 0)),
        ),
        out_shape=jax.ShapeDtypeStruct((count, columns), jnp.float32),
        compiler_params=pltpu.CompilerParams(vmem_limit_bytes=VMEM_BYTES),
        cost_estimate=pl.CostEstimate(
            flops=2 * count * width * columns, bytes_accessed=2 * (count + columns) * width, transcendentals=0
        ),
    )(jnp.reshape(place, (1,)).astype(jnp.int32), rows, *pieces)


def gathered_transposed_kernel(count, place, *refs):
    factors, pieces, out = refs[:count], refs[count:-1], refs[-1]
    size, half = pieces[0].shape[0], pieces[3].shape[0]
    for i, (bit, skip) in enumerate(((0, 0), (1, 0), (2, 0), (3, 0), (3, half))):
        start = pl.multiple_of(block_columns(place, bit, size) + skip, half)
        total = None
        for p in range(count):
            value = mul_nt(factors[p][...], pieces[5 * p + i][...])
            total = value if total is None else total + value
        out[:, pl.ds(start, pieces[i].shape[0])] = low(total)


def gathered_times_transposed(factors, place, pieces):
    count, rows = len(factors), factors[0].shape[0]
    width = 4 * pieces[0][0].shape[0]
    tile = min(256, rows)
    flat = [piece for some in pieces for piece in some]
    whole = [pl.BlockSpec(piece.shape, lambda i, place: (0, 0)) for piece in flat]
    wides = [pl.BlockSpec((tile, factor.shape[1]), lambda i, place: (i, 0)) for factor in factors]
    columns = sum(factor.shape[1] for factor in factors)
    return pl.pallas_call(
        functools.partial(gathered_transposed_kernel, count),
        grid_spec=pltpu.PrefetchScalarGridSpec(
            num_scalar_prefetch=1,
            grid=(rows // tile,),
            in_specs=wides + whole,
            out_specs=pl.BlockSpec((tile, width), lambda i, place: (i, 0)),
        ),
        out_shape=jax.ShapeDtypeStruct((rows, width), jnp.bfloat16),
        compiler_params=pltpu.CompilerParams(vmem_limit_bytes=VMEM_BYTES),
        cost_estimate=pl.CostEstimate(
            flops=2 * rows * width * columns, bytes_accessed=2 * (rows + columns) * width, transcendentals=0
        ),
    )(jnp.reshape(place, (1,)).astype(jnp.int32), *factors, *flat)


def join_kernel(squares, source, target):
    lines, _, columns = source.shape
    part = columns // squares
    for i in range(lines):
        for j in range(squares):
            at = (j * lines + i) * part
            target[:, at : at + part] = source[i, :, j * part : (j + 1) * part]


def columns_join(parts, squares):
    lines, rows, columns = parts.shape
    tile = 176 if rows % 176 == 0 else rows
    return pl.pallas_call(
        functools.partial(join_kernel, squares),
        grid=(rows // tile,),
        in_specs=[pl.BlockSpec((lines, tile, columns), lambda i: (0, i, 0))],
        out_specs=pl.BlockSpec((tile, lines * columns), lambda i: (i, 0)),
        out_shape=jax.ShapeDtypeStruct((rows, lines * columns), parts.dtype),
        compiler_params=pltpu.CompilerParams(vmem_limit_bytes=VMEM_BYTES),
        cost_estimate=pl.CostEstimate(flops=0, bytes_accessed=4 * parts.size, transcendentals=0),
    )(parts)


def flip(value, axis, bit):
    devices = range(lax.axis_size(axis))
    return lax.ppermute(value, axis, [(i, i ^ bit) for i in devices])


def shift(value, axis, distance):
    count = lax.axis_size(axis)
    return lax.ppermute(value, axis, [(i, (i + distance) % count) for i in range(count)])


def from_behind(block, axis, distance):
    devices = range(lax.axis_size(axis))
    route = [(i - distance, i) for i in devices if i - distance in devices]
    return lax.ppermute(block, axis, route)


def tie(value, *earlier):
    return lax.optimization_barrier((value,) + earlier)[0]


def put(buffer, piece, *start):
    return lax.dynamic_update_slice(buffer, piece, start)


def wide(value):
    return value.astype(jnp.float32)


def gather_line(shard):
    count, place = lax.axis_size("fsdp"), lax.axis_index("fsdp")
    pieces = [shard] + [shift(shard, "fsdp", d) for d in range(1, count)]
    order = [(place - i) % count for i in range(count)]
    return jnp.concatenate([lax.select_n(which, *pieces) for which in order], axis=0)


class Square:
    def __init__(self, own):
        self.own = own
        self.half = own.shape[0] // 2
        self.beside = flip(own, "ctx", 1)
        self.across = flip(own, "ctx", 2)

    def forward(self, *earlier):
        upper = self.beside[: self.half]
        lower = self.across[self.half :]
        if earlier:
            upper, lower = lax.optimization_barrier((upper, lower) + earlier)[:2]
        self.upper = flip(upper, "ctx", 2)
        self.lower = flip(lower, "ctx", 1)
        return self

    def done(self):
        return (self.upper, self.lower)

    def pieces(self):
        return [self.own, self.beside, self.across, self.upper, self.lower]

    def far(self):
        return jnp.concatenate([self.upper, self.lower], axis=0)


def both_sides(rows):
    if lax.axis_size("tp") == 2:
        return rows, flip(rows, "tp", 1)
    every = lax.all_gather(rows, "tp", axis=0, tiled=True)
    half = every.shape[0] // 2
    return every[:half], every[half:]


def core_sum(mine, other):
    if lax.axis_size("tp") == 2:
        return wide(mine) + wide(flip(other, "tp", 1))
    both = jnp.concatenate([mine, other], axis=0)
    return wide(lax.psum_scatter(both, "tp", scatter_dimension=0, tiled=True))


def neighbour_columns(rows):
    width = rows.shape[1] // 4
    place = lax.axis_index("ctx")
    return [lax.dynamic_slice_in_dim(rows, (place ^ bit) * width, width, 1) for bit in range(4)]


class Line:
    def __init__(self, own):
        count, place = lax.axis_size("fsdp"), lax.axis_index("fsdp")
        own = own.reshape(count, own.shape[0] // count, own.shape[1])

        def part(distance):
            return lax.dynamic_index_in_dim(own, (place + distance) % count, 0, keepdims=False)

        self.kept = part(0)
        self.sent = [low(part(distance)) for distance in range(1, count)]
        self.arrived = [shift(piece, "fsdp", distance + 1) for distance, piece in enumerate(self.sent)]

    def total(self, *late):
        total = self.kept
        for part in lax.optimization_barrier(tuple(self.arrived) + late)[: len(self.arrived)]:
            total = total + wide(part)
        return total


class Scatter:
    def __init__(self, columns, grads):
        self.columns, self.grads = columns, grads
        self.half = columns[0].shape[1] // 2
        self.mine = outer_rows(columns[0], grads)
        beside, across = (
            jnp.concatenate([self.side(3, 1), self.side(1, 1)], axis=1),
            jnp.concatenate([self.side(3, 0), self.side(2, 0)], axis=1),
        )
        self.sent = [low(outer_rows(beside, grads)), low(outer_rows(across, grads))]
        self.first = (flip(self.sent[0], "ctx", 1), flip(self.sent[1], "ctx", 2))

    def side(self, bit, lower):
        return self.columns[bit][:, lower * self.half : (lower + 1) * self.half]

    def second(self, *earlier):
        first = self.first
        if earlier:
            first = lax.optimization_barrier(first + earlier)[:2]
        beside, across = (wide(part) for part in first)
        upper = low(outer_rows(self.side(1, 0), self.grads) + across[: self.half])
        lower = low(outer_rows(self.side(2, 1), self.grads) + beside[: self.half])
        self.last = (flip(upper, "ctx", 1), flip(lower, "ctx", 2))
        self.kept = (beside, across)
        return upper, lower

    def own(self, *ties):
        beside_upper, across_lower = self.last
        if ties:
            beside_upper, across_lower = lax.optimization_barrier(self.last + ties)[:2]
        beside, across = self.kept
        own = self.mine
        upper = own[: self.half] + wide(beside_upper) + across[self.half :]
        lower = own[self.half :] + beside[self.half :] + wide(across_lower)
        return jnp.concatenate([upper, lower], axis=0)


def butterfly(value, axes):
    for axis in axes:
        count, bit = lax.axis_size(axis), 1
        while bit < count:
            value = value + flip(value, axis, bit)
            bit *= 2
    return value


def rms_scale(values, floor_value):
    return lax.rsqrt(jnp.mean(values * values, axis=-1, keepdims=True) + floor_value)


def norm_backward(grad_normed, inputs, scale, gain):
    normed = inputs * scale
    weighted = grad_normed * gain
    return (
        scale * (weighted - normed * jnp.mean(weighted * normed, axis=-1, keepdims=True)),
        normed,
    )


def times(left, right):
    return jnp.dot(left, right, preferred_element_type=jnp.float32)


def times_transposed(left, right):
    return lax.dot_general(
        left, right, (((1,), (1,)), ((), ())), preferred_element_type=jnp.float32
    )


def outer_rows(left, right):
    return lax.dot_general(
        left, right, (((0,), (0,)), ((), ())), preferred_element_type=jnp.float32
    )


def rows_mine(rows):
    count = rows.shape[1] // lax.axis_size("tp")
    return lax.dynamic_slice_in_dim(rows, lax.axis_index("tp") * count, count, 1)


def rows_scatter(partial):
    if lax.axis_size("tp") != 2:
        return wide(lax.psum_scatter(partial, "tp", scatter_dimension=1, tiled=True))
    count = partial.shape[1] // 2
    other = lax.dynamic_slice_in_dim(partial, (1 - lax.axis_index("tp")) * count, count, 1)
    return wide(rows_mine(partial)) + wide(flip(other, "tp", 1))


def rows_full(mine):
    if lax.axis_size("tp") != 2:
        return lax.all_gather(mine, "tp", axis=1, tiled=True)
    other = flip(mine, "tp", 1)
    lower = lax.axis_index("tp") == 0
    return jnp.concatenate([jnp.where(lower, mine, other), jnp.where(lower, other, mine)], axis=1)


def by_head(parts):
    heads = range(parts[0].shape[-1] // LANES)
    return jnp.concatenate([part[..., h * LANES : (h + 1) * LANES] for h in heads for part in parts], axis=-1)


def by_kind(joined):
    return [
        jnp.concatenate(
            [
                some[..., at : at + LANES]
                for some in joined
                for at in range(kind * LANES, some.shape[-1], 3 * LANES)
            ],
            axis=-1,
        )
        for kind in range(3)
    ]


def pass_states(own, transfer, forward, *beside):
    rule = "shij,shjk->shik" if forward == 1 else "shji,shjk->shik"
    leaving = own
    entered = low(jnp.zeros_like(own))
    for repeat in range(lax.axis_size("ctx") - 1):
        entered = from_behind(low(leaving), "ctx", forward)
        if repeat == 1 and beside:
            entered = tie(entered, *beside)
        leaving = own + jnp.einsum(rule, transfer, entered, preferred_element_type=jnp.float32)
    return wide(entered)


def local(
    block_input,
    doc_start,
    gain_mix,
    query_weight,
    key_weight,
    value_weight,
    beta_weight,
    beta_bias,
    conv_weight,
    gain_o,
    out_weight,
    gain_ffn,
    gate_weight,
    up_weight,
    down_weight,
    out_grad,
):
    seq_count, local_len, width = block_input.shape
    row_count = seq_count * local_len
    heads_here = beta_weight.shape[1]
    taps = conv_weight.shape[1]
    parts = 2 if heads_here % 2 == 0 else 1
    part_heads = heads_here // parts
    group = 2 if part_heads % 2 == 0 else 1
    part_cols = 3 * part_heads * LANES
    spare = LANES - heads_here
    units_here = gate_weight.shape[1]
    shard_rows = gate_weight.shape[0]

    joined = by_head([low(query_weight), low(key_weight), low(value_weight)])
    shards = [joined[:, p * part_cols : (p + 1) * part_cols] for p in range(parts)]
    shards[0] = jnp.concatenate([shards[0], jnp.pad(low(beta_weight), ((0, 0), (0, spare)))], axis=1)
    shards.append(low(out_weight).T)
    lines = []
    for shard in shards[:parts]:
        lines.append(gather_line(tie(shard, lines[-1]) if lines else shard))
    units = units_here // 4
    pieces = jnp.stack([low(gate_weight).T, low(up_weight).T, low(down_weight)])
    pieces = pieces.reshape(3, 4, units, shard_rows).transpose(1, 0, 2, 3)
    ffn_swapped = lax.all_to_all(pieces.reshape(4, 3 * units, shard_rows), "ctx", 0, 0)
    ffn_line = ffn_swapped.transpose(1, 0, 2).reshape(3 * units, 4 * shard_rows)
    line_count = lax.axis_size("fsdp")

    ctx_place = lax.axis_index("ctx")
    first_pos = ctx_place * local_len
    starts = doc_start - first_pos
    col, row = starts[:, :, None], starts[:, None, :]
    conv = by_head([conv_weight[0], conv_weight[1], conv_weight[2]])
    bias = jnp.pad(beta_bias, (0, spare))[None]
    gain_head = gain_o[None]
    tokens = block_input.reshape(row_count, width)
    inputs = wide(tokens)
    normed_mix = low(inputs * rms_scale(inputs, EPSILON) * gain_mix)
    grads_mine = rows_mine(out_grad).reshape(-1, width)

    square = Square(tie(lines[0], ffn_swapped)).forward(normed_mix)
    gate_up_parts = tie(ffn_line[None, : 2 * units], lines[parts - 1], *square.done())
    gate_up_parts = lax.all_gather(gate_up_parts, "fsdp", axis=0, tiled=True)
    down_parts = lax.all_gather(ffn_line[None, 2 * units :], "fsdp", axis=0, tiled=True)
    mix_full, kept, pre = [], [], []
    for p in range(parts):
        mix_full.append(square.pieces())
        arrived = square.done()
        ends = normed_mix.reshape(seq_count, local_len, width)[:, local_len - HALO :].reshape(seq_count * HALO, width)
        ends = gathered_times(ends, ctx_place, mix_full[p])
        ends = low(ends)
        halo = from_behind(ends[:, :part_cols].reshape(seq_count, HALO, part_cols), "ctx", 1)
        pre.append(gathered_times(tie(normed_mix, ends), ctx_place, mix_full[p]))
        if p == parts - 1:
            lines.append(gather_line(tie(shards[-1], pre[p])))
        square = Square(tie(lines[p + 1], halo, pre[p], *arrived))
        halo = wide(halo)
        convs = conv[:, p * part_cols : (p + 1) * part_cols]
        kept.append(
            [halo, convs]
            + list(
                mixer_forward(
                    pre[p], pre[0], bias, halo, convs, col, row, taps, p * part_heads, part_heads, group
                )
            )
        )
        square.forward(kept[p][2])
        if p == 0:
            grad_square = Square(tie(grads_mine, kept[p][2], *square.done()))
    out_full = square.pieces()

    inputs_mine = wide(tie(rows_mine(block_input).reshape(-1, width), kept[0][2]))
    gate_up_full = columns_join(gate_up_parts, 4)
    finals = jnp.concatenate([some[4] for some in kept], axis=1)
    transfer = low(finals[..., LANES:])
    first = tie(finals[..., :LANES], gate_up_full, grad_square.beside, grad_square.across)
    entering = pass_states(first, transfer, 1)
    entered = [entering[:, p * part_heads : (p + 1) * part_heads] for p in range(parts)]
    grad_square.forward(entering)
    grad_rows = [both_sides(part) for part in (grad_square.own, grad_square.beside, grad_square.across)]
    mixed_rows = []
    for p in range(parts):
        own, carry = kept[p][2:4]
        mixed_rows.append(mixer_output(own, carry, entered[p], gain_head, group))
    mixed_rows = jnp.concatenate(mixed_rows, axis=1)
    mixed_rows = tie(mixed_rows, *(other for _, other in grad_rows))
    grad_rows.append(both_sides(grad_square.far()))

    branch = gathered_times_transposed([mixed_rows], ctx_place, [out_full]).reshape(seq_count, local_len, width)
    branch = tie(branch, down_parts)
    residual = inputs_mine + rows_scatter(branch).reshape(-1, width)
    scale_ffn = rms_scale(residual, EPSILON)
    square = Square(low(residual * scale_ffn * gain_ffn))
    ffn_full = (gate_up_full, columns_join(down_parts, 4))

    ffn_rows = [both_sides(square.own)]
    ffn_out = [ffn_both(ffn_rows[0], grad_rows[0], *ffn_full)]
    square.forward(ffn_out[0][0][0])
    ffn_rows.append(both_sides(tie(square.beside, ffn_out[0][0][0])))
    ffn_out.append(ffn_both(ffn_rows[1], grad_rows[1], *ffn_full))
    ffn_rows.append(both_sides(tie(square.across, ffn_out[0][0][0])))
    mine, other = ffn_rows[2]
    ffn_out.append(ffn_both((tie(mine, ffn_out[1][0][0], *square.done()), other), grad_rows[2], *ffn_full))
    beside_sums, across_sums = (low(core_sum(*(side[1] for side in ffn_out[bit]))) for bit in (1, 2))
    ffn_rows.append(both_sides(square.far()))
    mine, other = ffn_rows[3]
    ffn_out.append(ffn_both((tie(mine, beside_sums, across_sums), other), grad_rows[3], *ffn_full))
    near_sums = (flip(beside_sums, "ctx", 1), flip(across_sums, "ctx", 2))
    mine, other = (side[1] for side in ffn_out[3])
    far_sums = low(core_sum(mine, tie(other, *near_sums)))
    acts = [side[0] for outs in ffn_out for side in outs]
    own_sums = core_sum(*(side[1] for side in ffn_out[0]))
    result_low = []
    for bit in (1, 2):
        mine, other = (side[2] for side in ffn_out[bit])
        result_low.append(low(core_sum(tie(mine, far_sums), other)))
    acts[0] = tie(acts[0], far_sums, own_sums, *result_low)
    far_sums = flip(far_sums, "ctx", 3)
    sums = ffn_weights(
        acts,
        [side for sides in ffn_rows for side in sides],
        [side for sides in grad_rows for side in sides],
        line_count,
        4,
    )

    far_sums, sums = lax.optimization_barrier((far_sums, sums))
    result_near = [flip(tie(part, far_sums), "ctx", bit) for part, bit in zip(result_low, (1, 2))]
    grad_normed = own_sums + wide(near_sums[0]) + wide(near_sums[1]) + wide(far_sums)
    back_ffn, unit_ffn = norm_backward(grad_normed, residual, scale_ffn, gain_ffn)
    grad_residual = wide(grads_mine) + back_ffn
    gain_ffn_part = jnp.sum(grad_normed * unit_ffn, axis=0)
    grad_branch = rows_full(low(grad_residual).reshape(seq_count, -1, width)).reshape(row_count, width)
    grad_heads = gathered_times(grad_branch, ctx_place, out_full)
    backs, acrosses, gain_o_part = [], [], 0.0
    for p in range(parts):
        _, _, own, carry, _, _, _, _ = kept[p]
        back, across, gain_part = mixer_output_backward(
            own, carry, entered[p], gain_head, grad_heads, p * part_heads, group
        )
        backs.append(back)
        acrosses.append(across)
        gain_o_part = gain_o_part + jnp.sum(gain_part, axis=(0, 1, 2))
    grad_end = pass_states(jnp.concatenate(acrosses, axis=1), transfer, -1, *result_near)
    total = lax.psum_scatter(sums, "fsdp", scatter_dimension=0, tiled=True)

    out_grad_w = low(outer_rows(grad_branch, mixed_rows))
    out_part = out_grad_w
    out_grad_w = lax.psum_scatter(out_grad_w, ("ctx", "fsdp"), scatter_dimension=0, tiled=True)

    mine, other = (side[2] for side in ffn_out[0])
    result_own = core_sum(mine, tie(other, grad_branch))
    mine, other = (side[2] for side in ffn_out[3])
    result_far = flip(tie(low(core_sum(mine, tie(other, grad_branch))), grad_end), "ctx", 3)
    columns = neighbour_columns(normed_mix)
    grad_mixes, mix_grads, conv_parts = [None] * parts, [None] * parts, [None] * parts
    logits = 0.0
    scatter = None
    for p in reversed(range(parts)):
        halo, convs, own, carry, final, inverses, updates, states = kept[p]
        heads = slice(p * part_heads, (p + 1) * part_heads)
        back = tie(backs[p], out_part) if scatter is None else tie(backs[p], total, *scatter.sent)
        grad_mix, tail, before, conv_parts[p], logit = mixer_backward(
            pre[p], pre[0], bias, halo, convs, col, row, back, inverses, updates, states,
            entered[p], grad_end[:, heads], taps, p * part_heads, part_heads, group,
        )
        logits = logits + logit
        tail = low(tail + from_behind(before, "ctx", -1))
        grad_mix = put(grad_mix.reshape(seq_count, local_len, -1), tail, 0, local_len - HALO, 0)
        grad_mix = grad_mix.reshape(row_count, -1)
        if scatter is not None:
            earlier_ready = scatter.second(before)
            earlier_scatter = scatter
        else:
            grad_mix = tie(grad_mix, result_far)
        if p == 0:
            grad_mix = jnp.concatenate([grad_mix, low(logits)], axis=1)
        grad_mixes[p] = grad_mix
        scatter = Scatter(columns, grad_mix)
        if p > 0:
            result_far = tie(result_far, *scatter.sent)
    result = result_own + wide(result_near[0]) + wide(result_near[1])
    result = result + wide(result_far)
    block_output = rows_full(low(residual + result).reshape(seq_count, -1, width))
    ready = (block_output, scatter.mine)
    if parts > 1:
        ready = ready + tuple(earlier_ready) + (earlier_scatter.mine,)
    ready = scatter.second(*ready)
    grad_mixes[0] = tie(grad_mixes[0], *ready)
    mix_back = tie(gathered_times_transposed(grad_mixes, ctx_place, mix_full), *scatter.last)
    mix_back = rows_scatter(mix_back.reshape(seq_count, local_len, width)).reshape(-1, width)
    back_mix, unit_mix = norm_backward(mix_back, inputs_mine, rms_scale(inputs_mine, EPSILON), gain_mix)
    input_grad = rows_full(low(grad_residual + back_mix).reshape(seq_count, -1, width))
    gain_mix_part = jnp.sum(mix_back * unit_mix, axis=0)

    conv_cols = jnp.concatenate([jnp.sum(part, axis=0)[:taps] for part in conv_parts], axis=1)
    gains = butterfly(jnp.concatenate([gain_mix_part, gain_ffn_part, gain_o_part]), ("tp",))
    conv_kinds = jnp.stack(by_kind([conv_cols]))
    sums = jnp.concatenate([gains, conv_kinds.reshape(-1), jnp.sum(logits, axis=0)])
    last_line = Line(scatter.own())
    for p in range(1, parts):
        own = low(earlier_scatter.own(*last_line.sent))
        mix_grads[p] = lax.psum_scatter(own, "fsdp", scatter_dimension=0, tiled=True)
    sums = butterfly(tie(sums, input_grad, *last_line.sent), ("ctx",))
    mix_grads[0] = last_line.total(sums)
    count = lax.axis_size("fsdp")
    bit = 1
    while bit < count // 2:
        sums = sums + flip(sums, "fsdp", bit)
        bit *= 2
    for p in range(1, parts):
        mix_grads[p] = wide(tie(mix_grads[p], sums))
    if count > 1:
        sums = sums + flip(sums, "fsdp", bit)
    query_grad, key_grad, value_grad = by_kind([grad[:, :part_cols] for grad in mix_grads])
    beta_grad = mix_grads[0][:, part_cols : part_cols + heads_here]
    ends = [width, 2 * width, 2 * width + LANES, sums.shape[0] - LANES]
    gain_mix_grad, gain_ffn_grad, gain_o_grad, conv_grad, bias_grad = jnp.split(sums, ends)
    conv_grad = conv_grad.reshape(conv_kinds.shape)
    bias_grad = bias_grad[:heads_here]
    out_grad_w = wide(tie(out_grad_w, *scatter.last)).T
    pieces = tie(total, *scatter.last).reshape(3 * units, 4, shard_rows).transpose(1, 0, 2)
    arrived = lax.all_to_all(pieces, "ctx", 0, 0).reshape(4, 3, units, shard_rows)
    gate_grad, up_grad, down_grad = (wide(arrived[:, i].reshape(units_here, shard_rows)) for i in range(3))

    return (
        block_output,
        input_grad,
        gain_mix_grad,
        query_grad,
        key_grad,
        value_grad,
        beta_grad,
        bias_grad,
        conv_grad,
        gain_o_grad,
        out_grad_w,
        gain_ffn_grad,
        gate_grad.T,
        up_grad.T,
        down_grad,
    )


def solution(mesh):
    placed = (
        P("fsdp", "ctx", None),
        P("fsdp", "ctx"),
        P(),
        P(("ctx", "fsdp"), "tp"),
        P(("ctx", "fsdp"), "tp"),
        P(("ctx", "fsdp"), "tp"),
        P(("ctx", "fsdp"), "tp"),
        P("tp"),
        P(None, None, "tp"),
        P(),
        P("tp", ("ctx", "fsdp")),
        P(),
        P(("ctx", "fsdp"), "tp"),
        P(("ctx", "fsdp"), "tp"),
        P("tp", ("ctx", "fsdp")),
        P("fsdp", "ctx", None),
    )
    return jax.shard_map(
        local,
        mesh=mesh,
        in_specs=placed,
        out_specs=(
            P("fsdp", "ctx", None),
            P("fsdp", "ctx", None),
            P(),
            P(("ctx", "fsdp"), "tp"),
            P(("ctx", "fsdp"), "tp"),
            P(("ctx", "fsdp"), "tp"),
            P(("ctx", "fsdp"), "tp"),
            P("tp"),
            P(None, None, "tp"),
            P(),
            P("tp", ("ctx", "fsdp")),
            P(),
            P(("ctx", "fsdp"), "tp"),
            P(("ctx", "fsdp"), "tp"),
            P("tp", ("ctx", "fsdp")),
        ),
        check_vma=False,
    )
```

```python
import functools
import math
import jax
import jax.numpy as jnp
from jax import lax
from jax.experimental import pallas as pl
from jax.experimental.pallas import tpu as pltpu
from jax.sharding import PartitionSpec as P

LANES = 128
CHUNK = 128
HALO = 8
EPSILON = 1e-06
HEAD_FLOOR = 0.01
VMEM_BYTES = 60 * 1024 * 1024


def low(value):
    return value.astype(jnp.bfloat16)


def mul_nn(left, right):
    return lax.dot_general(low(left), low(right), (((1,), (0,)), ((), ())), preferred_element_type=jnp.float32)


def mul_nt(left, right):
    return lax.dot_general(low(left), low(right), (((1,), (1,)), ((), ())), preferred_element_type=jnp.float32)


def mul_tn(left, right):
    return lax.dot_general(low(left), low(right), (((0,), (0,)), ((), ())), preferred_element_type=jnp.float32)


def iota(shape, axis):
    return lax.broadcasted_iota(jnp.int32, shape, axis)


def chunk_masks(col, row, first):
    size = col.shape[0]
    same = col == row
    order, other = iota((size, size), 0), iota((size, size), 1)
    upto = same & (order >= other)
    below = same & (order > other)
    carried = (col < first).astype(jnp.float32)
    last = (col == row[:, size - 1 :]).astype(jnp.float32)
    keep = (row[:, size - 1 :] < first).astype(jnp.float32)
    return upto, below, carried, last, keep


def invert_units(systems):
    size = systems[0].shape[0]
    order, other = iota((size, size), 0), iota((size, size), 1)
    identity = (order == other).astype(jnp.float32)
    span = 1
    found = None
    while span < size:
        pair = (order // (2 * span) == other // (2 * span)) & (order // span != other // span)
        parts = [jnp.where(pair, system, 0.0) for system in systems]
        if found is None:
            found = [identity - part for part in parts]
        else:
            right = [mul_nn(part, value) for part, value in zip(parts, found)]
            found = [value - mul_nn(value, part) for value, part in zip(found, right)]
        span *= 2
    return found


def conv_rows(ext, conv, col, offset, size, lane, taps):
    total = None
    moved = []
    position = iota((size, 1), 0) + offset
    for tap in range(taps):
        back = taps - 1 - tap
        values = ext[pl.ds(HALO + offset - back, size), lane : lane + LANES]
        values = jnp.where(position - back >= col, values, 0.0)
        moved.append(values)
        term = conv[tap : tap + 1, lane : lane + LANES] * values
        total = term if total is None else total + term
    return total, moved


def unit(values):
    return values * lax.rsqrt(jnp.sum(values * values, axis=-1, keepdims=True) + EPSILON)


def head_column(values, head):
    return jnp.sum(jnp.where(iota(values.shape, 1) == head, values, 0.0), axis=-1, keepdims=True)


def forward_kernel(taps, heads, first, pre, beta, bias, halo, conv, col_ref, row_ref, own, carry, final, inv, upd, states, ext):
    length = pre.shape[0]
    ext[:HALO] = halo[0]
    ext[HALO:] = pre[...]
    head = first + pl.program_id(1) * heads
    jobs = [(i, j) for j in range(length // CHUNK) for i in range(heads)]
    data = {}
    for j in range(length // CHUNK):
        rows = pl.ds(j * CHUNK, CHUNK)
        col, row = col_ref[0, rows], row_ref[0, :, rows]
        masks = chunk_masks(col, row, j * CHUNK)
        strengths = jax.nn.sigmoid(beta[rows] + bias[...])
        for i in range(heads):
            acts = []
            for kind in range(3):
                total, _ = conv_rows(ext, conv, col, j * CHUNK, CHUNK, (3 * i + kind) * LANES, taps)
                acts.append(total * jax.nn.sigmoid(total))
            query, key, value = unit(acts[0]), unit(acts[1]), acts[2]
            strength = head_column(strengths, head + i)
            grams = mul_nt(jnp.concatenate([low(key), low(query)], axis=0), key)
            system = jnp.where(masks[1], strength * grams[:CHUNK], 0.0)
            scores = low(jnp.where(masks[0], grams[CHUNK:], 0.0))
            data[i, j] = (low(query), low(key), value, strength, scores, masks, system)
    inverses = dict(zip(jobs, invert_units([data[job][6] for job in jobs])))
    for i in range(heads):
        state = jnp.concatenate(
            [
                jnp.zeros((LANES, LANES), jnp.float32),
                (iota((LANES, LANES), 0) == iota((LANES, LANES), 1)).astype(jnp.float32),
            ],
            axis=1,
        )
        final[0, i] = state
    for j in range(length // CHUNK):
        rows = pl.ds(j * CHUNK, CHUNK)
        for i in range(heads):
            query, key, value, strength, scores, masks, _ = data[i, j]
            _, _, carried, last, keep = masks
            inverse = low(inverses[i, j])
            state = final[0, i]
            state_low = low(state)
            read = mul_nn(jnp.concatenate([key, query], axis=0), state_low)
            wide = jnp.concatenate([value, jnp.zeros_like(value)], axis=1)
            targets = strength * (wide - carried * read[:CHUNK])
            update = low(mul_nn(inverse, targets))
            result = carried * read[CHUNK:] + mul_nn(scores, update)
            final[0, i] = keep * state + mul_tn(key * low(last), update)
            lanes = slice(i * LANES, (i + 1) * LANES)
            own[rows, lanes] = result[:, :LANES]
            carry[rows, lanes] = low(result[:, LANES:])
            inv[0, i, j] = inverse
            upd[0, i, j] = update
            states[0, i, j] = state_low


def mixer_forward(pre, logit, bias, halo, conv, col, row, taps, first, heads_here, group):
    seqs, length = col.shape[0], col.shape[1]
    steps = heads_here // group
    chunks = length // CHUNK
    wide = 3 * LANES * group
    rows = seqs * length

    def tile(*tail, kind):
        return jax.ShapeDtypeStruct((seqs, heads_here) + tail, kind)

    def spec(*tail):
        return pl.BlockSpec((1, group) + tail, lambda s, h: (s, h) + (0,) * len(tail))

    flat = pl.BlockSpec((length, LANES * group), lambda s, h: (s, h))
    last = logit.shape[1] // LANES - 1
    return pl.pallas_call(
        functools.partial(forward_kernel, taps, group, first),
        grid=(seqs, steps),
        in_specs=[
            pl.BlockSpec((length, wide), lambda s, h: (s, h)),
            pl.BlockSpec((length, LANES), lambda s, h: (s, last)),
            pl.BlockSpec((1, LANES), lambda s, h: (0, 0)),
            pl.BlockSpec((1, HALO, wide), lambda s, h: (s, 0, h)),
            pl.BlockSpec((conv.shape[0], wide), lambda s, h: (0, h)),
            pl.BlockSpec((1, length, 1), lambda s, h: (s, 0, 0)),
            pl.BlockSpec((1, 1, length), lambda s, h: (s, 0, 0)),
        ],
        out_specs=[
            flat,
            flat,
            spec(LANES, 2 * LANES),
            spec(chunks, CHUNK, CHUNK),
            spec(chunks, CHUNK, 2 * LANES),
            spec(chunks, LANES, 2 * LANES),
        ],
        out_shape=[
            jax.ShapeDtypeStruct((rows, heads_here * LANES), jnp.float32),
            jax.ShapeDtypeStruct((rows, heads_here * LANES), jnp.bfloat16),
            tile(LANES, 2 * LANES, kind=jnp.float32),
            tile(chunks, CHUNK, CHUNK, kind=jnp.bfloat16),
            tile(chunks, CHUNK, 2 * LANES, kind=jnp.bfloat16),
            tile(chunks, LANES, 2 * LANES, kind=jnp.bfloat16),
        ],
        scratch_shapes=[pltpu.VMEM((length + HALO, wide), jnp.float32)],
        compiler_params=pltpu.CompilerParams(vmem_limit_bytes=VMEM_BYTES),
        cost_estimate=pl.CostEstimate(
            flops=60 * rows * heads_here * CHUNK * LANES, bytes_accessed=40 * rows * heads_here * LANES, transcendentals=0
        ),
    )(pre, logit, bias, halo, conv, col, row)


def backward_kernel(
    taps, heads, first, pre, beta, bias, halo, conv, col_ref, row_ref, grad_ref, inv, upd, states, start, end,
    grad_pre, tail, before, conv_grad, logits, ext, grad_ext,
):
    length = pre.shape[0]
    step = pl.program_id(1)
    head = first + step * heads
    ext[:HALO] = halo[0]
    ext[HALO:] = pre[...]
    grad_ext[...] = jnp.zeros_like(grad_ext)

    @pl.when(step == 0)
    def _():
        logits[...] = jnp.zeros_like(logits)

    grad_states = [end[0, i] for i in range(heads)]
    entry = [low(start[0, i]) for i in range(heads)]
    tap_sums = {}
    for j in reversed(range(length // CHUNK)):
        offset = j * CHUNK
        rows = pl.ds(offset, CHUNK)
        col, row = col_ref[0, rows], row_ref[0, :, rows]
        upto, below, carried, last, keep = chunk_masks(col, row, offset)
        strengths = jax.nn.sigmoid(beta[rows] + bias[...])
        grad_logit = jnp.zeros((CHUNK, LANES), jnp.float32)
        for i in range(heads):
            raw, taps_in = [], []
            for kind in range(3):
                total, moved = conv_rows(ext, conv, col, offset, CHUNK, (3 * i + kind) * LANES, taps)
                raw.append(total)
                taps_in.append(moved)
            gates = [jax.nn.sigmoid(total) for total in raw]
            acts = [total * gate for total, gate in zip(raw, gates)]
            scales = [lax.rsqrt(jnp.sum(act * act, axis=-1, keepdims=True) + EPSILON) for act in acts[:2]]
            query, key, value = acts[0] * scales[0], acts[1] * scales[1], acts[2]
            strength = head_column(strengths, head + i)
            lanes = slice(i * LANES, (i + 1) * LANES)
            query_low, key_low = low(query), low(key)
            grams = mul_nt(jnp.concatenate([key_low, query_low], axis=0), key_low)
            gram = jnp.where(below, grams[:CHUNK], 0.0)
            scores = jnp.where(upto, grams[CHUNK:], 0.0)
            inverse = inv[0, i, j]
            update = upd[0, i, j]
            update = low(update[:, :LANES].astype(jnp.float32) + mul_nn(update[:, LANES:], entry[i]))
            state = states[0, i, j]
            state = low(state[:, :LANES].astype(jnp.float32) + mul_nn(state[:, LANES:], entry[i]))
            grad_out = grad_ref[rows, lanes]
            grad_state = grad_states[i]
            grad_state_low = low(grad_state)
            key_last = key_low * low(last)
            grad_update = mul_tn(scores, grad_out) + mul_nn(key_last, grad_state_low)
            grad_target = mul_tn(inverse, grad_update)
            weighted = strength * grad_target
            passed = carried * weighted
            out_carried = carried * grad_out.astype(jnp.float32)
            query_carried = query_low * low(carried)
            grad_states[i] = (
                keep * grad_state + mul_tn(query_carried, grad_out) - mul_tn(key_low, passed)
            )
            grad_scores = jnp.where(upto, mul_nt(grad_out, update), 0.0)
            grad_system = jnp.where(below, mul_nt(grad_target, update), 0.0)
            remainder = value - carried * mul_nn(key_low, state)
            grad_strength = jnp.sum(grad_target * remainder - grad_system * gram, axis=-1, keepdims=True)
            scaled = strength * grad_system
            from_state = mul_nt(jnp.concatenate([low(out_carried), low(passed)], axis=0), state)
            from_keys = mul_nn(jnp.concatenate([low(grad_scores), low(scaled + scaled.T)], axis=0), key_low)
            grad_query = from_state[:CHUNK] + from_keys[:CHUNK]
            grad_key = (
                mul_tn(grad_scores, query_low)
                + last * mul_nt(update, grad_state_low)
                - from_state[CHUNK:]
                - from_keys[CHUNK:]
            )
            grad_logit = grad_logit + jnp.where(
                iota((CHUNK, LANES), 1) == head + i, grad_strength * strength * (1.0 - strength), 0.0
            )
            grads = [
                scales[0] * (grad_query - query * jnp.sum(grad_query * query, axis=-1, keepdims=True)),
                scales[1] * (grad_key - key * jnp.sum(grad_key * key, axis=-1, keepdims=True)),
                weighted,
            ]
            position = iota((CHUNK, 1), 0) + offset
            for kind in range(3):
                gate, total = gates[kind], raw[kind]
                grad_conv = grads[kind] * gate * (1.0 + total * (1.0 - gate))
                lane = (3 * i + kind) * LANES
                for tap in range(taps):
                    back = taps - 1 - tap
                    part = jnp.sum(grad_conv * taps_in[kind][tap], axis=0, keepdims=True)
                    spot = (i, kind, tap)
                    tap_sums[spot] = part if spot not in tap_sums else tap_sums[spot] + part
                    back_part = jnp.where(
                        position - back >= col, grad_conv * conv[tap : tap + 1, lane : lane + LANES], 0.0
                    )
                    where = pl.ds(HALO + offset - back, CHUNK)
                    grad_ext[where, lane : lane + LANES] += back_part
        logits[rows] += grad_logit
    grad_pre[...] = low(grad_ext[HALO:])
    before[0] = grad_ext[:HALO]
    tail[0] = grad_ext[length:]
    for i in range(heads):
        for kind in range(3):
            lane = (3 * i + kind) * LANES
            for tap in range(taps):
                conv_grad[0, tap : tap + 1, lane : lane + LANES] = tap_sums[i, kind, tap]


def mixer_backward(
    pre, logit, bias, halo, conv, col, row, grad_mixed, inv, upd, states, start, end, taps, first, heads_here, group
):
    seqs, length = col.shape[0], col.shape[1]
    steps = heads_here // group
    chunks = length // CHUNK
    wide = 3 * LANES * group
    rows = seqs * length

    def spec(*tail):
        return pl.BlockSpec((1, group) + tail, lambda s, h: (s, h) + (0,) * len(tail))

    last = logit.shape[1] // LANES - 1
    part = pl.BlockSpec((1, HALO, wide), lambda s, h: (s, 0, h))
    edge = jax.ShapeDtypeStruct((seqs, HALO, 3 * LANES * heads_here), jnp.float32)
    return pl.pallas_call(
        functools.partial(backward_kernel, taps, group, first),
        grid=(seqs, steps),
        in_specs=[
            pl.BlockSpec((length, wide), lambda s, h: (s, h)),
            pl.BlockSpec((length, LANES), lambda s, h: (s, last)),
            pl.BlockSpec((1, LANES), lambda s, h: (0, 0)),
            part,
            pl.BlockSpec((conv.shape[0], wide), lambda s, h: (0, h)),
            pl.BlockSpec((1, length, 1), lambda s, h: (s, 0, 0)),
            pl.BlockSpec((1, 1, length), lambda s, h: (s, 0, 0)),
            pl.BlockSpec((length, LANES * group), lambda s, h: (s, h)),
            spec(chunks, CHUNK, CHUNK),
            spec(chunks, CHUNK, 2 * LANES),
            spec(chunks, LANES, 2 * LANES),
            spec(LANES, LANES),
            spec(LANES, LANES),
        ],
        out_specs=[
            pl.BlockSpec((length, wide), lambda s, h: (s, h)),
            part,
            part,
            part,
            pl.BlockSpec((length, LANES), lambda s, h: (s, 0)),
        ],
        out_shape=[
            jax.ShapeDtypeStruct((rows, 3 * LANES * heads_here), jnp.bfloat16),
            edge,
            edge,
            edge,
            jax.ShapeDtypeStruct((rows, LANES), jnp.float32),
        ],
        scratch_shapes=[
            pltpu.VMEM((length + HALO, wide), jnp.float32),
            pltpu.VMEM((length + HALO, wide), jnp.float32),
        ],
        compiler_params=pltpu.CompilerParams(vmem_limit_bytes=VMEM_BYTES),
        cost_estimate=pl.CostEstimate(
            flops=60 * rows * heads_here * CHUNK * LANES, bytes_accessed=40 * rows * heads_here * LANES, transcendentals=0
        ),
    )(pre, logit, bias, halo, conv, col, row, grad_mixed, inv, upd, states, start, end)


def mixed_rows_of(own, carry, start):
    return own + mul_nn(carry, start)


def output_kernel(heads, own, carry, start, gain, out):
    for i in range(heads):
        lanes = slice(i * LANES, (i + 1) * LANES)
        mixed = mixed_rows_of(own[:, lanes], carry[:, lanes], start[0, i])
        scale = lax.rsqrt(jnp.mean(mixed * mixed, axis=-1, keepdims=True) + HEAD_FLOOR)
        out[:, lanes] = low(mixed * scale * gain[...])


def output_backward_kernel(heads, own, carry, start, gain, grad, out, across, gain_grad):
    total = jnp.zeros((1, LANES), jnp.float32)
    for i in range(heads):
        lanes = slice(i * LANES, (i + 1) * LANES)
        carried = carry[:, lanes]
        mixed = mixed_rows_of(own[:, lanes], carried, start[0, i])
        scale = lax.rsqrt(jnp.mean(mixed * mixed, axis=-1, keepdims=True) + HEAD_FLOOR)
        normed = mixed * scale
        upper = grad[:, lanes].astype(jnp.float32)
        total = total + jnp.sum(upper * normed, axis=0, keepdims=True)
        weighted = upper * gain[...]
        back = scale * (weighted - normed * jnp.mean(weighted * normed, axis=-1, keepdims=True))
        out[:, lanes] = low(back)
        across[0, i] = mul_tn(carried, back)
    gain_grad[0, 0] = total


def mixer_output(own, carry, start, gain, group):
    seqs, heads_here = start.shape[:2]
    rows = own.shape[0]
    length = rows // seqs
    flat = pl.BlockSpec((length, LANES * group), lambda s, h: (s, h))
    square = pl.BlockSpec((1, group, LANES, LANES), lambda s, h: (s, h, 0, 0))
    return pl.pallas_call(
        functools.partial(output_kernel, group),
        grid=(seqs, heads_here // group),
        in_specs=[flat, flat, square, pl.BlockSpec((1, LANES), lambda s, h: (0, 0))],
        out_specs=flat,
        out_shape=jax.ShapeDtypeStruct(own.shape, jnp.bfloat16),
        compiler_params=pltpu.CompilerParams(vmem_limit_bytes=VMEM_BYTES),
        cost_estimate=pl.CostEstimate(
            flops=2 * own.size * LANES, bytes_accessed=8 * own.size, transcendentals=0
        ),
    )(own, carry, start, gain)


def mixer_output_backward(own, carry, start, gain, grad, first, group):
    seqs, heads_here = start.shape[:2]
    rows = own.shape[0]
    length = rows // seqs
    steps = heads_here // group
    flat = pl.BlockSpec((length, LANES * group), lambda s, h: (s, h))
    base = first // group
    shifted = pl.BlockSpec((length, LANES * group), lambda s, h: (s, base + h))
    square = pl.BlockSpec((1, group, LANES, LANES), lambda s, h: (s, h, 0, 0))
    return pl.pallas_call(
        functools.partial(output_backward_kernel, group),
        grid=(seqs, steps),
        in_specs=[flat, flat, square, pl.BlockSpec((1, LANES), lambda s, h: (0, 0)), shifted],
        out_specs=[flat, square, pl.BlockSpec((1, 1, 1, LANES), lambda s, h: (s, h, 0, 0))],
        out_shape=[
            jax.ShapeDtypeStruct(own.shape, jnp.bfloat16),
            jax.ShapeDtypeStruct(start.shape, jnp.float32),
            jax.ShapeDtypeStruct((seqs, steps, 1, LANES), jnp.float32),
        ],
        compiler_params=pltpu.CompilerParams(vmem_limit_bytes=VMEM_BYTES),
        cost_estimate=pl.CostEstimate(
            flops=4 * own.size * LANES, bytes_accessed=12 * own.size, transcendentals=0
        ),
    )(own, carry, start, gain, grad)


def ffn_kernel(mine, other, mine_grads, other_grads, gate_w, up_w, down_w, *outs):
    rows = jnp.concatenate([mine[...], other[...]], axis=0)
    grads = jnp.concatenate([mine_grads[...], other_grads[...]], axis=0)
    half = mine.shape[0]
    gate = mul_nt(rows, gate_w[...])
    up = mul_nt(rows, up_w[...])
    grad_hidden = mul_nt(grads, down_w[...])
    sigmoid = jax.nn.sigmoid(gate)
    active = gate * sigmoid
    kept = low(active * up)
    back_gate = low(grad_hidden * up * sigmoid * (1.0 + gate * (1.0 - sigmoid)))
    back_up = low(grad_hidden * active)
    grad_rows = low(mul_nn(back_gate, gate_w[...]) + mul_nn(back_up, up_w[...]))
    result = low(mul_nn(kept, down_w[...]))
    for side in range(2):
        here = slice(side * half, (side + 1) * half)
        acts, grad_out, result_out = outs[3 * side : 3 * side + 3]
        for kind, value in enumerate((back_gate, back_up, kept)):
            acts[kind] = value[here]
        grad_out[...] = grad_rows[here]
        result_out[...] = result[here]


def ffn_both(rows, grads, gate_up, down):
    count, width = rows[0].shape
    units = down.shape[0]
    tile = min(256, count)
    wide_rows = pl.BlockSpec((tile, width), lambda i: (i, 0))
    narrow = pl.BlockSpec((3, tile, units), lambda i: (0, i, 0))

    def third(index):
        return pl.BlockSpec((units, width), lambda i: (index, 0))

    flat = jax.ShapeDtypeStruct((count, width), jnp.bfloat16)
    outs = pl.pallas_call(
        ffn_kernel,
        grid=(count // tile,),
        in_specs=[wide_rows] * 4 + [third(0), third(1), third(0)],
        out_specs=[narrow, wide_rows, wide_rows] * 2,
        out_shape=[jax.ShapeDtypeStruct((3, count, units), jnp.bfloat16), flat, flat] * 2,
        compiler_params=pltpu.CompilerParams(vmem_limit_bytes=VMEM_BYTES),
        cost_estimate=pl.CostEstimate(
            flops=24 * count * width * units, bytes_accessed=16 * count * width + 6 * units * width, transcendentals=0
        ),
    )(*rows, *grads, gate_up, gate_up, down)
    return outs[:3], outs[3:]


def ffn_weights_kernel(count, lines, *refs):
    acts, rows, grads = refs[:count], refs[count : 2 * count], refs[2 * count : 3 * count]
    out, total = refs[-2:]
    part = out.shape[-1]

    def add(sources):
        for i in range(count):
            value = mul_tn(acts[i][0], sources[i][...])
            if i == 0:
                total[...] = value
            else:
                total[...] += value

    @pl.when(pl.program_id(0) < 2)
    def _():
        add(rows)

    @pl.when(pl.program_id(0) == 2)
    def _():
        add(grads)

    for line in range(lines):
        out[line, 0] = low(total[:, line * part : (line + 1) * part])


def ffn_weights(acts, rows, grads, lines, squares):
    count, width = len(acts), rows[0].shape[1]
    size, units = acts[0].shape[1:]
    block = width // squares
    part = block // lines
    act_spec = pl.BlockSpec((1, size, units), lambda k, c: (k, 0, 0))
    row_spec = pl.BlockSpec((size, block), lambda k, c: (0, jnp.where(k < 2, c, squares - 1)))
    grad_spec = pl.BlockSpec((size, block), lambda k, c: (0, jnp.where(k < 2, 0, c)))
    return pl.pallas_call(
        functools.partial(ffn_weights_kernel, count, lines),
        grid=(3, squares),
        in_specs=[act_spec] * count + [row_spec] * count + [grad_spec] * count,
        out_specs=pl.BlockSpec((lines, 1, units, part), lambda k, c: (0, k, 0, c)),
        out_shape=jax.ShapeDtypeStruct((lines, 3, units, squares * part), jnp.bfloat16),
        scratch_shapes=[pltpu.VMEM((units, block), jnp.float32)],
        compiler_params=pltpu.CompilerParams(vmem_limit_bytes=VMEM_BYTES),
        cost_estimate=pl.CostEstimate(
            flops=6 * count * size * width * units, bytes_accessed=8 * count * size * width, transcendentals=0
        ),
    )(*acts, *rows, *grads)


def block_columns(place, bit, size):
    return pl.multiple_of((place[0] ^ bit) * size, size)


def gathered_kernel(place, rows, *refs):
    out = refs[-1]
    own, beside, across, upper, lower = refs[:-1]
    size, half = own.shape[0], upper.shape[0]
    total = None
    for bit, skip, ref in ((0, 0, own), (1, 0, beside), (2, 0, across), (3, 0, upper), (3, half, lower)):
        start = pl.multiple_of(block_columns(place, bit, size) + skip, half)
        value = mul_nn(rows[:, pl.ds(start, ref.shape[0])], ref[...])
        total = value if total is None else total + value
    out[...] = total


def gathered_times(rows, place, pieces):
    count, width = rows.shape
    columns = pieces[0].shape[1]
    tile = min(256, count)
    whole = [pl.BlockSpec(piece.shape, lambda i, place: (0, 0)) for piece in pieces]
    return pl.pallas_call(
        gathered_kernel,
        grid_spec=pltpu.PrefetchScalarGridSpec(
            num_scalar_prefetch=1,
            grid=(count // tile,),
            in_specs=[pl.BlockSpec((tile, width), lambda i, place: (i, 0))] + whole,
            out_specs=pl.BlockSpec((tile, columns), lambda i, place: (i, 0)),
        ),
        out_shape=jax.ShapeDtypeStruct((count, columns), jnp.float32),
        compiler_params=pltpu.CompilerParams(vmem_limit_bytes=VMEM_BYTES),
        cost_estimate=pl.CostEstimate(
            flops=2 * count * width * columns, bytes_accessed=2 * (count + columns) * width, transcendentals=0
        ),
    )(jnp.reshape(place, (1,)).astype(jnp.int32), rows, *pieces)


def gathered_transposed_kernel(count, place, *refs):
    factors, pieces, out = refs[:count], refs[count:-1], refs[-1]
    size, half = pieces[0].shape[0], pieces[3].shape[0]
    for i, (bit, skip) in enumerate(((0, 0), (1, 0), (2, 0), (3, 0), (3, half))):
        start = pl.multiple_of(block_columns(place, bit, size) + skip, half)
        total = None
        for p in range(count):
            value = mul_nt(factors[p][...], pieces[5 * p + i][...])
            total = value if total is None else total + value
        out[:, pl.ds(start, pieces[i].shape[0])] = low(total)


def gathered_times_transposed(factors, place, pieces):
    count, rows = len(factors), factors[0].shape[0]
    width = 4 * pieces[0][0].shape[0]
    tile = min(256, rows)
    flat = [piece for some in pieces for piece in some]
    whole = [pl.BlockSpec(piece.shape, lambda i, place: (0, 0)) for piece in flat]
    wides = [pl.BlockSpec((tile, factor.shape[1]), lambda i, place: (i, 0)) for factor in factors]
    columns = sum(factor.shape[1] for factor in factors)
    return pl.pallas_call(
        functools.partial(gathered_transposed_kernel, count),
        grid_spec=pltpu.PrefetchScalarGridSpec(
            num_scalar_prefetch=1,
            grid=(rows // tile,),
            in_specs=wides + whole,
            out_specs=pl.BlockSpec((tile, width), lambda i, place: (i, 0)),
        ),
        out_shape=jax.ShapeDtypeStruct((rows, width), jnp.bfloat16),
        compiler_params=pltpu.CompilerParams(vmem_limit_bytes=VMEM_BYTES),
        cost_estimate=pl.CostEstimate(
            flops=2 * rows * width * columns, bytes_accessed=2 * (rows + columns) * width, transcendentals=0
        ),
    )(jnp.reshape(place, (1,)).astype(jnp.int32), *factors, *flat)


def join_kernel(squares, source, target):
    lines, _, columns = source.shape
    part = columns // squares
    for i in range(lines):
        for j in range(squares):
            at = (j * lines + i) * part
            target[:, at : at + part] = source[i, :, j * part : (j + 1) * part]


def columns_join(parts, squares):
    lines, rows, columns = parts.shape
    tile = 176 if rows % 176 == 0 else rows
    return pl.pallas_call(
        functools.partial(join_kernel, squares),
        grid=(rows // tile,),
        in_specs=[pl.BlockSpec((lines, tile, columns), lambda i: (0, i, 0))],
        out_specs=pl.BlockSpec((tile, lines * columns), lambda i: (i, 0)),
        out_shape=jax.ShapeDtypeStruct((rows, lines * columns), parts.dtype),
        compiler_params=pltpu.CompilerParams(vmem_limit_bytes=VMEM_BYTES),
        cost_estimate=pl.CostEstimate(flops=0, bytes_accessed=4 * parts.size, transcendentals=0),
    )(parts)


def flip(value, axis, bit):
    devices = range(lax.axis_size(axis))
    return lax.ppermute(value, axis, [(i, i ^ bit) for i in devices])


def shift(value, axis, distance):
    count = lax.axis_size(axis)
    return lax.ppermute(value, axis, [(i, (i + distance) % count) for i in range(count)])


def from_behind(block, axis, distance):
    devices = range(lax.axis_size(axis))
    route = [(i - distance, i) for i in devices if i - distance in devices]
    return lax.ppermute(block, axis, route)


def tie(value, *earlier):
    return lax.optimization_barrier((value,) + earlier)[0]


def put(buffer, piece, *start):
    return lax.dynamic_update_slice(buffer, piece, start)


def wide(value):
    return value.astype(jnp.float32)


def gather_line(shard):
    count, place = lax.axis_size("fsdp"), lax.axis_index("fsdp")
    pieces = [shard] + [shift(shard, "fsdp", d) for d in range(1, count)]
    order = [(place - i) % count for i in range(count)]
    return jnp.concatenate([lax.select_n(which, *pieces) for which in order], axis=0)


class Square:
    def __init__(self, own):
        self.own = own
        self.half = own.shape[0] // 2
        self.beside = flip(own, "ctx", 1)
        self.across = flip(own, "ctx", 2)

    def forward(self, *earlier):
        upper = self.beside[: self.half]
        lower = self.across[self.half :]
        if earlier:
            upper, lower = lax.optimization_barrier((upper, lower) + earlier)[:2]
        self.upper = flip(upper, "ctx", 2)
        self.lower = flip(lower, "ctx", 1)
        return self

    def done(self):
        return (self.upper, self.lower)

    def pieces(self):
        return [self.own, self.beside, self.across, self.upper, self.lower]

    def far(self):
        return jnp.concatenate([self.upper, self.lower], axis=0)


def both_sides(rows):
    if lax.axis_size("tp") == 2:
        return rows, flip(rows, "tp", 1)
    every = lax.all_gather(rows, "tp", axis=0, tiled=True)
    half = every.shape[0] // 2
    return every[:half], every[half:]


def core_sum(mine, other):
    if lax.axis_size("tp") == 2:
        return wide(mine) + wide(flip(other, "tp", 1))
    both = jnp.concatenate([mine, other], axis=0)
    return wide(lax.psum_scatter(both, "tp", scatter_dimension=0, tiled=True))


def neighbour_columns(rows):
    width = rows.shape[1] // 4
    place = lax.axis_index("ctx")
    return [lax.dynamic_slice_in_dim(rows, (place ^ bit) * width, width, 1) for bit in range(4)]


class Line:
    def __init__(self, own):
        count, place = lax.axis_size("fsdp"), lax.axis_index("fsdp")
        own = own.reshape(count, own.shape[0] // count, own.shape[1])

        def part(distance):
            return lax.dynamic_index_in_dim(own, (place + distance) % count, 0, keepdims=False)

        self.kept = part(0)
        self.sent = [low(part(distance)) for distance in range(1, count)]
        self.arrived = [shift(piece, "fsdp", distance + 1) for distance, piece in enumerate(self.sent)]

    def total(self, *late):
        total = self.kept
        for part in lax.optimization_barrier(tuple(self.arrived) + late)[: len(self.arrived)]:
            total = total + wide(part)
        return total


class Scatter:
    def __init__(self, columns, grads):
        self.columns, self.grads = columns, grads
        self.half = columns[0].shape[1] // 2
        self.mine = outer_rows(columns[0], grads)
        beside, across = (
            jnp.concatenate([self.side(3, 1), self.side(1, 1)], axis=1),
            jnp.concatenate([self.side(3, 0), self.side(2, 0)], axis=1),
        )
        self.sent = [low(outer_rows(beside, grads)), low(outer_rows(across, grads))]
        self.first = (flip(self.sent[0], "ctx", 1), flip(self.sent[1], "ctx", 2))

    def side(self, bit, lower):
        return self.columns[bit][:, lower * self.half : (lower + 1) * self.half]

    def second(self, *earlier):
        first = self.first
        if earlier:
            first = lax.optimization_barrier(first + earlier)[:2]
        beside, across = (wide(part) for part in first)
        upper = low(outer_rows(self.side(1, 0), self.grads) + across[: self.half])
        lower = low(outer_rows(self.side(2, 1), self.grads) + beside[: self.half])
        self.last = (flip(upper, "ctx", 1), flip(lower, "ctx", 2))
        self.kept = (beside, across)
        return upper, lower

    def own(self, *ties):
        beside_upper, across_lower = self.last
        if ties:
            beside_upper, across_lower = lax.optimization_barrier(self.last + ties)[:2]
        beside, across = self.kept
        own = self.mine
        upper = own[: self.half] + wide(beside_upper) + across[self.half :]
        lower = own[self.half :] + beside[self.half :] + wide(across_lower)
        return jnp.concatenate([upper, lower], axis=0)


def butterfly(value, axes):
    for axis in axes:
        count, bit = lax.axis_size(axis), 1
        while bit < count:
            value = value + flip(value, axis, bit)
            bit *= 2
    return value


def rms_scale(values, floor_value):
    return lax.rsqrt(jnp.mean(values * values, axis=-1, keepdims=True) + floor_value)


def norm_backward(grad_normed, inputs, scale, gain):
    normed = inputs * scale
    weighted = grad_normed * gain
    return (
        scale * (weighted - normed * jnp.mean(weighted * normed, axis=-1, keepdims=True)),
        normed,
    )


def times(left, right):
    return jnp.dot(left, right, preferred_element_type=jnp.float32)


def times_transposed(left, right):
    return lax.dot_general(
        left, right, (((1,), (1,)), ((), ())), preferred_element_type=jnp.float32
    )


def outer_rows(left, right):
    return lax.dot_general(
        left, right, (((0,), (0,)), ((), ())), preferred_element_type=jnp.float32
    )


def rows_mine(rows):
    count = rows.shape[1] // lax.axis_size("tp")
    return lax.dynamic_slice_in_dim(rows, lax.axis_index("tp") * count, count, 1)


def rows_scatter(partial):
    if lax.axis_size("tp") != 2:
        return wide(lax.psum_scatter(partial, "tp", scatter_dimension=1, tiled=True))
    count = partial.shape[1] // 2
    other = lax.dynamic_slice_in_dim(partial, (1 - lax.axis_index("tp")) * count, count, 1)
    return wide(rows_mine(partial)) + wide(flip(other, "tp", 1))


def rows_full(mine):
    if lax.axis_size("tp") != 2:
        return lax.all_gather(mine, "tp", axis=1, tiled=True)
    other = flip(mine, "tp", 1)
    lower = lax.axis_index("tp") == 0
    return jnp.concatenate([jnp.where(lower, mine, other), jnp.where(lower, other, mine)], axis=1)


def by_head(parts):
    heads = range(parts[0].shape[-1] // LANES)
    return jnp.concatenate([part[..., h * LANES : (h + 1) * LANES] for h in heads for part in parts], axis=-1)


def by_kind(joined):
    return [
        jnp.concatenate(
            [
                some[..., at : at + LANES]
                for some in joined
                for at in range(kind * LANES, some.shape[-1], 3 * LANES)
            ],
            axis=-1,
        )
        for kind in range(3)
    ]


def pass_states(own, transfer, forward, *beside):
    rule = "shij,shjk->shik" if forward == 1 else "shji,shjk->shik"
    leaving = own
    entered = low(jnp.zeros_like(own))
    for repeat in range(lax.axis_size("ctx") - 1):
        entered = from_behind(low(leaving), "ctx", forward)
        if repeat == 1 and beside:
            entered = tie(entered, *beside)
        leaving = own + jnp.einsum(rule, transfer, entered, preferred_element_type=jnp.float32)
    return wide(entered)


def local(
    block_input,
    doc_start,
    gain_mix,
    query_weight,
    key_weight,
    value_weight,
    beta_weight,
    beta_bias,
    conv_weight,
    gain_o,
    out_weight,
    gain_ffn,
    gate_weight,
    up_weight,
    down_weight,
    out_grad,
):
    seq_count, local_len, width = block_input.shape
    row_count = seq_count * local_len
    heads_here = beta_weight.shape[1]
    taps = conv_weight.shape[1]
    parts = 2 if heads_here % 2 == 0 else 1
    part_heads = heads_here // parts
    group = 2 if part_heads % 2 == 0 else 1
    part_cols = 3 * part_heads * LANES
    spare = LANES - heads_here
    units_here = gate_weight.shape[1]
    shard_rows = gate_weight.shape[0]

    joined = by_head([low(query_weight), low(key_weight), low(value_weight)])
    shards = [joined[:, p * part_cols : (p + 1) * part_cols] for p in range(parts)]
    shards[0] = jnp.concatenate([shards[0], jnp.pad(low(beta_weight), ((0, 0), (0, spare)))], axis=1)
    shards.append(low(out_weight).T)
    lines = []
    for shard in shards[:parts]:
        lines.append(gather_line(tie(shard, lines[-1]) if lines else shard))
    units = units_here // 4
    pieces = jnp.stack([low(gate_weight).T, low(up_weight).T, low(down_weight)])
    pieces = pieces.reshape(3, 4, units, shard_rows).transpose(1, 0, 2, 3)
    ffn_swapped = lax.all_to_all(pieces.reshape(4, 3 * units, shard_rows), "ctx", 0, 0)
    ffn_line = ffn_swapped.transpose(1, 0, 2).reshape(3 * units, 4 * shard_rows)
    line_count = lax.axis_size("fsdp")

    ctx_place = lax.axis_index("ctx")
    first_pos = ctx_place * local_len
    starts = doc_start - first_pos
    col, row = starts[:, :, None], starts[:, None, :]
    conv = by_head([conv_weight[0], conv_weight[1], conv_weight[2]])
    bias = jnp.pad(beta_bias, (0, spare))[None]
    gain_head = gain_o[None]
    tokens = block_input.reshape(row_count, width)
    inputs = wide(tokens)
    normed_mix = low(inputs * rms_scale(inputs, EPSILON) * gain_mix)
    grads_mine = rows_mine(out_grad).reshape(-1, width)

    square = Square(tie(lines[0], ffn_swapped)).forward(normed_mix)
    gate_up_parts = tie(ffn_line[None, : 2 * units], lines[parts - 1], *square.done())
    gate_up_parts = lax.all_gather(gate_up_parts, "fsdp", axis=0, tiled=True)
    down_parts = lax.all_gather(ffn_line[None, 2 * units :], "fsdp", axis=0, tiled=True)
    mix_full, kept, pre = [], [], []
    for p in range(parts):
        mix_full.append(square.pieces())
        arrived = square.done()
        ends = normed_mix.reshape(seq_count, local_len, width)[:, local_len - HALO :].reshape(seq_count * HALO, width)
        ends = gathered_times(ends, ctx_place, mix_full[p])
        ends = low(ends)
        halo = from_behind(ends[:, :part_cols].reshape(seq_count, HALO, part_cols), "ctx", 1)
        pre.append(gathered_times(tie(normed_mix, ends), ctx_place, mix_full[p]))
        if p == parts - 1:
            lines.append(gather_line(tie(shards[-1], pre[p])))
        square = Square(tie(lines[p + 1], halo, pre[p], *arrived))
        halo = wide(halo)
        convs = conv[:, p * part_cols : (p + 1) * part_cols]
        kept.append(
            [halo, convs]
            + list(
                mixer_forward(
                    pre[p], pre[0], bias, halo, convs, col, row, taps, p * part_heads, part_heads, group
                )
            )
        )
        square.forward(kept[p][2])
        if p == 0:
            grad_square = Square(tie(grads_mine, kept[p][2], *square.done()))
    out_full = square.pieces()

    inputs_mine = wide(tie(rows_mine(block_input).reshape(-1, width), kept[0][2]))
    gate_up_full = columns_join(gate_up_parts, 4)
    finals = jnp.concatenate([some[4] for some in kept], axis=1)
    transfer = low(finals[..., LANES:])
    first = tie(finals[..., :LANES], gate_up_full, grad_square.beside, grad_square.across)
    entering = pass_states(first, transfer, 1)
    entered = [entering[:, p * part_heads : (p + 1) * part_heads] for p in range(parts)]
    grad_square.forward(entering)
    grad_rows = [both_sides(part) for part in (grad_square.own, grad_square.beside, grad_square.across)]
    mixed_rows = []
    for p in range(parts):
        own, carry = kept[p][2:4]
        mixed_rows.append(mixer_output(own, carry, entered[p], gain_head, group))
    mixed_rows = jnp.concatenate(mixed_rows, axis=1)
    mixed_rows = tie(mixed_rows, *(other for _, other in grad_rows))
    grad_rows.append(both_sides(grad_square.far()))

    branch = gathered_times_transposed([mixed_rows], ctx_place, [out_full]).reshape(seq_count, local_len, width)
    branch = tie(branch, down_parts)
    residual = inputs_mine + rows_scatter(branch).reshape(-1, width)
    scale_ffn = rms_scale(residual, EPSILON)
    square = Square(low(residual * scale_ffn * gain_ffn))
    ffn_full = (gate_up_full, columns_join(down_parts, 4))

    ffn_rows = [both_sides(square.own)]
    ffn_out = [ffn_both(ffn_rows[0], grad_rows[0], *ffn_full)]
    square.forward(ffn_out[0][0][0])
    ffn_rows.append(both_sides(tie(square.beside, ffn_out[0][0][0])))
    ffn_out.append(ffn_both(ffn_rows[1], grad_rows[1], *ffn_full))
    ffn_rows.append(both_sides(tie(square.across, ffn_out[0][0][0])))
    mine, other = ffn_rows[2]
    ffn_out.append(ffn_both((tie(mine, ffn_out[1][0][0], *square.done()), other), grad_rows[2], *ffn_full))
    beside_sums, across_sums = (low(core_sum(*(side[1] for side in ffn_out[bit]))) for bit in (1, 2))
    ffn_rows.append(both_sides(square.far()))
    mine, other = ffn_rows[3]
    ffn_out.append(ffn_both((tie(mine, beside_sums, across_sums), other), grad_rows[3], *ffn_full))
    near_sums = (flip(beside_sums, "ctx", 1), flip(across_sums, "ctx", 2))
    mine, other = (side[1] for side in ffn_out[3])
    far_sums = low(core_sum(mine, tie(other, *near_sums)))
    acts = [side[0] for outs in ffn_out for side in outs]
    own_sums = core_sum(*(side[1] for side in ffn_out[0]))
    result_low = []
    for bit in (1, 2):
        mine, other = (side[2] for side in ffn_out[bit])
        result_low.append(low(core_sum(tie(mine, far_sums), other)))
    acts[0] = tie(acts[0], far_sums, own_sums, *result_low)
    far_sums = flip(far_sums, "ctx", 3)
    sums = ffn_weights(
        acts,
        [side for sides in ffn_rows for side in sides],
        [side for sides in grad_rows for side in sides],
        line_count,
        4,
    )

    far_sums, sums = lax.optimization_barrier((far_sums, sums))
    result_near = [flip(tie(part, far_sums), "ctx", bit) for part, bit in zip(result_low, (1, 2))]
    grad_normed = own_sums + wide(near_sums[0]) + wide(near_sums[1]) + wide(far_sums)
    back_ffn, unit_ffn = norm_backward(grad_normed, residual, scale_ffn, gain_ffn)
    grad_residual = wide(grads_mine) + back_ffn
    gain_ffn_part = jnp.sum(grad_normed * unit_ffn, axis=0)
    grad_branch = rows_full(low(grad_residual).reshape(seq_count, -1, width)).reshape(row_count, width)
    grad_heads = gathered_times(grad_branch, ctx_place, out_full)
    backs, acrosses, gain_o_part = [], [], 0.0
    for p in range(parts):
        _, _, own, carry, _, _, _, _ = kept[p]
        back, across, gain_part = mixer_output_backward(
            own, carry, entered[p], gain_head, grad_heads, p * part_heads, group
        )
        backs.append(back)
        acrosses.append(across)
        gain_o_part = gain_o_part + jnp.sum(gain_part, axis=(0, 1, 2))
    grad_end = pass_states(jnp.concatenate(acrosses, axis=1), transfer, -1, *result_near)
    total = lax.psum_scatter(sums, "fsdp", scatter_dimension=0, tiled=True)

    out_grad_w = low(outer_rows(grad_branch, mixed_rows))
    out_part = out_grad_w
    out_grad_w = lax.psum_scatter(out_grad_w, ("ctx", "fsdp"), scatter_dimension=0, tiled=True)

    mine, other = (side[2] for side in ffn_out[0])
    result_own = core_sum(mine, tie(other, grad_branch))
    mine, other = (side[2] for side in ffn_out[3])
    result_far = flip(tie(low(core_sum(mine, tie(other, grad_branch))), grad_end), "ctx", 3)
    columns = neighbour_columns(normed_mix)
    grad_mixes, mix_grads, conv_parts = [None] * parts, [None] * parts, [None] * parts
    logits = 0.0
    scatter = None
    for p in reversed(range(parts)):
        halo, convs, own, carry, final, inverses, updates, states = kept[p]
        heads = slice(p * part_heads, (p + 1) * part_heads)
        back = tie(backs[p], out_part) if scatter is None else tie(backs[p], total, *scatter.sent)
        grad_mix, tail, before, conv_parts[p], logit = mixer_backward(
            pre[p], pre[0], bias, halo, convs, col, row, back, inverses, updates, states,
            entered[p], grad_end[:, heads], taps, p * part_heads, part_heads, group,
        )
        logits = logits + logit
        tail = low(tail + from_behind(before, "ctx", -1))
        grad_mix = put(grad_mix.reshape(seq_count, local_len, -1), tail, 0, local_len - HALO, 0)
        grad_mix = grad_mix.reshape(row_count, -1)
        if scatter is not None:
            earlier_ready = scatter.second(before)
            earlier_scatter = scatter
        else:
            grad_mix = tie(grad_mix, result_far)
        if p == 0:
            grad_mix = jnp.concatenate([grad_mix, low(logits)], axis=1)
        grad_mixes[p] = grad_mix
        scatter = Scatter(columns, grad_mix)
        if p > 0:
            result_far = tie(result_far, *scatter.sent)
    result = result_own + wide(result_near[0]) + wide(result_near[1])
    result = result + wide(result_far)
    block_output = rows_full(low(residual + result).reshape(seq_count, -1, width))
    ready = (block_output, scatter.mine)
    if parts > 1:
        ready = ready + tuple(earlier_ready) + (earlier_scatter.mine,)
    ready = scatter.second(*ready)
    grad_mixes[0] = tie(grad_mixes[0], *ready)
    mix_back = tie(gathered_times_transposed(grad_mixes, ctx_place, mix_full), *scatter.last)
    mix_back = rows_scatter(mix_back.reshape(seq_count, local_len, width)).reshape(-1, width)
    back_mix, unit_mix = norm_backward(mix_back, inputs_mine, rms_scale(inputs_mine, EPSILON), gain_mix)
    input_grad = rows_full(low(grad_residual + back_mix).reshape(seq_count, -1, width))
    gain_mix_part = jnp.sum(mix_back * unit_mix, axis=0)

    conv_cols = jnp.concatenate([jnp.sum(part, axis=0)[:taps] for part in conv_parts], axis=1)
    gains = butterfly(jnp.concatenate([gain_mix_part, gain_ffn_part, gain_o_part]), ("tp",))
    sums = jnp.concatenate([gains, conv_cols.reshape(-1), jnp.sum(logits, axis=0)])
    last_line = Line(scatter.own())
    for p in range(1, parts):
        own = low(earlier_scatter.own(*last_line.sent))
        mix_grads[p] = lax.psum_scatter(own, "fsdp", scatter_dimension=0, tiled=True)
    sums = butterfly(tie(sums, input_grad, *last_line.sent), ("ctx",))
    mix_grads[0] = last_line.total(sums)
    count = lax.axis_size("fsdp")
    bit = 1
    while bit < count // 2:
        sums = sums + flip(sums, "fsdp", bit)
        bit *= 2
    for p in range(1, parts):
        mix_grads[p] = wide(tie(mix_grads[p], sums))
    if count > 1:
        sums = sums + flip(sums, "fsdp", bit)
    query_grad, key_grad, value_grad = by_kind([grad[:, :part_cols] for grad in mix_grads])
    beta_grad = mix_grads[0][:, part_cols : part_cols + heads_here]
    ends = [width, 2 * width, 2 * width + LANES, sums.shape[0] - LANES]
    gain_mix_grad, gain_ffn_grad, gain_o_grad, conv_grad, bias_grad = jnp.split(sums, ends)
    conv_grad = jnp.stack(by_kind([conv_grad.reshape(taps, -1)]))
    bias_grad = bias_grad[:heads_here]
    out_grad_w = wide(tie(out_grad_w, *scatter.last)).T
    pieces = tie(total, *scatter.last).reshape(3 * units, 4, shard_rows).transpose(1, 0, 2)
    arrived = lax.all_to_all(pieces, "ctx", 0, 0).reshape(4, 3, units, shard_rows)
    gate_grad, up_grad, down_grad = (wide(arrived[:, i].reshape(units_here, shard_rows)) for i in range(3))

    return (
        block_output,
        input_grad,
        gain_mix_grad,
        query_grad,
        key_grad,
        value_grad,
        beta_grad,
        bias_grad,
        conv_grad,
        gain_o_grad,
        out_grad_w,
        gain_ffn_grad,
        gate_grad.T,
        up_grad.T,
        down_grad,
    )


def solution(mesh):
    placed = (
        P("fsdp", "ctx", None),
        P("fsdp", "ctx"),
        P(),
        P(("ctx", "fsdp"), "tp"),
        P(("ctx", "fsdp"), "tp"),
        P(("ctx", "fsdp"), "tp"),
        P(("ctx", "fsdp"), "tp"),
        P("tp"),
        P(None, None, "tp"),
        P(),
        P("tp", ("ctx", "fsdp")),
        P(),
        P(("ctx", "fsdp"), "tp"),
        P(("ctx", "fsdp"), "tp"),
        P("tp", ("ctx", "fsdp")),
        P("fsdp", "ctx", None),
    )
    return jax.shard_map(
        local,
        mesh=mesh,
        in_specs=placed,
        out_specs=(
            P("fsdp", "ctx", None),
            P("fsdp", "ctx", None),
            P(),
            P(("ctx", "fsdp"), "tp"),
            P(("ctx", "fsdp"), "tp"),
            P(("ctx", "fsdp"), "tp"),
            P(("ctx", "fsdp"), "tp"),
            P("tp"),
            P(None, None, "tp"),
            P(),
            P("tp", ("ctx", "fsdp")),
            P(),
            P(("ctx", "fsdp"), "tp"),
            P(("ctx", "fsdp"), "tp"),
            P("tp", ("ctx", "fsdp")),
        ),
        check_vma=False,
    )
```
